32 devices in a mesh: segment: 4 (over y, x), mp: 2 (over core), dp: 4 (over z).
Axes of the slice: x: 2, y: 2, z: 4, core: 2. Of those that a mesh axis runs over, the one named last changes fastest.
Arguments:
- text_rows: bfloat16 [4, 512, 1024], P(None, 'dp'), may hold values from -6 to 6
- durations: int32 [4, 4, 128], P(None, 'dp'), may hold values from 1 to 16, 512 in all within a row
- unit_targets: int32 [4, 2048], P(None, 'dp'), may hold values from 0 to 9999
- w_in: bfloat16 [4, 1024, 8192], P('segment', None, 'mp'), may hold values from -0.1875 to 0.1875
- w_out: bfloat16 [4, 8192, 1024], P('segment', 'mp'), may hold values from -0.0625 to 0.0625
- w_unit: bfloat16 [1024, 10240], P(None, ('segment', 'mp')), as said below
Outputs:
- loss: float32 [4], P('dp')
- grad_in: float32 [4, 1024, 8192], P('segment', 'dp', 'mp')
- grad_out: float32 [4, 8192, 1024], P('segment', 'mp', 'dp')
- grad_unit: float32 [1024, 10240], P('dp', ('segment', 'mp'))
The draws below stay inside these ranges and needn't reach their ends.
Inputs may be any that keep to these rules, and one draw needn't show every extreme that they name: Within each micro-batch and each index of dp the 128 durations sum to exactly 512, and one of them equals 16. `w_unit`: entries of order 3 / sqrt(1024) in most columns, some columns much larger.
All inputs are finite; a program needn't handle non-finite values.
Results may differ from the reference program's by a relative error of at most 0.035.
Values may be sent and summed in bfloat16 or wider, within the bound.
No kernel may reach another device: no remote copies, remote signals or barrier semaphores. Data moves between devices by JAX's collectives and lax.ppermute only.
A program may use at most 256 MiB of HBM per device.

```python
import math
import jax
import jax.numpy as jnp
import numpy as np
from jax import lax

D = 1024
FF = 8192
V = 10240
MICRO = 4
ROWS_DEV = 128
UNITS_DEV = 512
TEXT = 512
UNITS = 2048
N_SEGMENT = 4
N_DP = 4


def draw_w_unit(key, part):
    key_a = jax.random.fold_in(jax.random.fold_in(key, 7), 0)
    spread = 3.0 / math.sqrt(D)
    values = jax.random.truncated_normal(key_a, -6.0, 6.0, (D, V), jnp.float32) * spread
    return values.astype(jnp.bfloat16)


def touch_ends(array, own_key, smallest, top_value):
    place = [jax.random.randint(jax.random.fold_in(own_key, axis), (), 0, length) for axis, length in enumerate(array.shape)]
    main_axis = array.shape.index(max(array.shape))
    neighbour = place[:main_axis] + [(place[main_axis] + 1) % array.shape[main_axis]] + place[main_axis + 1:]
    return array.at[tuple(place)].set(smallest).at[tuple(neighbour)].set(top_value)


def shard_levels(stream_key, dims, cuts, low, top_value):
    factor_of, own = 1.0, jax.random.fold_in(stream_key, 6)
    for dim, blocks in cuts:
        draws = jnp.exp(jax.random.uniform(jax.random.fold_in(own, dim), (blocks,), jnp.float32, low / len(cuts), top_value / len(cuts)))
        factor_of = factor_of * jnp.repeat(draws, dims[dim] // blocks).reshape([-1 if axis == dim else 1 for axis in range(len(dims))])
    return factor_of


def cumulative_ranks(amount, skew):
    loads = [(1 << 20) // math.isqrt(standing ** skew) + 1 for standing in range(1, amount + 1)]
    scale = 1 + sum(loads) // (1 << 30)
    return np.cumsum(np.array([max(1, weight // scale) for weight in loads]))


def ranked(key, dims, count, lean):
    listing = cumulative_ranks(count, lean)
    ticket = jax.random.randint(jax.random.fold_in(key, 1), dims, 0, int(listing[count - 1]))
    rank = jnp.searchsorted(jnp.asarray(listing, jnp.int32), ticket, side="right")
    return jax.random.permutation(jax.random.fold_in(key, 2), count)[rank].astype(jnp.int32)


def split_up(amount, total, reach, skew):
    loads = [(1 << 20) // math.isqrt(rank ** skew) + 1 for rank in range(2, amount + 1)]
    rest, holding = total - reach - (amount - 1), [1] * (amount - 1)
    while rest > 0:
        movable = [i for i in range(amount - 1) if holding[i] < reach]
        mass, budget = sum([loads[i] for i in movable]), rest
        for i in movable:
            addition = min(reach - holding[i], max(1, budget * loads[i] // mass), rest)
            holding[i] = holding[i] + addition
            rest = rest - addition
    return np.array([reach] + holding)


def uneven_parts(own_key, number_of, total, bound, skew):
    if number_of == 2:
        one = jax.random.randint(own_key, (), max(1, total - bound), min(bound, total - 1) + 1)
        return jnp.stack([one, total - one])
    sizes = jnp.asarray(split_up(number_of, total, bound, skew), jnp.int32)
    pairs = (number_of - 1) // 2
    source_of, sink = sizes[1:1 + 2 * pairs:2], sizes[2:2 + 2 * pairs:2]
    margin = jnp.minimum(source_of - 1, bound - sink)
    shifted = jax.random.randint(jax.random.fold_in(own_key, 1), (pairs,), 0, 1 << 20) % (margin + 1)
    sizes = sizes.at[1:1 + 2 * pairs:2].set(source_of - shifted).at[2:2 + 2 * pairs:2].set(sink + shifted)
    return sizes[jax.random.permutation(jax.random.fold_in(own_key, 2), number_of)]


def centred(key, extent, width, reach, cuts=(), held_as=jnp.bfloat16):
    level = shard_levels(key, extent, cuts, -0.22, 0.18) if cuts else 1.0
    drawn = jax.random.normal(key, extent, jnp.float32) * width * level
    return jnp.minimum(jnp.maximum(drawn, -reach), reach).astype(held_as)


def setup_inputs(seed: int = 0) -> dict:
    streams_of = jax.random.split(jax.random.key(seed), 7)
    text_rows = centred(streams_of[0], (MICRO, TEXT, D), 1.0, 6.0, ((1, 4),))
    durations = jax.vmap(lambda own: uneven_parts(own, ROWS_DEV, UNITS_DEV, 16, 2))(jax.random.split(streams_of[1], MICRO * N_DP)).reshape((MICRO, N_DP, ROWS_DEV)).astype(jnp.int32)
    unit_targets = touch_ends(ranked(streams_of[2], (MICRO, UNITS), min(V, 10000), 2), jax.random.fold_in(streams_of[2], 3), 0, (min(V, 10000)) - 1).astype(jnp.int32)
    w_in = centred(streams_of[3], (N_SEGMENT, D, FF), D ** -0.5, 0.1875, ((0, 4), (2, 2)))
    w_out = centred(streams_of[4], (N_SEGMENT, FF, D), FF ** -0.5, 0.0625, ((0, 4), (1, 2)))
    w_unit = draw_w_unit(jax.random.fold_in(streams_of[6], 71), 0)
    return {"text_rows": text_rows, "durations": durations, "unit_targets": unit_targets, "w_in": w_in, "w_out": w_out, "w_unit": w_unit}


def gelu_parts(pre_vals):
    coeff = 0.7978845608
    inner = coeff * (pre_vals + 0.044715 * pre_vals * pre_vals * pre_vals)
    tanh_val = jnp.tanh(inner)
    value = 0.5 * pre_vals * (1.0 + tanh_val)
    slope = 0.5 * (1.0 + tanh_val) + 0.5 * pre_vals * (1.0 - tanh_val * tanh_val) * coeff * (1.0 + 3.0 * 0.044715 * pre_vals * pre_vals)
    return (value, slope)

def row_scale(rows_in):
    floats = rows_in.astype(jnp.float32)
    return lax.rsqrt(lax.optimization_barrier(jnp.mean(floats * floats, axis=-1, keepdims=True)) + 1e-06)

def norm_back(rows_in, grads):
    scale = row_scale(rows_in)
    normal = rows_in.astype(jnp.float32) * scale
    return scale * (grads - normal * lax.optimization_barrier(jnp.mean(grads * normal, axis=-1, keepdims=True)))

def section(rows_in, first, second):
    normed = (rows_in.astype(jnp.float32) * row_scale(rows_in)).astype(jnp.bfloat16)
    pre_vals = jnp.dot(normed, first, preferred_element_type=jnp.float32)
    value, slope = gelu_parts(pre_vals)
    hidden = value.astype(jnp.bfloat16)
    return (normed, hidden, slope)

def reference(text_rows, durations, unit_targets, w_in, w_out, w_unit):
    total_rows = MICRO * TEXT
    rows_now = text_rows.reshape(total_rows, D)
    stored = []
    for segment_id in range(N_SEGMENT):
        stored.append(rows_now)
        normed, hidden, slope = section(rows_now, w_in[segment_id], w_out[segment_id])
        rows_now = (rows_now.astype(jnp.float32) + jnp.dot(hidden, w_out[segment_id], preferred_element_type=jnp.float32)).astype(jnp.bfloat16)
    final_norm = (rows_now.astype(jnp.float32) * row_scale(rows_now)).astype(jnp.bfloat16)
    logits = jnp.dot(final_norm, w_unit, preferred_element_type=jnp.float32)
    ends = jnp.cumsum(durations, axis=-1)
    positions = jnp.arange(UNITS_DEV, dtype=jnp.int32)
    row_local = lax.optimization_barrier(jnp.sum((ends[:, :, None, :] <= positions[None, None, :, None]).astype(jnp.int32), axis=-1))
    block_ids = jnp.arange(MICRO * N_DP, dtype=jnp.int32).reshape(MICRO, N_DP, 1)
    row_global = (block_ids * ROWS_DEV + row_local).reshape(-1).astype(jnp.int32)
    target_flat = unit_targets.reshape(-1).astype(jnp.int32)
    counts = jnp.zeros((total_rows, V), jnp.float32).at[row_global, target_flat].add(1.0)
    duration_f = durations.reshape(total_rows).astype(jnp.float32)
    peak = lax.optimization_barrier(jnp.max(logits, axis=-1))
    lse = peak + jnp.log(lax.optimization_barrier(jnp.sum(jnp.exp(logits - peak[:, None]), axis=-1)))
    denom = float(MICRO * UNITS)
    loss_terms = duration_f * lse - lax.optimization_barrier(jnp.sum(counts * logits, axis=-1))
    loss = lax.optimization_barrier(jnp.sum(loss_terms.reshape(MICRO, N_DP, ROWS_DEV), axis=(0, 2))) / denom
    dlogits = ((duration_f[:, None] * jnp.exp(logits - lse[:, None]) - counts) / denom).astype(jnp.bfloat16)
    grad_unit = jnp.dot(final_norm.T, dlogits, preferred_element_type=jnp.float32)
    dnorm = jnp.dot(dlogits, w_unit.T, preferred_element_type=jnp.float32).astype(jnp.bfloat16)
    grads = norm_back(rows_now, dnorm.astype(jnp.float32)).astype(jnp.bfloat16)
    grads_in = []
    grads_out = []
    for segment_id in reversed(range(N_SEGMENT)):
        rows_in = stored[segment_id]
        normed, hidden, slope = section(rows_in, w_in[segment_id], w_out[segment_id])
        grads_out.append(jnp.dot(hidden.T, grads, preferred_element_type=jnp.float32))
        dhidden = jnp.dot(grads, w_out[segment_id].T, preferred_element_type=jnp.float32)
        dpre = (dhidden * slope).astype(jnp.bfloat16)
        grads_in.append(jnp.dot(normed.T, dpre, preferred_element_type=jnp.float32))
        dnormed = jnp.dot(dpre, w_in[segment_id].T, preferred_element_type=jnp.float32)
        grads = (grads.astype(jnp.float32) + norm_back(rows_in, dnormed)).astype(jnp.bfloat16)
    grad_in = jnp.stack(grads_in[::-1], axis=0)
    grad_out = jnp.stack(grads_out[::-1], axis=0)
    return (loss, grad_in, grad_out, grad_unit)
```

```python
import jax
import jax.numpy as jnp
from jax import lax
from jax.sharding import PartitionSpec as P

CHUNKS = 4


def shifted(block, axis, distance):
    devices = range(lax.axis_size(axis))
    route = [(i - distance, i) for i in devices if i - distance in devices]
    return lax.ppermute(block, axis, route)


def gelu_parts(pre_vals):
    coeff = 0.7978845608
    inner = coeff * (pre_vals + 0.044715 * pre_vals * pre_vals * pre_vals)
    tanh_val = jnp.tanh(inner)
    value = 0.5 * pre_vals * (1.0 + tanh_val)
    slope = 0.5 * (1.0 + tanh_val) + 0.5 * pre_vals * (1.0 - tanh_val * tanh_val) * coeff * (
        1.0 + 3.0 * 0.044715 * pre_vals * pre_vals
    )
    return (value, slope)


def row_scale(rows_in):
    floats = rows_in.astype(jnp.float32)
    return lax.rsqrt(jnp.mean(floats * floats, axis=-1, keepdims=True) + 1e-06)


def normalised(rows_in):
    return (rows_in.astype(jnp.float32) * row_scale(rows_in)).astype(jnp.bfloat16)


def norm_back(rows_in, grads):
    scale = row_scale(rows_in)
    normal = rows_in.astype(jnp.float32) * scale
    return scale * (grads - normal * jnp.mean(grads * normal, axis=-1, keepdims=True))


def dot(a, b):
    return jnp.dot(a, b, preferred_element_type=jnp.float32)


def dot_t(a, b):
    return lax.dot_general(a, b, (((1,), (1,)), ((), ())), preferred_element_type=jnp.float32)


def t_dot(a, b):
    return lax.dot_general(a, b, (((0,), (0,)), ((), ())), preferred_element_type=jnp.float32)


def mp_sum(partial_value):
    if lax.axis_size("mp") != 2:
        return lax.psum(partial_value, "mp")
    mine = partial_value.astype(jnp.bfloat16)
    other = lax.ppermute(mine, "mp", [(0, 1), (1, 0)])
    return mine.astype(jnp.float32) + other.astype(jnp.float32)


def mp_stats(stats):
    if lax.axis_size("mp") != 2:
        return lax.all_gather(stats, "mp")
    other = lax.ppermute(stats, "mp", [(0, 1), (1, 0)])
    return jnp.stack([stats, other])


def unit_counts(ends, targets, ids):
    positions = jnp.arange(targets.shape[1], dtype=jnp.int32)
    row_local = jnp.sum((ends[:, None, :] <= positions[None, :, None]).astype(jnp.int32), axis=-1)
    rows = jnp.arange(ends.shape[1], dtype=jnp.int32)
    row_onehot = (row_local[:, :, None] == rows[None, None, :]).astype(jnp.bfloat16)
    hits = (targets[:, :, None] == ids[None, None, :]).astype(jnp.bfloat16)
    counts = jnp.einsum("mur,muv->mrv", row_onehot, hits, preferred_element_type=jnp.float32)
    return counts.astype(jnp.bfloat16)


def pick(options, index):
    chosen = None
    for at, option in options:
        chosen = option if chosen is None else jnp.where(index == at, option, chosen)
    return chosen


def on_device(text_rows, durations, unit_targets, w_in, w_out, w_unit):
    micro, row_count, width = text_rows.shape
    segments = lax.axis_size("segment")
    mp_size = lax.axis_size("mp")
    dp_size = lax.axis_size("dp")
    seg = lax.axis_index("segment")
    mp_at = lax.axis_index("mp")
    dp_at = lax.axis_index("dp")
    is_last = seg == segments - 1
    first = w_in[0]
    second = w_out[0]
    chunks = CHUNKS
    rows = micro * row_count // chunks
    text = text_rows.reshape(chunks, rows, width)
    vocab_part = w_unit.shape[1]
    unit_count = unit_targets.shape[1]
    denom = float(micro * unit_count * dp_size)
    lengths = durations[:, 0, :]
    length_f = lengths.astype(jnp.float32).reshape(chunks, rows, 1)
    ends = jnp.cumsum(lengths, axis=-1)

    w_head = lax.all_gather(w_unit, "segment", axis=1, tiled=True)
    part_ids = jnp.arange(vocab_part, dtype=jnp.int32)
    shard_ids = (jnp.arange(segments, dtype=jnp.int32) * mp_size + mp_at) * vocab_part
    head_ids = (shard_ids[:, None] + part_ids[None, :]).reshape(-1)
    head_counts = unit_counts(ends, unit_targets, head_ids).reshape(chunks, rows, -1)

    def forward(rows_in):
        value, _ = gelu_parts(dot(normalised(rows_in), first))
        summed = mp_sum(dot(value.astype(jnp.bfloat16), second))
        return (rows_in.astype(jnp.float32) + summed).astype(jnp.bfloat16)

    def head(final_rows, at):
        counts = head_counts[at].astype(jnp.float32)
        logits = dot(normalised(final_rows), w_head)
        peak = jnp.max(logits, axis=-1)
        total = jnp.sum(jnp.exp(logits - peak[:, None]), axis=-1)
        target = jnp.sum(counts * logits, axis=-1)
        stats = mp_stats(jnp.stack([peak, total, target]))
        top = jnp.max(stats[:, 0], axis=0)
        lse = top + jnp.log(jnp.sum(stats[:, 1] * jnp.exp(stats[:, 0] - top[None]), axis=0))
        loss_rows = length_f[at][:, 0] * lse - jnp.sum(stats[:, 2], axis=0)
        dlogits = (length_f[at] * jnp.exp(logits - lse[:, None]) - counts) / denom
        dnorm = mp_sum(dot_t(dlogits.astype(jnp.bfloat16), w_head)).astype(jnp.bfloat16)
        grad = norm_back(final_rows, dnorm.astype(jnp.float32)).astype(jnp.bfloat16)
        return lse, jnp.sum(loss_rows), grad

    def backward(rows_in, grad_rows):
        _, slope = gelu_parts(dot(normalised(rows_in), first))
        dpre = (dot_t(grad_rows, second) * slope).astype(jnp.bfloat16)
        summed = mp_sum(dot_t(dpre, first))
        return (grad_rows.astype(jnp.float32) + norm_back(rows_in, summed)).astype(jnp.bfloat16)

    inputs, all_inputs, all_grads = [], [], []
    finals, lses, losses = [], [], []
    outgoing = going_back = None
    for clock in range(2 * segments + chunks - 1):
        f_out = b_out = None
        if clock < segments + chunks - 1:
            own = text[min(clock, chunks - 1)]
            rows_in = own
            if clock > 0:
                rows_in = jnp.where(seg == 0, own, shifted(outgoing, "segment", 1))
            inputs.append(rows_in)
            all_inputs.append(lax.all_gather(rows_in, "dp"))
            f_out = forward(rows_in)
        if clock >= segments:
            at = clock - segments
            grad_rows = None
            if clock > segments:
                grad_rows = shifted(going_back, "segment", -1)
            if at < chunks:
                finals.append(outgoing)
                lse, loss_part, grad_final = head(outgoing, at)
                lses.append(lse)
                losses.append(loss_part)
                grad_rows = (
                    grad_final if grad_rows is None else jnp.where(is_last, grad_final, grad_rows)
                )
            options = []
            for other in range(segments):
                stage = clock - 2 * segments + 1 + 2 * other
                if 0 <= stage < len(inputs):
                    options.append((other, inputs[stage]))
            all_grads.append(lax.all_gather(grad_rows, "dp"))
            if clock < 2 * segments + chunks - 2:
                b_out = backward(pick(options, seg), grad_rows)
        outgoing, going_back = f_out, b_out

    final_rows = jnp.stack(finals)
    lse_rows = jnp.stack(lses)
    loss_sum = sum(losses)
    final_rows, lse_rows, loss_sum = lax.psum(
        (
            jnp.where(is_last, final_rows, jnp.zeros_like(final_rows)),
            jnp.where(is_last, lse_rows, 0.0),
            jnp.where(is_last, loss_sum, 0.0),
        ),
        "segment",
    )
    loss = (loss_sum / denom)[None]
    final_norm = normalised(final_rows).reshape(micro * row_count, width)
    own_ids = (seg * mp_size + mp_at) * vocab_part + part_ids
    own_counts = unit_counts(ends, unit_targets, own_ids).reshape(micro * row_count, vocab_part)
    own_logits = dot(final_norm, w_unit)
    own_length = length_f.reshape(-1, 1)
    own_exp = jnp.exp(own_logits - lse_rows.reshape(-1, 1))
    own_dlogits = ((own_length * own_exp - own_counts.astype(jnp.float32)) / denom).astype(
        jnp.bfloat16
    )
    grad_unit = t_dot(final_norm, own_dlogits)
    sum_unit = lax.psum_scatter(grad_unit, "dp", scatter_dimension=0, tiled=True)

    x_all = lax.dynamic_slice_in_dim(jnp.stack(all_inputs), seg, chunks, 0)
    g_all = lax.dynamic_slice_in_dim(jnp.stack(all_grads), segments - 1 - seg, chunks, 0)
    x_all = x_all.reshape(-1, width)
    g_all = g_all.reshape(-1, width)
    n_all = normalised(x_all)
    value, slope = gelu_parts(dot(n_all, first))
    dpre = (dot_t(g_all, second) * slope).astype(jnp.bfloat16)
    share = width // dp_size
    n_share = lax.dynamic_slice_in_dim(n_all, dp_at * share, share, 1)
    g_share = lax.dynamic_slice_in_dim(g_all, dp_at * share, share, 1)
    sum_first = t_dot(n_share, dpre)
    sum_second = t_dot(value.astype(jnp.bfloat16), g_share)
    return (loss, sum_first[None], sum_second[None], sum_unit)


def solution(mesh):
    placed = (
        P(None, "dp", None),
        P(None, "dp", None),
        P(None, "dp"),
        P("segment", None, "mp"),
        P("segment", "mp", None),
        P(None, ("segment", "mp")),
    )
    return jax.shard_map(
        on_device,
        mesh=mesh,
        in_specs=placed,
        out_specs=(
            P("dp"),
            P("segment", "dp", "mp"),
            P("segment", "mp", "dp"),
            P("dp", ("segment", "mp")),
        ),
        check_vma=False,
    )
```

```python
import functools
import jax
import jax.numpy as jnp
from jax import lax
from jax.experimental import pallas as pl
from jax.experimental.pallas import tpu as pltpu
from jax.sharding import PartitionSpec as P

CHUNKS = 4
BF16 = jnp.bfloat16
F32 = jnp.float32
MIB = 1024 * 1024


def shifted(block, axis, distance):
    devices = range(lax.axis_size(axis))
    route = [(i - distance, i) for i in devices if i - distance in devices]
    return lax.ppermute(block, axis, route)


def swapped(block):
    return lax.ppermute(block, "mp", [(0, 1), (1, 0)])


def gelu_parts(pre_vals):
    coeff = 0.7978845608
    square = pre_vals * pre_vals
    inner = coeff * pre_vals * (1.0 + 0.044715 * square)
    half = 0.5 * (1.0 + jnp.tanh(inner))
    value = pre_vals * half
    slope = half + 2.0 * value * (1.0 - half) * coeff * (1.0 + 3.0 * 0.044715 * square)
    return (value, slope)


def row_scale(rows_in):
    floats = rows_in.astype(F32)
    return lax.rsqrt(jnp.mean(floats * floats, axis=-1, keepdims=True) + 1e-06)


def normalised(rows_in):
    return (rows_in.astype(F32) * row_scale(rows_in)).astype(BF16)


def norm_back(rows_in, grads):
    scale = row_scale(rows_in)
    normal = rows_in.astype(F32) * scale
    return scale * (grads - normal * jnp.mean(grads * normal, axis=-1, keepdims=True))


def dot(a, b):
    return jnp.dot(a, b, preferred_element_type=F32)


def dot_t(a, b):
    return lax.dot_general(a, b, (((1,), (1,)), ((), ())), preferred_element_type=F32)


def t_dot(a, b):
    return lax.dot_general(a, b, (((0,), (0,)), ((), ())), preferred_element_type=F32)


def tile_of(size, most):
    if size <= most:
        return size
    return max(t for t in range(128, most + 1, 128) if size % t == 0)


def params(limit):
    return pltpu.CompilerParams(vmem_limit_bytes=limit * MIB)


def added(refs):
    total = refs[0][...].astype(F32)
    for ref in refs[1:]:
        total = total + ref[...].astype(F32)
    return total


def chosen(index, candidates):
    value = candidates[0][1]
    for at, option in candidates[1:]:
        value = jnp.where(index == at, option, value)
    return value


def forward_kernel(where, own, arrived, w_in, w_out, rows_out, part, normed, total):
    step = pl.program_id(0)

    @pl.when(step == 0)
    def _():
        rows = jnp.where(where[0] == 0, own[...], arrived[...])
        rows_out[...] = rows
        normed[...] = normalised(rows)
        total[...] = jnp.zeros_like(total)

    value, _ = gelu_parts(dot(normed[...], w_in[...]))
    total[...] += dot(value.astype(BF16), w_out[...])

    @pl.when(step == pl.num_programs(0) - 1)
    def _():
        part[...] = total[...].astype(part.dtype)


def forward_section(where, own, arrived, w_in, w_out, part_type):
    rows, width = own.shape
    hidden = w_in.shape[1]
    tile = tile_of(hidden, 512)
    whole = pl.BlockSpec((rows, width), lambda j, s: (0, 0))
    return pl.pallas_call(
        forward_kernel,
        grid_spec=pltpu.PrefetchScalarGridSpec(
            num_scalar_prefetch=1,
            grid=(hidden // tile,),
            in_specs=[
                whole,
                whole,
                pl.BlockSpec((width, tile), lambda j, s: (0, j)),
                pl.BlockSpec((tile, width), lambda j, s: (j, 0)),
            ],
            out_specs=[whole, whole],
            scratch_shapes=[pltpu.VMEM((rows, width), BF16), pltpu.VMEM((rows, width), F32)],
        ),
        out_shape=[
            jax.ShapeDtypeStruct((rows, width), BF16),
            jax.ShapeDtypeStruct((rows, width), part_type),
        ],
        compiler_params=params(32),
        cost_estimate=pl.CostEstimate(
            flops=4 * rows * width * hidden,
            bytes_accessed=4 * width * hidden,
            transcendentals=rows * hidden,
        ),
        name="section_forward",
    )(where, own, arrived, w_in, w_out)


def finish_forward_kernel(*refs):
    refs[-1][...] = added(refs[:-1]).astype(BF16)


def finish_forward(rows, pieces):
    return pl.pallas_call(
        finish_forward_kernel,
        out_shape=jax.ShapeDtypeStruct(rows.shape, BF16),
        compiler_params=params(16),
        name="finish_forward",
    )(rows, *pieces)


def finish_backward_kernel(rows, grads, *refs):
    summed = added(refs[:-1])
    refs[-1][...] = (grads[...].astype(F32) + norm_back(rows[...], summed)).astype(BF16)


def finish_backward(rows, grads, pieces):
    return pl.pallas_call(
        finish_backward_kernel,
        out_shape=jax.ShapeDtypeStruct(rows.shape, BF16),
        compiler_params=params(16),
        name="finish_backward",
    )(rows, grads, *pieces)


def backward_kernel(owners, pieces, last, has_arrived, where, *refs):
    stashed, refs = refs[: len(owners)], refs[len(owners) :]
    final = None
    if pieces:
        final, parts, refs = refs[0], refs[1 : 1 + pieces], refs[1 + pieces :]
    if has_arrived:
        arrived, refs = refs[0], refs[1:]
    w_in, w_out, rows_out, grads_out, part, normed, total = refs
    step = pl.program_id(0)

    @pl.when(step == 0)
    def _():
        rows = chosen(where[0], [(at, ref[...]) for at, ref in zip(owners, stashed)])
        grads = None
        if pieces:
            dnorm = added(parts).astype(BF16).astype(F32)
            grads = norm_back(final[...], dnorm).astype(BF16)
        if has_arrived:
            grads = arrived[...] if grads is None else jnp.where(where[0] == last, grads, arrived[...])
        rows_out[...] = rows
        grads_out[...] = grads
        normed[...] = normalised(rows)
        total[...] = jnp.zeros_like(total)

    _, slope = gelu_parts(dot(normed[...], w_in[...]))
    dpre = (dot_t(grads_out[...], w_out[...]) * slope).astype(BF16)
    total[...] += dot_t(dpre, w_in[...])

    @pl.when(step == pl.num_programs(0) - 1)
    def _():
        part[...] = total[...].astype(part.dtype)


def backward_section(where, last, options, final, parts, arrived, w_in, w_out, part_type):
    width, hidden = w_in.shape
    rows = options[0][1].shape[0]
    tile = tile_of(hidden, 512)
    whole = pl.BlockSpec((rows, width), lambda j, s: (0, 0))
    operands = [option for _, option in options]
    if parts:
        operands += [final, *parts]
    if arrived is not None:
        operands.append(arrived)
    body = functools.partial(
        backward_kernel, tuple(at for at, _ in options), len(parts), last, arrived is not None
    )
    return pl.pallas_call(
        body,
        grid_spec=pltpu.PrefetchScalarGridSpec(
            num_scalar_prefetch=1,
            grid=(hidden // tile,),
            in_specs=[whole] * len(operands)
            + [
                pl.BlockSpec((width, tile), lambda j, s: (0, j)),
                pl.BlockSpec((tile, width), lambda j, s: (j, 0)),
            ],
            out_specs=[whole, whole, whole],
            scratch_shapes=[pltpu.VMEM((rows, width), BF16), pltpu.VMEM((rows, width), F32)],
        ),
        out_shape=[
            jax.ShapeDtypeStruct((rows, width), BF16),
            jax.ShapeDtypeStruct((rows, width), BF16),
            jax.ShapeDtypeStruct((rows, width), part_type),
        ],
        compiler_params=params(32),
        cost_estimate=pl.CostEstimate(
            flops=6 * rows * width * hidden,
            bytes_accessed=4 * width * hidden,
            transcendentals=rows * hidden,
        ),
        name="section_backward",
    )(where, *operands, w_in, w_out)


def lane_fill(columns, shape):
    lane = lax.broadcasted_iota(jnp.int32, shape, 1)
    filled = jnp.zeros(shape, F32)
    for at, column in enumerate(columns):
        filled = jnp.where(lane == at, column, filled)
    return filled


def logits_kernel(final, w_head, counts, logits, stats, normed, peak, total, target):
    step = pl.program_id(0)

    @pl.when(step == 0)
    def _():
        normed[...] = normalised(final[...])
        peak[...] = jnp.full_like(peak, -jnp.inf)
        total[...] = jnp.zeros_like(total)
        target[...] = jnp.zeros_like(target)

    values = dot(normed[...], w_head[...])
    logits[...] = values
    higher = jnp.maximum(peak[...], jnp.max(values, axis=-1, keepdims=True))
    total[...] = total[...] * jnp.exp(peak[...] - higher) + jnp.sum(
        jnp.exp(values - higher), axis=-1, keepdims=True
    )
    peak[...] = higher
    target[...] += jnp.sum(counts[...].astype(F32) * values, axis=-1, keepdims=True)

    @pl.when(step == pl.num_programs(0) - 1)
    def _():
        stats[...] = lane_fill([peak[...], total[...], target[...]], stats.shape)


def head_logits(final, w_head, counts, at):
    rows, width = final.shape
    vocab = w_head.shape[1]
    tile = tile_of(vocab, 1024)
    return pl.pallas_call(
        logits_kernel,
        grid=(vocab // tile,),
        in_specs=[
            pl.BlockSpec((rows, width), lambda j: (0, 0)),
            pl.BlockSpec((width, tile), lambda j: (0, j)),
            pl.BlockSpec((None, rows, tile), lambda j: (at, 0, j)),
        ],
        out_specs=[
            pl.BlockSpec((rows, tile), lambda j: (0, j)),
            pl.BlockSpec((rows, 128), lambda j: (0, 0)),
        ],
        out_shape=[
            jax.ShapeDtypeStruct((rows, vocab), F32),
            jax.ShapeDtypeStruct((rows, 128), F32),
        ],
        scratch_shapes=[pltpu.VMEM((rows, width), BF16)] + [pltpu.VMEM((rows, 1), F32)] * 3,
        compiler_params=params(32),
        cost_estimate=pl.CostEstimate(
            flops=2 * rows * width * vocab,
            bytes_accessed=2 * width * vocab + 6 * rows * vocab,
            transcendentals=rows * vocab,
        ),
        name="head_logits",
    )(final, w_head, counts)


def head_grads_kernel(shards, denom, *refs):
    stats, refs = refs[:shards], refs[shards:]
    lengths, logits, counts, w_head, part, results, lse, total = refs
    step = pl.program_id(0)

    @pl.when(step == 0)
    def _():
        tables = [ref[...] for ref in stats]
        top = tables[0][:, 0:1]
        for table in tables[1:]:
            top = jnp.maximum(top, table[:, 0:1])
        mass = sum(table[:, 1:2] * jnp.exp(table[:, 0:1] - top) for table in tables)
        target = sum(table[:, 2:3] for table in tables)
        lse[...] = top + jnp.log(mass)
        results[...] = lane_fill([lse[...], lengths[...] * lse[...] - target], results.shape)
        total[...] = jnp.zeros_like(total)

    exped = lengths[...] * jnp.exp(logits[...] - lse[...])
    dlogits = ((exped - counts[...].astype(F32)) / denom).astype(BF16)
    total[...] += dot_t(dlogits, w_head[...])

    @pl.when(step == pl.num_programs(0) - 1)
    def _():
        part[...] = total[...].astype(part.dtype)


def head_grads(stats, lengths, logits, counts, at, w_head, denom, part_type):
    rows, vocab = logits.shape
    width = w_head.shape[0]
    tile = tile_of(vocab, 1024)
    return pl.pallas_call(
        functools.partial(head_grads_kernel, len(stats), denom),
        grid=(vocab // tile,),
        in_specs=[pl.BlockSpec((rows, 128), lambda j: (0, 0))] * len(stats)
        + [
            pl.BlockSpec((None, rows, 1), lambda j: (at, 0, 0)),
            pl.BlockSpec((rows, tile), lambda j: (0, j)),
            pl.BlockSpec((None, rows, tile), lambda j: (at, 0, j)),
            pl.BlockSpec((width, tile), lambda j: (0, j)),
        ],
        out_specs=[
            pl.BlockSpec((rows, width), lambda j: (0, 0)),
            pl.BlockSpec((rows, 128), lambda j: (0, 0)),
        ],
        out_shape=[
            jax.ShapeDtypeStruct((rows, width), part_type),
            jax.ShapeDtypeStruct((rows, 128), F32),
        ],
        scratch_shapes=[pltpu.VMEM((rows, 1), F32), pltpu.VMEM((rows, width), F32)],
        compiler_params=params(32),
        cost_estimate=pl.CostEstimate(
            flops=2 * rows * width * vocab,
            bytes_accessed=2 * width * vocab + 6 * rows * vocab,
            transcendentals=rows * vocab,
        ),
        name="head_grads",
    )(*stats, lengths, logits, counts, w_head)


def weight_kernel(blocks, adding, share, where, *refs):
    x_refs, refs = refs[:blocks], refs[blocks:]
    g_refs, refs = refs[:blocks], refs[blocks:]
    w_in, w_out, refs = refs[0], refs[1], refs[2:]
    if adding:
        old_first, old_second, refs = refs[0], refs[1], refs[2:]
    first, second, normed, grads, normed_t, grads_t = refs
    count = x_refs[0].shape[0]

    @pl.when(pl.program_id(0) == 0)
    def _():
        columns = pl.ds(pl.multiple_of(where[0] * share, share), share)
        for at in range(blocks):
            place = pl.ds(at * count, count)
            normed[place, :] = normalised(x_refs[at][...])
            grads[place, :] = g_refs[at][...]
        normed_t[...] = normed[:, columns].astype(F32).T.astype(BF16)
        grads_t[...] = grads[:, columns].astype(F32).T.astype(BF16)

    total_first = old_first[...] if adding else None
    total_second = None
    rows = normed.shape[0]
    part = min(256, rows)
    for at in range(rows // part):
        place = pl.ds(at * part, part)
        value, slope = gelu_parts(dot(normed[place, :], w_in[...]))
        dpre = (dot_t(grads[place, :], w_out[...]) * slope).astype(BF16)
        now_first = dot(normed_t[:, place], dpre)
        now_second = dot(grads_t[:, place], value.astype(BF16))
        total_first = now_first if total_first is None else total_first + now_first
        total_second = now_second if total_second is None else total_second + now_second
    first[...] = total_first
    total_second = total_second.T
    second[...] = old_second[...] + total_second if adding else total_second


def weight_grads(where, x_parts, g_parts, w_in, w_out, old, share):
    width, hidden = w_in.shape
    tile = tile_of(hidden, 512)
    blocks = len(g_parts)
    count = g_parts[0].shape[0]
    rows = blocks * count
    in_specs = [
        pl.BlockSpec((None, None, count, width), index) for _, index in x_parts
    ]
    in_specs += [pl.BlockSpec((count, width), lambda j, s: (0, 0))] * blocks
    in_specs += [
        pl.BlockSpec((width, tile), lambda j, s: (0, j)),
        pl.BlockSpec((tile, width), lambda j, s: (j, 0)),
    ]
    grad_specs = [
        pl.BlockSpec((share, tile), lambda j, s: (0, j)),
        pl.BlockSpec((tile, share), lambda j, s: (j, 0)),
    ]
    adding = old is not None
    aliases = {}
    if adding:
        in_specs += grad_specs
        aliases = {1 + 2 * blocks + 2: 0, 1 + 2 * blocks + 3: 1}
    return pl.pallas_call(
        functools.partial(weight_kernel, blocks, adding, share),
        grid_spec=pltpu.PrefetchScalarGridSpec(
            num_scalar_prefetch=1,
            grid=(hidden // tile,),
            in_specs=in_specs,
            out_specs=grad_specs,
            scratch_shapes=[
                pltpu.VMEM((rows, width), BF16),
                pltpu.VMEM((rows, width), BF16),
                pltpu.VMEM((share, rows), BF16),
                pltpu.VMEM((share, rows), BF16),
            ],
        ),
        out_shape=[
            jax.ShapeDtypeStruct((share, hidden), F32),
            jax.ShapeDtypeStruct((hidden, share), F32),
        ],
        input_output_aliases=aliases,
        compiler_params=params(48),
        cost_estimate=pl.CostEstimate(
            flops=4 * rows * (width + share) * hidden,
            bytes_accessed=4 * width * hidden + 16 * share * hidden,
            transcendentals=rows * hidden,
        ),
        name="weight_grads",
    )(where, *[x for x, _ in x_parts], *g_parts, w_in, w_out, *(old or ()))


def unit_counts(ends, targets, ids):
    positions = jnp.arange(targets.shape[1], dtype=jnp.int32)
    row_local = jnp.sum((ends[:, None, :] <= positions[None, :, None]).astype(jnp.int32), axis=-1)
    rows = jnp.arange(ends.shape[1], dtype=jnp.int32)
    row_onehot = (row_local[:, :, None] == rows[None, None, :]).astype(BF16)
    hits = (targets[:, :, None] == ids[None, None, :]).astype(BF16)
    counts = jnp.einsum("mur,muv->mrv", row_onehot, hits, preferred_element_type=F32)
    return counts.astype(BF16)


def on_device(text_rows, durations, unit_targets, w_in, w_out, w_unit):
    micro, row_count, width = text_rows.shape
    segments = lax.axis_size("segment")
    mp_size = lax.axis_size("mp")
    dp_size = lax.axis_size("dp")
    seg = lax.axis_index("segment")
    mp_at = lax.axis_index("mp")
    dp_at = lax.axis_index("dp")
    last = segments - 1
    is_last = seg == last
    seg_ref = seg.astype(jnp.int32)[None]
    dp_ref = dp_at.astype(jnp.int32)[None]
    pair = mp_size == 2
    part_type = BF16 if pair else F32
    first = w_in[0]
    second = w_out[0]
    chunks = CHUNKS
    rows = micro * row_count // chunks
    text = [t for t in text_rows.reshape(chunks, rows, width)]
    vocab_part = w_unit.shape[1]
    unit_count = unit_targets.shape[1]
    denom = float(micro * unit_count * dp_size)
    lengths = durations[:, 0, :]
    length_f = lengths.astype(F32).reshape(chunks, rows, 1)
    ends = jnp.cumsum(lengths, axis=-1)

    w_head = lax.all_gather(w_unit, "segment", axis=1, tiled=True)
    part_ids = jnp.arange(vocab_part, dtype=jnp.int32)
    shard_ids = (jnp.arange(segments, dtype=jnp.int32) * mp_size + mp_at) * vocab_part
    head_ids = (shard_ids[:, None] + part_ids[None, :]).reshape(-1)
    head_counts = unit_counts(ends, unit_targets, head_ids).reshape(chunks, rows, -1)
    own_ids = (seg * mp_size + mp_at) * vocab_part + part_ids
    own_counts = unit_counts(ends, unit_targets, own_ids).reshape(micro * row_count, vocab_part)

    def mp_pieces(part):
        if pair:
            return [part, swapped(part)]
        return [lax.psum(part, "mp")]

    def mp_tables(stats):
        if pair:
            return [stats, swapped(stats)]
        return [t for t in lax.all_gather(stats, "mp")]

    def my_half(block):
        if not pair:
            return block
        half = rows // 2
        return lax.dynamic_slice_in_dim(block, mp_at * half, half, 0)

    def other_half(block):
        half = rows // 2
        return lax.dynamic_slice_in_dim(block, (1 - mp_at) * half, half, 0)

    def gather_grads(block):
        if not pair:
            return [t for t in lax.all_gather(block, "dp")]
        mine = my_half(block)
        own = [mine]
        theirs = [other_half(block)]
        for distance in range(1, dp_size):
            route = [(i, (i + distance) % dp_size) for i in range(dp_size)]
            came = lax.ppermute(mine, "dp", route)
            own.append(came)
            theirs.append(swapped(came))
        return own + theirs

    stash, grads, finals, results, sent = [], [], [], [], []
    sums = None
    x_mine = x_theirs = None
    outgoing = going_back = None

    def x_parts(at):
        if not pair:
            return [
                (x_mine, lambda j, s, k=k: (k, at, 0, 0)) for k in range(dp_size)
            ]
        return [
            (source, lambda j, s, k=k: (lax.rem(s[0] + dp_size - k, dp_size), at, 0, 0))
            for source in (x_mine, x_theirs)
            for k in range(dp_size)
        ]

    for clock in range(2 * segments + chunks - 1):
        f_out = b_out = None
        if clock < segments + chunks - 1:
            own = text[min(clock, chunks - 1)]
            arrived = own if clock == 0 else shifted(outgoing, "segment", 1)
            rows_in, part = forward_section(seg_ref, own, arrived, first, second, part_type)
            stash.append(rows_in)
            f_out = finish_forward(rows_in, mp_pieces(part))
        if clock >= segments:
            at = clock - segments
            arrived = None if at == 0 else shifted(going_back, "segment", -1)
            parts = []
            if at < chunks:
                finals.append(outgoing)
                sent.append(
                    [lax.ppermute(outgoing, "segment", [(last, to)]) for to in range(last)]
                )
                logits, stats = head_logits(outgoing, w_head, head_counts, at)
                part, result = head_grads(
                    mp_tables(stats), length_f, logits, head_counts, at, w_head, denom, part_type
                )
                results.append(result[:, 0:2])
                parts = mp_pieces(part)
            options = []
            for other in range(segments):
                stage = clock - 2 * segments + 1 + 2 * other
                if 0 <= stage < len(stash):
                    options.append((other, stash[stage]))
            rows_in, grad_rows, part = backward_section(
                seg_ref, last, options, outgoing, parts, arrived, first, second, part_type
            )
            grads.append(grad_rows)
            if clock < 2 * segments + chunks - 2:
                b_out = finish_backward(rows_in, grad_rows, mp_pieces(part))
        if clock == segments + chunks - 2:
            x_half = jnp.stack(
                [
                    chosen(seg, [(s, my_half(stash[b + s])) for s in range(segments)])
                    for b in range(chunks)
                ]
            )
            x_mine = lax.all_gather(x_half, "dp")
            x_theirs = swapped(x_mine) if pair else None
        if clock >= 2 * segments - 1:
            at = clock - 2 * segments + 1
            block = chosen(seg, [(s, grads[at + last - s]) for s in range(segments)])
            sums = weight_grads(
                dp_ref, x_parts(at), gather_grads(block), first, second, sums, width // dp_size
            )
        outgoing, going_back = f_out, b_out

    results = lax.all_gather(jnp.stack(results), "segment")[last]
    loss = (jnp.sum(results[:, :, 1]) / denom)[None]
    final_rows = jnp.concatenate(
        [
            chosen(seg, [(last, finals[b])] + [(to, sent[b][to]) for to in range(last)])
            for b in range(chunks)
        ]
    )
    final_norm = normalised(final_rows)
    own_logits = dot(final_norm, w_unit)
    own_exp = jnp.exp(own_logits - results[:, :, 0].reshape(-1, 1))
    own_dlogits = (
        (length_f.reshape(-1, 1) * own_exp - own_counts.astype(F32)) / denom
    ).astype(BF16)
    grad_unit = t_dot(final_norm, own_dlogits).astype(BF16)
    sum_unit = lax.psum_scatter(grad_unit, "dp", scatter_dimension=0, tiled=True).astype(F32)
    return (loss, sums[0][None], sums[1][None], sum_unit)


def solution(mesh):
    placed = (
        P(None, "dp", None),
        P(None, "dp", None),
        P(None, "dp"),
        P("segment", None, "mp"),
        P("segment", "mp", None),
        P(None, ("segment", "mp")),
    )
    return jax.shard_map(
        on_device,
        mesh=mesh,
        in_specs=placed,
        out_specs=(
            P("dp"),
            P("segment", "dp", "mp"),
            P("segment", "mp", "dp"),
            P("dp", ("segment", "mp")),
        ),
        check_vma=False,
    )
```

```python
import functools
import jax
import jax.numpy as jnp
from jax import lax
from jax.experimental import pallas as pl
from jax.experimental.pallas import tpu as pltpu
from jax.sharding import PartitionSpec as P

CHUNKS = 2
VMEM_MIB = 60
BF16 = jnp.bfloat16
F32 = jnp.float32
MIB = 1024 * 1024


def shifted(block, axis, distance):
    devices = range(lax.axis_size(axis))
    route = [(i - distance, i) for i in devices if i - distance in devices]
    return lax.ppermute(block, axis, route)


def swapped(block):
    return lax.ppermute(block, "mp", [(0, 1), (1, 0)])


def gelu_parts(pre_vals):
    coeff = 0.7978845608
    square = pre_vals * pre_vals
    inner = coeff * pre_vals * (1.0 + 0.044715 * square)
    half = 0.5 * (1.0 + jnp.tanh(inner))
    value = pre_vals * half
    slope = half + 2.0 * value * (1.0 - half) * coeff * (1.0 + 3.0 * 0.044715 * square)
    return (value, slope)


def row_scale(rows_in):
    floats = rows_in.astype(F32)
    return lax.rsqrt(jnp.mean(floats * floats, axis=-1, keepdims=True) + 1e-06)


def normalised(rows_in):
    return (rows_in.astype(F32) * row_scale(rows_in)).astype(BF16)


def norm_back(rows_in, grads):
    scale = row_scale(rows_in)
    normal = rows_in.astype(F32) * scale
    return scale * (grads - normal * jnp.mean(grads * normal, axis=-1, keepdims=True))


def dot(a, b):
    return jnp.dot(a, b, preferred_element_type=F32)


def dot_t(a, b):
    return lax.dot_general(a, b, (((1,), (1,)), ((), ())), preferred_element_type=F32)


def t_dot(a, b):
    return lax.dot_general(a, b, (((0,), (0,)), ((), ())), preferred_element_type=F32)


def tile_of(size, most):
    if size <= most:
        return size
    return max(t for t in range(128, most + 1, 128) if size % t == 0)


def params(limit):
    return pltpu.CompilerParams(vmem_limit_bytes=limit * MIB)


def added(refs):
    total = refs[0][...].astype(F32)
    for ref in refs[1:]:
        total = total + ref[...].astype(F32)
    return total


def chosen(index, candidates):
    value = candidates[0][1]
    for at, option in candidates[1:]:
        value = jnp.where(index == at, option, value)
    return value


def gathered(halves, place):
    if len(halves) == 1:
        return halves[0][...]
    mine, theirs = (half[...] for half in halves)
    first = jnp.where(place == 0, mine, theirs)
    second = jnp.where(place == 0, theirs, mine)
    return jnp.concatenate([first, second], axis=0)


def part_of(block, place, parts):
    rows = block.shape[0] // parts
    if parts == 1:
        return block[...]
    return block[pl.ds(pl.multiple_of(place * rows, rows), rows), :]


def whole_spec(shape):
    return pl.BlockSpec(shape, lambda *_: (0,) * len(shape))


def emit_parts(total, place, keep, send):
    if send is None:
        keep[...] = total[...]
        return
    keep[...] = part_of(total, place, 2)
    send[...] = part_of(total, 1 - place, 2).astype(send.dtype)


def forward_kernel(halves, where, own, *refs):
    arrived, refs = refs[:halves], refs[halves:]
    w_in, w_out, rows_out, mine_out, keep, *send, whole, normed, total = refs
    step = pl.program_id(0)

    @pl.when(step == 0)
    def _():
        rows = jnp.where(where[0] == 0, own[...], gathered(arrived, where[1]))
        rows_out[...] = rows
        whole[...] = rows
        mine_out[...] = part_of(whole, where[1], halves)
        normed[...] = normalised(rows)
        total[...] = jnp.zeros_like(total)

    value, _ = gelu_parts(dot(normed[...], w_in[...]))
    total[...] += dot(value.astype(BF16), w_out[...])

    @pl.when(step == pl.num_programs(0) - 1)
    def _():
        emit_parts(total, where[1], keep, send[0] if send else None)


def forward_section(where, own, arrived, w_in, w_out):
    rows, width = own.shape
    hidden = w_in.shape[1]
    tile = tile_of(hidden, 512)
    halves = len(arrived)
    full, part = (rows, width), (rows // halves, width)
    shapes = [(full, BF16), (part, BF16), (part, F32)] + [(part, BF16)] * (halves - 1)
    return pl.pallas_call(
        functools.partial(forward_kernel, halves),
        grid_spec=pltpu.PrefetchScalarGridSpec(
            num_scalar_prefetch=1,
            grid=(hidden // tile,),
            in_specs=[
                whole_spec(full),
                *[whole_spec(part)] * halves,
                pl.BlockSpec((width, tile), lambda j, s: (0, j)),
                pl.BlockSpec((tile, width), lambda j, s: (j, 0)),
            ],
            out_specs=[whole_spec(shape) for shape, _ in shapes],
            scratch_shapes=[pltpu.VMEM(full, BF16), pltpu.VMEM(full, BF16), pltpu.VMEM(full, F32)],
        ),
        out_shape=[jax.ShapeDtypeStruct(*shape) for shape in shapes],
        compiler_params=params(VMEM_MIB),
        cost_estimate=pl.CostEstimate(
            flops=4 * rows * width * hidden,
            bytes_accessed=4 * width * hidden,
            transcendentals=rows * hidden,
        ),
        name="section_forward",
    )(where, own, *arrived, w_in, w_out)


def finish_forward_kernel(*refs):
    refs[-1][...] = added(refs[:-1]).astype(BF16)


def finish_forward(rows, pieces):
    return pl.pallas_call(
        finish_forward_kernel,
        out_shape=jax.ShapeDtypeStruct(rows.shape, BF16),
        compiler_params=params(VMEM_MIB),
        name="finish_forward",
    )(rows, *pieces)


def finish_backward_kernel(rows, grads, *refs):
    summed = added(refs[:-1])
    refs[-1][...] = (grads[...].astype(F32) + norm_back(rows[...], summed)).astype(BF16)


def finish_backward(rows, grads, pieces):
    return pl.pallas_call(
        finish_backward_kernel,
        out_shape=jax.ShapeDtypeStruct(rows.shape, BF16),
        compiler_params=params(VMEM_MIB),
        name="finish_backward",
    )(rows, grads, *pieces)


def backward_kernel(owners, halves, pieces, last, has_arrived, where, *refs):
    stashed, refs = refs[: len(owners)], refs[len(owners) :]
    if pieces:
        final, refs = refs[:halves], refs[halves:]
        parts, refs = refs[:pieces], refs[pieces:]
    if has_arrived:
        arrived, refs = refs[:halves], refs[halves:]
    w_in, w_out, mine_rows, mine_grads, keep, *send, rows, grads, normed, total = refs
    step = pl.program_id(0)

    @pl.when(step == 0)
    def _():
        rows[...] = chosen(where[0], [(at, ref[...]) for at, ref in zip(owners, stashed)])
        here = None
        if pieces:
            dnorm = added(parts).astype(BF16).astype(F32)
            here = norm_back(gathered(final, where[1]), dnorm).astype(BF16)
        if has_arrived:
            came = gathered(arrived, where[1])
            here = came if here is None else jnp.where(where[0] == last, here, came)
        grads[...] = here
        mine_rows[...] = part_of(rows, where[1], halves)
        mine_grads[...] = part_of(grads, where[1], halves)
        normed[...] = normalised(rows[...])
        total[...] = jnp.zeros_like(total)

    _, slope = gelu_parts(dot(normed[...], w_in[...]))
    dpre = (dot_t(grads[...], w_out[...]) * slope).astype(BF16)
    total[...] += dot_t(dpre, w_in[...])

    @pl.when(step == pl.num_programs(0) - 1)
    def _():
        emit_parts(total, where[1], keep, send[0] if send else None)


def backward_section(where, last, halves, options, final, parts, arrived, w_in, w_out):
    width, hidden = w_in.shape
    rows = options[0][1].shape[0]
    tile = tile_of(hidden, 512)
    full, part = (rows, width), (rows // halves, width)
    operands = [option for _, option in options]
    specs = [whole_spec(full)] * len(options)
    if parts:
        operands += [*final, *parts]
        specs += [whole_spec(part)] * halves + [whole_spec(full)] * len(parts)
    if arrived is not None:
        operands += arrived
        specs += [whole_spec(part)] * halves
    body = functools.partial(
        backward_kernel,
        tuple(at for at, _ in options),
        halves,
        len(parts),
        last,
        arrived is not None,
    )
    shapes = [(part, BF16), (part, BF16), (part, F32)] + [(part, BF16)] * (halves - 1)
    return pl.pallas_call(
        body,
        grid_spec=pltpu.PrefetchScalarGridSpec(
            num_scalar_prefetch=1,
            grid=(hidden // tile,),
            in_specs=specs
            + [
                pl.BlockSpec((width, tile), lambda j, s: (0, j)),
                pl.BlockSpec((tile, width), lambda j, s: (j, 0)),
            ],
            out_specs=[whole_spec(shape) for shape, _ in shapes],
            scratch_shapes=[pltpu.VMEM(full, BF16)] * 3 + [pltpu.VMEM(full, F32)],
        ),
        out_shape=[jax.ShapeDtypeStruct(*shape) for shape in shapes],
        compiler_params=params(VMEM_MIB),
        cost_estimate=pl.CostEstimate(
            flops=6 * rows * width * hidden,
            bytes_accessed=4 * width * hidden,
            transcendentals=rows * hidden,
        ),
        name="section_backward",
    )(where, *operands, w_in, w_out)


def lane_fill(columns, shape):
    lane = lax.broadcasted_iota(jnp.int32, shape, 1)
    filled = jnp.zeros(shape, F32)
    for at, column in enumerate(columns):
        filled = jnp.where(lane == at, column, filled)
    return filled


def shard_specs(count, width, tile, tiles):
    def index(shard, i, t):
        before, after = i < shard, i > shard
        return (0, jnp.where(before, 0, jnp.where(after, tiles - 1, t)))

    return [
        pl.BlockSpec((width, tile), lambda i, t, s, k=k: index(k, i, t)) for k in range(count)
    ]


def logits_kernel(halves, where, *refs):
    final, refs = refs[:halves], refs[halves:]
    *shards, counts, logits, stats, normed, peak, total, target = refs
    shard, step = pl.program_id(0), pl.program_id(1)
    is_first = (shard == 0) & (step == 0)
    is_end = (shard == pl.num_programs(0) - 1) & (step == pl.num_programs(1) - 1)

    @pl.when(is_first)
    def _():
        normed[...] = normalised(gathered(final, where[1]))
        peak[...] = jnp.full_like(peak, -jnp.inf)
        total[...] = jnp.zeros_like(total)
        target[...] = jnp.zeros_like(target)

    for at, w_part in enumerate(shards):

        @pl.when(shard == at)
        def _(w_part=w_part):
            values = dot(normed[...], w_part[...])
            logits[...] = values
            higher = jnp.maximum(peak[...], jnp.max(values, axis=-1, keepdims=True))
            total[...] = total[...] * jnp.exp(peak[...] - higher) + jnp.sum(
                jnp.exp(values - higher), axis=-1, keepdims=True
            )
            peak[...] = higher
            target[...] += jnp.sum(counts[...].astype(F32) * values, axis=-1, keepdims=True)

    @pl.when(is_end)
    def _():
        stats[...] = lane_fill([peak[...], total[...], target[...]], stats.shape)


def head_logits(where, final, shards, counts, at):
    halves = len(final)
    half, width = final[0].shape
    rows = half * halves
    vocab = shards[0].shape[1]
    tile = tile_of(vocab, 640)
    tiles = vocab // tile
    return pl.pallas_call(
        functools.partial(logits_kernel, halves),
        grid_spec=pltpu.PrefetchScalarGridSpec(
            num_scalar_prefetch=1,
            grid=(len(shards), tiles),
            in_specs=[
                *[whole_spec((half, width))] * halves,
                *shard_specs(len(shards), width, tile, tiles),
                pl.BlockSpec((None, None, rows, tile), lambda i, t, s: (i, at, 0, t)),
            ],
            out_specs=[
                pl.BlockSpec((None, rows, tile), lambda i, t, s: (i, 0, t)),
                whole_spec((rows, 128)),
            ],
            scratch_shapes=[pltpu.VMEM((rows, width), BF16)] + [pltpu.VMEM((rows, 1), F32)] * 3,
        ),
        out_shape=[
            jax.ShapeDtypeStruct((len(shards), rows, vocab), F32),
            jax.ShapeDtypeStruct((rows, 128), F32),
        ],
        compiler_params=params(VMEM_MIB),
        cost_estimate=pl.CostEstimate(
            flops=2 * rows * width * vocab * len(shards),
            bytes_accessed=(2 * width + 6 * rows) * vocab * len(shards),
            transcendentals=rows * vocab * len(shards),
        ),
        name="head_logits",
    )(where, *final, *shards, counts)


def head_grads_kernel(tables, denom, where, *refs):
    stats, refs = refs[:tables], refs[tables:]
    lengths, logits, counts, *shards, part, results, lse, total = refs
    shard, step = pl.program_id(0), pl.program_id(1)
    is_first = (shard == 0) & (step == 0)
    is_end = (shard == pl.num_programs(0) - 1) & (step == pl.num_programs(1) - 1)

    @pl.when(is_first)
    def _():
        values = [ref[...] for ref in stats]
        top = values[0][:, 0:1]
        for table in values[1:]:
            top = jnp.maximum(top, table[:, 0:1])
        mass = sum(table[:, 1:2] * jnp.exp(table[:, 0:1] - top) for table in values)
        target = sum(table[:, 2:3] for table in values)
        lse[...] = top + jnp.log(mass)
        results[...] = lane_fill([lse[...], lengths[...] * lse[...] - target], results.shape)
        total[...] = jnp.zeros_like(total)

    for at, w_part in enumerate(shards):

        @pl.when(shard == at)
        def _(w_part=w_part):
            exped = lengths[...] * jnp.exp(logits[...] - lse[...])
            dlogits = ((exped - counts[...].astype(F32)) / denom).astype(BF16)
            total[...] += dot_t(dlogits, w_part[...])

    @pl.when(is_end)
    def _():
        part[...] = total[...].astype(part.dtype)


def head_grads(where, stats, lengths, logits, counts, at, shards, denom, part_type):
    count, rows, vocab = logits.shape
    width = shards[0].shape[0]
    tile = tile_of(vocab, 640)
    tiles = vocab // tile
    return pl.pallas_call(
        functools.partial(head_grads_kernel, len(stats), denom),
        grid_spec=pltpu.PrefetchScalarGridSpec(
            num_scalar_prefetch=1,
            grid=(count, tiles),
            in_specs=[whole_spec((rows, 128))] * len(stats)
            + [
                pl.BlockSpec((None, rows, 1), lambda i, t, s: (at, 0, 0)),
                pl.BlockSpec((None, rows, tile), lambda i, t, s: (i, 0, t)),
                pl.BlockSpec((None, None, rows, tile), lambda i, t, s: (i, at, 0, t)),
                *shard_specs(count, width, tile, tiles),
            ],
            out_specs=[whole_spec((rows, width)), whole_spec((rows, 128))],
            scratch_shapes=[pltpu.VMEM((rows, 1), F32), pltpu.VMEM((rows, width), F32)],
        ),
        out_shape=[
            jax.ShapeDtypeStruct((rows, width), part_type),
            jax.ShapeDtypeStruct((rows, 128), F32),
        ],
        compiler_params=params(VMEM_MIB),
        cost_estimate=pl.CostEstimate(
            flops=2 * rows * width * vocab * count,
            bytes_accessed=(2 * width + 6 * rows) * vocab * count,
            transcendentals=rows * vocab * count,
        ),
        name="head_grads",
    )(where, *stats, lengths, logits, counts, *shards)


def weight_kernel(blocks, adding, share, where, *refs):
    x_refs, refs = refs[:blocks], refs[blocks:]
    g_refs, refs = refs[:blocks], refs[blocks:]
    w_in, w_out, refs = refs[0], refs[1], refs[2:]
    if adding:
        old_first, old_second, refs = refs[0], refs[1], refs[2:]
    first, second, normed, grads, normed_t, grads_t = refs
    count = x_refs[0].shape[0]

    @pl.when(pl.program_id(0) == 0)
    def _():
        columns = pl.ds(pl.multiple_of(where[0] * share, share), share)
        for at in range(blocks):
            place = pl.ds(at * count, count)
            normed[place, :] = normalised(x_refs[at][...])
            grads[place, :] = g_refs[at][...]
        normed_t[...] = normed[:, columns].astype(F32).T.astype(BF16)
        grads_t[...] = grads[:, columns].astype(F32).T.astype(BF16)

    total_first = old_first[...] if adding else None
    total_second = None
    rows = normed.shape[0]
    part = min(256, rows)
    for at in range(rows // part):
        place = pl.ds(at * part, part)
        value, slope = gelu_parts(dot(normed[place, :], w_in[...]))
        dpre = (dot_t(grads[place, :], w_out[...]) * slope).astype(BF16)
        now_first = dot(normed_t[:, place], dpre)
        now_second = dot(grads_t[:, place], value.astype(BF16))
        total_first = now_first if total_first is None else total_first + now_first
        total_second = now_second if total_second is None else total_second + now_second
    first[...] = total_first
    total_second = total_second.T
    second[...] = old_second[...] + total_second if adding else total_second


def weight_grads(where, x_parts, g_parts, w_in, w_out, old, share):
    width, hidden = w_in.shape
    tile = tile_of(hidden, 512)
    blocks = len(g_parts)
    count = g_parts[0].shape[0]
    rows = blocks * count
    in_specs = [
        pl.BlockSpec((None, None, count, width), index) for _, index in x_parts
    ]
    in_specs += [pl.BlockSpec((count, width), lambda j, s: (0, 0))] * blocks
    in_specs += [
        pl.BlockSpec((width, tile), lambda j, s: (0, j)),
        pl.BlockSpec((tile, width), lambda j, s: (j, 0)),
    ]
    grad_specs = [
        pl.BlockSpec((share, tile), lambda j, s: (0, j)),
        pl.BlockSpec((tile, share), lambda j, s: (j, 0)),
    ]
    adding = old is not None
    aliases = {}
    if adding:
        in_specs += grad_specs
        aliases = {1 + 2 * blocks + 2: 0, 1 + 2 * blocks + 3: 1}
    return pl.pallas_call(
        functools.partial(weight_kernel, blocks, adding, share),
        grid_spec=pltpu.PrefetchScalarGridSpec(
            num_scalar_prefetch=1,
            grid=(hidden // tile,),
            in_specs=in_specs,
            out_specs=grad_specs,
            scratch_shapes=[
                pltpu.VMEM((rows, width), BF16),
                pltpu.VMEM((rows, width), BF16),
                pltpu.VMEM((share, rows), BF16),
                pltpu.VMEM((share, rows), BF16),
            ],
        ),
        out_shape=[
            jax.ShapeDtypeStruct((share, hidden), F32),
            jax.ShapeDtypeStruct((hidden, share), F32),
        ],
        input_output_aliases=aliases,
        compiler_params=params(VMEM_MIB),
        cost_estimate=pl.CostEstimate(
            flops=4 * rows * (width + share) * hidden,
            bytes_accessed=4 * width * hidden + 16 * share * hidden,
            transcendentals=rows * hidden,
        ),
        name="weight_grads",
    )(where, *[x for x, _ in x_parts], *g_parts, w_in, w_out, *(old or ()))


def unit_counts(ends, targets, ids):
    positions = jnp.arange(targets.shape[1], dtype=jnp.int32)
    row_local = jnp.sum((ends[:, None, :] <= positions[None, :, None]).astype(jnp.int32), axis=-1)
    rows = jnp.arange(ends.shape[1], dtype=jnp.int32)
    row_onehot = (row_local[:, :, None] == rows[None, None, :]).astype(BF16)
    hits = (targets[:, :, None] == ids[None, None, :]).astype(BF16)
    counts = jnp.einsum("mur,muv->mrv", row_onehot, hits, preferred_element_type=F32)
    return counts.astype(BF16)


def on_device(text_rows, durations, unit_targets, w_in, w_out, w_unit):
    micro, row_count, width = text_rows.shape
    segments = lax.axis_size("segment")
    mp_size = lax.axis_size("mp")
    dp_size = lax.axis_size("dp")
    seg = lax.axis_index("segment").astype(jnp.int32)
    mp_at = lax.axis_index("mp").astype(jnp.int32)
    dp_at = lax.axis_index("dp").astype(jnp.int32)
    last = segments - 1
    pair = mp_size == 2
    halves = 2 if pair else 1
    part_type = BF16 if pair else F32
    where = jnp.stack([seg, mp_at])
    first = w_in[0]
    second = w_out[0]
    chunks = CHUNKS
    rows = micro * row_count // chunks
    text = [t for t in text_rows.reshape(chunks, rows, width)]
    vocab_part = w_unit.shape[1]
    unit_count = unit_targets.shape[1]
    denom = float(micro * unit_count * dp_size)
    lengths = durations[:, 0, :]
    length_f = lengths.astype(F32).reshape(chunks, rows, 1)
    ends = jnp.cumsum(lengths, axis=-1)

    shards = [w_unit] + [lax.ppermute(w_unit, "segment", [(j, last)]) for j in range(last)]
    part_ids = jnp.arange(vocab_part, dtype=jnp.int32)
    head_counts = jnp.stack(
        [
            unit_counts(ends, unit_targets, (j * mp_size + mp_at) * vocab_part + part_ids)
            for j in [last, *range(last)]
        ]
    ).reshape(segments, chunks, rows, vocab_part)
    own_ids = (seg * mp_size + mp_at) * vocab_part + part_ids
    own_counts = unit_counts(ends, unit_targets, own_ids).reshape(micro * row_count, vocab_part)

    def both(part):
        return [part, swapped(part)] if pair else [part]

    def reduced(keep, send):
        return [keep, swapped(send[0])] if pair else [lax.psum(keep, "mp")]

    def mp_pieces(part):
        return [part, swapped(part)] if pair else [lax.psum(part, "mp")]

    def mp_tables(stats):
        if pair:
            return [stats, swapped(stats)]
        return [t for t in lax.all_gather(stats, "mp")]

    def gather_grads(mine, theirs):
        if not pair:
            return [t for t in lax.all_gather(mine, "dp")]
        own, other = [mine], [theirs]
        for distance in range(1, dp_size):
            route = [(i, (i + distance) % dp_size) for i in range(dp_size)]
            came = lax.ppermute(mine, "dp", route)
            own.append(came)
            other.append(swapped(came))
        return own + other

    stash, x_halves, grads, finals, results, sent = [], [], [], [], [], []
    sums = None
    x_mine = x_theirs = None
    f_hop = b_hop = None

    def x_parts(at):
        if not pair:
            return [(x_mine, lambda j, s, k=k: (k, at, 0, 0)) for k in range(dp_size)]
        return [
            (source, lambda j, s, k=k: (lax.rem(s[0] + dp_size - k, dp_size), at, 0, 0))
            for source in (x_mine, x_theirs)
            for k in range(dp_size)
        ]

    clocks = 2 * segments + chunks - 1
    for clock in range(clocks):
        f_out = b_out = None
        if clock < segments + chunks - 1:
            own = text[min(clock, chunks - 1)]
            arrived = [own[: rows // halves]] * halves
            if clock > 0:
                arrived = both(shifted(f_hop, "segment", 1))
            rows_in, mine, keep, *send = forward_section(where, own, arrived, first, second)
            stash.append(rows_in)
            x_halves.append(mine)
            f_out = finish_forward(mine, reduced(keep, send))
        if clock >= segments:
            at = clock - segments
            arrived = None if at == 0 else both(shifted(b_hop, "segment", -1))
            if clock < clocks - 1:
                parts = []
                final = None
                if at < chunks:
                    final = both(f_hop)
                    finals.append(final)
                    sent.append(
                        [lax.ppermute(f_hop, "segment", [(last, to)]) for to in range(last)]
                    )
                    logits, stats = head_logits(where, final, shards, head_counts, at)
                    part, result = head_grads(
                        where,
                        mp_tables(stats),
                        length_f,
                        logits,
                        head_counts,
                        at,
                        shards,
                        denom,
                        part_type,
                    )
                    results.append(result[:, 0:2])
                    parts = mp_pieces(part)
                options = []
                for other in range(segments):
                    stage = clock - 2 * segments + 1 + 2 * other
                    if 0 <= stage < len(stash):
                        options.append((other, stash[stage]))
                mine, g_mine, keep, *send = backward_section(
                    where, last, halves, options, final, parts, arrived, first, second
                )
                grads.append(g_mine)
                b_out = finish_backward(mine, g_mine, reduced(keep, send))
            else:
                grads.append(arrived[0])
        if clock == segments + chunks - 2:
            x_half = jnp.stack(
                [
                    chosen(seg, [(s, x_halves[b + s]) for s in range(segments)])
                    for b in range(chunks)
                ]
            )
            x_mine = lax.all_gather(x_half, "dp")
            x_theirs = swapped(x_mine) if pair else None
        if clock >= 2 * segments - 1:
            at = clock - 2 * segments + 1
            mine = chosen(seg, [(s, grads[at + last - s]) for s in range(segments)])
            theirs = swapped(mine) if pair else None
            sums = weight_grads(
                dp_at[None],
                x_parts(at),
                gather_grads(mine, theirs),
                first,
                second,
                sums,
                width // dp_size,
            )
        f_hop, b_hop = f_out, b_out

    results = jnp.stack(results)
    results = chosen(
        seg,
        [(last, results)]
        + [(to, lax.ppermute(results, "segment", [(last, to)])) for to in range(last)],
    )
    loss = (jnp.sum(results[:, :, 1]) / denom)[None]
    final_rows = []
    for b in range(chunks):
        mine = chosen(seg, [(last, finals[b][0])] + [(to, sent[b][to]) for to in range(last)])
        pieces = both(mine)
        if pair:
            pieces = [
                jnp.where(mp_at == 0, pieces[0], pieces[1]),
                jnp.where(mp_at == 0, pieces[1], pieces[0]),
            ]
        final_rows += pieces
    final_norm = normalised(jnp.concatenate(final_rows))
    own_logits = dot(final_norm, w_unit)
    own_exp = jnp.exp(own_logits - results[:, :, 0].reshape(-1, 1))
    own_dlogits = (
        (length_f.reshape(-1, 1) * own_exp - own_counts.astype(F32)) / denom
    ).astype(BF16)
    grad_unit = t_dot(final_norm, own_dlogits).astype(BF16)
    sum_unit = lax.psum_scatter(grad_unit, "dp", scatter_dimension=0, tiled=True).astype(F32)
    return (loss, sums[0][None], sums[1][None], sum_unit)


def solution(mesh):
    placed = (
        P(None, "dp", None),
        P(None, "dp", None),
        P(None, "dp"),
        P("segment", None, "mp"),
        P("segment", "mp", None),
        P(None, ("segment", "mp")),
    )
    return jax.shard_map(
        on_device,
        mesh=mesh,
        in_specs=placed,
        out_specs=(
            P("dp"),
            P("segment", "dp", "mp"),
            P("segment", "mp", "dp"),
            P("dp", ("segment", "mp")),
        ),
        check_vma=False,
    )
```

```python
import functools
import jax
import jax.numpy as jnp
from jax import lax
from jax.experimental import pallas as pl
from jax.experimental.pallas import tpu as pltpu
from jax.sharding import PartitionSpec as P

CHUNKS = 2
VMEM_MIB = 58
SMALL_MIB = 16
BF16 = jnp.bfloat16
F32 = jnp.float32
MIB = 1024 * 1024


def shifted(block, axis, distance):
    devices = range(lax.axis_size(axis))
    route = [(i - distance, i) for i in devices if i - distance in devices]
    return lax.ppermute(block, axis, route)


def swapped(block):
    return lax.ppermute(block, "mp", [(0, 1), (1, 0)])


def gelu_parts(pre_vals):
    coeff = 0.7978845608
    square = pre_vals * pre_vals
    inner = coeff * pre_vals * (1.0 + 0.044715 * square)
    half = 0.5 * (1.0 + jnp.tanh(inner))
    value = pre_vals * half
    slope = half + 2.0 * value * (1.0 - half) * coeff * (1.0 + 3.0 * 0.044715 * square)
    return (value, slope)


def row_scale(rows_in):
    floats = rows_in.astype(F32)
    return lax.rsqrt(jnp.mean(floats * floats, axis=-1, keepdims=True) + 1e-06)


def normalised(rows_in):
    return (rows_in.astype(F32) * row_scale(rows_in)).astype(BF16)


def norm_back(rows_in, grads):
    scale = row_scale(rows_in)
    normal = rows_in.astype(F32) * scale
    return scale * (grads - normal * jnp.mean(grads * normal, axis=-1, keepdims=True))


def dot(a, b):
    return jnp.dot(a, b, preferred_element_type=F32)


def dot_t(a, b):
    return lax.dot_general(a, b, (((1,), (1,)), ((), ())), preferred_element_type=F32)


def t_dot(a, b):
    return lax.dot_general(a, b, (((0,), (0,)), ((), ())), preferred_element_type=F32)


def tile_of(size, most):
    if size <= most:
        return size
    return max(t for t in range(128, most + 1, 128) if size % t == 0)


def pieces_of(size):
    return [(at, min(256, size - at)) for at in range(0, size, 256)]


def cost(flops, bytes_accessed, transcendentals):
    return pl.CostEstimate(
        flops=flops // 16,
        bytes_accessed=bytes_accessed // 16,
        transcendentals=transcendentals // 16,
    )


def params(limit):
    return pltpu.CompilerParams(vmem_limit_bytes=limit * MIB)


def added(refs):
    total = refs[0][...].astype(F32)
    for ref in refs[1:]:
        total = total + ref[...].astype(F32)
    return total


def chosen(index, candidates):
    value = candidates[0][1]
    for at, option in candidates[1:]:
        value = jnp.where(index == at, option, value)
    return value


def gathered(halves, place):
    if len(halves) == 1:
        return halves[0][...]
    mine, theirs = (half[...] for half in halves)
    first = jnp.where(place == 0, mine, theirs)
    second = jnp.where(place == 0, theirs, mine)
    return jnp.concatenate([first, second], axis=0)


def part_of(block, place, parts):
    rows = block.shape[0] // parts
    if parts == 1:
        return block[...]
    return block[pl.ds(pl.multiple_of(place * rows, rows), rows), :]


def whole_spec(shape):
    return pl.BlockSpec(shape, lambda *_: (0,) * len(shape))


def emit_parts(total, place, keep, send):
    if send is None:
        keep[...] = total[...]
        return
    keep[...] = part_of(total, place, 2)
    send[...] = part_of(total, 1 - place, 2).astype(send.dtype)


def forward_kernel(halves, where, own, *refs):
    arrived, refs = refs[:halves], refs[halves:]
    w_in, w_out, rows_out, mine_out, keep, *send, whole, normed, total = refs
    step = pl.program_id(0)

    @pl.when(step == 0)
    def _():
        rows = jnp.where(where[0] == 0, own[...], gathered(arrived, where[1]))
        rows_out[...] = rows
        whole[...] = rows
        mine_out[...] = part_of(whole, where[1], halves)
        normed[...] = normalised(rows)
        total[...] = jnp.zeros_like(total)

    values = []
    for at, size in pieces_of(w_in.shape[1]):
        value, _ = gelu_parts(dot(normed[...], w_in[:, at : at + size]))
        values.append(value.astype(BF16))
    total[...] += dot(jnp.concatenate(values, axis=1), w_out[...])

    @pl.when(step == pl.num_programs(0) - 1)
    def _():
        emit_parts(total, where[1], keep, send[0] if send else None)


def forward_section(where, own, arrived, w_in, w_out):
    rows, width = own.shape
    hidden = w_in.shape[1]
    tile = tile_of(hidden, 1024)
    halves = len(arrived)
    full, part = (rows, width), (rows // halves, width)
    shapes = [(full, BF16), (part, BF16), (part, F32)] + [(part, BF16)] * (halves - 1)
    return pl.pallas_call(
        functools.partial(forward_kernel, halves),
        grid_spec=pltpu.PrefetchScalarGridSpec(
            num_scalar_prefetch=1,
            grid=(hidden // tile,),
            in_specs=[
                whole_spec(full),
                *[whole_spec(part)] * halves,
                pl.BlockSpec((width, tile), lambda j, s: (0, j)),
                pl.BlockSpec((tile, width), lambda j, s: (j, 0)),
            ],
            out_specs=[whole_spec(shape) for shape, _ in shapes],
            scratch_shapes=[pltpu.VMEM(full, BF16), pltpu.VMEM(full, BF16), pltpu.VMEM(full, F32)],
        ),
        out_shape=[jax.ShapeDtypeStruct(*shape) for shape in shapes],
        compiler_params=params(VMEM_MIB),
        cost_estimate=cost(
            flops=4 * rows * width * hidden,
            bytes_accessed=4 * width * hidden,
            transcendentals=rows * hidden,
        ),
        name="section_forward",
    )(where, own, *arrived, w_in, w_out)


def finish_forward_kernel(*refs):
    refs[-1][...] = added(refs[:-1]).astype(BF16)


def finish_forward(rows, pieces):
    return pl.pallas_call(
        finish_forward_kernel,
        out_shape=jax.ShapeDtypeStruct(rows.shape, BF16),
        compiler_params=params(SMALL_MIB),
        name="finish_forward",
    )(rows, *pieces)


def finish_backward_kernel(rows, grads, *refs):
    summed = added(refs[:-1])
    refs[-1][...] = (grads[...].astype(F32) + norm_back(rows[...], summed)).astype(BF16)


def finish_backward(rows, grads, pieces):
    return pl.pallas_call(
        finish_backward_kernel,
        out_shape=jax.ShapeDtypeStruct(rows.shape, BF16),
        compiler_params=params(SMALL_MIB),
        name="finish_backward",
    )(rows, grads, *pieces)


def backward_kernel(owners, halves, pieces, last, has_arrived, where, *refs):
    stashed, refs = refs[: len(owners)], refs[len(owners) :]
    if pieces:
        final, refs = refs[:halves], refs[halves:]
        parts, refs = refs[:pieces], refs[pieces:]
    if has_arrived:
        arrived, refs = refs[:halves], refs[halves:]
    w_in, w_out, mine_rows, mine_grads, keep, *send, rows, grads, normed, total = refs
    step = pl.program_id(0)

    @pl.when(step == 0)
    def _():
        rows[...] = chosen(where[0], [(at, ref[...]) for at, ref in zip(owners, stashed)])
        here = None
        if pieces:
            dnorm = added(parts).astype(BF16).astype(F32)
            here = norm_back(gathered(final, where[1]), dnorm).astype(BF16)
        if has_arrived:
            came = gathered(arrived, where[1])
            here = came if here is None else jnp.where(where[0] == last, here, came)
        grads[...] = here
        mine_rows[...] = part_of(rows, where[1], halves)
        mine_grads[...] = part_of(grads, where[1], halves)
        normed[...] = normalised(rows[...])
        total[...] = jnp.zeros_like(total)

    dpres = []
    for at, size in pieces_of(w_in.shape[1]):
        _, slope = gelu_parts(dot(normed[...], w_in[:, at : at + size]))
        dpres.append((dot_t(grads[...], w_out[at : at + size, :]) * slope).astype(BF16))
    total[...] += dot_t(jnp.concatenate(dpres, axis=1), w_in[...])

    @pl.when(step == pl.num_programs(0) - 1)
    def _():
        emit_parts(total, where[1], keep, send[0] if send else None)


def backward_section(where, last, halves, options, final, parts, arrived, w_in, w_out):
    width, hidden = w_in.shape
    rows = options[0][1].shape[0]
    tile = tile_of(hidden, 1024)
    full, part = (rows, width), (rows // halves, width)
    operands = [option for _, option in options]
    specs = [whole_spec(full)] * len(options)
    if parts:
        operands += [*final, *parts]
        specs += [whole_spec(part)] * halves + [whole_spec(full)] * len(parts)
    if arrived is not None:
        operands += arrived
        specs += [whole_spec(part)] * halves
    body = functools.partial(
        backward_kernel,
        tuple(at for at, _ in options),
        halves,
        len(parts),
        last,
        arrived is not None,
    )
    shapes = [(part, BF16), (part, BF16), (part, F32)] + [(part, BF16)] * (halves - 1)
    return pl.pallas_call(
        body,
        grid_spec=pltpu.PrefetchScalarGridSpec(
            num_scalar_prefetch=1,
            grid=(hidden // tile,),
            in_specs=specs
            + [
                pl.BlockSpec((width, tile), lambda j, s: (0, j)),
                pl.BlockSpec((tile, width), lambda j, s: (j, 0)),
            ],
            out_specs=[whole_spec(shape) for shape, _ in shapes],
            scratch_shapes=[pltpu.VMEM(full, BF16)] * 3 + [pltpu.VMEM(full, F32)],
        ),
        out_shape=[jax.ShapeDtypeStruct(*shape) for shape in shapes],
        compiler_params=params(VMEM_MIB),
        cost_estimate=cost(
            flops=6 * rows * width * hidden,
            bytes_accessed=4 * width * hidden,
            transcendentals=rows * hidden,
        ),
        name="section_backward",
    )(where, *operands, w_in, w_out)


def lane_fill(columns, shape):
    lane = lax.broadcasted_iota(jnp.int32, shape, 1)
    filled = jnp.zeros(shape, F32)
    for at, column in enumerate(columns):
        filled = jnp.where(lane == at, column, filled)
    return filled


def shard_specs(count, shape, tiles, lead=()):
    def index(shard, i, t):
        before, after = i < shard, i > shard
        return (*lead, 0, jnp.where(before, 0, jnp.where(after, tiles - 1, t)))

    block = (None,) * len(lead) + shape
    return [pl.BlockSpec(block, lambda i, t, s, k=k: index(k, i, t)) for k in range(count)]


def logits_kernel(halves, count, where, *refs):
    final, refs = refs[:halves], refs[halves:]
    shards, refs = refs[:count], refs[count:]
    counts, refs = refs[:count], refs[count:]
    logits, stats, normed, peak, total, target = refs
    shard, step = pl.program_id(0), pl.program_id(1)
    is_first = (shard == 0) & (step == 0)
    is_end = (shard == pl.num_programs(0) - 1) & (step == pl.num_programs(1) - 1)
    lanes = peak.shape[1]

    @pl.when(is_first)
    def _():
        normed[...] = normalised(gathered(final, where[1]))
        peak[...] = jnp.full_like(peak, -1e30)
        total[...] = jnp.zeros_like(total)
        target[...] = jnp.zeros_like(target)

    for at in range(count):

        @pl.when(shard == at)
        def _(w_part=shards[at], hits=counts[at]):
            columns = []
            for start, size in pieces_of(w_part.shape[1]):
                values = dot(normed[...], w_part[:, start : start + size])
                logits[:, start : start + size] = values
                counted = hits[:, start : start + size].astype(F32) * values
                columns += [
                    (values[:, c : c + lanes], counted[:, c : c + lanes])
                    for c in range(0, size, lanes)
                ]
            higher = peak[...]
            for values, _ in columns:
                higher = jnp.maximum(higher, values)
            mass = total[...] * jnp.exp(peak[...] - higher)
            summed = target[...]
            for values, counted in columns:
                mass = mass + jnp.exp(values - higher)
                summed = summed + counted
            peak[...] = higher
            total[...] = mass
            target[...] = summed

    @pl.when(is_end)
    def _():
        top = jnp.max(peak[...], axis=-1, keepdims=True)
        mass = jnp.sum(total[...] * jnp.exp(peak[...] - top), axis=-1, keepdims=True)
        summed = jnp.sum(target[...], axis=-1, keepdims=True)
        stats[...] = lane_fill([top, mass, summed], stats.shape)


def head_logits(where, final, shards, counts, at):
    halves = len(final)
    count = len(shards)
    half, width = final[0].shape
    rows = half * halves
    vocab = shards[0].shape[1]
    lanes = 128 if vocab % 128 == 0 else vocab
    tile = tile_of(vocab, 640)
    tiles = vocab // tile
    return pl.pallas_call(
        functools.partial(logits_kernel, halves, count),
        grid_spec=pltpu.PrefetchScalarGridSpec(
            num_scalar_prefetch=1,
            grid=(count, tiles),
            in_specs=[
                *[whole_spec((half, width))] * halves,
                *shard_specs(count, (width, tile), tiles),
                *shard_specs(count, (rows, tile), tiles, (at,)),
            ],
            out_specs=[
                pl.BlockSpec((None, rows, tile), lambda i, t, s: (i, 0, t)),
                whole_spec((rows, 128)),
            ],
            scratch_shapes=[pltpu.VMEM((rows, width), BF16)] + [pltpu.VMEM((rows, lanes), F32)] * 3,
        ),
        out_shape=[
            jax.ShapeDtypeStruct((count, rows, vocab), F32),
            jax.ShapeDtypeStruct((rows, 128), F32),
        ],
        compiler_params=params(VMEM_MIB),
        cost_estimate=cost(
            flops=2 * rows * width * vocab * count,
            bytes_accessed=(2 * width + 6 * rows) * vocab * count,
            transcendentals=rows * vocab * count,
        ),
        name="head_logits",
    )(where, *final, *shards, *counts)


def head_grads_kernel(tables, count, denom, where, *refs):
    stats, refs = refs[:tables], refs[tables:]
    lengths, logits, refs = refs[0], refs[1], refs[2:]
    shards, refs = refs[:count], refs[count:]
    counts, refs = refs[:count], refs[count:]
    part, results, shift, total = refs
    shard, step = pl.program_id(0), pl.program_id(1)
    is_first = (shard == 0) & (step == 0)
    is_end = (shard == pl.num_programs(0) - 1) & (step == pl.num_programs(1) - 1)

    @pl.when(is_first)
    def _():
        values = [ref[...] for ref in stats]
        top = values[0][:, 0:1]
        for table in values[1:]:
            top = jnp.maximum(top, table[:, 0:1])
        mass = sum(table[:, 1:2] * jnp.exp(table[:, 0:1] - top) for table in values)
        target = sum(table[:, 2:3] for table in values)
        lse = top + jnp.log(mass)
        shift[...] = lse - jnp.log(lengths[...] * (1.0 / denom))
        results[...] = lane_fill([shift[...], lengths[...] * lse - target], results.shape)
        total[...] = jnp.zeros_like(total)

    for at in range(count):

        @pl.when(shard == at)
        def _(w_part=shards[at], hits=counts[at]):
            columns = []
            for start, size in pieces_of(w_part.shape[1]):
                exped = jnp.exp(logits[:, start : start + size] - shift[...])
                counted = hits[:, start : start + size].astype(F32) * (1.0 / denom)
                columns.append((exped - counted).astype(BF16))
            total[...] += dot_t(jnp.concatenate(columns, axis=1), w_part[...])

    @pl.when(is_end)
    def _():
        part[...] = total[...].astype(part.dtype)


def head_grads(where, stats, lengths, logits, counts, at, shards, denom, part_type):
    count, rows, vocab = logits.shape
    width = shards[0].shape[0]
    tile = tile_of(vocab, 640)
    tiles = vocab // tile
    return pl.pallas_call(
        functools.partial(head_grads_kernel, len(stats), count, denom),
        grid_spec=pltpu.PrefetchScalarGridSpec(
            num_scalar_prefetch=1,
            grid=(count, tiles),
            in_specs=[whole_spec((rows, 128))] * len(stats)
            + [
                pl.BlockSpec((None, rows, 1), lambda i, t, s: (at, 0, 0)),
                pl.BlockSpec((None, rows, tile), lambda i, t, s: (i, 0, t)),
                *shard_specs(count, (width, tile), tiles),
                *shard_specs(count, (rows, tile), tiles, (at,)),
            ],
            out_specs=[whole_spec((rows, width)), whole_spec((rows, 128))],
            scratch_shapes=[pltpu.VMEM((rows, 1), F32), pltpu.VMEM((rows, width), F32)],
        ),
        out_shape=[
            jax.ShapeDtypeStruct((rows, width), part_type),
            jax.ShapeDtypeStruct((rows, 128), F32),
        ],
        compiler_params=params(VMEM_MIB),
        cost_estimate=cost(
            flops=2 * rows * width * vocab * count,
            bytes_accessed=(2 * width + 6 * rows) * vocab * count,
            transcendentals=rows * vocab * count,
        ),
        name="head_grads",
    )(where, *stats, lengths, logits, *shards, *counts)


def unit_kernel(blocks, tables, share, denom, where, *refs):
    x_refs, refs = refs[: len(blocks)], refs[len(blocks) :]
    shifts, refs = refs[:tables], refs[tables:]
    counts, refs = refs[:tables], refs[tables:]
    w_unit, grad, normed, normed_t = refs
    half = x_refs[0].shape[0]
    rows = normed.shape[0] // tables

    @pl.when(pl.program_id(0) == 0)
    def _():
        for ref, (base, theirs) in zip(x_refs, blocks):
            side = 0
            if theirs is not None:
                side = 1 - where[1] if theirs else where[1]
            place = pl.ds(pl.multiple_of(base + side * half, half), half)
            normed[place, :] = normalised(ref[...])
        columns = pl.ds(pl.multiple_of(where[0] * share, share), share)
        normed_t[...] = normed[:, columns].astype(F32).T.astype(BF16)

    total = None
    for k in range(tables):
        place = pl.ds(k * rows, rows)
        exped = jnp.exp(dot(normed[place, :], w_unit[...]) - shifts[k][...])
        dlogits = (exped - counts[k][...].astype(F32) * (1.0 / denom)).astype(BF16)
        now = dot(normed_t[:, place], dlogits)
        total = now if total is None else total + now
    grad[...] = total


def unit_grads(where, x_parts, shifts, counts, w_unit, denom, share):
    width, vocab = w_unit.shape
    tile = tile_of(vocab, 256)
    half = x_parts[0][0].shape[2]
    rows = shifts[0].shape[0]
    tables = len(shifts)
    blocks = tuple(block for _, _, block in x_parts)
    return pl.pallas_call(
        functools.partial(unit_kernel, blocks, tables, share, denom),
        grid_spec=pltpu.PrefetchScalarGridSpec(
            num_scalar_prefetch=1,
            grid=(vocab // tile,),
            in_specs=[pl.BlockSpec((None, None, half, width), index) for _, index, _ in x_parts]
            + [whole_spec((rows, 1))] * tables
            + [pl.BlockSpec((rows, tile), lambda j, s: (0, j))] * tables
            + [pl.BlockSpec((width, tile), lambda j, s: (0, j))],
            out_specs=pl.BlockSpec((share, tile), lambda j, s: (0, j)),
            scratch_shapes=[
                pltpu.VMEM((rows * tables, width), BF16),
                pltpu.VMEM((share, rows * tables), BF16),
            ],
        ),
        out_shape=jax.ShapeDtypeStruct((share, vocab), F32),
        compiler_params=params(VMEM_MIB),
        cost_estimate=cost(
            flops=2 * rows * tables * (width + share) * vocab,
            bytes_accessed=2 * (width + rows * tables) * vocab,
            transcendentals=rows * tables * vocab,
        ),
        name="unit_grads",
    )(where, *[x for x, _, _ in x_parts], *shifts, *counts, w_unit)


def weight_kernel(blocks, adding, share, where, *refs):
    x_refs, refs = refs[:blocks], refs[blocks:]
    g_refs, refs = refs[:blocks], refs[blocks:]
    w_in, w_out, refs = refs[0], refs[1], refs[2:]
    if adding:
        old_first, old_second, refs = refs[0], refs[1], refs[2:]
    first, second, normed, grads, normed_t, grads_t = refs
    count = x_refs[0].shape[0]

    @pl.when(pl.program_id(0) == 0)
    def _():
        columns = pl.ds(pl.multiple_of(where[0] * share, share), share)
        for at in range(blocks):
            place = pl.ds(at * count, count)
            normed[place, :] = normalised(x_refs[at][...])
            grads[place, :] = g_refs[at][...]
        normed_t[...] = normed[:, columns].astype(F32).T.astype(BF16)
        grads_t[...] = grads[:, columns].astype(F32).T.astype(BF16)

    total_first = old_first[...] if adding else None
    total_second = None
    rows = normed.shape[0]
    part = min(256, rows)
    for at in range(rows // part):
        place = pl.ds(at * part, part)
        value, slope = gelu_parts(dot(normed[place, :], w_in[...]))
        dpre = (dot_t(grads[place, :], w_out[...]) * slope).astype(BF16)
        now_first = dot(normed_t[:, place], dpre)
        now_second = dot(grads_t[:, place], value.astype(BF16))
        total_first = now_first if total_first is None else total_first + now_first
        total_second = now_second if total_second is None else total_second + now_second
    first[...] = total_first
    total_second = total_second.T
    second[...] = old_second[...] + total_second if adding else total_second


def weight_grads(where, x_parts, g_parts, w_in, w_out, old, share):
    width, hidden = w_in.shape
    tile = tile_of(hidden, 512)
    blocks = len(g_parts)
    count = g_parts[0][0].shape[1]
    rows = blocks * count
    in_specs = [pl.BlockSpec((None, None, count, width), index) for _, index in x_parts]
    in_specs += [pl.BlockSpec((None, count, width), index) for _, index in g_parts]
    in_specs += [
        pl.BlockSpec((width, tile), lambda j, s: (0, j)),
        pl.BlockSpec((tile, width), lambda j, s: (j, 0)),
    ]
    grad_specs = [
        pl.BlockSpec((share, tile), lambda j, s: (0, j)),
        pl.BlockSpec((tile, share), lambda j, s: (j, 0)),
    ]
    adding = old is not None
    aliases = {}
    if adding:
        in_specs += grad_specs
        aliases = {1 + 2 * blocks + 2: 0, 1 + 2 * blocks + 3: 1}
    return pl.pallas_call(
        functools.partial(weight_kernel, blocks, adding, share),
        grid_spec=pltpu.PrefetchScalarGridSpec(
            num_scalar_prefetch=1,
            grid=(hidden // tile,),
            in_specs=in_specs,
            out_specs=grad_specs,
            scratch_shapes=[
                pltpu.VMEM((rows, width), BF16),
                pltpu.VMEM((rows, width), BF16),
                pltpu.VMEM((share, rows), BF16),
                pltpu.VMEM((share, rows), BF16),
            ],
        ),
        out_shape=[
            jax.ShapeDtypeStruct((share, hidden), F32),
            jax.ShapeDtypeStruct((hidden, share), F32),
        ],
        input_output_aliases=aliases,
        compiler_params=params(VMEM_MIB),
        cost_estimate=cost(
            flops=4 * rows * (width + share) * hidden,
            bytes_accessed=4 * width * hidden + 16 * share * hidden,
            transcendentals=rows * hidden,
        ),
        name="weight_grads",
    )(where, *[x for x, _ in x_parts], *[g for g, _ in g_parts], w_in, w_out, *(old or ()))


def unit_counts(ends, targets, ids):
    positions = jnp.arange(targets.shape[1], dtype=jnp.int32)
    row_local = jnp.sum((ends[:, None, :] <= positions[None, :, None]).astype(jnp.int32), axis=-1)
    rows = jnp.arange(ends.shape[1], dtype=jnp.int32)
    row_onehot = (row_local[:, :, None] == rows[None, None, :]).astype(BF16)
    hits = (targets[:, :, None] == ids[None, None, :]).astype(BF16)
    counts = jnp.einsum("mur,muv->mrv", row_onehot, hits, preferred_element_type=F32)
    return counts.astype(BF16)


def on_device(text_rows, durations, unit_targets, w_in, w_out, w_unit):
    micro, row_count, width = text_rows.shape
    segments = lax.axis_size("segment")
    mp_size = lax.axis_size("mp")
    dp_size = lax.axis_size("dp")
    seg = lax.axis_index("segment").astype(jnp.int32)
    mp_at = lax.axis_index("mp").astype(jnp.int32)
    dp_at = lax.axis_index("dp").astype(jnp.int32)
    last = segments - 1
    pair = mp_size == 2
    halves = 2 if pair else 1
    part_type = BF16 if pair else F32
    where = jnp.stack([seg, mp_at])
    first = w_in[0]
    second = w_out[0]
    chunks = CHUNKS
    rows = micro * row_count // chunks
    text = [t for t in text_rows.reshape(chunks, rows, width)]
    vocab_part = w_unit.shape[1]
    unit_count = unit_targets.shape[1]
    denom = float(micro * unit_count * dp_size)
    lengths = durations[:, 0, :]
    length_f = lengths.astype(F32).reshape(chunks, rows, 1)
    ends = jnp.cumsum(lengths, axis=-1)

    shards = [w_unit] + [lax.ppermute(w_unit, "segment", [(j, last)]) for j in range(last)]
    part_ids = jnp.arange(vocab_part, dtype=jnp.int32)
    head_counts = [
        unit_counts(ends, unit_targets, (j * mp_size + mp_at) * vocab_part + part_ids).reshape(
            chunks, rows, vocab_part
        )
        for j in [last, *range(last)]
    ]
    own_ids = (seg * mp_size + mp_at) * vocab_part + part_ids

    def around(block):
        came = [block]
        for distance in range(1, dp_size):
            route = [(i, (i + distance) % dp_size) for i in range(dp_size)]
            came.append(lax.ppermute(block, "dp", route))
        return came

    own_counts = [
        unit_counts(packed[:, unit_count:], packed[:, :unit_count], own_ids).reshape(
            micro * row_count, vocab_part
        )
        for packed in around(jnp.concatenate([unit_targets, ends], axis=1))
    ]

    def both(part):
        return [part, swapped(part)] if pair else [part]

    def reduced(keep, send):
        return [keep, swapped(send[0])] if pair else [lax.psum(keep, "mp")]

    def mp_pieces(part):
        return [part, swapped(part)] if pair else [lax.psum(part, "mp")]

    def mp_tables(stats):
        if pair:
            return [stats, swapped(stats)]
        return [t for t in lax.all_gather(stats, "mp")]

    def gathered_rows(mine):
        came = lax.all_gather(mine, "dp")
        return [came, swapped(came)] if pair else [came]

    stash, x_halves, grads, finals, results, sent = [], [], [], [], [], []
    sums = None
    x_gathered = None
    f_hop = b_hop = None

    def x_parts(at):
        return [
            (source, lambda j, s, k=k: (k, at, 0, 0))
            for source in x_gathered
            for k in range(dp_size)
        ]

    def g_parts(sources):
        return [
            (source, lambda j, s, k=k: (k, 0, 0)) for source in sources for k in range(dp_size)
        ]

    clocks = 2 * segments + chunks - 1
    for clock in range(clocks):
        f_out = b_out = None
        if clock < segments + chunks - 1:
            own = text[min(clock, chunks - 1)]
            arrived = [own[: rows // halves]] * halves
            if clock > 0:
                arrived = both(shifted(f_hop, "segment", 1))
            rows_in, mine, keep, *send = forward_section(where, own, arrived, first, second)
            stash.append(rows_in)
            x_halves.append(mine)
            f_out = finish_forward(mine, reduced(keep, send))
        if clock >= segments:
            at = clock - segments
            arrived = None if at == 0 else both(shifted(b_hop, "segment", -1))
            if clock == segments + chunks:
                unit_rows = gathered_rows(
                    jnp.stack(
                        [
                            chosen(
                                seg,
                                [(last, finals[b][0])] + [(to, sent[b][to]) for to in range(last)],
                            )
                            for b in range(chunks)
                        ]
                    )
                )
            if clock < clocks - 1:
                parts = []
                final = None
                if at < chunks:
                    final = both(f_hop)
                    finals.append(final)
                    sent.append(
                        [lax.ppermute(f_hop, "segment", [(last, to)]) for to in range(last)]
                    )
                    logits, stats = head_logits(where, final, shards, head_counts, at)
                    part, result = head_grads(
                        where,
                        mp_tables(stats),
                        length_f,
                        logits,
                        head_counts,
                        at,
                        shards,
                        denom,
                        part_type,
                    )
                    results.append(result[:, 0:2])
                    parts = mp_pieces(part)
                options = []
                for other in range(segments):
                    stage = clock - 2 * segments + 1 + 2 * other
                    if 0 <= stage < len(stash):
                        options.append((other, stash[stage]))
                mine, g_mine, keep, *send = backward_section(
                    where, last, halves, options, final, parts, arrived, first, second
                )
                grads.append(g_mine)
                b_out = finish_backward(mine, g_mine, reduced(keep, send))
            else:
                grads.append(arrived[0])
        if clock == segments + chunks - 2:
            x_half = jnp.stack(
                [
                    chosen(seg, [(s, x_halves[b + s]) for s in range(segments)])
                    for b in range(chunks)
                ]
            )
            x_gathered = gathered_rows(x_half)
        if clock >= 2 * segments - 1:
            at = clock - 2 * segments + 1
            mine = chosen(seg, [(s, grads[at + last - s]) for s in range(segments)])
            sums = weight_grads(
                dp_at[None],
                x_parts(at),
                g_parts(gathered_rows(mine)),
                first,
                second,
                sums,
                width // dp_size,
            )
        f_hop, b_hop = f_out, b_out

    results = jnp.stack(results)
    results = chosen(
        seg,
        [(last, results)]
        + [(to, lax.ppermute(results, "segment", [(last, to)])) for to in range(last)],
    )
    loss = (jnp.sum(results[:, :, 1]) / denom)[None]
    shifts = around(results[:, :, 0].reshape(-1, 1))
    unit_parts = [
        (
            source,
            lambda j, s, k=k, b=b: (lax.rem(s[0] + dp_size - k, dp_size), b, 0, 0),
            ((k * chunks + b) * rows, bool(at) if pair else None),
        )
        for at, source in enumerate(unit_rows)
        for k in range(dp_size)
        for b in range(chunks)
    ]
    sum_unit = unit_grads(
        jnp.stack([dp_at, mp_at]), unit_parts, shifts, own_counts, w_unit, denom, width // dp_size
    )
    return (loss, sums[0][None], sums[1][None], sum_unit)


def solution(mesh):
    placed = (
        P(None, "dp", None),
        P(None, "dp", None),
        P(None, "dp"),
        P("segment", None, "mp"),
        P("segment", "mp", None),
        P(None, ("segment", "mp")),
    )
    return jax.shard_map(
        on_device,
        mesh=mesh,
        in_specs=placed,
        out_specs=(
            P("dp"),
            P("segment", "dp", "mp"),
            P("segment", "mp", "dp"),
            P("dp", ("segment", "mp")),
        ),
        check_vma=False,
    )
```

```python
import functools
import jax
import jax.numpy as jnp
from jax import lax
from jax.experimental import pallas as pl
from jax.experimental.pallas import tpu as pltpu
from jax.sharding import PartitionSpec as P

CHUNKS = 2
VMEM_MIB = 58
BF16 = jnp.bfloat16
F32 = jnp.float32
MIB = 1024 * 1024


def shifted(block, axis, distance):
    devices = range(lax.axis_size(axis))
    route = [(i - distance, i) for i in devices if i - distance in devices]
    return lax.ppermute(block, axis, route)


def swapped(block):
    return lax.ppermute(block, "mp", [(0, 1), (1, 0)])


def gelu_parts(pre_vals):
    coeff = 0.7978845608
    square = pre_vals * pre_vals
    inner = coeff * pre_vals * (1.0 + 0.044715 * square)
    half = 0.5 * (1.0 + jnp.tanh(inner))
    value = pre_vals * half
    slope = half + 2.0 * value * (1.0 - half) * coeff * (1.0 + 3.0 * 0.044715 * square)
    return (value, slope)


def row_scale(rows_in):
    floats = rows_in.astype(F32)
    return lax.rsqrt(jnp.mean(floats * floats, axis=-1, keepdims=True) + 1e-06)


def normalised(rows_in):
    return (rows_in.astype(F32) * row_scale(rows_in)).astype(BF16)


def norm_back(rows_in, grads):
    scale = row_scale(rows_in)
    normal = rows_in.astype(F32) * scale
    return scale * (grads - normal * jnp.mean(grads * normal, axis=-1, keepdims=True))


def dot(a, b):
    return jnp.dot(a, b, preferred_element_type=F32)


def dot_t(a, b):
    return lax.dot_general(a, b, (((1,), (1,)), ((), ())), preferred_element_type=F32)


def t_dot(a, b):
    return lax.dot_general(a, b, (((0,), (0,)), ((), ())), preferred_element_type=F32)


def tile_of(size, most):
    if size <= most:
        return size
    return max(t for t in range(128, most + 1, 128) if size % t == 0)


def pieces_of(size):
    return [(at, min(256, size - at)) for at in range(0, size, 256)]


def cost(flops, bytes_accessed, transcendentals):
    return pl.CostEstimate(
        flops=flops,
        bytes_accessed=bytes_accessed,
        transcendentals=transcendentals,
    )


def params(limit):
    return pltpu.CompilerParams(vmem_limit_bytes=limit * MIB)


def chosen(index, candidates):
    value = candidates[0][1]
    for at, option in candidates[1:]:
        value = jnp.where(index == at, option, value)
    return value


def gathered(halves, place):
    if len(halves) == 1:
        return halves[0][...]
    mine, theirs = (half[...] for half in halves)
    first = jnp.where(place == 0, mine, theirs)
    second = jnp.where(place == 0, theirs, mine)
    return jnp.concatenate([first, second], axis=0)


def part_of(block, place, parts):
    rows = block.shape[0] // parts
    if parts == 1:
        return block[...]
    return block[pl.ds(pl.multiple_of(place * rows, rows), rows), :]


def whole_spec(shape):
    return pl.BlockSpec(shape, lambda *_: (0,) * len(shape))


def forward_kernel(halves, has_arrived, where, own, *refs):
    if has_arrived:
        arrived, refs = refs[:halves], refs[halves:]
    w_in, w_out, rows_out, mine_out, keep, *send, whole, normed, total = refs
    step = pl.program_id(0)

    @pl.when(step == 0)
    def _():
        rows = own[...]
        if has_arrived:
            rows = jnp.where(where[0] == 0, rows, gathered(arrived, where[1]))
        rows_out[...] = rows
        whole[...] = rows
        mine_out[...] = part_of(whole, where[1], halves)
        normed[...] = normalised(rows)
        total[...] = jnp.zeros_like(total)

    values = []
    for at, size in pieces_of(w_in.shape[1]):
        value, _ = gelu_parts(dot(normed[...], w_in[:, at : at + size]))
        values.append(value.astype(BF16))
    total[...] += dot(jnp.concatenate(values, axis=1), w_out[...])

    @pl.when(step == pl.num_programs(0) - 1)
    def _():
        if send:
            keep[...] = part_of(total, where[1], 2) + part_of(whole, where[1], 2).astype(F32)
            send[0][...] = part_of(total, 1 - where[1], 2).astype(send[0].dtype)
        else:
            keep[...] = total[...]


def forward_section(where, text, at, halves, arrived, w_in, w_out):
    _, rows, width = text.shape
    hidden = w_in.shape[1]
    tile = tile_of(hidden, 1024)
    full, part = (rows, width), (rows // halves, width)
    shapes = [(full, BF16), (part, BF16), (part, F32)] + [(part, BF16)] * (halves - 1)
    return pl.pallas_call(
        functools.partial(forward_kernel, halves, bool(arrived)),
        grid_spec=pltpu.PrefetchScalarGridSpec(
            num_scalar_prefetch=1,
            grid=(hidden // tile,),
            in_specs=[
                pl.BlockSpec((None, rows, width), lambda j, s: (at, 0, 0)),
                *[whole_spec(part)] * len(arrived),
                pl.BlockSpec((width, tile), lambda j, s: (0, j)),
                pl.BlockSpec((tile, width), lambda j, s: (j, 0)),
            ],
            out_specs=[whole_spec(shape) for shape, _ in shapes],
            scratch_shapes=[pltpu.VMEM(full, BF16), pltpu.VMEM(full, BF16), pltpu.VMEM(full, F32)],
        ),
        out_shape=[jax.ShapeDtypeStruct(*shape) for shape in shapes],
        compiler_params=params(VMEM_MIB),
        cost_estimate=cost(
            flops=4 * rows * width * hidden,
            bytes_accessed=4 * width * hidden,
            transcendentals=rows * hidden,
        ),
        name="section_forward",
    )(where, text, *arrived, w_in, w_out)


def total_of(pieces):
    total = pieces[0].astype(F32)
    for piece in pieces[1:]:
        total = total + piece.astype(F32)
    return total


def finish_backward(rows, grads, pieces):
    return (grads.astype(F32) + norm_back(rows, total_of(pieces))).astype(BF16)


def backward_kernel(owners, halves, where, *refs):
    stashed, refs = refs[: len(owners)], refs[len(owners) :]
    arrived, refs = refs[:halves], refs[halves:]
    w_in, w_out, mine_rows, keep, *send, rows, grads, normed, total = refs
    step = pl.program_id(0)

    @pl.when(step == 0)
    def _():
        rows[...] = chosen(where[0], [(at, ref[...]) for at, ref in zip(owners, stashed)])
        grads[...] = gathered(arrived, where[1])
        mine_rows[...] = part_of(rows, where[1], halves)
        normed[...] = normalised(rows[...])
        total[...] = jnp.zeros_like(total)

    dpres = []
    for at, size in pieces_of(w_in.shape[1]):
        _, slope = gelu_parts(dot(normed[...], w_in[:, at : at + size]))
        dpres.append((dot_t(grads[...], w_out[at : at + size, :]) * slope).astype(BF16))
    total[...] += dot_t(jnp.concatenate(dpres, axis=1), w_in[...])

    @pl.when(step == pl.num_programs(0) - 1)
    def _():
        if send:
            keep[...] = part_of(total, where[1], 2)
            send[0][...] = part_of(total, 1 - where[1], 2).astype(send[0].dtype)
        else:
            keep[...] = total[...]


def backward_section(where, halves, options, arrived, w_in, w_out):
    width, hidden = w_in.shape
    rows = options[0][1].shape[0]
    tile = tile_of(hidden, 1024)
    full, part = (rows, width), (rows // halves, width)
    shapes = [(part, BF16), (part, F32)] + [(part, BF16)] * (halves - 1)
    return pl.pallas_call(
        functools.partial(backward_kernel, tuple(at for at, _ in options), halves),
        grid_spec=pltpu.PrefetchScalarGridSpec(
            num_scalar_prefetch=1,
            grid=(hidden // tile,),
            in_specs=[whole_spec(full)] * len(options)
            + [whole_spec(part)] * halves
            + [
                pl.BlockSpec((width, tile), lambda j, s: (0, j)),
                pl.BlockSpec((tile, width), lambda j, s: (j, 0)),
            ],
            out_specs=[whole_spec(shape) for shape, _ in shapes],
            scratch_shapes=[pltpu.VMEM(full, BF16)] * 3 + [pltpu.VMEM(full, F32)],
        ),
        out_shape=[jax.ShapeDtypeStruct(*shape) for shape in shapes],
        compiler_params=params(VMEM_MIB),
        cost_estimate=cost(
            flops=6 * rows * width * hidden,
            bytes_accessed=4 * width * hidden,
            transcendentals=rows * hidden,
        ),
        name="section_backward",
    )(where, *[option for _, option in options], *arrived, w_in, w_out)


def lane_fill(columns, shape):
    lane = lax.broadcasted_iota(jnp.int32, shape, 1)
    filled = jnp.zeros(shape, F32)
    for at, column in enumerate(columns):
        filled = jnp.where(lane == at, column, filled)
    return filled


def logits_kernel(halves, where, *refs):
    final, refs = refs[:halves], refs[halves:]
    w_unit, counts, logits, stats, normed, peak, total, target = refs
    step = pl.program_id(0)
    lanes = peak.shape[1]

    @pl.when(step == 0)
    def _():
        normed[...] = normalised(gathered(final, where[1]))
        peak[...] = jnp.full_like(peak, -1e30)
        total[...] = jnp.zeros_like(total)
        target[...] = jnp.zeros_like(target)

    columns = []
    for start, size in pieces_of(w_unit.shape[1]):
        values = dot(normed[...], w_unit[:, start : start + size])
        logits[:, start : start + size] = values
        counted = counts[:, start : start + size].astype(F32) * values
        columns += [
            (values[:, c : c + lanes], counted[:, c : c + lanes]) for c in range(0, size, lanes)
        ]
    higher = peak[...]
    for values, _ in columns:
        higher = jnp.maximum(higher, values)
    mass = total[...] * jnp.exp(peak[...] - higher)
    summed = target[...]
    for values, counted in columns:
        mass = mass + jnp.exp(values - higher)
        summed = summed + counted
    peak[...] = higher
    total[...] = mass
    target[...] = summed

    @pl.when(step == pl.num_programs(0) - 1)
    def _():
        top = jnp.max(peak[...], axis=-1, keepdims=True)
        mass = jnp.sum(total[...] * jnp.exp(peak[...] - top), axis=-1, keepdims=True)
        summed = jnp.sum(target[...], axis=-1, keepdims=True)
        stats[...] = lane_fill([top, mass, summed], stats.shape)


def head_logits(where, final, w_unit, counts, at):
    halves = len(final)
    half, width = final[0].shape
    rows = half * halves
    vocab = w_unit.shape[1]
    lanes = 128 if vocab % 128 == 0 else vocab
    tile = tile_of(vocab, 640)
    return pl.pallas_call(
        functools.partial(logits_kernel, halves),
        grid_spec=pltpu.PrefetchScalarGridSpec(
            num_scalar_prefetch=1,
            grid=(vocab // tile,),
            in_specs=[
                *[whole_spec((half, width))] * halves,
                pl.BlockSpec((width, tile), lambda t, s: (0, t)),
                pl.BlockSpec((None, rows, tile), lambda t, s: (at, 0, t)),
            ],
            out_specs=[
                pl.BlockSpec((rows, tile), lambda t, s: (0, t)),
                whole_spec((rows, 128)),
            ],
            scratch_shapes=[pltpu.VMEM((rows, width), BF16)] + [pltpu.VMEM((rows, lanes), F32)] * 3,
        ),
        out_shape=[
            jax.ShapeDtypeStruct((rows, vocab), F32),
            jax.ShapeDtypeStruct((rows, 128), F32),
        ],
        compiler_params=params(VMEM_MIB),
        cost_estimate=cost(
            flops=2 * rows * width * vocab,
            bytes_accessed=(2 * width + 6 * rows) * vocab,
            transcendentals=rows * vocab,
        ),
        name="head_logits",
    )(where, *final, w_unit, counts)


def head_grads_kernel(denom, halves, where, *refs):
    stats, lengths, logits, counts, w_unit, keep, *send, results, shift, total = refs
    step = pl.program_id(0)

    @pl.when(step == 0)
    def _():
        values = [stats[at] for at in range(stats.shape[0])]
        top = values[0][:, 0:1]
        for table in values[1:]:
            top = jnp.maximum(top, table[:, 0:1])
        mass = sum(table[:, 1:2] * jnp.exp(table[:, 0:1] - top) for table in values)
        target = sum(table[:, 2:3] for table in values)
        lse = top + jnp.log(mass)
        shift[...] = lse - jnp.log(lengths[...] * (1.0 / denom))
        results[...] = lane_fill([shift[...], lengths[...] * lse - target], results.shape)
        total[...] = jnp.zeros_like(total)

    columns = []
    for start, size in pieces_of(w_unit.shape[1]):
        exped = jnp.exp(logits[:, start : start + size] - shift[...])
        counted = counts[:, start : start + size].astype(F32) * (1.0 / denom)
        columns.append((exped - counted).astype(BF16))
    total[...] += dot_t(jnp.concatenate(columns, axis=1), w_unit[...])

    @pl.when(step == pl.num_programs(0) - 1)
    def _():
        if send:
            keep[...] = part_of(total, where[1], 2)
            send[0][...] = part_of(total, 1 - where[1], 2).astype(send[0].dtype)
        else:
            keep[...] = total[...]


def head_grads(where, halves, stats, lengths, logits, counts, at, w_unit, denom):
    rows, vocab = logits.shape
    width = w_unit.shape[0]
    tile = tile_of(vocab, 640)
    part = (rows // halves, width)
    shapes = [(part, F32)] + [(part, BF16)] * (halves - 1) + [((rows, 128), F32)]
    return pl.pallas_call(
        functools.partial(head_grads_kernel, denom, halves),
        grid_spec=pltpu.PrefetchScalarGridSpec(
            num_scalar_prefetch=1,
            grid=(vocab // tile,),
            in_specs=[
                whole_spec(stats.shape),
                pl.BlockSpec((None, rows, 1), lambda t, s: (at, 0, 0)),
                pl.BlockSpec((rows, tile), lambda t, s: (0, t)),
                pl.BlockSpec((None, rows, tile), lambda t, s: (at, 0, t)),
                pl.BlockSpec((width, tile), lambda t, s: (0, t)),
            ],
            out_specs=[whole_spec(shape) for shape, _ in shapes],
            scratch_shapes=[pltpu.VMEM((rows, 1), F32), pltpu.VMEM((rows, width), F32)],
        ),
        out_shape=[jax.ShapeDtypeStruct(*shape) for shape in shapes],
        compiler_params=params(VMEM_MIB),
        cost_estimate=cost(
            flops=2 * rows * width * vocab,
            bytes_accessed=(2 * width + 6 * rows) * vocab,
            transcendentals=rows * vocab,
        ),
        name="head_grads",
    )(where, stats, lengths, logits, counts, w_unit)


def unit_kernel(blocks, tables, share, denom, where, *refs):
    x_refs, refs = refs[: len(blocks)], refs[len(blocks) :]
    shifts, refs = refs[:tables], refs[tables:]
    counts, refs = refs[:tables], refs[tables:]
    w_unit, grad, normed, normed_t = refs
    half = x_refs[0].shape[0]
    rows = normed.shape[0] // tables

    @pl.when(pl.program_id(0) == 0)
    def _():
        for ref, (base, theirs) in zip(x_refs, blocks):
            side = 0
            if theirs is not None:
                side = 1 - where[1] if theirs else where[1]
            place = pl.ds(pl.multiple_of(base + side * half, half), half)
            normed[place, :] = normalised(ref[...])
        columns = pl.ds(pl.multiple_of(where[0] * share, share), share)
        normed_t[...] = normed[:, columns].astype(F32).T.astype(BF16)

    logits = dot(normed[...], w_unit[...])
    dlogits = []
    for k in range(tables):
        exped = jnp.exp(logits[k * rows : (k + 1) * rows] - shifts[k][...])
        counted = counts[k][...].astype(F32) * (1.0 / denom)
        dlogits.append((exped - counted).astype(BF16))
    grad[...] = dot(normed_t[...], jnp.concatenate(dlogits, axis=0))


def unit_grads(where, x_parts, shifts, counts, w_unit, denom, share):
    width, vocab = w_unit.shape
    tile = tile_of(vocab, 256)
    half = x_parts[0][0].shape[2]
    rows = shifts[0].shape[0]
    tables = len(shifts)
    blocks = tuple(block for _, _, block in x_parts)
    return pl.pallas_call(
        functools.partial(unit_kernel, blocks, tables, share, denom),
        grid_spec=pltpu.PrefetchScalarGridSpec(
            num_scalar_prefetch=1,
            grid=(vocab // tile,),
            in_specs=[pl.BlockSpec((None, None, half, width), index) for _, index, _ in x_parts]
            + [whole_spec((rows, 1))] * tables
            + [pl.BlockSpec((rows, tile), lambda j, s: (0, j))] * tables
            + [pl.BlockSpec((width, tile), lambda j, s: (0, j))],
            out_specs=pl.BlockSpec((share, tile), lambda j, s: (0, j)),
            scratch_shapes=[
                pltpu.VMEM((rows * tables, width), BF16),
                pltpu.VMEM((share, rows * tables), BF16),
            ],
        ),
        out_shape=jax.ShapeDtypeStruct((share, vocab), F32),
        compiler_params=params(VMEM_MIB),
        cost_estimate=cost(
            flops=2 * rows * tables * (width + share) * vocab,
            bytes_accessed=2 * (width + rows * tables) * vocab,
            transcendentals=rows * tables * vocab,
        ),
        name="unit_grads",
    )(where, *[x for x, _, _ in x_parts], *shifts, *counts, w_unit)


def weight_kernel(blocks, adding, share, where, *refs):
    x_refs, refs = refs[:blocks], refs[blocks:]
    g_refs, refs = refs[:blocks], refs[blocks:]
    w_in, w_out, refs = refs[0], refs[1], refs[2:]
    if adding:
        old_first, old_second, refs = refs[0], refs[1], refs[2:]
    first, second, normed, grads, normed_t, grads_t = refs
    count = x_refs[0].shape[0]

    @pl.when(pl.program_id(0) == 0)
    def _():
        columns = pl.ds(pl.multiple_of(where[0] * share, share), share)
        for at in range(blocks):
            place = pl.ds(at * count, count)
            normed[place, :] = normalised(x_refs[at][...])
            grads[place, :] = g_refs[at][...]
        normed_t[...] = normed[:, columns].astype(F32).T.astype(BF16)
        grads_t[...] = grads[:, columns].astype(F32).T.astype(BF16)

    for at, size in pieces_of(w_in.shape[1]):
        value, slope = gelu_parts(dot(normed[...], w_in[:, at : at + size]))
        dpre = (dot_t(grads[...], w_out[at : at + size, :]) * slope).astype(BF16)
        now_first = dot(normed_t[...], dpre)
        now_second = dot(grads_t[...], value.astype(BF16)).T
        if adding:
            now_first = old_first[:, at : at + size] + now_first
            now_second = old_second[at : at + size, :] + now_second
        first[:, at : at + size] = now_first
        second[at : at + size, :] = now_second


def weight_grads(where, x_parts, g_parts, w_in, w_out, old, share):
    width, hidden = w_in.shape
    tile = tile_of(hidden, 512)
    blocks = len(g_parts)
    count = g_parts[0][0].shape[1]
    rows = blocks * count
    in_specs = [pl.BlockSpec((None, None, count, width), index) for _, index in x_parts]
    in_specs += [pl.BlockSpec((None, count, width), index) for _, index in g_parts]
    in_specs += [
        pl.BlockSpec((width, tile), lambda j, s: (0, j)),
        pl.BlockSpec((tile, width), lambda j, s: (j, 0)),
    ]
    grad_specs = [
        pl.BlockSpec((share, tile), lambda j, s: (0, j)),
        pl.BlockSpec((tile, share), lambda j, s: (j, 0)),
    ]
    adding = old is not None
    aliases = {}
    if adding:
        in_specs += grad_specs
        aliases = {1 + 2 * blocks + 2: 0, 1 + 2 * blocks + 3: 1}
    return pl.pallas_call(
        functools.partial(weight_kernel, blocks, adding, share),
        grid_spec=pltpu.PrefetchScalarGridSpec(
            num_scalar_prefetch=1,
            grid=(hidden // tile,),
            in_specs=in_specs,
            out_specs=grad_specs,
            scratch_shapes=[
                pltpu.VMEM((rows, width), BF16),
                pltpu.VMEM((rows, width), BF16),
                pltpu.VMEM((share, rows), BF16),
                pltpu.VMEM((share, rows), BF16),
            ],
        ),
        out_shape=[
            jax.ShapeDtypeStruct((share, hidden), F32),
            jax.ShapeDtypeStruct((hidden, share), F32),
        ],
        input_output_aliases=aliases,
        compiler_params=params(VMEM_MIB),
        cost_estimate=cost(
            flops=4 * rows * (width + share) * hidden,
            bytes_accessed=4 * width * hidden + 16 * share * hidden,
            transcendentals=rows * hidden,
        ),
        name="weight_grads",
    )(where, *[x for x, _ in x_parts], *[g for g, _ in g_parts], w_in, w_out, *(old or ()))


def unit_counts(ends, targets, ids):
    positions = jnp.arange(targets.shape[1], dtype=jnp.int32)
    row_local = jnp.sum((ends[:, None, :] <= positions[None, :, None]).astype(jnp.int32), axis=-1)
    rows = jnp.arange(ends.shape[1], dtype=jnp.int32)
    row_onehot = (row_local[:, :, None] == rows[None, None, :]).astype(BF16)
    hits = (targets[:, :, None] == ids[None, None, :]).astype(BF16)
    counts = jnp.einsum("mur,muv->mrv", row_onehot, hits, preferred_element_type=F32)
    return counts.astype(BF16)


def on_device(text_rows, durations, unit_targets, w_in, w_out, w_unit):
    micro, row_count, width = text_rows.shape
    segments = lax.axis_size("segment")
    mp_size = lax.axis_size("mp")
    dp_size = lax.axis_size("dp")
    seg = lax.axis_index("segment").astype(jnp.int32)
    mp_at = lax.axis_index("mp").astype(jnp.int32)
    dp_at = lax.axis_index("dp").astype(jnp.int32)
    last = segments - 1
    pair = mp_size == 2
    halves = 2 if pair else 1
    where = jnp.stack([seg, mp_at])
    first = w_in[0]
    second = w_out[0]
    chunks = CHUNKS
    rows = micro * row_count // chunks
    text = text_rows.reshape(chunks, rows, width)
    vocab_part = w_unit.shape[1]
    unit_count = unit_targets.shape[1]
    denom = float(micro * unit_count * dp_size)
    lengths = durations[:, 0, :]
    length_f = lengths.astype(F32).reshape(chunks, rows, 1)
    ends = jnp.cumsum(lengths, axis=-1)
    own_ids = (seg * mp_size + mp_at) * vocab_part + jnp.arange(vocab_part, dtype=jnp.int32)

    def around(block):
        came = [block]
        for distance in range(1, dp_size):
            route = [(i, (i + distance) % dp_size) for i in range(dp_size)]
            came.append(lax.ppermute(block, "dp", route))
        return came

    unit_hits = [
        unit_counts(packed[:, unit_count:], packed[:, :unit_count], own_ids)
        for packed in around(jnp.concatenate([unit_targets, ends], axis=1))
    ]
    head_counts = unit_hits[0].reshape(chunks, rows, vocab_part)
    unit_hits = [hits.reshape(micro * row_count, vocab_part) for hits in unit_hits]

    def both(part):
        return [part, swapped(part)] if pair else [part]

    def reduced(keep, send):
        return [keep, swapped(send[0])] if pair else [lax.psum(keep, "mp")]

    def gathered_rows(mine):
        came = lax.all_gather(mine, "dp")
        return [came, swapped(came)] if pair else [came]

    stash, x_halves, grads, finals, results = [], [], [], [], []
    sums = None
    x_gathered = None
    f_hop = b_hop = None

    def x_parts(at):
        return [
            (source, lambda j, s, k=k: (k, at, 0, 0))
            for source in x_gathered
            for k in range(dp_size)
        ]

    def g_parts(sources):
        return [
            (source, lambda j, s, k=k: (k, 0, 0)) for source in sources for k in range(dp_size)
        ]

    clocks = 2 * segments + chunks - 1
    for clock in range(clocks):
        f_out = b_out = None
        if clock < segments + chunks - 1:
            arrived = [] if clock == 0 else both(shifted(f_hop, "segment", 1))
            rows_in, mine, keep, *send = forward_section(
                where, text, min(clock, chunks - 1), halves, arrived, first, second
            )
            stash.append(rows_in)
            x_halves.append(mine)
            pieces = reduced(keep, send)
            f_out = total_of(pieces if pair else [mine, *pieces]).astype(BF16)
        if clock >= segments:
            at = clock - segments
            arrived = None if at == 0 else shifted(b_hop, "segment", -1)
            if at < chunks:
                final = chosen(
                    seg,
                    [(last, f_hop)]
                    + [(to, lax.ppermute(f_hop, "segment", [(last, to)])) for to in range(last)],
                )
                finals.append(final)
                logits, stats = head_logits(where, both(final), w_unit, head_counts, at)
                tables = lax.all_gather(stats[:, 0:3], ("segment", "mp"))
                keep, *send, result = head_grads(
                    where, halves, tables, length_f, logits, head_counts, at, w_unit, denom
                )
                results.append(result[:, 0:2])
                dnorm = total_of(reduced(keep, send)).astype(BF16)
                dnorm = total_of(
                    [dnorm]
                    + [lax.ppermute(dnorm, "segment", [(j, last)]) for j in range(last)]
                ).astype(BF16)
                grad_final = norm_back(final, dnorm.astype(F32)).astype(BF16)
                arrived = (
                    grad_final if arrived is None else jnp.where(seg == last, grad_final, arrived)
                )
            grads.append(arrived)
            if clock < clocks - 1:
                options = []
                for other in range(segments):
                    stage = clock - 2 * segments + 1 + 2 * other
                    if 0 <= stage < len(stash):
                        options.append((other, stash[stage]))
                mine, keep, *send = backward_section(
                    where, halves, options, both(arrived), first, second
                )
                b_out = finish_backward(mine, arrived, reduced(keep, send))
        if clock == segments + chunks - 2:
            x_half = jnp.stack(
                [
                    chosen(seg, [(s, x_halves[b + s]) for s in range(segments)])
                    for b in range(chunks)
                ]
            )
            x_gathered = gathered_rows(x_half)
        if clock == segments + chunks - 1:
            unit_rows = gathered_rows(jnp.stack(finals))
        if clock >= 2 * segments - 1:
            at = clock - 2 * segments + 1
            mine = chosen(seg, [(s, grads[at + last - s]) for s in range(segments)])
            sums = weight_grads(
                dp_at[None],
                x_parts(at),
                g_parts(gathered_rows(mine)),
                first,
                second,
                sums,
                width // dp_size,
            )
        f_hop, b_hop = f_out, b_out

    results = jnp.stack(results)
    loss = (jnp.sum(results[:, :, 1]) / denom)[None]
    shifts = around(results[:, :, 0].reshape(-1, 1))
    unit_parts = [
        (
            source,
            lambda j, s, k=k, b=b: (lax.rem(s[0] + dp_size - k, dp_size), b, 0, 0),
            ((k * chunks + b) * rows, bool(at) if pair else None),
        )
        for at, source in enumerate(unit_rows)
        for k in range(dp_size)
        for b in range(chunks)
    ]
    sum_unit = unit_grads(
        jnp.stack([dp_at, mp_at]), unit_parts, shifts, unit_hits, w_unit, denom, width // dp_size
    )
    return (loss, sums[0][None], sums[1][None], sum_unit)


def solution(mesh):
    placed = (
        P(None, "dp", None),
        P(None, "dp", None),
        P(None, "dp"),
        P("segment", None, "mp"),
        P("segment", "mp", None),
        P(None, ("segment", "mp")),
    )
    return jax.shard_map(
        on_device,
        mesh=mesh,
        in_specs=placed,
        out_specs=(
            P("dp"),
            P("segment", "dp", "mp"),
            P("segment", "mp", "dp"),
            P("dp", ("segment", "mp")),
        ),
        check_vma=False,
    )
```

```python
import functools
import jax
import jax.numpy as jnp
from jax import lax
from jax.experimental import pallas as pl
from jax.experimental.pallas import tpu as pltpu
from jax.sharding import PartitionSpec as P

CHUNKS = 2
VMEM_MIB = 58
BF16 = jnp.bfloat16
F32 = jnp.float32
MIB = 1024 * 1024


def shifted(block, axis, distance):
    devices = range(lax.axis_size(axis))
    route = [(i - distance, i) for i in devices if i - distance in devices]
    return lax.ppermute(block, axis, route)


def swapped(block):
    return lax.ppermute(block, "mp", [(0, 1), (1, 0)])


def gelu_parts(pre_vals):
    coeff = 0.7978845608
    pre = pre_vals.astype(BF16)
    square = pre * pre
    inner = pre * (square * BF16(coeff * 0.044715) + BF16(coeff))
    half = jnp.tanh(inner) * BF16(0.5) + BF16(0.5)
    value = pre * half
    bend = square * BF16(6.0 * coeff * 0.044715) + BF16(2.0 * coeff)
    slope = half + value * (BF16(1.0) - half) * bend
    return (value, slope)


def row_scale(rows_in):
    floats = rows_in.astype(F32)
    return lax.rsqrt(jnp.mean(floats * floats, axis=-1, keepdims=True) + 1e-06)


def normalised(rows_in):
    return (rows_in.astype(F32) * row_scale(rows_in)).astype(BF16)


def norm_back(rows_in, grads):
    scale = row_scale(rows_in)
    normal = rows_in.astype(F32) * scale
    return scale * (grads - normal * jnp.mean(grads * normal, axis=-1, keepdims=True))


def dot(a, b):
    return jnp.dot(a, b, preferred_element_type=F32)


def dot_t(a, b):
    return lax.dot_general(a, b, (((1,), (1,)), ((), ())), preferred_element_type=F32)


def t_dot(a, b):
    return lax.dot_general(a, b, (((0,), (0,)), ((), ())), preferred_element_type=F32)


def tile_of(size, most):
    if size <= most:
        return size
    return max(t for t in range(128, most + 1, 128) if size % t == 0)


def pieces_of(size):
    return [(at, min(256, size - at)) for at in range(0, size, 256)]


def cost(flops, bytes_accessed, transcendentals):
    return pl.CostEstimate(
        flops=flops,
        bytes_accessed=bytes_accessed,
        transcendentals=transcendentals,
    )


def params(limit):
    return pltpu.CompilerParams(vmem_limit_bytes=limit * MIB)


def chosen(index, candidates):
    value = candidates[0][1]
    for at, option in candidates[1:]:
        value = jnp.where(index == at, option, value)
    return value


def gathered(halves, place):
    if len(halves) == 1:
        return halves[0][...]
    mine, theirs = (half[...] for half in halves)
    first = jnp.where(place == 0, mine, theirs)
    second = jnp.where(place == 0, theirs, mine)
    return jnp.concatenate([first, second], axis=0)


def part_of(block, place, parts):
    rows = block.shape[0] // parts
    if parts == 1:
        return block[...]
    return block[pl.ds(pl.multiple_of(place * rows, rows), rows), :]


def whole_spec(shape):
    return pl.BlockSpec(shape, lambda *_: (0,) * len(shape))


def forward_kernel(halves, has_arrived, ties, where, own, *refs):
    refs = refs[ties:]
    if has_arrived:
        arrived, refs = refs[:halves], refs[halves:]
    live = where[2] == 1
    w_in, w_out, rows_out, mine_out, keep, *send, whole, normed, total = refs
    step = pl.program_id(0)

    @pl.when(step == 0)
    def _():
        rows = own[...]
        if has_arrived:
            rows = jnp.where(where[0] == 0, rows, gathered(arrived, where[1]))
        rows_out[...] = rows
        whole[...] = rows
        mine_out[...] = part_of(whole, where[1], halves)
        normed[...] = normalised(rows)
        total[...] = jnp.zeros_like(total)

    @pl.when(live)
    def _():
        values = []
        for at, size in pieces_of(w_in.shape[1]):
            value, _ = gelu_parts(dot(normed[...], w_in[:, at : at + size]))
            values.append(value)
        total[...] += dot(jnp.concatenate(values, axis=1), w_out[...])

    @pl.when(step == pl.num_programs(0) - 1)
    def _():
        if send:
            keep[...] = part_of(total, where[1], 2) + part_of(whole, where[1], 2).astype(F32)
            send[0][...] = part_of(total, 1 - where[1], 2).astype(send[0].dtype)
        else:
            keep[...] = total[...]


def forward_section(where, text, at, halves, arrived, w_in, w_out, ties):
    _, rows, width = text.shape
    hidden = w_in.shape[1]
    tile = tile_of(hidden, 1024)
    full, part = (rows, width), (rows // halves, width)
    shapes = [(full, BF16), (part, BF16), (part, F32)] + [(part, BF16)] * (halves - 1)
    return pl.pallas_call(
        functools.partial(forward_kernel, halves, bool(arrived), len(ties)),
        grid_spec=pltpu.PrefetchScalarGridSpec(
            num_scalar_prefetch=1,
            grid=(hidden // tile,),
            in_specs=[
                pl.BlockSpec((None, rows, width), lambda j, s: (at, 0, 0)),
                *[pl.BlockSpec(memory_space=pl.ANY)] * len(ties),
                *[whole_spec(part)] * len(arrived),
                pl.BlockSpec((width, tile), lambda j, s: (0, j * s[2])),
                pl.BlockSpec((tile, width), lambda j, s: (j * s[2], 0)),
            ],
            out_specs=[whole_spec(shape) for shape, _ in shapes],
            scratch_shapes=[pltpu.VMEM(full, BF16), pltpu.VMEM(full, BF16), pltpu.VMEM(full, F32)],
        ),
        out_shape=[jax.ShapeDtypeStruct(*shape) for shape in shapes],
        compiler_params=params(VMEM_MIB),
        cost_estimate=cost(
            flops=4 * rows * width * hidden,
            bytes_accessed=4 * width * hidden,
            transcendentals=rows * hidden,
        ),
        name="section_forward",
    )(where, text, *ties, *arrived, w_in, w_out)


def total_of(pieces):
    total = pieces[0].astype(F32)
    for piece in pieces[1:]:
        total = total + piece.astype(F32)
    return total


def finish_backward(rows, grads, pieces):
    return (grads.astype(F32) + norm_back(rows, total_of(pieces))).astype(BF16)


def backward_kernel(owners, halves, ties, where, *refs):
    refs = refs[ties:]
    live = where[2] == 1
    stashed, refs = refs[: len(owners)], refs[len(owners) :]
    arrived, refs = refs[:halves], refs[halves:]
    w_in, w_out, mine_rows, keep, *send, rows, grads, normed, total = refs
    step = pl.program_id(0)

    @pl.when(step == 0)
    def _():
        rows[...] = chosen(where[0], [(at, ref[...]) for at, ref in zip(owners, stashed)])
        grads[...] = gathered(arrived, where[1])
        mine_rows[...] = part_of(rows, where[1], halves)
        normed[...] = normalised(rows[...])
        total[...] = jnp.zeros_like(total)

    @pl.when(live)
    def _():
        dpres = []
        for at, size in pieces_of(w_in.shape[1]):
            _, slope = gelu_parts(dot(normed[...], w_in[:, at : at + size]))
            dpres.append(dot_t(grads[...], w_out[at : at + size, :]).astype(BF16) * slope)
        total[...] += dot_t(jnp.concatenate(dpres, axis=1), w_in[...])

    @pl.when(step == pl.num_programs(0) - 1)
    def _():
        if send:
            keep[...] = part_of(total, where[1], 2)
            send[0][...] = part_of(total, 1 - where[1], 2).astype(send[0].dtype)
        else:
            keep[...] = total[...]


def backward_section(where, halves, options, arrived, w_in, w_out, ties):
    width, hidden = w_in.shape
    rows = options[0][1].shape[0]
    tile = tile_of(hidden, 1024)
    full, part = (rows, width), (rows // halves, width)
    shapes = [(part, BF16), (part, F32)] + [(part, BF16)] * (halves - 1)
    return pl.pallas_call(
        functools.partial(backward_kernel, tuple(at for at, _ in options), halves, len(ties)),
        grid_spec=pltpu.PrefetchScalarGridSpec(
            num_scalar_prefetch=1,
            grid=(hidden // tile,),
            in_specs=[pl.BlockSpec(memory_space=pl.ANY)] * len(ties)
            + [whole_spec(full)] * len(options)
            + [whole_spec(part)] * halves
            + [
                pl.BlockSpec((width, tile), lambda j, s: (0, j * s[2])),
                pl.BlockSpec((tile, width), lambda j, s: (j * s[2], 0)),
            ],
            out_specs=[whole_spec(shape) for shape, _ in shapes],
            scratch_shapes=[pltpu.VMEM(full, BF16)] * 3 + [pltpu.VMEM(full, F32)],
        ),
        out_shape=[jax.ShapeDtypeStruct(*shape) for shape in shapes],
        compiler_params=params(VMEM_MIB),
        cost_estimate=cost(
            flops=6 * rows * width * hidden,
            bytes_accessed=4 * width * hidden,
            transcendentals=rows * hidden,
        ),
        name="section_backward",
    )(where, *ties, *[option for _, option in options], *arrived, w_in, w_out)


def row_table(rows):
    pad = jnp.zeros((8 - len(rows), rows[0].shape[1]), F32)
    return jnp.concatenate([*rows, pad], axis=0)


def as_row(column):
    return jnp.broadcast_to(column, (column.shape[0], 128)).T[0:1, :]


def as_columns(row):
    return jnp.broadcast_to(row, (128, row.shape[1])).T


def logits_kernel(halves, where, *refs):
    final, refs = refs[:halves], refs[halves:]
    w_unit, counts, logits, stats, normed, peak, total, target = refs
    step = pl.program_id(0)
    lanes = peak.shape[1]

    @pl.when(step == 0)
    def _():
        normed[...] = normalised(gathered(final, where[1]))
        peak[...] = jnp.full_like(peak, -1e30)
        total[...] = jnp.zeros_like(total)
        target[...] = jnp.zeros_like(target)

    columns = []
    for start, size in pieces_of(w_unit.shape[1]):
        values = dot(normed[...], w_unit[:, start : start + size])
        logits[:, start : start + size] = values
        counted = counts[:, start : start + size].astype(F32) * values
        columns += [
            (values[:, c : c + lanes], counted[:, c : c + lanes]) for c in range(0, size, lanes)
        ]
    higher = peak[...]
    for values, _ in columns:
        higher = jnp.maximum(higher, values)
    mass = total[...] * jnp.exp(peak[...] - higher)
    summed = target[...]
    for values, counted in columns:
        mass = mass + jnp.exp(values - higher)
        summed = summed + counted
    peak[...] = higher
    total[...] = mass
    target[...] = summed

    @pl.when(step == pl.num_programs(0) - 1)
    def _():
        top = jnp.max(peak[...], axis=-1, keepdims=True)
        mass = jnp.sum(total[...] * jnp.exp(peak[...] - top), axis=-1, keepdims=True)
        summed = jnp.sum(target[...], axis=-1, keepdims=True)
        stats[...] = row_table([as_row(top), as_row(mass), as_row(summed)])


def head_logits(where, final, w_unit, counts, at):
    halves = len(final)
    half, width = final[0].shape
    rows = half * halves
    vocab = w_unit.shape[1]
    lanes = 128 if vocab % 128 == 0 else vocab
    tile = tile_of(vocab, 640)
    return pl.pallas_call(
        functools.partial(logits_kernel, halves),
        grid_spec=pltpu.PrefetchScalarGridSpec(
            num_scalar_prefetch=1,
            grid=(vocab // tile,),
            in_specs=[
                *[whole_spec((half, width))] * halves,
                pl.BlockSpec((width, tile), lambda t, s: (0, t)),
                pl.BlockSpec((None, rows, tile), lambda t, s: (at, 0, t)),
            ],
            out_specs=[
                pl.BlockSpec((rows, tile), lambda t, s: (0, t)),
                whole_spec((8, rows)),
            ],
            scratch_shapes=[pltpu.VMEM((rows, width), BF16)] + [pltpu.VMEM((rows, lanes), F32)] * 3,
        ),
        out_shape=[
            jax.ShapeDtypeStruct((rows, vocab), F32),
            jax.ShapeDtypeStruct((8, rows), F32),
        ],
        compiler_params=params(VMEM_MIB),
        cost_estimate=cost(
            flops=2 * rows * width * vocab,
            bytes_accessed=(2 * width + 6 * rows) * vocab,
            transcendentals=rows * vocab,
        ),
        name="head_logits",
    )(where, *final, w_unit, counts)


def head_grads_kernel(denom, halves, tables, where, *refs):
    stats, refs = refs[:tables], refs[tables:]
    lengths, logits, counts, w_unit, keep, *send, results, shift, total = refs
    step = pl.program_id(0)

    @pl.when(step == 0)
    def _():
        values = [ref[...] for ref in stats]
        top = values[0][0:1, :]
        for table in values[1:]:
            top = jnp.maximum(top, table[0:1, :])
        mass = sum(table[1:2, :] * jnp.exp(table[0:1, :] - top) for table in values)
        target = sum(table[2:3, :] for table in values)
        lse = top + jnp.log(mass)
        moved = lse - jnp.log(lengths[...] * (1.0 / denom))
        shift[...] = as_columns(moved)
        results[...] = row_table([moved, lengths[...] * lse - target])
        total[...] = jnp.zeros_like(total)

    columns = []
    for start, size in pieces_of(w_unit.shape[1]):
        exped = jnp.exp(logits[:, start : start + size] - shift[:, 0:1])
        counted = counts[:, start : start + size].astype(F32) * (1.0 / denom)
        columns.append((exped - counted).astype(BF16))
    total[...] += dot_t(jnp.concatenate(columns, axis=1), w_unit[...])

    @pl.when(step == pl.num_programs(0) - 1)
    def _():
        if send:
            keep[...] = part_of(total, where[1], 2)
            send[0][...] = part_of(total, 1 - where[1], 2).astype(send[0].dtype)
        else:
            keep[...] = total[...]


def head_grads(where, halves, stats, lengths, logits, counts, at, w_unit, denom):
    rows, vocab = logits.shape
    width = w_unit.shape[0]
    tile = tile_of(vocab, 640)
    part = (rows // halves, width)
    shapes = [(part, F32)] + [(part, BF16)] * (halves - 1) + [((8, rows), F32)]
    return pl.pallas_call(
        functools.partial(head_grads_kernel, denom, halves, len(stats)),
        grid_spec=pltpu.PrefetchScalarGridSpec(
            num_scalar_prefetch=1,
            grid=(vocab // tile,),
            in_specs=[
                *[whole_spec((8, rows))] * len(stats),
                pl.BlockSpec((None, 1, rows), lambda t, s: (at, 0, 0)),
                pl.BlockSpec((rows, tile), lambda t, s: (0, t)),
                pl.BlockSpec((None, rows, tile), lambda t, s: (at, 0, t)),
                pl.BlockSpec((width, tile), lambda t, s: (0, t)),
            ],
            out_specs=[whole_spec(shape) for shape, _ in shapes],
            scratch_shapes=[pltpu.VMEM((rows, 128), F32), pltpu.VMEM((rows, width), F32)],
        ),
        out_shape=[jax.ShapeDtypeStruct(*shape) for shape in shapes],
        compiler_params=params(VMEM_MIB),
        cost_estimate=cost(
            flops=2 * rows * width * vocab,
            bytes_accessed=(2 * width + 6 * rows) * vocab,
            transcendentals=rows * vocab,
        ),
        name="head_grads",
    )(where, *stats, lengths, logits, counts, w_unit)


def unit_kernel(blocks, tables, share, denom, where, *refs):
    x_refs, refs = refs[: len(blocks)], refs[len(blocks) :]
    shifts, refs = refs[:tables], refs[tables:]
    counts, refs = refs[:tables], refs[tables:]
    w_unit, grad, normed, normed_t, *columns_of = refs
    half = x_refs[0].shape[0]
    rows = normed.shape[0] // tables

    @pl.when(pl.program_id(0) == 0)
    def _():
        for ref, (base, theirs) in zip(x_refs, blocks):
            side = 0
            if theirs is not None:
                side = 1 - where[1] if theirs else where[1]
            place = pl.ds(pl.multiple_of(base + side * half, half), half)
            normed[place, :] = normalised(ref[...])
        columns = pl.ds(pl.multiple_of(where[0] * share, share), share)
        normed_t[...] = normed[:, columns].astype(F32).T.astype(BF16)
        for shift, column in zip(shifts, columns_of):
            column[...] = as_columns(shift[...])

    logits = dot(normed[...], w_unit[...])
    dlogits = []
    for k in range(tables):
        exped = jnp.exp(logits[k * rows : (k + 1) * rows] - columns_of[k][:, 0:1])
        counted = counts[k][...].astype(F32) * (1.0 / denom)
        dlogits.append((exped - counted).astype(BF16))
    grad[...] = dot(normed_t[...], jnp.concatenate(dlogits, axis=0))


def unit_grads(where, x_parts, shifts, counts, w_unit, denom, share):
    width, vocab = w_unit.shape
    tile = tile_of(vocab, 256)
    half = x_parts[0][0].shape[2]
    rows = shifts[0].shape[1]
    tables = len(shifts)
    blocks = tuple(block for _, _, block in x_parts)
    return pl.pallas_call(
        functools.partial(unit_kernel, blocks, tables, share, denom),
        grid_spec=pltpu.PrefetchScalarGridSpec(
            num_scalar_prefetch=1,
            grid=(vocab // tile,),
            in_specs=[pl.BlockSpec((None, None, half, width), index) for _, index, _ in x_parts]
            + [whole_spec((1, rows))] * tables
            + [pl.BlockSpec((rows, tile), lambda j, s: (0, j))] * tables
            + [pl.BlockSpec((width, tile), lambda j, s: (0, j))],
            out_specs=pl.BlockSpec((share, tile), lambda j, s: (0, j)),
            scratch_shapes=[
                pltpu.VMEM((rows * tables, width), BF16),
                pltpu.VMEM((share, rows * tables), BF16),
                *[pltpu.VMEM((rows, 128), F32)] * tables,
            ],
        ),
        out_shape=jax.ShapeDtypeStruct((share, vocab), F32),
        compiler_params=params(VMEM_MIB),
        cost_estimate=cost(
            flops=2 * rows * tables * (width + share) * vocab,
            bytes_accessed=2 * (width + rows * tables) * vocab,
            transcendentals=rows * tables * vocab,
        ),
        name="unit_grads",
    )(where, *[x for x, _, _ in x_parts], *shifts, *counts, w_unit)


def weight_kernel(blocks, adding, share, where, *refs):
    x_refs, refs = refs[:blocks], refs[blocks:]
    g_refs, refs = refs[:blocks], refs[blocks:]
    w_in, w_out, refs = refs[0], refs[1], refs[2:]
    if adding:
        old_first, old_second, refs = refs[0], refs[1], refs[2:]
    first, second, normed, grads, normed_t, grads_t = refs
    count = x_refs[0].shape[0]

    @pl.when(pl.program_id(0) == 0)
    def _():
        columns = pl.ds(pl.multiple_of(where[0] * share, share), share)
        for at in range(blocks):
            place = pl.ds(at * count, count)
            normed[place, :] = normalised(x_refs[at][...])
            grads[place, :] = g_refs[at][...]
        normed_t[...] = normed[:, columns].astype(F32).T.astype(BF16)
        grads_t[...] = grads[:, columns].astype(F32).T.astype(BF16)

    for at, size in pieces_of(w_in.shape[1]):
        value, slope = gelu_parts(dot(normed[...], w_in[:, at : at + size]))
        dpre = dot_t(grads[...], w_out[at : at + size, :]).astype(BF16) * slope
        now_first = dot(normed_t[...], dpre)
        now_second = dot(grads_t[...], value).T
        if adding:
            now_first = old_first[:, at : at + size] + now_first
            now_second = old_second[at : at + size, :] + now_second
        first[:, at : at + size] = now_first
        second[at : at + size, :] = now_second


def weight_grads(where, x_parts, g_parts, w_in, w_out, old, share):
    width, hidden = w_in.shape
    tile = tile_of(hidden, 512)
    blocks = len(g_parts)
    count = g_parts[0][0].shape[1]
    rows = blocks * count
    in_specs = [pl.BlockSpec((None, None, count, width), index) for _, index in x_parts]
    in_specs += [pl.BlockSpec((None, count, width), index) for _, index in g_parts]
    in_specs += [
        pl.BlockSpec((width, tile), lambda j, s: (0, j)),
        pl.BlockSpec((tile, width), lambda j, s: (j, 0)),
    ]
    grad_specs = [
        pl.BlockSpec((share, tile), lambda j, s: (0, j)),
        pl.BlockSpec((tile, share), lambda j, s: (j, 0)),
    ]
    adding = old is not None
    aliases = {}
    if adding:
        in_specs += grad_specs
        aliases = {1 + 2 * blocks + 2: 0, 1 + 2 * blocks + 3: 1}
    return pl.pallas_call(
        functools.partial(weight_kernel, blocks, adding, share),
        grid_spec=pltpu.PrefetchScalarGridSpec(
            num_scalar_prefetch=1,
            grid=(hidden // tile,),
            in_specs=in_specs,
            out_specs=grad_specs,
            scratch_shapes=[
                pltpu.VMEM((rows, width), BF16),
                pltpu.VMEM((rows, width), BF16),
                pltpu.VMEM((share, rows), BF16),
                pltpu.VMEM((share, rows), BF16),
            ],
        ),
        out_shape=[
            jax.ShapeDtypeStruct((share, hidden), F32),
            jax.ShapeDtypeStruct((hidden, share), F32),
        ],
        input_output_aliases=aliases,
        compiler_params=params(VMEM_MIB),
        cost_estimate=cost(
            flops=4 * rows * (width + share) * hidden,
            bytes_accessed=4 * width * hidden + 16 * share * hidden,
            transcendentals=rows * hidden,
        ),
        name="weight_grads",
    )(where, *[x for x, _ in x_parts], *[g for g, _ in g_parts], w_in, w_out, *(old or ()))


def unit_counts(ends, targets, ids):
    positions = jnp.arange(targets.shape[1], dtype=jnp.int32)
    row_local = jnp.sum((ends[:, None, :] <= positions[None, :, None]).astype(jnp.int32), axis=-1)
    rows = jnp.arange(ends.shape[1], dtype=jnp.int32)
    row_onehot = (row_local[:, :, None] == rows[None, None, :]).astype(BF16)
    hits = (targets[:, :, None] == ids[None, None, :]).astype(BF16)
    counts = jnp.einsum("mur,muv->mrv", row_onehot, hits, preferred_element_type=F32)
    return counts.astype(BF16)


def on_device(text_rows, durations, unit_targets, w_in, w_out, w_unit):
    micro, row_count, width = text_rows.shape
    segments = lax.axis_size("segment")
    mp_size = lax.axis_size("mp")
    dp_size = lax.axis_size("dp")
    seg = lax.axis_index("segment").astype(jnp.int32)
    mp_at = lax.axis_index("mp").astype(jnp.int32)
    dp_at = lax.axis_index("dp").astype(jnp.int32)
    last = segments - 1
    pair = mp_size == 2
    halves = 2 if pair else 1
    chunks = CHUNKS
    def place(live_at):
        live = (live_at >= 0) & (live_at < chunks)
        return jnp.stack([seg, mp_at, jnp.asarray(live, jnp.int32)])

    first = w_in[0]
    second = w_out[0]
    rows = micro * row_count // chunks
    text = text_rows.reshape(chunks, rows, width)
    vocab_part = w_unit.shape[1]
    unit_count = unit_targets.shape[1]
    denom = float(micro * unit_count * dp_size)
    lengths = durations[:, 0, :]
    length_f = lengths.astype(F32).reshape(chunks, 1, rows)
    ends = jnp.cumsum(lengths, axis=-1)
    own_ids = (seg * mp_size + mp_at) * vocab_part + jnp.arange(vocab_part, dtype=jnp.int32)

    def around(block):
        came = [block]
        for distance in range(1, dp_size):
            route = [(i, (i + distance) % dp_size) for i in range(dp_size)]
            came.append(lax.ppermute(block, "dp", route))
        return came

    unit_hits = [
        unit_counts(packed[:, unit_count:], packed[:, :unit_count], own_ids)
        for packed in around(jnp.concatenate([unit_targets, ends], axis=1))
    ]
    head_counts = unit_hits[0].reshape(chunks, rows, vocab_part)
    unit_hits = [hits.reshape(micro * row_count, vocab_part) for hits in unit_hits]

    def both(part):
        return [part, swapped(part)] if pair else [part]

    def reduced(keep, send):
        return [keep, swapped(send[0])] if pair else [lax.psum(keep, "mp")]

    def gathered_rows(mine):
        came = lax.all_gather(mine, "dp")
        return [came, swapped(came)] if pair else [came]

    def all_tables(table):
        if not pair:
            return [t for t in lax.all_gather(table, ("segment", "mp"))]
        count = segments * mp_size
        return [table] + [
            lax.ppermute(table, ("segment", "mp"), [(i, (i + k) % count) for i in range(count)])
            for k in range(1, count)
        ]

    stash, x_halves, grads, finals, results = [], [], [], [], []
    sums = None
    x_gathered = None
    f_hop = b_hop = None

    def x_parts(at, side):
        return [
            (x_gathered[side], lambda j, s, k=k: (k, at, 0, 0)) for k in range(dp_size)
        ]

    clocks = 2 * segments + chunks - 1
    for clock in range(clocks):
        f_out = b_out = None
        f_ties, b_ties = [], []
        head_at = clock - segments
        if 0 <= head_at < chunks:
            final = chosen(
                seg,
                [(last, f_hop)]
                + [(to, lax.ppermute(f_hop, "segment", [(last, to)])) for to in range(last)],
            )
            finals.append(final)
            logits, stats = head_logits(place(0), both(final), w_unit, head_counts, head_at)
            f_ties = [logits]
        if clock < segments + chunks - 1:
            arrived = [] if clock == 0 else both(shifted(f_hop, "segment", 1))
            if clock == segments - 1:
                f_ties = unit_hits
            rows_in, mine, keep, *send = forward_section(
                place(clock - seg),
                text,
                min(clock, chunks - 1),
                halves,
                arrived,
                first,
                second,
                f_ties,
            )
            stash.append(rows_in)
            x_halves.append(mine)
            pieces = reduced(keep, send)
            f_out = total_of(pieces if pair else [mine, *pieces]).astype(BF16)
        if clock == segments + chunks - 2:
            x_half = jnp.stack(
                [
                    chosen(seg, [(s, x_halves[b + s]) for s in range(segments)])
                    for b in range(chunks)
                ]
            )
            x_gathered = gathered_rows(x_half)
        if clock >= segments:
            arrived = None if head_at == 0 else shifted(b_hop, "segment", -1)
            if head_at < chunks:
                keep, *send, result = head_grads(
                    place(0),
                    halves,
                    all_tables(stats),
                    length_f,
                    logits,
                    head_counts,
                    head_at,
                    w_unit,
                    denom,
                )
                results.append(result)
                dnorm = total_of(reduced(keep, send)).astype(BF16)
                dnorm = total_of(
                    [dnorm]
                    + [lax.ppermute(dnorm, "segment", [(j, last)]) for j in range(last)]
                ).astype(BF16)
                grad_final = norm_back(final, dnorm.astype(F32)).astype(BF16)
                arrived = (
                    grad_final if arrived is None else jnp.where(seg == last, grad_final, arrived)
                )
                if head_at == chunks - 1:
                    unit_rows = gathered_rows(jnp.stack(finals))
                    shifts = around(
                        jnp.concatenate([result[0:1, :] for result in results], axis=1)
                    )
            grads.append(arrived)
            if clock < clocks - 1:
                options = []
                for other in range(segments):
                    stage = clock - 2 * segments + 1 + 2 * other
                    if 0 <= stage < len(stash):
                        options.append((other, stash[stage]))
                if clock == clocks - 3:
                    b_ties = [*shifts, *x_gathered]
                if clock == clocks - 2:
                    b_ties = unit_rows
                mine, keep, *send = backward_section(
                    place(head_at - last + seg),
                    halves,
                    options,
                    both(arrived),
                    first,
                    second,
                    b_ties,
                )
                b_out = finish_backward(mine, arrived, reduced(keep, send))
        if clock >= 2 * segments - 1:
            at = clock - 2 * segments + 1
            mine = chosen(seg, [(s, grads[at + last - s]) for s in range(segments)])
            for side, source in enumerate(gathered_rows(mine)):
                sums = weight_grads(
                    dp_at[None],
                    x_parts(at, side),
                    [(source, lambda j, s, k=k: (k, 0, 0)) for k in range(dp_size)],
                    first,
                    second,
                    sums,
                    width // dp_size,
                )
        f_hop, b_hop = f_out, b_out

    loss = (sum(jnp.sum(result[1, :]) for result in results) / denom)[None]
    unit_parts = [
        (
            source,
            lambda j, s, k=k, b=b: (lax.rem(s[0] + dp_size - k, dp_size), b, 0, 0),
            ((k * chunks + b) * rows, bool(at) if pair else None),
        )
        for at, source in enumerate(unit_rows)
        for k in range(dp_size)
        for b in range(chunks)
    ]
    sum_unit = unit_grads(
        jnp.stack([dp_at, mp_at]), unit_parts, shifts, unit_hits, w_unit, denom, width // dp_size
    )
    return (loss, sums[0][None], sums[1][None], sum_unit)


def solution(mesh):
    placed = (
        P(None, "dp", None),
        P(None, "dp", None),
        P(None, "dp"),
        P("segment", None, "mp"),
        P("segment", "mp", None),
        P(None, ("segment", "mp")),
    )
    return jax.shard_map(
        on_device,
        mesh=mesh,
        in_specs=placed,
        out_specs=(
            P("dp"),
            P("segment", "dp", "mp"),
            P("segment", "mp", "dp"),
            P("dp", ("segment", "mp")),
        ),
        check_vma=False,
    )
```

```python
import functools
import jax
import jax.numpy as jnp
from jax import lax
from jax.experimental import pallas as pl
from jax.experimental.pallas import tpu as pltpu
from jax.sharding import PartitionSpec as P

CHUNKS = 2
VMEM_MIB = 60
BF16 = jnp.bfloat16
F32 = jnp.float32
MIB = 1024 * 1024


def shifted(block, axis, distance):
    devices = range(lax.axis_size(axis))
    route = [(i - distance, i) for i in devices if i - distance in devices]
    return lax.ppermute(block, axis, route)


def swapped(block):
    return lax.ppermute(block, "mp", [(0, 1), (1, 0)])


def gelu_parts(pre_vals):
    coeff = 0.7978845608
    pre = pre_vals.astype(BF16)
    square = pre * pre
    inner = pre * (square * BF16(coeff * 0.044715) + BF16(coeff))
    half = jnp.tanh(inner) * BF16(0.5) + BF16(0.5)
    value = pre * half
    bend = square * BF16(6.0 * coeff * 0.044715) + BF16(2.0 * coeff)
    slope = half + value * (BF16(1.0) - half) * bend
    return (value, slope)


def row_scale(rows_in):
    floats = rows_in.astype(F32)
    return lax.rsqrt(jnp.mean(floats * floats, axis=-1, keepdims=True) + 1e-06)


def normalised(rows_in):
    return (rows_in.astype(F32) * row_scale(rows_in)).astype(BF16)


def norm_back(rows_in, grads):
    scale = row_scale(rows_in)
    normal = rows_in.astype(F32) * scale
    return scale * (grads - normal * jnp.mean(grads * normal, axis=-1, keepdims=True))


def dot(a, b):
    return jnp.dot(a, b, preferred_element_type=F32)


def dot_t(a, b):
    return lax.dot_general(a, b, (((1,), (1,)), ((), ())), preferred_element_type=F32)


def t_dot(a, b):
    return lax.dot_general(a, b, (((0,), (0,)), ((), ())), preferred_element_type=F32)


def tile_of(size, most):
    if size <= most:
        return size
    return max(t for t in range(128, most + 1, 128) if size % t == 0)


def pieces_of(size):
    return [(at, min(256, size - at)) for at in range(0, size, 256)]


def cost(flops, bytes_accessed, transcendentals):
    return pl.CostEstimate(
        flops=flops,
        bytes_accessed=bytes_accessed,
        transcendentals=transcendentals,
    )


def params(limit):
    return pltpu.CompilerParams(vmem_limit_bytes=limit * MIB)


def chosen(index, candidates):
    value = candidates[0][1]
    for at, option in candidates[1:]:
        value = jnp.where(index == at, option, value)
    return value


def gathered(halves, place):
    if len(halves) == 1:
        return halves[0][...]
    mine, theirs = (half[...] for half in halves)
    first = jnp.where(place == 0, mine, theirs)
    second = jnp.where(place == 0, theirs, mine)
    return jnp.concatenate([first, second], axis=0)


def part_of(block, place, parts):
    rows = block.shape[0] // parts
    if parts == 1:
        return block[...]
    return block[pl.ds(pl.multiple_of(place * rows, rows), rows), :]


def whole_spec(shape):
    return pl.BlockSpec(shape, lambda *_: (0,) * len(shape))


def keep_live(live, arrived, before, after):
    for came, old, new in zip(arrived, before, after):
        new[...] = jnp.where(live, came[...], old[...])


def forward_kernel(halves, stage, ties, where, *refs):
    refs = refs[ties:]
    if stage == 0:
        own, refs = refs[0], refs[1:]
    else:
        arrived, refs = refs[:halves], refs[halves:]
        before, refs = refs[:halves], refs[halves:]
    w_in, w_out, refs = refs[0], refs[1], refs[2:]
    after, refs = refs[:halves], refs[halves:]
    keep, *send, whole, normed, total = refs
    step = pl.program_id(0)
    live = where[0] == stage

    @pl.when(step == 0)
    def _():
        if stage == 0:
            whole[...] = own[...]
            after[0][...] = part_of(whole, where[1], halves)
            if halves == 2:
                after[1][...] = part_of(whole, 1 - where[1], halves)
        else:
            whole[...] = gathered(arrived, where[1])
            keep_live(live, arrived, before, after)
        normed[...] = normalised(whole[...])
        total[...] = jnp.zeros_like(total)

    @pl.when(live)
    def _():
        values = []
        for at, size in pieces_of(w_in.shape[1]):
            value, _ = gelu_parts(dot(normed[...], w_in[:, at : at + size]))
            values.append(value)
        total[...] += dot(jnp.concatenate(values, axis=1), w_out[...])

    @pl.when(step == pl.num_programs(0) - 1)
    def _():
        if send:
            keep[...] = part_of(total, where[1], 2) + part_of(whole, where[1], 2).astype(F32)
            send[0][...] = part_of(total, 1 - where[1], 2).astype(send[0].dtype)
        else:
            keep[...] = total[...]


def forward_section(where, stage, halves, text, at, arrived, before, w_in, w_out, ties):
    _, rows, width = text.shape
    hidden = w_in.shape[1]
    tile = tile_of(hidden, 1024)
    full, part = (rows, width), (rows // halves, width)
    shapes = [(part, BF16)] * halves + [(part, F32)] + [(part, BF16)] * (halves - 1)
    if stage == 0:
        operands = [text]
        specs = [pl.BlockSpec((None, rows, width), lambda j, s: (at, 0, 0))]
    else:
        operands = [*arrived, *before]
        specs = [whole_spec(part)] * len(operands)
    return pl.pallas_call(
        functools.partial(forward_kernel, halves, stage, len(ties)),
        grid_spec=pltpu.PrefetchScalarGridSpec(
            num_scalar_prefetch=1,
            grid=(hidden // tile,),
            in_specs=[pl.BlockSpec(memory_space=pl.ANY)] * len(ties)
            + specs
            + [
                pl.BlockSpec((width, tile), lambda j, s: (0, jnp.where(s[0] == stage, j, 0))),
                pl.BlockSpec((tile, width), lambda j, s: (jnp.where(s[0] == stage, j, 0), 0)),
            ],
            out_specs=[whole_spec(shape) for shape, _ in shapes],
            scratch_shapes=[pltpu.VMEM(full, BF16), pltpu.VMEM(full, BF16), pltpu.VMEM(full, F32)],
        ),
        out_shape=[jax.ShapeDtypeStruct(*shape) for shape in shapes],
        compiler_params=params(VMEM_MIB),
        cost_estimate=cost(
            flops=4 * rows * width * hidden,
            bytes_accessed=4 * width * hidden,
            transcendentals=rows * hidden,
        ),
        name="section_forward",
    )(where, *ties, *operands, w_in, w_out)


def total_of(pieces):
    total = pieces[0].astype(F32)
    for piece in pieces[1:]:
        total = total + piece.astype(F32)
    return total


def finish_backward(rows, grads, pieces):
    return (grads.astype(F32) + norm_back(rows, total_of(pieces))).astype(BF16)


def backward_kernel(halves, owner, old, ties, where, *refs):
    refs = refs[ties:]
    stash, refs = refs[:halves], refs[halves:]
    arrived, refs = refs[:halves], refs[halves:]
    before, refs = refs[:old], refs[old:]
    w_in, w_out, refs = refs[0], refs[1], refs[2:]
    after, refs = refs[:halves], refs[halves:]
    keep, *send, grads, normed, total = refs
    step = pl.program_id(0)
    live = where[0] == owner

    @pl.when(step == 0)
    def _():
        grads[...] = gathered(arrived, where[1])
        keep_live(live, arrived, before if old else arrived, after)
        normed[...] = normalised(gathered(stash, where[1]))
        total[...] = jnp.zeros_like(total)

    @pl.when(live)
    def _():
        dpres = []
        for at, size in pieces_of(w_in.shape[1]):
            _, slope = gelu_parts(dot(normed[...], w_in[:, at : at + size]))
            dpres.append(dot_t(grads[...], w_out[at : at + size, :]).astype(BF16) * slope)
        total[...] += dot_t(jnp.concatenate(dpres, axis=1), w_in[...])

    @pl.when(step == pl.num_programs(0) - 1)
    def _():
        if send:
            keep[...] = part_of(total, where[1], 2)
            send[0][...] = part_of(total, 1 - where[1], 2).astype(send[0].dtype)
        else:
            keep[...] = total[...]


def backward_section(where, owner, stash, arrived, before, w_in, w_out, ties):
    width, hidden = w_in.shape
    halves = len(stash)
    part = stash[0].shape
    full = (part[0] * halves, width)
    tile = tile_of(hidden, 1024)
    shapes = [(part, BF16)] * halves + [(part, F32)] + [(part, BF16)] * (halves - 1)
    operands = [*stash, *arrived, *before]
    return pl.pallas_call(
        functools.partial(backward_kernel, halves, owner, len(before), len(ties)),
        grid_spec=pltpu.PrefetchScalarGridSpec(
            num_scalar_prefetch=1,
            grid=(hidden // tile,),
            in_specs=[pl.BlockSpec(memory_space=pl.ANY)] * len(ties)
            + [whole_spec(part)] * len(operands)
            + [
                pl.BlockSpec((width, tile), lambda j, s: (0, jnp.where(s[0] == owner, j, 0))),
                pl.BlockSpec((tile, width), lambda j, s: (jnp.where(s[0] == owner, j, 0), 0)),
            ],
            out_specs=[whole_spec(shape) for shape, _ in shapes],
            scratch_shapes=[pltpu.VMEM(full, BF16)] * 2 + [pltpu.VMEM(full, F32)],
        ),
        out_shape=[jax.ShapeDtypeStruct(*shape) for shape in shapes],
        compiler_params=params(VMEM_MIB),
        cost_estimate=cost(
            flops=6 * full[0] * width * hidden,
            bytes_accessed=4 * width * hidden,
            transcendentals=full[0] * hidden,
        ),
        name="section_backward",
    )(where, *ties, *operands, w_in, w_out)


def pick_kernel(halves, owner, ties, where, *refs):
    refs = refs[ties:]
    arrived, before, after = refs[:halves], refs[halves : 2 * halves], refs[2 * halves :]
    keep_live(where[0] == owner, arrived, before, after)


def pick(where, owner, arrived, before, ties):
    halves = len(arrived)
    part = arrived[0].shape
    return pl.pallas_call(
        functools.partial(pick_kernel, halves, owner, len(ties)),
        grid_spec=pltpu.PrefetchScalarGridSpec(
            num_scalar_prefetch=1,
            grid=(1,),
            in_specs=[pl.BlockSpec(memory_space=pl.ANY)] * len(ties)
            + [whole_spec(part)] * (2 * halves),
            out_specs=[whole_spec(part)] * halves,
        ),
        out_shape=[jax.ShapeDtypeStruct(part, BF16)] * halves,
        compiler_params=params(VMEM_MIB),
        name="pick_grads",
    )(where, *ties, *arrived, *before)


def row_table(rows):
    pad = jnp.zeros((8 - len(rows), rows[0].shape[1]), F32)
    return jnp.concatenate([*rows, pad], axis=0)


def as_row(column):
    return jnp.broadcast_to(column, (column.shape[0], 128)).T[0:1, :]


def as_columns(row):
    return jnp.broadcast_to(row, (128, row.shape[1])).T


def logits_kernel(halves, chunks, where, *refs):
    finals, refs = refs[: halves * chunks], refs[halves * chunks :]
    w_unit, counts, logits, stats, normed, peak, total, target = refs
    step = pl.program_id(0)
    lanes = peak.shape[1]

    @pl.when(step == 0)
    def _():
        rows = normed.shape[0] // chunks
        for at in range(chunks):
            final = finals[at * halves : (at + 1) * halves]
            normed[at * rows : (at + 1) * rows, :] = normalised(gathered(final, where[1]))
        peak[...] = jnp.full_like(peak, -1e30)
        total[...] = jnp.zeros_like(total)
        target[...] = jnp.zeros_like(target)

    columns = []
    for start, size in pieces_of(w_unit.shape[1]):
        values = dot(normed[...], w_unit[:, start : start + size])
        logits[:, start : start + size] = values
        counted = counts[:, start : start + size].astype(F32) * values
        columns += [
            (values[:, c : c + lanes], counted[:, c : c + lanes]) for c in range(0, size, lanes)
        ]
    higher = peak[...]
    for values, _ in columns:
        higher = jnp.maximum(higher, values)
    mass = total[...] * jnp.exp(peak[...] - higher)
    summed = target[...]
    for values, counted in columns:
        mass = mass + jnp.exp(values - higher)
        summed = summed + counted
    peak[...] = higher
    total[...] = mass
    target[...] = summed

    @pl.when(step == pl.num_programs(0) - 1)
    def _():
        top = jnp.max(peak[...], axis=-1, keepdims=True)
        mass = jnp.sum(total[...] * jnp.exp(peak[...] - top), axis=-1, keepdims=True)
        summed = jnp.sum(target[...], axis=-1, keepdims=True)
        stats[...] = row_table([as_row(top), as_row(mass), as_row(summed)])


def head_logits(where, finals, w_unit, counts):
    halves, chunks = len(finals[0]), len(finals)
    half, width = finals[0][0].shape
    rows = half * halves * chunks
    vocab = w_unit.shape[1]
    lanes = 128 if vocab % 128 == 0 else vocab
    tile = tile_of(vocab, 640)
    return pl.pallas_call(
        functools.partial(logits_kernel, halves, chunks),
        grid_spec=pltpu.PrefetchScalarGridSpec(
            num_scalar_prefetch=1,
            grid=(vocab // tile,),
            in_specs=[
                *[whole_spec((half, width))] * (halves * chunks),
                pl.BlockSpec((width, tile), lambda t, s: (0, t)),
                pl.BlockSpec((rows, tile), lambda t, s: (0, t)),
            ],
            out_specs=[
                pl.BlockSpec((rows, tile), lambda t, s: (0, t)),
                whole_spec((8, rows)),
            ],
            scratch_shapes=[pltpu.VMEM((rows, width), BF16)] + [pltpu.VMEM((rows, lanes), F32)] * 3,
        ),
        out_shape=[
            jax.ShapeDtypeStruct((rows, vocab), F32),
            jax.ShapeDtypeStruct((8, rows), F32),
        ],
        compiler_params=params(VMEM_MIB),
        cost_estimate=cost(
            flops=2 * rows * width * vocab,
            bytes_accessed=(2 * width + 6 * rows) * vocab,
            transcendentals=rows * vocab,
        ),
        name="head_logits",
    )(where, *[half for final in finals for half in final], w_unit, counts)


def head_grads_kernel(denom, halves, chunks, tables, where, *refs):
    stats, refs = refs[:tables], refs[tables:]
    lengths, logits, counts, w_unit, *parts, results, shift, total = refs
    step = pl.program_id(0)

    @pl.when(step == 0)
    def _():
        values = [ref[...] for ref in stats]
        top = values[0][0:1, :]
        for table in values[1:]:
            top = jnp.maximum(top, table[0:1, :])
        mass = sum(table[1:2, :] * jnp.exp(table[0:1, :] - top) for table in values)
        target = sum(table[2:3, :] for table in values)
        lse = top + jnp.log(mass)
        moved = lse - jnp.log(lengths[...] * (1.0 / denom))
        shift[...] = as_columns(moved)
        results[...] = row_table([moved, lengths[...] * lse - target])
        total[...] = jnp.zeros_like(total)

    columns = []
    for start, size in pieces_of(w_unit.shape[1]):
        exped = jnp.exp(logits[:, start : start + size] - shift[:, 0:1])
        counted = counts[:, start : start + size].astype(F32) * (1.0 / denom)
        columns.append((exped - counted).astype(BF16))
    total[...] += dot_t(jnp.concatenate(columns, axis=1), w_unit[...])

    @pl.when(step == pl.num_programs(0) - 1)
    def _():
        half = total.shape[0] // (chunks * halves)
        for at in range(chunks):
            base = at * halves * half
            mine, theirs = base, base
            if halves == 2:
                mine, theirs = base + where[1] * half, base + (1 - where[1]) * half
                out = parts[chunks + at]
                out[...] = total[pl.ds(pl.multiple_of(theirs, half), half), :].astype(out.dtype)
                parts[at][...] = total[pl.ds(pl.multiple_of(mine, half), half), :]
            else:
                parts[at][...] = total[base : base + half, :]


def head_grads(where, halves, chunks, stats, lengths, logits, counts, w_unit, denom):
    rows, vocab = logits.shape
    width = w_unit.shape[0]
    tile = tile_of(vocab, 640)
    part = (rows // (halves * chunks), width)
    shapes = [(part, F32)] * chunks + [(part, BF16)] * (chunks * (halves - 1))
    shapes += [((8, rows), F32)]
    return pl.pallas_call(
        functools.partial(head_grads_kernel, denom, halves, chunks, len(stats)),
        grid_spec=pltpu.PrefetchScalarGridSpec(
            num_scalar_prefetch=1,
            grid=(vocab // tile,),
            in_specs=[
                *[whole_spec((8, rows))] * len(stats),
                whole_spec((1, rows)),
                pl.BlockSpec((rows, tile), lambda t, s: (0, t)),
                pl.BlockSpec((rows, tile), lambda t, s: (0, t)),
                pl.BlockSpec((width, tile), lambda t, s: (0, t)),
            ],
            out_specs=[whole_spec(shape) for shape, _ in shapes],
            scratch_shapes=[pltpu.VMEM((rows, 128), F32), pltpu.VMEM((rows, width), F32)],
        ),
        out_shape=[jax.ShapeDtypeStruct(*shape) for shape in shapes],
        compiler_params=params(VMEM_MIB),
        cost_estimate=cost(
            flops=2 * rows * width * vocab,
            bytes_accessed=(2 * width + 6 * rows) * vocab,
            transcendentals=rows * vocab,
        ),
        name="head_grads",
    )(where, *stats, lengths, logits, counts, w_unit)


def unit_kernel(blocks, tables, share, denom, where, *refs):
    x_refs, refs = refs[: len(blocks)], refs[len(blocks) :]
    shifts, refs = refs[:tables], refs[tables:]
    counts, refs = refs[:tables], refs[tables:]
    w_unit, grad, normed, normed_t, *columns_of = refs
    half = x_refs[0].shape[0]
    rows = normed.shape[0] // tables

    @pl.when(pl.program_id(0) == 0)
    def _():
        for ref, (base, theirs) in zip(x_refs, blocks):
            side = 0
            if theirs is not None:
                side = 1 - where[1] if theirs else where[1]
            place = pl.ds(pl.multiple_of(base + side * half, half), half)
            normed[place, :] = normalised(ref[...])
        columns = pl.ds(pl.multiple_of(where[0] * share, share), share)
        normed_t[...] = normed[:, columns].astype(F32).T.astype(BF16)
        for shift, column in zip(shifts, columns_of):
            column[...] = as_columns(shift[...])

    logits = dot(normed[...], w_unit[...])
    dlogits = []
    for k in range(tables):
        exped = jnp.exp(logits[k * rows : (k + 1) * rows] - columns_of[k][:, 0:1])
        counted = counts[k][...].astype(F32) * (1.0 / denom)
        dlogits.append((exped - counted).astype(BF16))
    grad[...] = dot(normed_t[...], jnp.concatenate(dlogits, axis=0))


def unit_grads(where, x_parts, shifts, counts, w_unit, denom, share):
    width, vocab = w_unit.shape
    tile = tile_of(vocab, 256)
    half = x_parts[0][0].shape[2]
    rows = shifts[0].shape[1]
    tables = len(shifts)
    blocks = tuple(block for _, _, block in x_parts)
    return pl.pallas_call(
        functools.partial(unit_kernel, blocks, tables, share, denom),
        grid_spec=pltpu.PrefetchScalarGridSpec(
            num_scalar_prefetch=1,
            grid=(vocab // tile,),
            in_specs=[pl.BlockSpec((None, None, half, width), index) for _, index, _ in x_parts]
            + [whole_spec((1, rows))] * tables
            + [pl.BlockSpec((rows, tile), lambda j, s: (0, j))] * tables
            + [pl.BlockSpec((width, tile), lambda j, s: (0, j))],
            out_specs=pl.BlockSpec((share, tile), lambda j, s: (0, j)),
            scratch_shapes=[
                pltpu.VMEM((rows * tables, width), BF16),
                pltpu.VMEM((share, rows * tables), BF16),
                *[pltpu.VMEM((rows, 128), F32)] * tables,
            ],
        ),
        out_shape=jax.ShapeDtypeStruct((share, vocab), F32),
        compiler_params=params(VMEM_MIB),
        cost_estimate=cost(
            flops=2 * rows * tables * (width + share) * vocab,
            bytes_accessed=2 * (width + rows * tables) * vocab,
            transcendentals=rows * tables * vocab,
        ),
        name="unit_grads",
    )(where, *[x for x, _, _ in x_parts], *shifts, *counts, w_unit)


def weight_kernel(blocks, adding, share, where, *refs):
    x_refs, refs = refs[:blocks], refs[blocks:]
    g_refs, refs = refs[:blocks], refs[blocks:]
    w_in, w_out, refs = refs[0], refs[1], refs[2:]
    if adding:
        old_first, old_second, refs = refs[0], refs[1], refs[2:]
    first, second, normed, grads, normed_t, grads_t = refs
    count = x_refs[0].shape[0]

    @pl.when(pl.program_id(0) == 0)
    def _():
        columns = pl.ds(pl.multiple_of(where[0] * share, share), share)
        for at in range(blocks):
            place = pl.ds(at * count, count)
            normed[place, :] = normalised(x_refs[at][...])
            grads[place, :] = g_refs[at][...]
        normed_t[...] = normed[:, columns].astype(F32).T.astype(BF16)
        grads_t[...] = grads[:, columns].astype(F32).T.astype(BF16)

    for at, size in pieces_of(w_in.shape[1]):
        value, slope = gelu_parts(dot(normed[...], w_in[:, at : at + size]))
        dpre = dot_t(grads[...], w_out[at : at + size, :]).astype(BF16) * slope
        now_first = dot(normed_t[...], dpre)
        now_second = dot(grads_t[...], value).T
        if adding:
            now_first = old_first[:, at : at + size] + now_first
            now_second = old_second[at : at + size, :] + now_second
        first[:, at : at + size] = now_first
        second[at : at + size, :] = now_second


def weight_grads(where, x_parts, g_parts, w_in, w_out, old, share):
    width, hidden = w_in.shape
    tile = tile_of(hidden, 512)
    blocks = len(g_parts)
    count = g_parts[0][0].shape[-2]
    rows = blocks * count
    in_specs = [
        pl.BlockSpec((None,) * (array.ndim - 2) + (count, width), index)
        for array, index in (*x_parts, *g_parts)
    ]
    in_specs += [
        pl.BlockSpec((width, tile), lambda j, s: (0, j)),
        pl.BlockSpec((tile, width), lambda j, s: (j, 0)),
    ]
    grad_specs = [
        pl.BlockSpec((share, tile), lambda j, s: (0, j)),
        pl.BlockSpec((tile, share), lambda j, s: (j, 0)),
    ]
    adding = old is not None
    aliases = {}
    if adding:
        in_specs += grad_specs
        aliases = {1 + 2 * blocks + 2: 0, 1 + 2 * blocks + 3: 1}
    return pl.pallas_call(
        functools.partial(weight_kernel, blocks, adding, share),
        grid_spec=pltpu.PrefetchScalarGridSpec(
            num_scalar_prefetch=1,
            grid=(hidden // tile,),
            in_specs=in_specs,
            out_specs=grad_specs,
            scratch_shapes=[
                pltpu.VMEM((rows, width), BF16),
                pltpu.VMEM((rows, width), BF16),
                pltpu.VMEM((share, rows), BF16),
                pltpu.VMEM((share, rows), BF16),
            ],
        ),
        out_shape=[
            jax.ShapeDtypeStruct((share, hidden), F32),
            jax.ShapeDtypeStruct((hidden, share), F32),
        ],
        input_output_aliases=aliases,
        compiler_params=params(VMEM_MIB),
        cost_estimate=cost(
            flops=4 * rows * (width + share) * hidden,
            bytes_accessed=4 * width * hidden + 16 * share * hidden,
            transcendentals=rows * hidden,
        ),
        name="weight_grads",
    )(where, *[x for x, _ in x_parts], *[g for g, _ in g_parts], w_in, w_out, *(old or ()))


def unit_counts(ends, targets, ids):
    positions = jnp.arange(targets.shape[1], dtype=jnp.int32)
    row_local = jnp.sum((ends[:, None, :] <= positions[None, :, None]).astype(jnp.int32), axis=-1)
    rows = jnp.arange(ends.shape[1], dtype=jnp.int32)
    row_onehot = (row_local[:, :, None] == rows[None, None, :]).astype(BF16)
    hits = (targets[:, :, None] == ids[None, None, :]).astype(BF16)
    counts = jnp.einsum("mur,muv->mrv", row_onehot, hits, preferred_element_type=F32)
    return counts.astype(BF16)


def on_device(text_rows, durations, unit_targets, w_in, w_out, w_unit):
    micro, row_count, width = text_rows.shape
    segments = lax.axis_size("segment")
    mp_size = lax.axis_size("mp")
    dp_size = lax.axis_size("dp")
    seg = lax.axis_index("segment").astype(jnp.int32)
    mp_at = lax.axis_index("mp").astype(jnp.int32)
    dp_at = lax.axis_index("dp").astype(jnp.int32)
    last = segments - 1
    pair = mp_size == 2
    halves = 2 if pair else 1
    chunks = CHUNKS
    where = jnp.stack([seg, mp_at])
    first = w_in[0]
    second = w_out[0]
    rows = micro * row_count // chunks
    text = text_rows.reshape(chunks, rows, width)
    vocab_part = w_unit.shape[1]
    unit_count = unit_targets.shape[1]
    denom = float(micro * unit_count * dp_size)
    lengths = durations[:, 0, :]
    length_f = lengths.astype(F32).reshape(1, micro * row_count)
    ends = jnp.cumsum(lengths, axis=-1)
    own_ids = (seg * mp_size + mp_at) * vocab_part + jnp.arange(vocab_part, dtype=jnp.int32)

    def around(block):
        came = [block]
        for distance in range(1, dp_size):
            route = [(i, (i + distance) % dp_size) for i in range(dp_size)]
            came.append(lax.ppermute(block, "dp", route))
        return came

    unit_hits = [
        unit_counts(packed[:, unit_count:], packed[:, :unit_count], own_ids)
        for packed in around(jnp.concatenate([unit_targets, ends], axis=1))
    ]
    unit_hits = [hits.reshape(micro * row_count, vocab_part) for hits in unit_hits]

    def both(part):
        return [part, swapped(part)] if pair else [part]

    def reduced(keep, send):
        return [keep, swapped(send[0])] if pair else [lax.psum(keep, "mp")]

    def gathered_rows(mine):
        came = lax.all_gather(mine, "dp")
        return [came, swapped(came)] if pair else [came]

    def all_tables(table):
        if not pair:
            return [t for t in lax.all_gather(table, ("segment", "mp"))]
        count = segments * mp_size
        return [table] + [
            lax.ppermute(table, ("segment", "mp"), [(i, (i + k) % count) for i in range(count)])
            for k in range(1, count)
        ]

    every = range(chunks)
    stash = [None] * chunks
    hops = [None] * chunks
    for stage in range(segments):
        for b in every:
            arrived = []
            if stage > 0:
                arrived = both(lax.ppermute(hops[b], "segment", [(stage - 1, stage)]))
            ties = unit_hits if stage == min(2, last) and b == 0 else []
            outs = forward_section(
                where, stage, halves, text, b, arrived, stash[b], first, second, ties
            )
            stash[b], keep, send = outs[:halves], outs[halves], outs[halves + 1 :]
            pieces = reduced(keep, send)
            hops[b] = total_of(pieces if pair else [stash[b][0], *pieces]).astype(BF16)
    x_gathered = gathered_rows(jnp.stack([stash[b][0] for b in every]))

    finals = []
    for b in every:
        options = [(last, hops[b])]
        options += [
            (to, lax.ppermute(hops[b], "segment", [(last, to)])) for to in range(last)
        ]
        finals.append(both(chosen(seg, options)))
    logits, stats = head_logits(where, finals, w_unit, unit_hits[0])
    *parts, result = head_grads(
        where, halves, chunks, all_tables(stats), length_f, logits, unit_hits[0], w_unit, denom
    )
    loss = (jnp.sum(result[1, :]) / denom)[None]
    shifts = around(result[0:1, :])
    unit_rows = gathered_rows(jnp.stack([final[0] for final in finals]))
    for b in every:
        dnorm = total_of(reduced(parts[b], parts[chunks + b : chunks + b + 1])).astype(BF16)
        dnorm = total_of(
            [dnorm] + [lax.ppermute(dnorm, "segment", [(j, last)]) for j in range(last)]
        ).astype(BF16)
        hops[b] = norm_back(finals[b][0], dnorm.astype(F32)).astype(BF16)

    grads = [[] for _ in every]
    for stage in range(last):
        owner = last - stage
        for b in every:
            came = hops[b]
            if stage > 0:
                came = lax.ppermute(came, "segment", [(owner + 1, owner)])
            ties = []
            if b == 0 and stage == last - 1:
                ties = [*shifts, *x_gathered, *unit_rows]
            outs = backward_section(
                where, owner, stash[b], both(came), grads[b], first, second, ties
            )
            grads[b], keep, send = outs[:halves], outs[halves], outs[halves + 1 :]
            hops[b] = finish_backward(stash[b][0], came, reduced(keep, send))

    unit_parts = [
        (
            source,
            lambda j, s, k=k, b=b: (lax.rem(s[0] + dp_size - k, dp_size), b, 0, 0),
            ((k * chunks + b) * rows, bool(at) if pair else None),
        )
        for at, source in enumerate(unit_rows)
        for k in range(dp_size)
        for b in range(chunks)
    ]
    sum_unit = unit_grads(
        jnp.stack([dp_at, mp_at]), unit_parts, shifts, unit_hits, w_unit, denom, width // dp_size
    )
    for b in every:
        arrived = both(lax.ppermute(hops[b], "segment", [(1, 0)]))
        grads[b] = pick(where, 0, arrived, grads[b], [sum_unit] if b == 0 else [])
    share = width // dp_size
    sums = weight_grads(
        dp_at[None],
        [(half, lambda j, s: (0, 0)) for b in every for half in stash[b]],
        [(half, lambda j, s: (0, 0)) for b in every for half in grads[b]],
        first,
        second,
        None,
        share,
    )
    for b in every:
        sources = gathered_rows(grads[b][0])
        others = [(side, k) for side in range(halves) for k in range(1, dp_size)]
        sums = weight_grads(
            dp_at[None],
            [
                (x_gathered[side], lambda j, s, k=k: (lax.rem(s[0] + k, dp_size), b, 0, 0))
                for side, k in others
            ],
            [
                (sources[side], lambda j, s, k=k: (lax.rem(s[0] + k, dp_size), 0, 0))
                for side, k in others
            ],
            first,
            second,
            sums,
            share,
        )
    return (loss, sums[0][None], sums[1][None], sum_unit)


def solution(mesh):
    placed = (
        P(None, "dp", None),
        P(None, "dp", None),
        P(None, "dp"),
        P("segment", None, "mp"),
        P("segment", "mp", None),
        P(None, ("segment", "mp")),
    )
    return jax.shard_map(
        on_device,
        mesh=mesh,
        in_specs=placed,
        out_specs=(
            P("dp"),
            P("segment", "dp", "mp"),
            P("segment", "mp", "dp"),
            P("dp", ("segment", "mp")),
        ),
        check_vma=False,
    )
```

```python
import functools
import jax
import jax.numpy as jnp
from jax import lax
from jax.experimental import pallas as pl
from jax.experimental.pallas import tpu as pltpu
from jax.sharding import PartitionSpec as P

CHUNKS = 2
VMEM_MIB = 60
BF16 = jnp.bfloat16
F32 = jnp.float32
MIB = 1024 * 1024


def shifted(block, axis, distance):
    devices = range(lax.axis_size(axis))
    route = [(i - distance, i) for i in devices if i - distance in devices]
    return lax.ppermute(block, axis, route)


def swapped(block):
    return lax.ppermute(block, "mp", [(0, 1), (1, 0)])


def gelu_parts(pre_vals):
    coeff = 0.7978845608
    pre = pre_vals.astype(BF16)
    square = pre * pre
    inner = pre * (square * BF16(coeff * 0.044715) + BF16(coeff))
    half = jnp.tanh(inner) * BF16(0.5) + BF16(0.5)
    value = pre * half
    bend = square * BF16(6.0 * coeff * 0.044715) + BF16(2.0 * coeff)
    slope = half + value * (BF16(1.0) - half) * bend
    return (value, slope)


def row_scale(rows_in):
    floats = rows_in.astype(F32)
    return lax.rsqrt(jnp.mean(floats * floats, axis=-1, keepdims=True) + 1e-06)


def normalised(rows_in):
    return (rows_in.astype(F32) * row_scale(rows_in)).astype(BF16)


def norm_back(rows_in, grads):
    scale = row_scale(rows_in)
    normal = rows_in.astype(F32) * scale
    return scale * (grads - normal * jnp.mean(grads * normal, axis=-1, keepdims=True))


def dot(a, b):
    return jnp.dot(a, b, preferred_element_type=F32)


def dot_t(a, b):
    return lax.dot_general(a, b, (((1,), (1,)), ((), ())), preferred_element_type=F32)


def t_dot(a, b):
    return lax.dot_general(a, b, (((0,), (0,)), ((), ())), preferred_element_type=F32)


def tile_of(size, most):
    if size <= most:
        return size
    return max(t for t in range(128, most + 1, 128) if size % t == 0)


def pieces_of(size):
    return [(at, min(256, size - at)) for at in range(0, size, 256)]


def cost(flops, bytes_accessed, transcendentals):
    return pl.CostEstimate(
        flops=flops,
        bytes_accessed=bytes_accessed,
        transcendentals=transcendentals,
    )


def params(limit):
    return pltpu.CompilerParams(vmem_limit_bytes=limit * MIB)


def chosen(index, candidates):
    value = candidates[0][1]
    for at, option in candidates[1:]:
        value = jnp.where(index == at, option, value)
    return value


def gathered(halves, place):
    if len(halves) == 1:
        return halves[0][...]
    mine, theirs = (half[...] for half in halves)
    first = jnp.where(place == 0, mine, theirs)
    second = jnp.where(place == 0, theirs, mine)
    return jnp.concatenate([first, second], axis=0)


def part_of(block, place, parts):
    rows = block.shape[0] // parts
    if parts == 1:
        return block[...]
    return block[pl.ds(pl.multiple_of(place * rows, rows), rows), :]


def whole_spec(shape):
    return pl.BlockSpec(shape, lambda *_: (0,) * len(shape))


def keep_live(live, arrived, before, after):
    for came, old, new in zip(arrived, before, after):
        new[...] = jnp.where(live, came[...], old[...])


def forward_kernel(halves, stage, ties, where, *refs):
    refs = refs[ties:]
    if stage == 0:
        own, refs = refs[0], refs[1:]
    else:
        arrived, refs = refs[:halves], refs[halves:]
        before, refs = refs[:halves], refs[halves:]
    w_in, w_out, refs = refs[0], refs[1], refs[2:]
    after, refs = refs[:halves], refs[halves:]
    keep, *send, whole, normed, total = refs
    step = pl.program_id(0)
    live = where[0] == stage

    @pl.when(step == 0)
    def _():
        if stage == 0:
            whole[...] = own[...]
            after[0][...] = part_of(whole, where[1], halves)
            if halves == 2:
                after[1][...] = part_of(whole, 1 - where[1], halves)
        else:
            whole[...] = gathered(arrived, where[1])
            keep_live(live, arrived, before, after)
        normed[...] = normalised(whole[...])
        total[...] = jnp.zeros_like(total)

    @pl.when(live)
    def _():
        values = []
        for at, size in pieces_of(w_in.shape[1]):
            value, _ = gelu_parts(dot(normed[...], w_in[:, at : at + size]))
            values.append(value)
        total[...] += dot(jnp.concatenate(values, axis=1), w_out[...])

    @pl.when(step == pl.num_programs(0) - 1)
    def _():
        if send:
            keep[...] = part_of(total, where[1], 2) + part_of(whole, where[1], 2).astype(F32)
            send[0][...] = part_of(total, 1 - where[1], 2).astype(send[0].dtype)
        else:
            keep[...] = total[...]


def forward_section(where, stage, halves, text, at, arrived, before, w_in, w_out, ties):
    _, rows, width = text.shape
    hidden = w_in.shape[1]
    tile = tile_of(hidden, 1024)
    full, part = (rows, width), (rows // halves, width)
    shapes = [(part, BF16)] * halves + [(part, F32)] + [(part, BF16)] * (halves - 1)
    if stage == 0:
        operands = [text]
        specs = [pl.BlockSpec((None, rows, width), lambda j, s: (at, 0, 0))]
    else:
        operands = [*arrived, *before]
        specs = [whole_spec(part)] * len(operands)
    return pl.pallas_call(
        functools.partial(forward_kernel, halves, stage, len(ties)),
        grid_spec=pltpu.PrefetchScalarGridSpec(
            num_scalar_prefetch=1,
            grid=(hidden // tile,),
            in_specs=[pl.BlockSpec(memory_space=pl.ANY)] * len(ties)
            + specs
            + [
                pl.BlockSpec((width, tile), lambda j, s: (0, jnp.where(s[0] == stage, j, 0))),
                pl.BlockSpec((tile, width), lambda j, s: (jnp.where(s[0] == stage, j, 0), 0)),
            ],
            out_specs=[whole_spec(shape) for shape, _ in shapes],
            scratch_shapes=[pltpu.VMEM(full, BF16), pltpu.VMEM(full, BF16), pltpu.VMEM(full, F32)],
        ),
        out_shape=[jax.ShapeDtypeStruct(*shape) for shape in shapes],
        compiler_params=params(VMEM_MIB),
        cost_estimate=cost(
            flops=4 * rows * width * hidden,
            bytes_accessed=4 * width * hidden,
            transcendentals=rows * hidden,
        ),
        name="section_forward",
    )(where, *ties, *operands, w_in, w_out)


def total_of(pieces):
    total = pieces[0].astype(F32)
    for piece in pieces[1:]:
        total = total + piece.astype(F32)
    return total


def finish_backward(rows, grads, pieces):
    return (grads.astype(F32) + norm_back(rows, total_of(pieces))).astype(BF16)


def backward_kernel(halves, owner, old, ties, where, *refs):
    refs = refs[ties:]
    stash, refs = refs[:halves], refs[halves:]
    arrived, refs = refs[:halves], refs[halves:]
    before, refs = refs[:old], refs[old:]
    w_in, w_out, refs = refs[0], refs[1], refs[2:]
    after, refs = refs[:halves], refs[halves:]
    keep, *send, grads, normed, total = refs
    step = pl.program_id(0)
    live = where[0] == owner

    @pl.when(step == 0)
    def _():
        grads[...] = gathered(arrived, where[1])
        keep_live(live, arrived, before if old else arrived, after)
        normed[...] = normalised(gathered(stash, where[1]))
        total[...] = jnp.zeros_like(total)

    @pl.when(live)
    def _():
        dpres = []
        for at, size in pieces_of(w_in.shape[1]):
            _, slope = gelu_parts(dot(normed[...], w_in[:, at : at + size]))
            dpres.append(dot_t(grads[...], w_out[at : at + size, :]).astype(BF16) * slope)
        total[...] += dot_t(jnp.concatenate(dpres, axis=1), w_in[...])

    @pl.when(step == pl.num_programs(0) - 1)
    def _():
        if send:
            keep[...] = part_of(total, where[1], 2)
            send[0][...] = part_of(total, 1 - where[1], 2).astype(send[0].dtype)
        else:
            keep[...] = total[...]


def backward_section(where, owner, stash, arrived, before, w_in, w_out, ties):
    width, hidden = w_in.shape
    halves = len(stash)
    part = stash[0].shape
    full = (part[0] * halves, width)
    tile = tile_of(hidden, 1024)
    shapes = [(part, BF16)] * halves + [(part, F32)] + [(part, BF16)] * (halves - 1)
    operands = [*stash, *arrived, *before]
    return pl.pallas_call(
        functools.partial(backward_kernel, halves, owner, len(before), len(ties)),
        grid_spec=pltpu.PrefetchScalarGridSpec(
            num_scalar_prefetch=1,
            grid=(hidden // tile,),
            in_specs=[pl.BlockSpec(memory_space=pl.ANY)] * len(ties)
            + [whole_spec(part)] * len(operands)
            + [
                pl.BlockSpec((width, tile), lambda j, s: (0, jnp.where(s[0] == owner, j, 0))),
                pl.BlockSpec((tile, width), lambda j, s: (jnp.where(s[0] == owner, j, 0), 0)),
            ],
            out_specs=[whole_spec(shape) for shape, _ in shapes],
            scratch_shapes=[pltpu.VMEM(full, BF16)] * 2 + [pltpu.VMEM(full, F32)],
        ),
        out_shape=[jax.ShapeDtypeStruct(*shape) for shape in shapes],
        compiler_params=params(VMEM_MIB),
        cost_estimate=cost(
            flops=6 * full[0] * width * hidden,
            bytes_accessed=4 * width * hidden,
            transcendentals=full[0] * hidden,
        ),
        name="section_backward",
    )(where, *ties, *operands, w_in, w_out)


def pick_kernel(halves, owner, ties, where, *refs):
    refs = refs[ties:]
    arrived, before, after = refs[:halves], refs[halves : 2 * halves], refs[2 * halves :]
    keep_live(where[0] == owner, arrived, before, after)


def pick(where, owner, arrived, before, ties):
    halves = len(arrived)
    part = arrived[0].shape
    return pl.pallas_call(
        functools.partial(pick_kernel, halves, owner, len(ties)),
        grid_spec=pltpu.PrefetchScalarGridSpec(
            num_scalar_prefetch=1,
            grid=(1,),
            in_specs=[pl.BlockSpec(memory_space=pl.ANY)] * len(ties)
            + [whole_spec(part)] * (2 * halves),
            out_specs=[whole_spec(part)] * halves,
        ),
        out_shape=[jax.ShapeDtypeStruct(part, BF16)] * halves,
        compiler_params=params(VMEM_MIB),
        name="pick_grads",
    )(where, *ties, *arrived, *before)


def row_table(rows):
    pad = jnp.zeros((8 - len(rows), rows[0].shape[1]), F32)
    return jnp.concatenate([*rows, pad], axis=0)


def as_row(column):
    return jnp.broadcast_to(column, (column.shape[0], 128)).T[0:1, :]


def as_columns(row):
    return jnp.broadcast_to(row, (128, row.shape[1])).T


def logits_kernel(halves, chunks, where, *refs):
    finals, refs = refs[: halves * chunks], refs[halves * chunks :]
    w_unit, counts, logits, stats, normed, peak, total, target = refs
    step = pl.program_id(0)
    lanes = peak.shape[1]

    @pl.when(step == 0)
    def _():
        rows = normed.shape[0] // chunks
        for at in range(chunks):
            final = finals[at * halves : (at + 1) * halves]
            normed[at * rows : (at + 1) * rows, :] = normalised(gathered(final, where[1]))
        peak[...] = jnp.full_like(peak, -1e30)
        total[...] = jnp.zeros_like(total)
        target[...] = jnp.zeros_like(target)

    columns = []
    for start, size in pieces_of(w_unit.shape[1]):
        values = dot(normed[...], w_unit[:, start : start + size])
        logits[:, start : start + size] = values
        counted = counts[:, start : start + size].astype(F32) * values
        columns += [
            (values[:, c : c + lanes], counted[:, c : c + lanes]) for c in range(0, size, lanes)
        ]
    higher = peak[...]
    for values, _ in columns:
        higher = jnp.maximum(higher, values)
    mass = total[...] * jnp.exp(peak[...] - higher)
    summed = target[...]
    for values, counted in columns:
        mass = mass + jnp.exp(values - higher)
        summed = summed + counted
    peak[...] = higher
    total[...] = mass
    target[...] = summed

    @pl.when(step == pl.num_programs(0) - 1)
    def _():
        top = jnp.max(peak[...], axis=-1, keepdims=True)
        mass = jnp.sum(total[...] * jnp.exp(peak[...] - top), axis=-1, keepdims=True)
        summed = jnp.sum(target[...], axis=-1, keepdims=True)
        stats[...] = row_table([as_row(top), as_row(mass), as_row(summed)])


def head_logits(where, finals, w_unit, counts):
    halves, chunks = len(finals[0]), len(finals)
    half, width = finals[0][0].shape
    rows = half * halves * chunks
    vocab = w_unit.shape[1]
    lanes = 128 if vocab % 128 == 0 else vocab
    tile = tile_of(vocab, 640)
    return pl.pallas_call(
        functools.partial(logits_kernel, halves, chunks),
        grid_spec=pltpu.PrefetchScalarGridSpec(
            num_scalar_prefetch=1,
            grid=(vocab // tile,),
            in_specs=[
                *[whole_spec((half, width))] * (halves * chunks),
                pl.BlockSpec((width, tile), lambda t, s: (0, t)),
                pl.BlockSpec((rows, tile), lambda t, s: (0, t)),
            ],
            out_specs=[
                pl.BlockSpec((rows, tile), lambda t, s: (0, t)),
                whole_spec((8, rows)),
            ],
            scratch_shapes=[pltpu.VMEM((rows, width), BF16)] + [pltpu.VMEM((rows, lanes), F32)] * 3,
        ),
        out_shape=[
            jax.ShapeDtypeStruct((rows, vocab), F32),
            jax.ShapeDtypeStruct((8, rows), F32),
        ],
        compiler_params=params(VMEM_MIB),
        cost_estimate=cost(
            flops=2 * rows * width * vocab,
            bytes_accessed=(2 * width + 6 * rows) * vocab,
            transcendentals=rows * vocab,
        ),
        name="head_logits",
    )(where, *[half for final in finals for half in final], w_unit, counts)


def head_grads_kernel(denom, halves, chunks, tables, where, *refs):
    stats, refs = refs[:tables], refs[tables:]
    lengths, logits, counts, w_unit, *parts, results, shift, total = refs
    step = pl.program_id(0)

    @pl.when(step == 0)
    def _():
        values = [ref[...] for ref in stats]
        top = values[0][0:1, :]
        for table in values[1:]:
            top = jnp.maximum(top, table[0:1, :])
        mass = sum(table[1:2, :] * jnp.exp(table[0:1, :] - top) for table in values)
        target = sum(table[2:3, :] for table in values)
        lse = top + jnp.log(mass)
        moved = lse - jnp.log(lengths[...] * (1.0 / denom))
        shift[...] = as_columns(moved)
        results[...] = row_table([moved, lengths[...] * lse - target])
        total[...] = jnp.zeros_like(total)

    columns = []
    for start, size in pieces_of(w_unit.shape[1]):
        exped = jnp.exp(logits[:, start : start + size] - shift[:, 0:1])
        counted = counts[:, start : start + size].astype(F32) * (1.0 / denom)
        columns.append((exped - counted).astype(BF16))
    total[...] += dot_t(jnp.concatenate(columns, axis=1), w_unit[...])

    @pl.when(step == pl.num_programs(0) - 1)
    def _():
        half = total.shape[0] // (chunks * halves)
        for at in range(chunks):
            base = at * halves * half
            mine, theirs = base, base
            if halves == 2:
                mine, theirs = base + where[1] * half, base + (1 - where[1]) * half
                out = parts[chunks + at]
                out[...] = total[pl.ds(pl.multiple_of(theirs, half), half), :].astype(out.dtype)
                parts[at][...] = total[pl.ds(pl.multiple_of(mine, half), half), :]
            else:
                parts[at][...] = total[base : base + half, :]


def head_grads(where, halves, chunks, stats, lengths, logits, counts, w_unit, denom):
    rows, vocab = logits.shape
    width = w_unit.shape[0]
    tile = tile_of(vocab, 640)
    part = (rows // (halves * chunks), width)
    shapes = [(part, F32)] * chunks + [(part, BF16)] * (chunks * (halves - 1))
    shapes += [((8, rows), F32)]
    return pl.pallas_call(
        functools.partial(head_grads_kernel, denom, halves, chunks, len(stats)),
        grid_spec=pltpu.PrefetchScalarGridSpec(
            num_scalar_prefetch=1,
            grid=(vocab // tile,),
            in_specs=[
                *[whole_spec((8, rows))] * len(stats),
                whole_spec((1, rows)),
                pl.BlockSpec((rows, tile), lambda t, s: (0, t)),
                pl.BlockSpec((rows, tile), lambda t, s: (0, t)),
                pl.BlockSpec((width, tile), lambda t, s: (0, t)),
            ],
            out_specs=[whole_spec(shape) for shape, _ in shapes],
            scratch_shapes=[pltpu.VMEM((rows, 128), F32), pltpu.VMEM((rows, width), F32)],
        ),
        out_shape=[jax.ShapeDtypeStruct(*shape) for shape in shapes],
        compiler_params=params(VMEM_MIB),
        cost_estimate=cost(
            flops=2 * rows * width * vocab,
            bytes_accessed=(2 * width + 6 * rows) * vocab,
            transcendentals=rows * vocab,
        ),
        name="head_grads",
    )(where, *stats, lengths, logits, counts, w_unit)


def unit_kernel(blocks, tables, share, denom, where, *refs):
    x_refs, refs = refs[: len(blocks)], refs[len(blocks) :]
    shifts, refs = refs[:tables], refs[tables:]
    counts, refs = refs[:tables], refs[tables:]
    w_unit, grad, normed, normed_t, *columns_of = refs
    half = x_refs[0].shape[0]
    rows = normed.shape[0] // tables

    @pl.when(pl.program_id(0) == 0)
    def _():
        for ref, base in zip(x_refs, blocks):
            normed[base : base + half, :] = normalised(ref[...])
        columns = pl.ds(pl.multiple_of(where[0] * share, share), share)
        normed_t[...] = normed[:, columns].astype(F32).T.astype(BF16)
        for shift, column in zip(shifts, columns_of):
            column[...] = as_columns(shift[...])

    logits = dot(normed[...], w_unit[...])
    dlogits = []
    for k in range(tables):
        exped = jnp.exp(logits[k * rows : (k + 1) * rows] - columns_of[k][:, 0:1])
        counted = counts[k][...].astype(F32) * (1.0 / denom)
        dlogits.append((exped - counted).astype(BF16))
    grad[...] = dot(normed_t[...], jnp.concatenate(dlogits, axis=0))


def unit_grads(where, x_parts, shifts, counts, w_unit, denom, share):
    width, vocab = w_unit.shape
    tile = tile_of(vocab, 256)
    half = x_parts[0][0].shape[-2]
    rows = shifts[0].shape[1]
    tables = len(shifts)
    blocks = tuple(block for _, _, block in x_parts)
    return pl.pallas_call(
        functools.partial(unit_kernel, blocks, tables, share, denom),
        grid_spec=pltpu.PrefetchScalarGridSpec(
            num_scalar_prefetch=1,
            grid=(vocab // tile,),
            in_specs=[pl.BlockSpec((None, None, None, half, width), index) for _, index, _ in x_parts]
            + [whole_spec((1, rows))] * tables
            + [pl.BlockSpec((rows, tile), lambda j, s: (0, j))] * tables
            + [pl.BlockSpec((width, tile), lambda j, s: (0, j))],
            out_specs=pl.BlockSpec((share, tile), lambda j, s: (0, j)),
            scratch_shapes=[
                pltpu.VMEM((rows * tables, width), BF16),
                pltpu.VMEM((share, rows * tables), BF16),
                *[pltpu.VMEM((rows, 128), F32)] * tables,
            ],
        ),
        out_shape=jax.ShapeDtypeStruct((share, vocab), F32),
        compiler_params=params(VMEM_MIB),
        cost_estimate=cost(
            flops=2 * rows * tables * (width + share) * vocab,
            bytes_accessed=2 * (width + rows * tables) * vocab,
            transcendentals=rows * tables * vocab,
        ),
        name="unit_grads",
    )(where, *[x for x, _, _ in x_parts], *shifts, *counts, w_unit)


def weight_kernel(blocks, adding, share, where, *refs):
    x_refs, refs = refs[:blocks], refs[blocks:]
    g_refs, refs = refs[:blocks], refs[blocks:]
    w_in, w_out, refs = refs[0], refs[1], refs[2:]
    if adding:
        old_first, old_second, refs = refs[0], refs[1], refs[2:]
    first, second, normed, grads, normed_t, grads_t = refs
    count = x_refs[0].shape[0]

    @pl.when(pl.program_id(0) == 0)
    def _():
        columns = pl.ds(pl.multiple_of(where[0] * share, share), share)
        for at in range(blocks):
            place = pl.ds(at * count, count)
            normed[place, :] = normalised(x_refs[at][...])
            grads[place, :] = g_refs[at][...]
        normed_t[...] = normed[:, columns].astype(F32).T.astype(BF16)
        grads_t[...] = grads[:, columns].astype(F32).T.astype(BF16)

    for at, size in pieces_of(w_in.shape[1]):
        value, slope = gelu_parts(dot(normed[...], w_in[:, at : at + size]))
        dpre = dot_t(grads[...], w_out[at : at + size, :]).astype(BF16) * slope
        now_first = dot(normed_t[...], dpre)
        now_second = dot(grads_t[...], value).T
        if adding:
            now_first = old_first[:, at : at + size] + now_first
            now_second = old_second[at : at + size, :] + now_second
        first[:, at : at + size] = now_first
        second[at : at + size, :] = now_second


def weight_grads(where, x_parts, g_parts, w_in, w_out, old, share):
    width, hidden = w_in.shape
    tile = tile_of(hidden, 512)
    blocks = len(g_parts)
    count = g_parts[0][0].shape[-2]
    rows = blocks * count
    in_specs = [
        pl.BlockSpec((None,) * (array.ndim - 2) + (count, width), index)
        for array, index in (*x_parts, *g_parts)
    ]
    in_specs += [
        pl.BlockSpec((width, tile), lambda j, s: (0, j)),
        pl.BlockSpec((tile, width), lambda j, s: (j, 0)),
    ]
    grad_specs = [
        pl.BlockSpec((share, tile), lambda j, s: (0, j)),
        pl.BlockSpec((tile, share), lambda j, s: (j, 0)),
    ]
    adding = old is not None
    aliases = {}
    if adding:
        in_specs += grad_specs
        aliases = {1 + 2 * blocks + 2: 0, 1 + 2 * blocks + 3: 1}
    return pl.pallas_call(
        functools.partial(weight_kernel, blocks, adding, share),
        grid_spec=pltpu.PrefetchScalarGridSpec(
            num_scalar_prefetch=1,
            grid=(hidden // tile,),
            in_specs=in_specs,
            out_specs=grad_specs,
            scratch_shapes=[
                pltpu.VMEM((rows, width), BF16),
                pltpu.VMEM((rows, width), BF16),
                pltpu.VMEM((share, rows), BF16),
                pltpu.VMEM((share, rows), BF16),
            ],
        ),
        out_shape=[
            jax.ShapeDtypeStruct((share, hidden), F32),
            jax.ShapeDtypeStruct((hidden, share), F32),
        ],
        input_output_aliases=aliases,
        compiler_params=params(VMEM_MIB),
        cost_estimate=cost(
            flops=4 * rows * (width + share) * hidden,
            bytes_accessed=4 * width * hidden + 16 * share * hidden,
            transcendentals=rows * hidden,
        ),
        name="weight_grads",
    )(where, *[x for x, _ in x_parts], *[g for g, _ in g_parts], w_in, w_out, *(old or ()))


def unit_counts(ends, targets, ids):
    positions = jnp.arange(targets.shape[1], dtype=jnp.int32)
    row_local = jnp.sum((ends[:, None, :] <= positions[None, :, None]).astype(jnp.int32), axis=-1)
    rows = jnp.arange(ends.shape[1], dtype=jnp.int32)
    row_onehot = (row_local[:, :, None] == rows[None, None, :]).astype(BF16)
    hits = (targets[:, :, None] == ids[None, None, :]).astype(BF16)
    counts = jnp.einsum("mur,muv->mrv", row_onehot, hits, preferred_element_type=F32)
    return counts.astype(BF16)


def on_device(text_rows, durations, unit_targets, w_in, w_out, w_unit):
    micro, row_count, width = text_rows.shape
    segments = lax.axis_size("segment")
    mp_size = lax.axis_size("mp")
    dp_size = lax.axis_size("dp")
    seg = lax.axis_index("segment").astype(jnp.int32)
    mp_at = lax.axis_index("mp").astype(jnp.int32)
    dp_at = lax.axis_index("dp").astype(jnp.int32)
    last = segments - 1
    pair = mp_size == 2
    halves = 2 if pair else 1
    chunks = CHUNKS
    where = jnp.stack([seg, mp_at])
    first = w_in[0]
    second = w_out[0]
    rows = micro * row_count // chunks
    text = text_rows.reshape(chunks, rows, width)
    vocab_part = w_unit.shape[1]
    unit_count = unit_targets.shape[1]
    denom = float(micro * unit_count * dp_size)
    lengths = durations[:, 0, :]
    length_f = lengths.astype(F32).reshape(1, micro * row_count)
    ends = jnp.cumsum(lengths, axis=-1)
    own_ids = (seg * mp_size + mp_at) * vocab_part + jnp.arange(vocab_part, dtype=jnp.int32)

    def around(block):
        came = [block]
        for distance in range(1, dp_size):
            route = [(i, (i + distance) % dp_size) for i in range(dp_size)]
            came.append(lax.ppermute(block, "dp", route))
        return came

    unit_hits = [
        unit_counts(packed[:, unit_count:], packed[:, :unit_count], own_ids)
        for packed in around(jnp.concatenate([unit_targets, ends], axis=1))
    ]
    unit_hits = [hits.reshape(micro * row_count, vocab_part) for hits in unit_hits]

    def both(part):
        return [part, swapped(part)] if pair else [part]

    def reduced(keep, send):
        return [keep, swapped(send[0])] if pair else [lax.psum(keep, "mp")]

    def gathered_rows(mine):
        if pair:
            came = lax.all_gather(mine, ("mp", "dp"))
            return came.reshape(mp_size, dp_size, *mine.shape)
        return lax.all_gather(mine, "dp")[None]

    def all_tables(table):
        if not pair:
            return [t for t in lax.all_gather(table, ("segment", "mp"))]
        count = segments * mp_size
        return [table] + [
            lax.ppermute(table, ("segment", "mp"), [(i, (i + k) % count) for i in range(count)])
            for k in range(1, count)
        ]

    every = range(chunks)
    stash = [None] * chunks
    hops = [None] * chunks
    for stage in range(segments):
        for b in every:
            arrived = []
            if stage > 0:
                arrived = both(lax.ppermute(hops[b], "segment", [(stage - 1, stage)]))
            ties = [hops[b - 1], *unit_hits[stage : stage + 1]] if b > 0 else []
            outs = forward_section(
                where, stage, halves, text, b, arrived, stash[b], first, second, ties
            )
            stash[b], keep, send = outs[:halves], outs[halves], outs[halves + 1 :]
            pieces = reduced(keep, send)
            hops[b] = total_of(pieces if pair else [stash[b][0], *pieces]).astype(BF16)
    x_gathered = gathered_rows(jnp.stack([stash[b][0] for b in every]))

    finals = []
    for b in every:
        options = [(last, hops[b])]
        options += [
            (to, lax.ppermute(hops[b], "segment", [(last, to)])) for to in range(last)
        ]
        finals.append(both(chosen(seg, options)))
    logits, stats = head_logits(where, finals, w_unit, unit_hits[0])
    *parts, result = head_grads(
        where, halves, chunks, all_tables(stats), length_f, logits, unit_hits[0], w_unit, denom
    )
    loss = (jnp.sum(result[1, :]) / denom)[None]
    shifts = around(result[0:1, :])
    unit_rows = gathered_rows(jnp.stack([final[0] for final in finals]))
    for b in every:
        dnorm = total_of(reduced(parts[b], parts[chunks + b : chunks + b + 1])).astype(BF16)
        dnorm = total_of(
            [dnorm] + [lax.ppermute(dnorm, "segment", [(j, last)]) for j in range(last)]
        ).astype(BF16)
        hops[b] = norm_back(finals[b][0], dnorm.astype(F32)).astype(BF16)

    grads = [[] for _ in every]
    for stage in range(last):
        owner = last - stage
        for b in every:
            came = hops[b]
            if stage > 0:
                came = lax.ppermute(came, "segment", [(owner + 1, owner)])
            ties = [hops[b - 1]] if b > 0 else []
            outs = backward_section(
                where, owner, stash[b], both(came), grads[b], first, second, ties
            )
            grads[b], keep, send = outs[:halves], outs[halves], outs[halves + 1 :]
            hops[b] = finish_backward(stash[b][0], came, reduced(keep, send))

    unit_parts = [
        (
            unit_rows,
            lambda j, s, side=side, k=k, b=b: (side, lax.rem(s[0] + dp_size - k, dp_size), b, 0, 0),
            (k * micro * row_count + b * rows + side * (rows // halves)),
        )
        for side in range(halves)
        for k in range(dp_size)
        for b in every
    ]
    sum_unit = unit_grads(
        dp_at[None], unit_parts, shifts, unit_hits, w_unit, denom, width // dp_size
    )
    share = width // dp_size
    sums = None
    sources = [None] * chunks

    def own_parts(halves_of):
        return [(half, lambda j, s: (0, 0)) for half in halves_of]

    def other_parts(array, tail):
        return [
            (array, lambda j, s, side=side, k=k: (side, lax.rem(s[0] + k, dp_size), *tail, 0, 0))
            for side in range(halves)
            for k in range(1, dp_size)
        ]

    def weight_step(x_parts, g_parts, sums):
        return weight_grads(dp_at[None], x_parts, g_parts, first, second, sums, share)

    waiting = ([], [])
    for b in every:
        arrived = both(lax.ppermute(hops[b], "segment", [(1, 0)]))
        ties = [sum_unit, sums[0]] if b == 1 else []
        grads[b] = pick(where, 0, arrived, grads[b], ties)
        source = gathered_rows(grads[b][0])
        x_parts = own_parts(stash[b]) + waiting[0]
        g_parts = own_parts(grads[b]) + waiting[1]
        sums = weight_step(x_parts, g_parts, sums)
        waiting = (other_parts(x_gathered, (b,)), other_parts(source, ()))
    sums = weight_step(*waiting, sums)
    return (loss, sums[0][None], sums[1][None], sum_unit)


def solution(mesh):
    placed = (
        P(None, "dp", None),
        P(None, "dp", None),
        P(None, "dp"),
        P("segment", None, "mp"),
        P("segment", "mp", None),
        P(None, ("segment", "mp")),
    )
    return jax.shard_map(
        on_device,
        mesh=mesh,
        in_specs=placed,
        out_specs=(
            P("dp"),
            P("segment", "dp", "mp"),
            P("segment", "mp", "dp"),
            P("dp", ("segment", "mp")),
        ),
        check_vma=False,
    )
```

```python
import functools
import jax
import jax.numpy as jnp
from jax import lax
from jax.experimental import pallas as pl
from jax.experimental.pallas import tpu as pltpu
from jax.sharding import PartitionSpec as P

CHUNKS = 2
VMEM_MIB = 60
BF16 = jnp.bfloat16
F32 = jnp.float32
MIB = 1024 * 1024


def shifted(block, axis, distance):
    devices = range(lax.axis_size(axis))
    route = [(i - distance, i) for i in devices if i - distance in devices]
    return lax.ppermute(block, axis, route)


def swapped(block):
    return lax.ppermute(block, "mp", [(0, 1), (1, 0)])


def gelu_parts(pre_vals):
    coeff = 0.7978845608
    pre = pre_vals.astype(BF16)
    square = pre * pre
    inner = pre * (square * BF16(coeff * 0.044715) + BF16(coeff))
    half = jnp.tanh(inner) * BF16(0.5) + BF16(0.5)
    value = pre * half
    bend = square * BF16(6.0 * coeff * 0.044715) + BF16(2.0 * coeff)
    slope = half + value * (BF16(1.0) - half) * bend
    return (value, slope)


def row_scale(rows_in):
    floats = rows_in.astype(F32)
    return lax.rsqrt(jnp.mean(floats * floats, axis=-1, keepdims=True) + 1e-06)


def normalised(rows_in):
    return (rows_in.astype(F32) * row_scale(rows_in)).astype(BF16)


def norm_back(rows_in, grads):
    scale = row_scale(rows_in)
    normal = rows_in.astype(F32) * scale
    return scale * (grads - normal * jnp.mean(grads * normal, axis=-1, keepdims=True))


def dot(a, b):
    return jnp.dot(a, b, preferred_element_type=F32)


def dot_t(a, b):
    return lax.dot_general(a, b, (((1,), (1,)), ((), ())), preferred_element_type=F32)


def t_dot(a, b):
    return lax.dot_general(a, b, (((0,), (0,)), ((), ())), preferred_element_type=F32)


def tile_of(size, most):
    if size <= most:
        return size
    return max(t for t in range(128, most + 1, 128) if size % t == 0)


def pieces_of(size):
    return [(at, min(256, size - at)) for at in range(0, size, 256)]


def cost(flops, bytes_accessed, transcendentals):
    return pl.CostEstimate(
        flops=flops,
        bytes_accessed=bytes_accessed,
        transcendentals=transcendentals,
    )


def params(limit):
    return pltpu.CompilerParams(vmem_limit_bytes=limit * MIB)


def chosen(index, candidates):
    value = candidates[0][1]
    for at, option in candidates[1:]:
        value = jnp.where(index == at, option, value)
    return value


def gathered(halves, place):
    if len(halves) == 1:
        return halves[0][...]
    mine, theirs = (half[...] for half in halves)
    first = jnp.where(place == 0, mine, theirs)
    second = jnp.where(place == 0, theirs, mine)
    return jnp.concatenate([first, second], axis=0)


def part_of(block, place, parts):
    rows = block.shape[0] // parts
    if parts == 1:
        return block[...]
    return block[pl.ds(pl.multiple_of(place * rows, rows), rows), :]


def whole_spec(shape):
    return pl.BlockSpec(shape, lambda *_: (0,) * len(shape))


def keep_live(live, arrived, before, after):
    for came, old, new in zip(arrived, before, after):
        new[...] = jnp.where(live, came[...], old[...])


def tile_copies(w_in, w_out, in_buf, out_buf, sems, tile):
    copies = []
    for at in range(w_in.shape[1] // tile):
        part = pl.ds(at * tile, tile)
        copies.append(
            (
                pltpu.make_async_copy(w_in.at[:, part], in_buf.at[:, part], sems.at[0, at]),
                pltpu.make_async_copy(w_out.at[part, :], out_buf.at[part, :], sems.at[1, at]),
            )
        )
    return copies


def emit(total, added, place, keep, send):
    if send:
        kept = part_of(total, place, 2)
        keep[...] = kept if added is None else kept + part_of(added, place, 2).astype(F32)
        send[0][...] = part_of(total, 1 - place, 2).astype(send[0].dtype)
    else:
        keep[...] = total[...]


def forward_kernel(halves, stage, ties, tile, where, *refs):
    refs = refs[ties:]
    if stage == 0:
        own, refs = refs[0], refs[1:]
    else:
        arrived, refs = refs[:halves], refs[halves:]
        before, refs = refs[:halves], refs[halves:]
    w_in, w_out, refs = refs[0], refs[1], refs[2:]
    after, refs = refs[:halves], refs[halves:]
    keep, *send, whole, normed, total, in_buf, out_buf, sems = refs
    live = where[0] == stage
    copies = tile_copies(w_in, w_out, in_buf, out_buf, sems, tile)

    @pl.when(live)
    def _():
        for pair in copies:
            for copy in pair:
                copy.start()

    if stage == 0:
        whole[...] = own[...]
        after[0][...] = part_of(whole, where[1], halves)
        if halves == 2:
            after[1][...] = part_of(whole, 1 - where[1], halves)
    else:
        whole[...] = gathered(arrived, where[1])
        keep_live(live, arrived, before, after)

    @pl.when(live)
    def _():
        normed[...] = normalised(whole[...])
        for index, pair in enumerate(copies):
            for copy in pair:
                copy.wait()
            values = []
            for at, size in pieces_of(tile):
                start = index * tile + at
                value, _ = gelu_parts(dot(normed[...], in_buf[:, start : start + size]))
                values.append(value)
            part = dot(
                jnp.concatenate(values, axis=1), out_buf[index * tile : (index + 1) * tile, :]
            )
            total[...] = part if index == 0 else total[...] + part
        emit(total, whole, where[1], keep, send)

    @pl.when(jnp.logical_not(live))
    def _():
        for ref in (keep, *send):
            ref[...] = jnp.zeros_like(ref)


def section_call(body, name, where, ties, operands, specs, w_in, w_out, shapes, scratch, flops):
    width, hidden = w_in.shape
    tile = tile_of(hidden, 1024)
    return pl.pallas_call(
        functools.partial(body, tile),
        grid_spec=pltpu.PrefetchScalarGridSpec(
            num_scalar_prefetch=1,
            grid=(1,),
            in_specs=[pl.BlockSpec(memory_space=pl.ANY)] * len(ties)
            + specs
            + [pl.BlockSpec(memory_space=pl.ANY)] * 2,
            out_specs=[whole_spec(shape) for shape, _ in shapes],
            scratch_shapes=scratch
            + [
                pltpu.VMEM((width, hidden), BF16),
                pltpu.VMEM((hidden, width), BF16),
                pltpu.SemaphoreType.DMA((2, hidden // tile)),
            ],
        ),
        out_shape=[jax.ShapeDtypeStruct(*shape) for shape in shapes],
        compiler_params=params(VMEM_MIB),
        cost_estimate=cost(
            flops=flops, bytes_accessed=4 * width * hidden, transcendentals=flops // 4096
        ),
        name=name,
    )(where, *ties, *operands, w_in, w_out)


def forward_section(where, stage, halves, text, at, arrived, before, w_in, w_out, ties):
    _, rows, width = text.shape
    full, part = (rows, width), (rows // halves, width)
    shapes = [(part, BF16)] * halves + [(part, F32)] + [(part, BF16)] * (halves - 1)
    if stage == 0:
        operands = [text]
        specs = [pl.BlockSpec((None, rows, width), lambda j, s: (at, 0, 0))]
    else:
        operands = [*arrived, *before]
        specs = [whole_spec(part)] * len(operands)

    def body(tile, *refs):
        forward_kernel(halves, stage, len(ties), tile, *refs)

    scratch = [pltpu.VMEM(full, BF16), pltpu.VMEM(full, BF16), pltpu.VMEM(full, F32)]
    flops = 4 * rows * width * w_in.shape[1]
    return section_call(
        body, "section_forward", where, ties, operands, specs, w_in, w_out, shapes, scratch, flops
    )


def total_of(pieces):
    total = pieces[0].astype(F32)
    for piece in pieces[1:]:
        total = total + piece.astype(F32)
    return total


def finish_backward(rows, grads, pieces):
    return (grads.astype(F32) + norm_back(rows, total_of(pieces))).astype(BF16)


def backward_kernel(halves, owner, old, ties, tile, where, *refs):
    refs = refs[ties:]
    stash, refs = refs[:halves], refs[halves:]
    arrived, refs = refs[:halves], refs[halves:]
    before, refs = refs[:old], refs[old:]
    w_in, w_out, refs = refs[0], refs[1], refs[2:]
    after, refs = refs[:halves], refs[halves:]
    keep, *send, grads, normed, total, in_buf, out_buf, sems = refs
    live = where[0] == owner
    copies = tile_copies(w_in, w_out, in_buf, out_buf, sems, tile)

    @pl.when(live)
    def _():
        for pair in copies:
            for copy in pair:
                copy.start()

    keep_live(live, arrived, before if old else arrived, after)

    @pl.when(live)
    def _():
        grads[...] = gathered(arrived, where[1])
        normed[...] = normalised(gathered(stash, where[1]))
        for index, pair in enumerate(copies):
            for copy in pair:
                copy.wait()
            dpres = []
            for at, size in pieces_of(tile):
                part = slice(index * tile + at, index * tile + at + size)
                _, slope = gelu_parts(dot(normed[...], in_buf[:, part]))
                dpres.append(dot_t(grads[...], out_buf[part, :]).astype(BF16) * slope)
            part = dot_t(
                jnp.concatenate(dpres, axis=1), in_buf[:, index * tile : (index + 1) * tile]
            )
            total[...] = part if index == 0 else total[...] + part
        emit(total, None, where[1], keep, send)

    @pl.when(jnp.logical_not(live))
    def _():
        for ref in (keep, *send):
            ref[...] = jnp.zeros_like(ref)


def backward_section(where, owner, stash, arrived, before, w_in, w_out, ties):
    halves = len(stash)
    part = stash[0].shape
    full = (part[0] * halves, part[1])
    shapes = [(part, BF16)] * halves + [(part, F32)] + [(part, BF16)] * (halves - 1)
    operands = [*stash, *arrived, *before]

    def body(tile, *refs):
        backward_kernel(halves, owner, len(before), len(ties), tile, *refs)

    scratch = [pltpu.VMEM(full, BF16)] * 2 + [pltpu.VMEM(full, F32)]
    flops = 6 * full[0] * full[1] * w_in.shape[1]
    specs = [whole_spec(part)] * len(operands)
    return section_call(
        body, "section_backward", where, ties, operands, specs, w_in, w_out, shapes, scratch, flops
    )


def pick_kernel(halves, owner, ties, where, *refs):
    refs = refs[ties:]
    arrived, before, after = refs[:halves], refs[halves : 2 * halves], refs[2 * halves :]
    keep_live(where[0] == owner, arrived, before, after)


def pick(where, owner, arrived, before, ties):
    halves = len(arrived)
    part = arrived[0].shape
    return pl.pallas_call(
        functools.partial(pick_kernel, halves, owner, len(ties)),
        grid_spec=pltpu.PrefetchScalarGridSpec(
            num_scalar_prefetch=1,
            grid=(1,),
            in_specs=[pl.BlockSpec(memory_space=pl.ANY)] * len(ties)
            + [whole_spec(part)] * (2 * halves),
            out_specs=[whole_spec(part)] * halves,
        ),
        out_shape=[jax.ShapeDtypeStruct(part, BF16)] * halves,
        compiler_params=params(VMEM_MIB),
        name="pick_grads",
    )(where, *ties, *arrived, *before)


def row_table(rows):
    pad = jnp.zeros((8 - len(rows), rows[0].shape[1]), F32)
    return jnp.concatenate([*rows, pad], axis=0)


def as_row(column):
    return jnp.broadcast_to(column, (column.shape[0], 128)).T[0:1, :]


def as_columns(row):
    return jnp.broadcast_to(row, (128, row.shape[1])).T


def logits_kernel(halves, chunks, ties, where, *refs):
    refs = refs[ties:]
    finals, refs = refs[: halves * chunks], refs[halves * chunks :]
    w_unit, counts, logits, stats, normed, peak, total, target = refs
    step = pl.program_id(0)
    lanes = peak.shape[1]

    @pl.when(step == 0)
    def _():
        rows = normed.shape[0] // chunks
        for at in range(chunks):
            final = finals[at * halves : (at + 1) * halves]
            normed[at * rows : (at + 1) * rows, :] = normalised(gathered(final, where[1]))
        peak[...] = jnp.full_like(peak, -1e30)
        total[...] = jnp.zeros_like(total)
        target[...] = jnp.zeros_like(target)

    columns = []
    for start, size in pieces_of(w_unit.shape[1]):
        values = dot(normed[...], w_unit[:, start : start + size])
        logits[:, start : start + size] = values
        counted = counts[:, start : start + size].astype(F32) * values
        columns += [
            (values[:, c : c + lanes], counted[:, c : c + lanes]) for c in range(0, size, lanes)
        ]
    higher = peak[...]
    for values, _ in columns:
        higher = jnp.maximum(higher, values)
    mass = total[...] * jnp.exp(peak[...] - higher)
    summed = target[...]
    for values, counted in columns:
        mass = mass + jnp.exp(values - higher)
        summed = summed + counted
    peak[...] = higher
    total[...] = mass
    target[...] = summed

    @pl.when(step == pl.num_programs(0) - 1)
    def _():
        top = jnp.max(peak[...], axis=-1, keepdims=True)
        mass = jnp.sum(total[...] * jnp.exp(peak[...] - top), axis=-1, keepdims=True)
        summed = jnp.sum(target[...], axis=-1, keepdims=True)
        stats[...] = row_table([as_row(top), as_row(mass), as_row(summed)])


def head_logits(where, finals, w_unit, counts, ties):
    halves, chunks = len(finals[0]), len(finals)
    half, width = finals[0][0].shape
    rows = half * halves * chunks
    vocab = w_unit.shape[1]
    lanes = 128 if vocab % 128 == 0 else vocab
    tile = tile_of(vocab, 640)
    return pl.pallas_call(
        functools.partial(logits_kernel, halves, chunks, len(ties)),
        grid_spec=pltpu.PrefetchScalarGridSpec(
            num_scalar_prefetch=1,
            grid=(vocab // tile,),
            in_specs=[
                *[pl.BlockSpec(memory_space=pl.ANY)] * len(ties),
                *[whole_spec((half, width))] * (halves * chunks),
                pl.BlockSpec((width, tile), lambda t, s: (0, t)),
                pl.BlockSpec((rows, tile), lambda t, s: (0, t)),
            ],
            out_specs=[
                pl.BlockSpec((rows, tile), lambda t, s: (0, t)),
                whole_spec((8, rows)),
            ],
            scratch_shapes=[pltpu.VMEM((rows, width), BF16)] + [pltpu.VMEM((rows, lanes), F32)] * 3,
        ),
        out_shape=[
            jax.ShapeDtypeStruct((rows, vocab), F32),
            jax.ShapeDtypeStruct((8, rows), F32),
        ],
        compiler_params=params(VMEM_MIB),
        cost_estimate=cost(
            flops=2 * rows * width * vocab,
            bytes_accessed=(2 * width + 6 * rows) * vocab,
            transcendentals=rows * vocab,
        ),
        name="head_logits",
    )(where, *ties, *[half for final in finals for half in final], w_unit, counts)


def head_grads_kernel(denom, halves, chunks, tables, ties, where, *refs):
    refs = refs[ties:]
    stats, refs = refs[:tables], refs[tables:]
    lengths, logits, counts, w_unit, *parts, results, shift, total = refs
    step = pl.program_id(0)

    @pl.when(step == 0)
    def _():
        values = [ref[...] for ref in stats]
        top = values[0][0:1, :]
        for table in values[1:]:
            top = jnp.maximum(top, table[0:1, :])
        mass = sum(table[1:2, :] * jnp.exp(table[0:1, :] - top) for table in values)
        target = sum(table[2:3, :] for table in values)
        lse = top + jnp.log(mass)
        moved = lse - jnp.log(lengths[...] * (1.0 / denom))
        shift[...] = as_columns(moved)
        results[...] = row_table([moved, lengths[...] * lse - target])
        total[...] = jnp.zeros_like(total)

    columns = []
    for start, size in pieces_of(w_unit.shape[1]):
        exped = jnp.exp(logits[:, start : start + size] - shift[:, 0:1])
        counted = counts[:, start : start + size].astype(F32) * (1.0 / denom)
        columns.append((exped - counted).astype(BF16))
    total[...] += dot_t(jnp.concatenate(columns, axis=1), w_unit[...])

    @pl.when(step == pl.num_programs(0) - 1)
    def _():
        half = total.shape[0] // (chunks * halves)
        for at in range(chunks):
            base, out = at * halves * half, slice(at * half, (at + 1) * half)
            if halves == 2:
                mine, theirs = base + where[1] * half, base + (1 - where[1]) * half
                given = total[pl.ds(pl.multiple_of(theirs, half), half), :]
                parts[1][out, :] = given.astype(parts[1].dtype)
                parts[0][out, :] = total[pl.ds(pl.multiple_of(mine, half), half), :]
            else:
                parts[0][out, :] = total[base : base + half, :]


def head_grads(where, halves, chunks, stats, lengths, logits, counts, w_unit, denom, ties):
    rows, vocab = logits.shape
    width = w_unit.shape[0]
    tile = tile_of(vocab, 640)
    part = (rows // halves, width)
    shapes = [(part, F32)] + [(part, BF16)] * (halves - 1) + [((8, rows), F32)]
    return pl.pallas_call(
        functools.partial(head_grads_kernel, denom, halves, chunks, len(stats), len(ties)),
        grid_spec=pltpu.PrefetchScalarGridSpec(
            num_scalar_prefetch=1,
            grid=(vocab // tile,),
            in_specs=[
                *[pl.BlockSpec(memory_space=pl.ANY)] * len(ties),
                *[whole_spec((8, rows))] * len(stats),
                whole_spec((1, rows)),
                pl.BlockSpec((rows, tile), lambda t, s: (0, t)),
                pl.BlockSpec((rows, tile), lambda t, s: (0, t)),
                pl.BlockSpec((width, tile), lambda t, s: (0, t)),
            ],
            out_specs=[whole_spec(shape) for shape, _ in shapes],
            scratch_shapes=[pltpu.VMEM((rows, 128), F32), pltpu.VMEM((rows, width), F32)],
        ),
        out_shape=[jax.ShapeDtypeStruct(*shape) for shape in shapes],
        compiler_params=params(VMEM_MIB),
        cost_estimate=cost(
            flops=2 * rows * width * vocab,
            bytes_accessed=(2 * width + 6 * rows) * vocab,
            transcendentals=rows * vocab,
        ),
        name="head_grads",
    )(where, *ties, *stats, lengths, logits, counts, w_unit)


def unit_kernel(tables, share, denom, where, *refs):
    gathered_x, refs = refs[0], refs[1:]
    shifts, refs = refs[:tables], refs[tables:]
    counts, refs = refs[:tables], refs[tables:]
    w_unit, grad, normed, normed_t, *columns_of = refs
    halves, dp_size, chunks, half, _ = gathered_x.shape
    rows = normed.shape[0] // tables

    @pl.when(pl.program_id(0) == 0)
    def _():
        for k in range(tables):
            owner = lax.rem(where[0] + dp_size - k, dp_size)
            for b in range(chunks):
                for side in range(halves):
                    base = k * rows + (b * halves + side) * half
                    normed[base : base + half, :] = normalised(gathered_x[side, owner, b])
        columns = pl.ds(pl.multiple_of(where[0] * share, share), share)
        normed_t[...] = normed[:, columns].astype(F32).T.astype(BF16)
        for shift, column in zip(shifts, columns_of):
            column[...] = as_columns(shift[...])

    logits = dot(normed[...], w_unit[...])
    dlogits = []
    for k in range(tables):
        exped = jnp.exp(logits[k * rows : (k + 1) * rows] - columns_of[k][:, 0:1])
        counted = counts[k][...].astype(F32) * (1.0 / denom)
        dlogits.append((exped - counted).astype(BF16))
    grad[...] = dot(normed_t[...], jnp.concatenate(dlogits, axis=0))


def unit_grads(where, gathered_x, shifts, counts, w_unit, denom, share):
    width, vocab = w_unit.shape
    tile = tile_of(vocab, 256)
    rows = shifts[0].shape[1]
    tables = len(shifts)
    return pl.pallas_call(
        functools.partial(unit_kernel, tables, share, denom),
        grid_spec=pltpu.PrefetchScalarGridSpec(
            num_scalar_prefetch=1,
            grid=(vocab // tile,),
            in_specs=[whole_spec(gathered_x.shape)]
            + [whole_spec((1, rows))] * tables
            + [pl.BlockSpec((rows, tile), lambda j, s: (0, j))] * tables
            + [pl.BlockSpec((width, tile), lambda j, s: (0, j))],
            out_specs=pl.BlockSpec((share, tile), lambda j, s: (0, j)),
            scratch_shapes=[
                pltpu.VMEM((rows * tables, width), BF16),
                pltpu.VMEM((share, rows * tables), BF16),
                *[pltpu.VMEM((rows, 128), F32)] * tables,
            ],
        ),
        out_shape=jax.ShapeDtypeStruct((share, vocab), F32),
        compiler_params=params(VMEM_MIB),
        cost_estimate=cost(
            flops=2 * rows * tables * (width + share) * vocab,
            bytes_accessed=2 * (width + rows * tables) * vocab,
            transcendentals=rows * tables * vocab,
        ),
        name="unit_grads",
    )(where, gathered_x, *shifts, *counts, w_unit)


def row_copies(sources, parts, me, dp_size, target, sems):
    copies = []
    base = 0
    for at, (slot, selected) in enumerate(parts):
        ref = sources[slot]
        if selected is not None:
            side, distance, rest = selected
            ref = ref.at[(side, lax.rem(me + distance, dp_size), *rest)]
        count = ref.shape[0]
        copies.append(
            pltpu.make_async_copy(ref, target.at[pl.ds(base, count), :], sems.at[at])
        )
        base += count
    return copies


def weight_kernel(x_parts, g_parts, sources, adding, share, dp_size, where, *refs):
    arrays, refs = refs[:sources], refs[sources:]
    w_in, w_out, refs = refs[0], refs[1], refs[2:]
    if adding:
        old_first, old_second, refs = refs[0], refs[1], refs[2:]
    first, second, normed, grads, normed_t, grads_t, x_sems, g_sems = refs

    @pl.when(pl.program_id(0) == 0)
    def _():
        columns = pl.ds(pl.multiple_of(where[0] * share, share), share)
        x_copies = row_copies(arrays, x_parts, where[0], dp_size, normed, x_sems)
        g_copies = row_copies(arrays, g_parts, where[0], dp_size, grads, g_sems)
        for copy in x_copies + g_copies:
            copy.start()
        for copy in x_copies:
            copy.wait()
        normed[...] = normalised(normed[...])
        normed_t[...] = normed[:, columns].astype(F32).T.astype(BF16)
        for copy in g_copies:
            copy.wait()
        grads_t[...] = grads[:, columns].astype(F32).T.astype(BF16)

    for at, size in pieces_of(w_in.shape[1]):
        value, slope = gelu_parts(dot(normed[...], w_in[:, at : at + size]))
        dpre = dot_t(grads[...], w_out[at : at + size, :]).astype(BF16) * slope
        now_first = dot(normed_t[...], dpre)
        now_second = dot(grads_t[...], value).T
        if adding:
            now_first = old_first[:, at : at + size] + now_first
            now_second = old_second[at : at + size, :] + now_second
        first[:, at : at + size] = now_first
        second[at : at + size, :] = now_second


def weight_grads(where, x_parts, g_parts, w_in, w_out, old, share):
    width, hidden = w_in.shape
    tile = tile_of(hidden, 1024)
    arrays, rows = [], 0
    slots = []
    for parts in (x_parts, g_parts):
        placed = []
        for array, selected in parts:
            known = [at for at, other in enumerate(arrays) if other is array]
            if not known:
                arrays.append(array)
            placed.append((known[0] if known else len(arrays) - 1, selected))
        slots.append(tuple(placed))
    rows = sum(array.shape[-2] for array, _ in x_parts)
    dp_size = width // share
    hbm = pl.BlockSpec(memory_space=pl.ANY)
    in_specs = [hbm] * len(arrays) + [
        pl.BlockSpec((width, tile), lambda j, s: (0, j)),
        pl.BlockSpec((tile, width), lambda j, s: (j, 0)),
    ]
    grad_specs = [
        pl.BlockSpec((share, tile), lambda j, s: (0, j)),
        pl.BlockSpec((tile, share), lambda j, s: (j, 0)),
    ]
    adding = old is not None
    aliases = {}
    if adding:
        in_specs += grad_specs
        aliases = {len(arrays) + 3: 0, len(arrays) + 4: 1}
    return pl.pallas_call(
        functools.partial(
            weight_kernel, slots[0], slots[1], len(arrays), adding, share, dp_size
        ),
        grid_spec=pltpu.PrefetchScalarGridSpec(
            num_scalar_prefetch=1,
            grid=(hidden // tile,),
            in_specs=in_specs,
            out_specs=grad_specs,
            scratch_shapes=[
                pltpu.VMEM((rows, width), BF16),
                pltpu.VMEM((rows, width), BF16),
                pltpu.VMEM((share, rows), BF16),
                pltpu.VMEM((share, rows), BF16),
                pltpu.SemaphoreType.DMA((len(x_parts),)),
                pltpu.SemaphoreType.DMA((len(g_parts),)),
            ],
        ),
        out_shape=[
            jax.ShapeDtypeStruct((share, hidden), F32),
            jax.ShapeDtypeStruct((hidden, share), F32),
        ],
        input_output_aliases=aliases,
        compiler_params=params(VMEM_MIB),
        cost_estimate=cost(
            flops=4 * rows * (width + share) * hidden,
            bytes_accessed=4 * width * hidden + 16 * share * hidden,
            transcendentals=rows * hidden,
        ),
        name="weight_grads",
    )(where, *arrays, w_in, w_out, *(old or ()))


def unit_counts(ends, targets, ids):
    positions = jnp.arange(targets.shape[1], dtype=jnp.int32)
    row_local = jnp.sum((ends[:, None, :] <= positions[None, :, None]).astype(jnp.int32), axis=-1)
    rows = jnp.arange(ends.shape[1], dtype=jnp.int32)
    row_onehot = (row_local[:, :, None] == rows[None, None, :]).astype(BF16)
    hits = (targets[:, :, None] == ids[None, None, :]).astype(BF16)
    counts = jnp.einsum("mur,muv->mrv", row_onehot, hits, preferred_element_type=F32)
    return counts.astype(BF16)


def on_device(text_rows, durations, unit_targets, w_in, w_out, w_unit):
    micro, row_count, width = text_rows.shape
    segments = lax.axis_size("segment")
    mp_size = lax.axis_size("mp")
    dp_size = lax.axis_size("dp")
    seg = lax.axis_index("segment").astype(jnp.int32)
    mp_at = lax.axis_index("mp").astype(jnp.int32)
    dp_at = lax.axis_index("dp").astype(jnp.int32)
    last = segments - 1
    pair = mp_size == 2
    halves = 2 if pair else 1
    chunks = CHUNKS
    where = jnp.stack([seg, mp_at])
    first = w_in[0]
    second = w_out[0]
    rows = micro * row_count // chunks
    text = text_rows.reshape(chunks, rows, width)
    vocab_part = w_unit.shape[1]
    unit_count = unit_targets.shape[1]
    denom = float(micro * unit_count * dp_size)
    lengths = durations[:, 0, :]
    length_f = lengths.astype(F32).reshape(1, micro * row_count)
    ends = jnp.cumsum(lengths, axis=-1)
    own_ids = (seg * mp_size + mp_at) * vocab_part + jnp.arange(vocab_part, dtype=jnp.int32)

    def around(block):
        came = [block]
        for distance in range(1, dp_size):
            route = [(i, (i + distance) % dp_size) for i in range(dp_size)]
            came.append(lax.ppermute(block, "dp", route))
        return came

    packed = lax.all_gather(jnp.concatenate([unit_targets, ends], axis=1), "dp")
    tables = [jnp.concatenate([unit_targets, ends], axis=1)] + [
        lax.dynamic_index_in_dim(packed, lax.rem(dp_at + dp_size - k, dp_size), 0, False)
        for k in range(1, dp_size)
    ]
    unit_hits = [
        unit_counts(table[:, unit_count:], table[:, :unit_count], own_ids).reshape(
            micro * row_count, vocab_part
        )
        for table in tables
    ]

    def both(part):
        return [part, swapped(part)] if pair else [part]

    def reduced(keep, send):
        return [keep, swapped(send[0])] if pair else [lax.psum(keep, "mp")]

    def gathered_rows(mine):
        if pair:
            came = lax.all_gather(mine, ("mp", "dp"))
            return came.reshape(mp_size, dp_size, *mine.shape)
        return lax.all_gather(mine, "dp")[None]

    def all_tables(table):
        if not pair:
            return [t for t in lax.all_gather(table, ("segment", "mp"))]
        count = segments * mp_size
        return [table] + [
            lax.ppermute(table, ("segment", "mp"), [(i, (i + k) % count) for i in range(count)])
            for k in range(1, count)
        ]

    every = range(chunks)
    stash = [None] * chunks
    hops = [None] * chunks
    for stage in range(segments):
        for b in every:
            arrived = []
            if stage > 0:
                arrived = both(lax.ppermute(hops[b], "segment", [(stage - 1, stage)]))
            ties = [hops[b - 1]] if b > 0 or stage > 0 else []
            if stage == 0 and b > 0:
                ties = [*ties, unit_hits[0]]
            outs = forward_section(
                where, stage, halves, text, b, arrived, stash[b], first, second, ties
            )
            stash[b], keep, send = outs[:halves], outs[halves], outs[halves + 1 :]
            pieces = reduced(keep, send)
            hops[b] = total_of(pieces if pair else [stash[b][0], *pieces]).astype(BF16)
    x_gathered = gathered_rows(jnp.stack([stash[b][0] for b in every]))

    finals = []
    for b in every:
        options = [(last, hops[b])]
        options += [
            (to, lax.ppermute(hops[b], "segment", [(last, to)])) for to in range(last)
        ]
        finals.append(both(chosen(seg, options)))
    logits, stats = head_logits(where, finals, w_unit, unit_hits[0], unit_hits[1:2])
    keep, *send, result = head_grads(
        where,
        halves,
        chunks,
        all_tables(stats),
        length_f,
        logits,
        unit_hits[0],
        w_unit,
        denom,
        unit_hits[2:3],
    )
    loss = (jnp.sum(result[1, :]) / denom)[None]
    shifts = around(result[0:1, :])
    unit_rows = gathered_rows(jnp.stack([final[0] for final in finals]))
    dnorm = total_of(reduced(keep, send)).astype(BF16)
    dnorm = total_of(
        [dnorm] + [lax.ppermute(dnorm, "segment", [(j, last)]) for j in range(last)]
    ).astype(BF16)
    half = rows // halves
    for b in every:
        grad_rows = dnorm[b * half : (b + 1) * half].astype(F32)
        hops[b] = norm_back(finals[b][0], grad_rows).astype(BF16)

    grads = [[] for _ in every]
    for stage in range(last):
        owner = last - stage
        for b in every:
            came = hops[b]
            if stage > 0:
                came = lax.ppermute(came, "segment", [(owner + 1, owner)])
            ties = unit_hits[3:] if b == 0 and stage == 0 else [hops[b - 1]]
            outs = backward_section(
                where, owner, stash[b], both(came), grads[b], first, second, ties
            )
            grads[b], keep, send = outs[:halves], outs[halves], outs[halves + 1 :]
            hops[b] = finish_backward(stash[b][0], came, reduced(keep, send))

    sum_unit = unit_grads(
        dp_at[None], unit_rows, shifts, unit_hits, w_unit, denom, width // dp_size
    )
    share = width // dp_size
    sums = None
    sources = [None] * chunks

    def own_parts(halves_of):
        return [(half, None) for half in halves_of]

    def other_parts(array, rest):
        return [(array, (side, k, rest)) for side in range(halves) for k in range(1, dp_size)]

    def weight_step(x_parts, g_parts, sums):
        return weight_grads(dp_at[None], x_parts, g_parts, first, second, sums, share)

    waiting = ([], [])
    for b in every:
        arrived = both(lax.ppermute(hops[b], "segment", [(1, 0)]))
        ties = [sums[0]] if b == 1 else []
        grads[b] = pick(where, 0, arrived, grads[b], ties)
        source = gathered_rows(grads[b][0])
        x_parts = own_parts(stash[b]) + waiting[0]
        g_parts = own_parts(grads[b]) + waiting[1]
        sums = weight_step(x_parts, g_parts, sums)
        waiting = (other_parts(x_gathered, (b,)), other_parts(source, ()))
    sums = weight_step(*waiting, sums)
    return (loss, sums[0][None], sums[1][None], sum_unit)


def solution(mesh):
    placed = (
        P(None, "dp", None),
        P(None, "dp", None),
        P(None, "dp"),
        P("segment", None, "mp"),
        P("segment", "mp", None),
        P(None, ("segment", "mp")),
    )
    return jax.shard_map(
        on_device,
        mesh=mesh,
        in_specs=placed,
        out_specs=(
            P("dp"),
            P("segment", "dp", "mp"),
            P("segment", "mp", "dp"),
            P("dp", ("segment", "mp")),
        ),
        check_vma=False,
    )
```

```python
import functools
import jax
import jax.numpy as jnp
from jax import lax
from jax.experimental import pallas as pl
from jax.experimental.pallas import tpu as pltpu
from jax.sharding import PartitionSpec as P

CHUNKS = 2
VMEM_MIB = 60
COST_SCALE = 4096
BF16 = jnp.bfloat16
F32 = jnp.float32
MIB = 1024 * 1024


def shifted(block, axis, distance):
    devices = range(lax.axis_size(axis))
    route = [(i - distance, i) for i in devices if i - distance in devices]
    return lax.ppermute(block, axis, route)


def swapped(block):
    return lax.ppermute(block, "mp", [(0, 1), (1, 0)])


def gelu_parts(pre_vals):
    coeff = 0.7978845608
    pre = pre_vals.astype(BF16)
    square = pre * pre
    inner = pre * (square * BF16(coeff * 0.044715) + BF16(coeff))
    half = jnp.tanh(inner) * BF16(0.5) + BF16(0.5)
    value = pre * half
    bend = square * BF16(6.0 * coeff * 0.044715) + BF16(2.0 * coeff)
    slope = half + value * (BF16(1.0) - half) * bend
    return (value, slope)


def row_scale(rows_in):
    floats = rows_in.astype(F32)
    return lax.rsqrt(jnp.mean(floats * floats, axis=-1, keepdims=True) + 1e-06)


def normalised(rows_in):
    return (rows_in.astype(F32) * row_scale(rows_in)).astype(BF16)


def norm_back(rows_in, grads):
    scale = row_scale(rows_in)
    normal = rows_in.astype(F32) * scale
    return scale * (grads - normal * jnp.mean(grads * normal, axis=-1, keepdims=True))


def dot(a, b):
    return jnp.dot(a, b, preferred_element_type=F32)


def dot_t(a, b):
    return lax.dot_general(a, b, (((1,), (1,)), ((), ())), preferred_element_type=F32)


def t_dot(a, b):
    return lax.dot_general(a, b, (((0,), (0,)), ((), ())), preferred_element_type=F32)


def tile_of(size, most):
    if size <= most:
        return size
    return max(t for t in range(128, most + 1, 128) if size % t == 0)


def pieces_of(size):
    return [(at, min(256, size - at)) for at in range(0, size, 256)]


def cost(flops, bytes_accessed, transcendentals):
    return pl.CostEstimate(
        flops=flops // COST_SCALE,
        bytes_accessed=bytes_accessed // COST_SCALE,
        transcendentals=transcendentals // COST_SCALE,
    )


def params(limit):
    return pltpu.CompilerParams(vmem_limit_bytes=limit * MIB)


def chosen(index, candidates):
    value = candidates[0][1]
    for at, option in candidates[1:]:
        value = jnp.where(index == at, option, value)
    return value


def gathered(halves, place):
    if len(halves) == 1:
        return halves[0][...]
    mine, theirs = (half[...] for half in halves)
    first = jnp.where(place == 0, mine, theirs)
    second = jnp.where(place == 0, theirs, mine)
    return jnp.concatenate([first, second], axis=0)


def part_of(block, place, parts):
    rows = block.shape[0] // parts
    if parts == 1:
        return block[...]
    return block[pl.ds(pl.multiple_of(place * rows, rows), rows), :]


def whole_spec(shape):
    return pl.BlockSpec(shape, lambda *_: (0,) * len(shape))


def keep_live(live, arrived, before, after):
    for came, old, new in zip(arrived, before, after):
        new[...] = jnp.where(live, came[...], old[...])


def tile_copies(w_in, w_out, in_buf, out_buf, sems, tile):
    copies = []
    for at in range(w_in.shape[1] // tile):
        part = pl.ds(at * tile, tile)
        copies.append(
            (
                pltpu.make_async_copy(w_in.at[:, part], in_buf.at[:, part], sems.at[0, at]),
                pltpu.make_async_copy(w_out.at[part, :], out_buf.at[part, :], sems.at[1, at]),
            )
        )
    return copies


def emit(total, added, place, keep, send):
    if send:
        kept = part_of(total, place, 2)
        keep[...] = kept if added is None else kept + part_of(added, place, 2).astype(F32)
        send[0][...] = part_of(total, 1 - place, 2).astype(send[0].dtype)
    else:
        keep[...] = total[...]


def forward_kernel(halves, stage, ties, tile, where, *refs):
    refs = refs[ties:]
    if stage == 0:
        own, refs = refs[0], refs[1:]
    else:
        arrived, refs = refs[:halves], refs[halves:]
        before, refs = refs[:halves], refs[halves:]
    w_in, w_out, refs = refs[0], refs[1], refs[2:]
    after, refs = refs[:halves], refs[halves:]
    keep, *send, whole, normed, total, in_buf, out_buf, sems = refs
    live = where[0] == stage
    copies = tile_copies(w_in, w_out, in_buf, out_buf, sems, tile)

    @pl.when(live)
    def _():
        for pair in copies:
            for copy in pair:
                copy.start()

    if stage == 0:
        whole[...] = own[...]
        after[0][...] = part_of(whole, where[1], halves)
        if halves == 2:
            after[1][...] = part_of(whole, 1 - where[1], halves)
    else:
        whole[...] = gathered(arrived, where[1])
        keep_live(live, arrived, before, after)

    @pl.when(live)
    def _():
        normed[...] = normalised(whole[...])
        for index, pair in enumerate(copies):
            for copy in pair:
                copy.wait()
            values = []
            for at, size in pieces_of(tile):
                start = index * tile + at
                value, _ = gelu_parts(dot(normed[...], in_buf[:, start : start + size]))
                values.append(value)
            part = dot(
                jnp.concatenate(values, axis=1), out_buf[index * tile : (index + 1) * tile, :]
            )
            total[...] = part if index == 0 else total[...] + part
        emit(total, whole, where[1], keep, send)

    @pl.when(jnp.logical_not(live))
    def _():
        for ref in (keep, *send):
            ref[...] = jnp.zeros_like(ref)


def section_call(body, name, where, ties, operands, specs, w_in, w_out, shapes, scratch, flops):
    width, hidden = w_in.shape
    tile = tile_of(hidden, 1024)
    return pl.pallas_call(
        functools.partial(body, tile),
        grid_spec=pltpu.PrefetchScalarGridSpec(
            num_scalar_prefetch=1,
            grid=(1,),
            in_specs=[pl.BlockSpec(memory_space=pl.ANY)] * len(ties)
            + specs
            + [pl.BlockSpec(memory_space=pl.ANY)] * 2,
            out_specs=[whole_spec(shape) for shape, _ in shapes],
            scratch_shapes=scratch
            + [
                pltpu.VMEM((width, hidden), BF16),
                pltpu.VMEM((hidden, width), BF16),
                pltpu.SemaphoreType.DMA((2, hidden // tile)),
            ],
        ),
        out_shape=[jax.ShapeDtypeStruct(*shape) for shape in shapes],
        compiler_params=params(VMEM_MIB),
        cost_estimate=cost(
            flops=flops, bytes_accessed=4 * width * hidden, transcendentals=flops // 4096
        ),
        name=name,
    )(where, *ties, *operands, w_in, w_out)


def forward_section(where, stage, halves, text, at, arrived, before, w_in, w_out, ties):
    _, rows, width = text.shape
    full, part = (rows, width), (rows // halves, width)
    shapes = [(part, BF16)] * halves + [(part, F32)] + [(part, BF16)] * (halves - 1)
    if stage == 0:
        operands = [text]
        specs = [pl.BlockSpec((None, rows, width), lambda j, s: (at, 0, 0))]
    else:
        operands = [*arrived, *before]
        specs = [whole_spec(part)] * len(operands)

    def body(tile, *refs):
        forward_kernel(halves, stage, len(ties), tile, *refs)

    scratch = [pltpu.VMEM(full, BF16), pltpu.VMEM(full, BF16), pltpu.VMEM(full, F32)]
    flops = 4 * rows * width * w_in.shape[1]
    return section_call(
        body, "section_forward", where, ties, operands, specs, w_in, w_out, shapes, scratch, flops
    )


def total_of(pieces):
    total = pieces[0].astype(F32)
    for piece in pieces[1:]:
        total = total + piece.astype(F32)
    return total


def finish_backward(rows, grads, pieces):
    return (grads.astype(F32) + norm_back(rows, total_of(pieces))).astype(BF16)


def backward_kernel(halves, owner, old, ties, tile, where, *refs):
    refs = refs[ties:]
    stash, refs = refs[:halves], refs[halves:]
    arrived, refs = refs[:halves], refs[halves:]
    before, refs = refs[:old], refs[old:]
    w_in, w_out, refs = refs[0], refs[1], refs[2:]
    after, refs = refs[:halves], refs[halves:]
    keep, *send, grads, normed, total, in_buf, out_buf, sems = refs
    live = where[0] == owner
    copies = tile_copies(w_in, w_out, in_buf, out_buf, sems, tile)

    @pl.when(live)
    def _():
        for pair in copies:
            for copy in pair:
                copy.start()

    keep_live(live, arrived, before if old else arrived, after)

    @pl.when(live)
    def _():
        grads[...] = gathered(arrived, where[1])
        normed[...] = normalised(gathered(stash, where[1]))
        for index, pair in enumerate(copies):
            for copy in pair:
                copy.wait()
            dpres = []
            for at, size in pieces_of(tile):
                part = slice(index * tile + at, index * tile + at + size)
                _, slope = gelu_parts(dot(normed[...], in_buf[:, part]))
                dpres.append(dot_t(grads[...], out_buf[part, :]).astype(BF16) * slope)
            part = dot_t(
                jnp.concatenate(dpres, axis=1), in_buf[:, index * tile : (index + 1) * tile]
            )
            total[...] = part if index == 0 else total[...] + part
        emit(total, None, where[1], keep, send)

    @pl.when(jnp.logical_not(live))
    def _():
        for ref in (keep, *send):
            ref[...] = jnp.zeros_like(ref)


def backward_section(where, owner, stash, arrived, before, w_in, w_out, ties):
    halves = len(stash)
    part = stash[0].shape
    full = (part[0] * halves, part[1])
    shapes = [(part, BF16)] * halves + [(part, F32)] + [(part, BF16)] * (halves - 1)
    operands = [*stash, *arrived, *before]

    def body(tile, *refs):
        backward_kernel(halves, owner, len(before), len(ties), tile, *refs)

    scratch = [pltpu.VMEM(full, BF16)] * 2 + [pltpu.VMEM(full, F32)]
    flops = 6 * full[0] * full[1] * w_in.shape[1]
    specs = [whole_spec(part)] * len(operands)
    return section_call(
        body, "section_backward", where, ties, operands, specs, w_in, w_out, shapes, scratch, flops
    )


def pick_kernel(halves, owner, ties, where, *refs):
    refs = refs[ties:]
    arrived, before, after = refs[:halves], refs[halves : 2 * halves], refs[2 * halves :]
    keep_live(where[0] == owner, arrived, before, after)


def pick(where, owner, arrived, before, ties):
    halves = len(arrived)
    part = arrived[0].shape
    return pl.pallas_call(
        functools.partial(pick_kernel, halves, owner, len(ties)),
        grid_spec=pltpu.PrefetchScalarGridSpec(
            num_scalar_prefetch=1,
            grid=(1,),
            in_specs=[pl.BlockSpec(memory_space=pl.ANY)] * len(ties)
            + [whole_spec(part)] * (2 * halves),
            out_specs=[whole_spec(part)] * halves,
        ),
        out_shape=[jax.ShapeDtypeStruct(part, BF16)] * halves,
        compiler_params=params(VMEM_MIB),
        name="pick_grads",
    )(where, *ties, *arrived, *before)


def row_table(rows):
    pad = jnp.zeros((8 - len(rows), rows[0].shape[1]), F32)
    return jnp.concatenate([*rows, pad], axis=0)


def as_row(column):
    return jnp.broadcast_to(column, (column.shape[0], 128)).T[0:1, :]


def as_columns(row):
    return jnp.broadcast_to(row, (128, row.shape[1])).T


def logits_kernel(halves, chunks, where, *refs):
    finals, refs = refs[: halves * chunks], refs[halves * chunks :]
    w_unit, counts, logits, stats, normed, peak, total, target = refs
    step = pl.program_id(0)
    lanes = peak.shape[1]

    @pl.when(step == 0)
    def _():
        rows = normed.shape[0] // chunks
        for at in range(chunks):
            final = finals[at * halves : (at + 1) * halves]
            normed[at * rows : (at + 1) * rows, :] = normalised(gathered(final, where[1]))
        peak[...] = jnp.full_like(peak, -1e30)
        total[...] = jnp.zeros_like(total)
        target[...] = jnp.zeros_like(target)

    columns = []
    for start, size in pieces_of(w_unit.shape[1]):
        values = dot(normed[...], w_unit[:, start : start + size])
        logits[:, start : start + size] = values
        counted = counts[:, start : start + size].astype(F32) * values
        columns += [
            (values[:, c : c + lanes], counted[:, c : c + lanes]) for c in range(0, size, lanes)
        ]
    higher = peak[...]
    for values, _ in columns:
        higher = jnp.maximum(higher, values)
    mass = total[...] * jnp.exp(peak[...] - higher)
    summed = target[...]
    for values, counted in columns:
        mass = mass + jnp.exp(values - higher)
        summed = summed + counted
    peak[...] = higher
    total[...] = mass
    target[...] = summed

    @pl.when(step == pl.num_programs(0) - 1)
    def _():
        top = jnp.max(peak[...], axis=-1, keepdims=True)
        mass = jnp.sum(total[...] * jnp.exp(peak[...] - top), axis=-1, keepdims=True)
        summed = jnp.sum(target[...], axis=-1, keepdims=True)
        stats[...] = row_table([as_row(top), as_row(mass), as_row(summed)])


def head_logits(where, finals, w_unit, counts):
    halves, chunks = len(finals[0]), len(finals)
    half, width = finals[0][0].shape
    rows = half * halves * chunks
    vocab = w_unit.shape[1]
    lanes = 128 if vocab % 128 == 0 else vocab
    tile = tile_of(vocab, 640)
    return pl.pallas_call(
        functools.partial(logits_kernel, halves, chunks),
        grid_spec=pltpu.PrefetchScalarGridSpec(
            num_scalar_prefetch=1,
            grid=(vocab // tile,),
            in_specs=[
                *[whole_spec((half, width))] * (halves * chunks),
                pl.BlockSpec((width, tile), lambda t, s: (0, t)),
                pl.BlockSpec((rows, tile), lambda t, s: (0, t)),
            ],
            out_specs=[
                pl.BlockSpec((rows, tile), lambda t, s: (0, t)),
                whole_spec((8, rows)),
                whole_spec((rows, width)),
            ],
            scratch_shapes=[pltpu.VMEM((rows, lanes), F32)] * 3,
        ),
        out_shape=[
            jax.ShapeDtypeStruct((rows, vocab), F32),
            jax.ShapeDtypeStruct((8, rows), F32),
            jax.ShapeDtypeStruct((rows, width), BF16),
        ],
        compiler_params=params(VMEM_MIB),
        cost_estimate=cost(
            flops=2 * rows * width * vocab,
            bytes_accessed=(2 * width + 6 * rows) * vocab,
            transcendentals=rows * vocab,
        ),
        name="head_logits",
    )(where, *[half for final in finals for half in final], w_unit, counts)


def head_grads_kernel(denom, halves, chunks, tables, ties, where, *refs):
    refs = refs[ties:]
    stats, refs = refs[:tables], refs[tables:]
    lengths, logits, counts, w_unit, normed, *parts, results, grad, shift, total, normed_t = refs
    step = pl.program_id(0)

    @pl.when(step == 0)
    def _():
        values = [ref[...] for ref in stats]
        top = values[0][0:1, :]
        for table in values[1:]:
            top = jnp.maximum(top, table[0:1, :])
        mass = sum(table[1:2, :] * jnp.exp(table[0:1, :] - top) for table in values)
        target = sum(table[2:3, :] for table in values)
        lse = top + jnp.log(mass)
        moved = lse - jnp.log(lengths[...] * (1.0 / denom))
        shift[...] = as_columns(moved)
        results[...] = row_table([moved, lengths[...] * lse - target])
        normed_t[...] = normed[...].astype(F32).T.astype(BF16)
        total[...] = jnp.zeros_like(total)

    columns = []
    for start, size in pieces_of(w_unit.shape[1]):
        exped = jnp.exp(logits[:, start : start + size] - shift[:, 0:1])
        counted = counts[:, start : start + size].astype(F32) * (1.0 / denom)
        columns.append((exped - counted).astype(BF16))
    dlogits = jnp.concatenate(columns, axis=1)
    total[...] += dot_t(dlogits, w_unit[...])
    grad[...] = dot(normed_t[...], dlogits).astype(BF16)

    @pl.when(step == pl.num_programs(0) - 1)
    def _():
        half = total.shape[0] // (chunks * halves)
        for at in range(chunks):
            base = at * halves * half
            if halves == 2:
                mine, theirs = base + where[1] * half, base + (1 - where[1]) * half
                out = parts[chunks + at]
                out[...] = total[pl.ds(pl.multiple_of(theirs, half), half), :].astype(out.dtype)
                parts[at][...] = total[pl.ds(pl.multiple_of(mine, half), half), :]
            else:
                parts[at][...] = total[base : base + half, :]


def head_grads(where, halves, chunks, stats, lengths, logits, counts, w_unit, normed, denom, ties):
    rows, vocab = logits.shape
    width = w_unit.shape[0]
    tile = tile_of(vocab, 640)
    part = (rows // (halves * chunks), width)
    shapes = [(part, F32)] * chunks + [(part, BF16)] * (chunks * (halves - 1))
    shapes += [((8, rows), F32)]
    return pl.pallas_call(
        functools.partial(head_grads_kernel, denom, halves, chunks, len(stats), len(ties)),
        grid_spec=pltpu.PrefetchScalarGridSpec(
            num_scalar_prefetch=1,
            grid=(vocab // tile,),
            in_specs=[
                *[pl.BlockSpec(memory_space=pl.ANY)] * len(ties),
                *[whole_spec((8, rows))] * len(stats),
                whole_spec((1, rows)),
                pl.BlockSpec((rows, tile), lambda t, s: (0, t)),
                pl.BlockSpec((rows, tile), lambda t, s: (0, t)),
                pl.BlockSpec((width, tile), lambda t, s: (0, t)),
                whole_spec((rows, width)),
            ],
            out_specs=[whole_spec(shape) for shape, _ in shapes]
            + [pl.BlockSpec((width, tile), lambda t, s: (0, t))],
            scratch_shapes=[
                pltpu.VMEM((rows, 128), F32),
                pltpu.VMEM((rows, width), F32),
                pltpu.VMEM((width, rows), BF16),
            ],
        ),
        out_shape=[jax.ShapeDtypeStruct(*shape) for shape in shapes]
        + [jax.ShapeDtypeStruct((width, vocab), BF16)],
        compiler_params=params(VMEM_MIB),
        cost_estimate=cost(
            flops=2 * rows * width * vocab,
            bytes_accessed=(2 * width + 6 * rows) * vocab,
            transcendentals=rows * vocab,
        ),
        name="head_grads",
    )(where, *ties, *stats, lengths, logits, counts, w_unit, normed)


def row_copies(sources, parts, me, dp_size, target, sems):
    copies = []
    base = 0
    for at, (slot, selected) in enumerate(parts):
        ref = sources[slot]
        if selected is not None:
            side, distance = selected
            ref = ref.at[side, lax.rem(me + distance, dp_size)]
        count = ref.shape[0]
        copies.append(
            pltpu.make_async_copy(ref, target.at[pl.ds(base, count), :], sems.at[at])
        )
        base += count
    return copies


def weight_kernel(x_parts, g_parts, sources, adding, share, dp_size, where, *refs):
    arrays, refs = refs[:sources], refs[sources:]
    w_in, w_out, refs = refs[0], refs[1], refs[2:]
    if adding:
        old_first, old_second, refs = refs[0], refs[1], refs[2:]
    first, second, normed, grads, normed_t, grads_t, x_sems, g_sems = refs

    @pl.when(pl.program_id(0) == 0)
    def _():
        columns = pl.ds(pl.multiple_of(where[0] * share, share), share)
        x_copies = row_copies(arrays, x_parts, where[0], dp_size, normed, x_sems)
        g_copies = row_copies(arrays, g_parts, where[0], dp_size, grads, g_sems)
        for copy in x_copies + g_copies:
            copy.start()
        for copy in x_copies:
            copy.wait()
        normed[...] = normalised(normed[...])
        normed_t[...] = normed[:, columns].astype(F32).T.astype(BF16)
        for copy in g_copies:
            copy.wait()
        grads_t[...] = grads[:, columns].astype(F32).T.astype(BF16)

    for at, size in pieces_of(w_in.shape[1]):
        value, slope = gelu_parts(dot(normed[...], w_in[:, at : at + size]))
        dpre = dot_t(grads[...], w_out[at : at + size, :]).astype(BF16) * slope
        now_first = dot(normed_t[...], dpre)
        now_second = dot(grads_t[...], value).T
        if adding:
            now_first = old_first[:, at : at + size] + now_first
            now_second = old_second[at : at + size, :] + now_second
        first[:, at : at + size] = now_first
        second[at : at + size, :] = now_second


def weight_grads(where, x_parts, g_parts, w_in, w_out, old, share):
    width, hidden = w_in.shape
    tile = tile_of(hidden, 1024)
    arrays, rows = [], 0
    slots = []
    for parts in (x_parts, g_parts):
        placed = []
        for array, selected in parts:
            known = [at for at, other in enumerate(arrays) if other is array]
            if not known:
                arrays.append(array)
            placed.append((known[0] if known else len(arrays) - 1, selected))
        slots.append(tuple(placed))
    rows = sum(array.shape[-2] for array, _ in x_parts)
    dp_size = width // share
    hbm = pl.BlockSpec(memory_space=pl.ANY)
    in_specs = [hbm] * len(arrays) + [
        pl.BlockSpec((width, tile), lambda j, s: (0, j)),
        pl.BlockSpec((tile, width), lambda j, s: (j, 0)),
    ]
    grad_specs = [
        pl.BlockSpec((share, tile), lambda j, s: (0, j)),
        pl.BlockSpec((tile, share), lambda j, s: (j, 0)),
    ]
    adding = old is not None
    aliases = {}
    if adding:
        in_specs += grad_specs
        aliases = {len(arrays) + 3: 0, len(arrays) + 4: 1}
    return pl.pallas_call(
        functools.partial(
            weight_kernel, slots[0], slots[1], len(arrays), adding, share, dp_size
        ),
        grid_spec=pltpu.PrefetchScalarGridSpec(
            num_scalar_prefetch=1,
            grid=(hidden // tile,),
            in_specs=in_specs,
            out_specs=grad_specs,
            scratch_shapes=[
                pltpu.VMEM((rows, width), BF16),
                pltpu.VMEM((rows, width), BF16),
                pltpu.VMEM((share, rows), BF16),
                pltpu.VMEM((share, rows), BF16),
                pltpu.SemaphoreType.DMA((len(x_parts),)),
                pltpu.SemaphoreType.DMA((len(g_parts),)),
            ],
        ),
        out_shape=[
            jax.ShapeDtypeStruct((share, hidden), F32),
            jax.ShapeDtypeStruct((hidden, share), F32),
        ],
        input_output_aliases=aliases,
        compiler_params=params(VMEM_MIB),
        cost_estimate=cost(
            flops=4 * rows * (width + share) * hidden,
            bytes_accessed=4 * width * hidden + 16 * share * hidden,
            transcendentals=rows * hidden,
        ),
        name="weight_grads",
    )(where, *arrays, w_in, w_out, *(old or ()))


def unit_counts(ends, targets, ids):
    positions = jnp.arange(targets.shape[1], dtype=jnp.int32)
    row_local = jnp.sum((ends[:, None, :] <= positions[None, :, None]).astype(jnp.int32), axis=-1)
    rows = jnp.arange(ends.shape[1], dtype=jnp.int32)
    row_onehot = (row_local[:, :, None] == rows[None, None, :]).astype(BF16)
    hits = (targets[:, :, None] == ids[None, None, :]).astype(BF16)
    counts = jnp.einsum("mur,muv->mrv", row_onehot, hits, preferred_element_type=F32)
    return counts.astype(BF16)


def on_device(text_rows, durations, unit_targets, w_in, w_out, w_unit):
    micro, row_count, width = text_rows.shape
    segments = lax.axis_size("segment")
    mp_size = lax.axis_size("mp")
    dp_size = lax.axis_size("dp")
    seg = lax.axis_index("segment").astype(jnp.int32)
    mp_at = lax.axis_index("mp").astype(jnp.int32)
    dp_at = lax.axis_index("dp").astype(jnp.int32)
    last = segments - 1
    pair = mp_size == 2
    halves = 2 if pair else 1
    chunks = CHUNKS
    where = jnp.stack([seg, mp_at])
    first = w_in[0]
    second = w_out[0]
    rows = micro * row_count // chunks
    text = text_rows.reshape(chunks, rows, width)
    vocab_part = w_unit.shape[1]
    unit_count = unit_targets.shape[1]
    denom = float(micro * unit_count * dp_size)
    lengths = durations[:, 0, :]
    length_f = lengths.astype(F32).reshape(1, micro * row_count)
    ends = jnp.cumsum(lengths, axis=-1)
    own_ids = (seg * mp_size + mp_at) * vocab_part + jnp.arange(vocab_part, dtype=jnp.int32)

    counts = unit_counts(ends, unit_targets, own_ids).reshape(micro * row_count, vocab_part)

    def both(part):
        return [part, swapped(part)] if pair else [part]

    def reduced(keep, send):
        return [keep, swapped(send[0])] if pair else [lax.psum(keep, "mp")]

    def gathered_rows(mine):
        if pair:
            came = lax.all_gather(mine, ("mp", "dp"))
            return came.reshape(mp_size, dp_size, *mine.shape)
        return lax.all_gather(mine, "dp")[None]

    def all_tables(table):
        if not pair:
            return [t for t in lax.all_gather(table, ("segment", "mp"))]
        count = segments * mp_size
        return [table] + [
            lax.ppermute(table, ("segment", "mp"), [(i, (i + k) % count) for i in range(count)])
            for k in range(1, count)
        ]

    every = range(chunks)
    stash = [None] * chunks
    x_rows = [None] * chunks
    hops = [None] * chunks
    for stage in range(segments):
        for b in every:
            arrived = []
            if stage > 0:
                arrived = both(lax.ppermute(hops[b], "segment", [(stage - 1, stage)]))
            if stage == last and b < chunks - 1:
                x_rows[b] = jnp.where(seg == last, arrived[0], stash[b][0])
            ties = [hops[b - 1]] if b > 0 or stage > 0 else []
            if stage == 0 and b > 0:
                ties = [*ties, counts]
            outs = forward_section(
                where, stage, halves, text, b, arrived, stash[b], first, second, ties
            )
            stash[b], keep, send = outs[:halves], outs[halves], outs[halves + 1 :]
            pieces = reduced(keep, send)
            hops[b] = total_of(pieces if pair else [stash[b][0], *pieces]).astype(BF16)
    x_rows[-1] = stash[-1][0]
    x_gathered = [gathered_rows(x) for x in x_rows]

    finals = []
    for b in every:
        options = [(last, hops[b])]
        options += [
            (to, lax.ppermute(hops[b], "segment", [(last, to)])) for to in range(last)
        ]
        finals.append(both(chosen(seg, options)))
    logits, stats, normed = head_logits(where, finals, w_unit, counts)
    *parts, result, grad_unit = head_grads(
        where,
        halves,
        chunks,
        all_tables(stats),
        length_f,
        logits,
        counts,
        w_unit,
        normed,
        denom,
        x_gathered,
    )
    loss = (jnp.sum(result[1, :]) / denom)[None]
    sum_unit = lax.psum_scatter(grad_unit, "dp", scatter_dimension=0, tiled=True)
    for b in every:
        dnorm = total_of(reduced(parts[b], parts[chunks + b : chunks + b + 1])).astype(BF16)
        dnorm = total_of(
            [dnorm] + [lax.ppermute(dnorm, "segment", [(j, last)]) for j in range(last)]
        ).astype(BF16)
        hops[b] = norm_back(finals[b][0], dnorm.astype(F32)).astype(BF16)

    grads = [[] for _ in every]
    for stage in range(last):
        owner = last - stage
        for b in every:
            came = hops[b]
            if stage > 0:
                came = lax.ppermute(came, "segment", [(owner + 1, owner)])
            ties = [] if b == 0 and stage == 0 else [hops[b - 1]]
            outs = backward_section(
                where, owner, stash[b], both(came), grads[b], first, second, ties
            )
            grads[b], keep, send = outs[:halves], outs[halves], outs[halves + 1 :]
            hops[b] = finish_backward(stash[b][0], came, reduced(keep, send))

    share = width // dp_size
    sums = None
    sources = [None] * chunks

    def own_parts(halves_of):
        return [(half, None) for half in halves_of]

    def other_parts(array):
        return [(array, (side, k)) for side in range(halves) for k in range(1, dp_size)]

    def weight_step(x_parts, g_parts, sums):
        return weight_grads(dp_at[None], x_parts, g_parts, first, second, sums, share)

    waiting = ([], [])
    for b in every:
        arrived = both(lax.ppermute(hops[b], "segment", [(1, 0)]))
        ties = [sums[0]] if b > 0 else []
        grads[b] = pick(where, 0, arrived, grads[b], ties)
        source = gathered_rows(grads[b][0])
        x_parts = own_parts(stash[b]) + waiting[0]
        g_parts = own_parts(grads[b]) + waiting[1]
        sums = weight_step(x_parts, g_parts, sums)
        waiting = (other_parts(x_gathered[b]), other_parts(source))
    sums = weight_step(*waiting, sums)
    return (loss, sums[0][None], sums[1][None], sum_unit.astype(F32))


def solution(mesh):
    placed = (
        P(None, "dp", None),
        P(None, "dp", None),
        P(None, "dp"),
        P("segment", None, "mp"),
        P("segment", "mp", None),
        P(None, ("segment", "mp")),
    )
    return jax.shard_map(
        on_device,
        mesh=mesh,
        in_specs=placed,
        out_specs=(
            P("dp"),
            P("segment", "dp", "mp"),
            P("segment", "mp", "dp"),
            P("dp", ("segment", "mp")),
        ),
        check_vma=False,
    )
```

```python
import functools
import jax
import jax.numpy as jnp
from jax import lax
from jax.experimental import pallas as pl
from jax.experimental.pallas import tpu as pltpu
from jax.sharding import PartitionSpec as P

CHUNKS = 2
VMEM_MIB = 60
COST_SCALE = 4096
BF16 = jnp.bfloat16
F32 = jnp.float32
MIB = 1024 * 1024


def shifted(block, axis, distance):
    devices = range(lax.axis_size(axis))
    route = [(i - distance, i) for i in devices if i - distance in devices]
    return lax.ppermute(block, axis, route)


def swapped(block):
    return lax.ppermute(block, "mp", [(0, 1), (1, 0)])


def gelu_parts(pre_vals):
    coeff = 0.7978845608
    pre = pre_vals.astype(BF16)
    square = pre * pre
    inner = pre * (square * BF16(coeff * 0.044715) + BF16(coeff))
    half = jnp.tanh(inner) * BF16(0.5) + BF16(0.5)
    value = pre * half
    bend = square * BF16(6.0 * coeff * 0.044715) + BF16(2.0 * coeff)
    slope = half + value * (BF16(1.0) - half) * bend
    return (value, slope)


def row_scale(rows_in):
    floats = rows_in.astype(F32)
    return lax.rsqrt(jnp.mean(floats * floats, axis=-1, keepdims=True) + 1e-06)


def normalised(rows_in):
    return (rows_in.astype(F32) * row_scale(rows_in)).astype(BF16)


def norm_back(rows_in, grads):
    scale = row_scale(rows_in)
    normal = rows_in.astype(F32) * scale
    return scale * (grads - normal * jnp.mean(grads * normal, axis=-1, keepdims=True))


def dot(a, b):
    return jnp.dot(a, b, preferred_element_type=F32)


def dot_t(a, b):
    return lax.dot_general(a, b, (((1,), (1,)), ((), ())), preferred_element_type=F32)


def t_dot(a, b):
    return lax.dot_general(a, b, (((0,), (0,)), ((), ())), preferred_element_type=F32)


def tile_of(size, most):
    if size <= most:
        return size
    return max(t for t in range(128, most + 1, 128) if size % t == 0)


def pieces_of(size):
    return [(at, min(256, size - at)) for at in range(0, size, 256)]


def cost(flops, bytes_accessed, transcendentals):
    return pl.CostEstimate(
        flops=flops // COST_SCALE,
        bytes_accessed=bytes_accessed // COST_SCALE,
        transcendentals=transcendentals // COST_SCALE,
    )


def params(limit):
    return pltpu.CompilerParams(vmem_limit_bytes=limit * MIB)


def chosen(index, candidates):
    value = candidates[0][1]
    for at, option in candidates[1:]:
        value = jnp.where(index == at, option, value)
    return value


def gathered(halves, place):
    if len(halves) == 1:
        return halves[0][...]
    mine, theirs = (half[...] for half in halves)
    first = jnp.where(place == 0, mine, theirs)
    second = jnp.where(place == 0, theirs, mine)
    return jnp.concatenate([first, second], axis=0)


def part_of(block, place, parts):
    rows = block.shape[0] // parts
    if parts == 1:
        return block[...]
    return block[pl.ds(pl.multiple_of(place * rows, rows), rows), :]


def whole_spec(shape):
    return pl.BlockSpec(shape, lambda *_: (0,) * len(shape))


def keep_live(live, arrived, before, after):
    for came, old, new in zip(arrived, before, after):
        new[...] = jnp.where(live, came[...], old[...])


def tile_copies(w_in, w_out, in_buf, out_buf, sems, tile):
    copies = []
    for at in range(w_in.shape[1] // tile):
        part = pl.ds(at * tile, tile)
        copies.append(
            (
                pltpu.make_async_copy(w_in.at[:, part], in_buf.at[:, part], sems.at[0, at]),
                pltpu.make_async_copy(w_out.at[part, :], out_buf.at[part, :], sems.at[1, at]),
            )
        )
    return copies


def emit(total, added, place, keep, send):
    if send:
        kept = part_of(total, place, 2)
        keep[...] = kept if added is None else kept + part_of(added, place, 2).astype(F32)
        send[0][...] = part_of(total, 1 - place, 2).astype(send[0].dtype)
    else:
        keep[...] = total[...]


def forward_kernel(halves, stage, ties, tile, where, *refs):
    refs = refs[ties:]
    if stage == 0:
        own, refs = refs[0], refs[1:]
    else:
        arrived, refs = refs[:halves], refs[halves:]
        before, refs = refs[:halves], refs[halves:]
    w_in, w_out, refs = refs[0], refs[1], refs[2:]
    after, refs = refs[:halves], refs[halves:]
    keep, *send, whole, normed, total, in_buf, out_buf, sems = refs
    live = where[0] == stage
    copies = tile_copies(w_in, w_out, in_buf, out_buf, sems, tile)

    @pl.when(live)
    def _():
        for pair in copies:
            for copy in pair:
                copy.start()

    if stage == 0:
        whole[...] = own[...]
        after[0][...] = part_of(whole, where[1], halves)
        if halves == 2:
            after[1][...] = part_of(whole, 1 - where[1], halves)
    else:
        whole[...] = gathered(arrived, where[1])
        keep_live(live, arrived, before, after)

    @pl.when(live)
    def _():
        normed[...] = normalised(whole[...])
        for index, pair in enumerate(copies):
            for copy in pair:
                copy.wait()
            values = []
            for at, size in pieces_of(tile):
                start = index * tile + at
                value, _ = gelu_parts(dot(normed[...], in_buf[:, start : start + size]))
                values.append(value)
            part = dot(
                jnp.concatenate(values, axis=1), out_buf[index * tile : (index + 1) * tile, :]
            )
            total[...] = part if index == 0 else total[...] + part
        emit(total, whole, where[1], keep, send)

    @pl.when(jnp.logical_not(live))
    def _():
        for ref in (keep, *send):
            ref[...] = jnp.zeros_like(ref)


def section_call(body, name, where, ties, operands, specs, w_in, w_out, shapes, scratch, flops):
    width, hidden = w_in.shape
    tile = tile_of(hidden, 1024)
    return pl.pallas_call(
        functools.partial(body, tile),
        grid_spec=pltpu.PrefetchScalarGridSpec(
            num_scalar_prefetch=1,
            grid=(1,),
            in_specs=[pl.BlockSpec(memory_space=pl.ANY)] * len(ties)
            + specs
            + [pl.BlockSpec(memory_space=pl.ANY)] * 2,
            out_specs=[whole_spec(shape) for shape, _ in shapes],
            scratch_shapes=scratch
            + [
                pltpu.VMEM((width, hidden), BF16),
                pltpu.VMEM((hidden, width), BF16),
                pltpu.SemaphoreType.DMA((2, hidden // tile)),
            ],
        ),
        out_shape=[jax.ShapeDtypeStruct(*shape) for shape in shapes],
        compiler_params=params(VMEM_MIB),
        cost_estimate=cost(
            flops=flops, bytes_accessed=4 * width * hidden, transcendentals=flops // 4096
        ),
        name=name,
    )(where, *ties, *operands, w_in, w_out)


def forward_section(where, stage, halves, text, at, arrived, before, w_in, w_out, ties):
    _, rows, width = text.shape
    full, part = (rows, width), (rows // halves, width)
    shapes = [(part, BF16)] * halves + [(part, F32)] + [(part, BF16)] * (halves - 1)
    if stage == 0:
        operands = [text]
        specs = [pl.BlockSpec((None, rows, width), lambda j, s: (at, 0, 0))]
    else:
        operands = [*arrived, *before]
        specs = [whole_spec(part)] * len(operands)

    def body(tile, *refs):
        forward_kernel(halves, stage, len(ties), tile, *refs)

    scratch = [pltpu.VMEM(full, BF16), pltpu.VMEM(full, BF16), pltpu.VMEM(full, F32)]
    flops = 4 * rows * width * w_in.shape[1]
    return section_call(
        body, "section_forward", where, ties, operands, specs, w_in, w_out, shapes, scratch, flops
    )


def total_of(pieces):
    total = pieces[0].astype(F32)
    for piece in pieces[1:]:
        total = total + piece.astype(F32)
    return total


def tied_sum_kernel(ties, *refs):
    refs = refs[ties:]
    total = refs[0][...].astype(F32)
    for ref in refs[1:-1]:
        total = total + ref[...].astype(F32)
    refs[-1][...] = total.astype(BF16)


def tied_sum(pieces, ties):
    if not ties:
        return total_of(pieces).astype(BF16)
    shape = pieces[0].shape
    return pl.pallas_call(
        functools.partial(tied_sum_kernel, len(ties)),
        grid=(1,),
        in_specs=[pl.BlockSpec(memory_space=pl.ANY)] * len(ties)
        + [whole_spec(shape)] * len(pieces),
        out_specs=whole_spec(shape),
        out_shape=jax.ShapeDtypeStruct(shape, BF16),
        compiler_params=params(VMEM_MIB),
        name="tied_sum",
    )(*ties, *pieces)


def finish_backward(rows, grads, pieces):
    return (grads.astype(F32) + norm_back(rows, total_of(pieces))).astype(BF16)


def backward_kernel(halves, owner, old, ties, tile, where, *refs):
    refs = refs[ties:]
    stash, refs = refs[:halves], refs[halves:]
    arrived, refs = refs[:halves], refs[halves:]
    before, refs = refs[:old], refs[old:]
    w_in, w_out, refs = refs[0], refs[1], refs[2:]
    after, refs = refs[:halves], refs[halves:]
    keep, *send, grads, normed, total, in_buf, out_buf, sems = refs
    live = where[0] == owner
    copies = tile_copies(w_in, w_out, in_buf, out_buf, sems, tile)

    @pl.when(live)
    def _():
        for pair in copies:
            for copy in pair:
                copy.start()

    keep_live(live, arrived, before if old else arrived, after)

    @pl.when(live)
    def _():
        grads[...] = gathered(arrived, where[1])
        normed[...] = normalised(gathered(stash, where[1]))
        for index, pair in enumerate(copies):
            for copy in pair:
                copy.wait()
            dpres = []
            for at, size in pieces_of(tile):
                part = slice(index * tile + at, index * tile + at + size)
                _, slope = gelu_parts(dot(normed[...], in_buf[:, part]))
                dpres.append(dot_t(grads[...], out_buf[part, :]).astype(BF16) * slope)
            part = dot_t(
                jnp.concatenate(dpres, axis=1), in_buf[:, index * tile : (index + 1) * tile]
            )
            total[...] = part if index == 0 else total[...] + part
        emit(total, None, where[1], keep, send)

    @pl.when(jnp.logical_not(live))
    def _():
        for ref in (keep, *send):
            ref[...] = jnp.zeros_like(ref)


def backward_section(where, owner, stash, arrived, before, w_in, w_out, ties):
    halves = len(stash)
    part = stash[0].shape
    full = (part[0] * halves, part[1])
    shapes = [(part, BF16)] * halves + [(part, F32)] + [(part, BF16)] * (halves - 1)
    operands = [*stash, *arrived, *before]

    def body(tile, *refs):
        backward_kernel(halves, owner, len(before), len(ties), tile, *refs)

    scratch = [pltpu.VMEM(full, BF16)] * 2 + [pltpu.VMEM(full, F32)]
    flops = 6 * full[0] * full[1] * w_in.shape[1]
    specs = [whole_spec(part)] * len(operands)
    return section_call(
        body, "section_backward", where, ties, operands, specs, w_in, w_out, shapes, scratch, flops
    )


def pick_kernel(halves, owner, ties, where, *refs):
    refs = refs[ties:]
    arrived, before, after = refs[:halves], refs[halves : 2 * halves], refs[2 * halves :]
    keep_live(where[0] == owner, arrived, before, after)


def pick(where, owner, arrived, before, ties):
    halves = len(arrived)
    part = arrived[0].shape
    return pl.pallas_call(
        functools.partial(pick_kernel, halves, owner, len(ties)),
        grid_spec=pltpu.PrefetchScalarGridSpec(
            num_scalar_prefetch=1,
            grid=(1,),
            in_specs=[pl.BlockSpec(memory_space=pl.ANY)] * len(ties)
            + [whole_spec(part)] * (2 * halves),
            out_specs=[whole_spec(part)] * halves,
        ),
        out_shape=[jax.ShapeDtypeStruct(part, BF16)] * halves,
        compiler_params=params(VMEM_MIB),
        name="pick_grads",
    )(where, *ties, *arrived, *before)


def row_table(rows):
    pad = jnp.zeros((8 - len(rows), rows[0].shape[1]), F32)
    return jnp.concatenate([*rows, pad], axis=0)


def as_row(column):
    return jnp.broadcast_to(column, (column.shape[0], 128)).T[0:1, :]


def as_columns(row):
    return jnp.broadcast_to(row, (128, row.shape[1])).T


def logits_kernel(halves, chunks, where, *refs):
    finals, refs = refs[: halves * chunks], refs[halves * chunks :]
    w_unit, counts, logits, stats, normed, peak, total, target = refs
    step = pl.program_id(0)
    lanes = peak.shape[1]

    @pl.when(step == 0)
    def _():
        rows = normed.shape[0] // chunks
        for at in range(chunks):
            final = finals[at * halves : (at + 1) * halves]
            normed[at * rows : (at + 1) * rows, :] = normalised(gathered(final, where[1]))
        peak[...] = jnp.full_like(peak, -1e30)
        total[...] = jnp.zeros_like(total)
        target[...] = jnp.zeros_like(target)

    columns = []
    for start, size in pieces_of(w_unit.shape[1]):
        values = dot(normed[...], w_unit[:, start : start + size])
        logits[:, start : start + size] = values
        counted = counts[:, start : start + size].astype(F32) * values
        columns += [
            (values[:, c : c + lanes], counted[:, c : c + lanes]) for c in range(0, size, lanes)
        ]
    higher = peak[...]
    for values, _ in columns:
        higher = jnp.maximum(higher, values)
    mass = total[...] * jnp.exp(peak[...] - higher)
    summed = target[...]
    for values, counted in columns:
        mass = mass + jnp.exp(values - higher)
        summed = summed + counted
    peak[...] = higher
    total[...] = mass
    target[...] = summed

    @pl.when(step == pl.num_programs(0) - 1)
    def _():
        top = jnp.max(peak[...], axis=-1, keepdims=True)
        mass = jnp.sum(total[...] * jnp.exp(peak[...] - top), axis=-1, keepdims=True)
        summed = jnp.sum(target[...], axis=-1, keepdims=True)
        stats[...] = row_table([as_row(top), as_row(mass), as_row(summed)])


def head_logits(where, finals, w_unit, counts):
    halves, chunks = len(finals[0]), len(finals)
    half, width = finals[0][0].shape
    rows = half * halves * chunks
    vocab = w_unit.shape[1]
    lanes = 128 if vocab % 128 == 0 else vocab
    tile = tile_of(vocab, 640)
    return pl.pallas_call(
        functools.partial(logits_kernel, halves, chunks),
        grid_spec=pltpu.PrefetchScalarGridSpec(
            num_scalar_prefetch=1,
            grid=(vocab // tile,),
            in_specs=[
                *[whole_spec((half, width))] * (halves * chunks),
                pl.BlockSpec((width, tile), lambda t, s: (0, t)),
                pl.BlockSpec((rows, tile), lambda t, s: (0, t)),
            ],
            out_specs=[
                pl.BlockSpec((rows, tile), lambda t, s: (0, t)),
                whole_spec((8, rows)),
                whole_spec((rows, width)),
            ],
            scratch_shapes=[pltpu.VMEM((rows, lanes), F32)] * 3,
        ),
        out_shape=[
            jax.ShapeDtypeStruct((rows, vocab), F32),
            jax.ShapeDtypeStruct((8, rows), F32),
            jax.ShapeDtypeStruct((rows, width), BF16),
        ],
        compiler_params=params(VMEM_MIB),
        cost_estimate=cost(
            flops=2 * rows * width * vocab,
            bytes_accessed=(2 * width + 6 * rows) * vocab,
            transcendentals=rows * vocab,
        ),
        name="head_logits",
    )(where, *[half for final in finals for half in final], w_unit, counts)


def head_grads_kernel(denom, halves, chunks, tables, ties, where, *refs):
    refs = refs[ties:]
    stats, refs = refs[:tables], refs[tables:]
    lengths, logits, counts, w_unit, normed, *parts, results, grad, shift, total, normed_t = refs
    step = pl.program_id(0)

    @pl.when(step == 0)
    def _():
        values = [ref[...] for ref in stats]
        top = values[0][0:1, :]
        for table in values[1:]:
            top = jnp.maximum(top, table[0:1, :])
        mass = sum(table[1:2, :] * jnp.exp(table[0:1, :] - top) for table in values)
        target = sum(table[2:3, :] for table in values)
        lse = top + jnp.log(mass)
        moved = lse - jnp.log(lengths[...] * (1.0 / denom))
        shift[...] = as_columns(moved)
        results[...] = row_table([moved, lengths[...] * lse - target])
        normed_t[...] = normed[...].astype(F32).T.astype(BF16)
        total[...] = jnp.zeros_like(total)

    columns = []
    for start, size in pieces_of(w_unit.shape[1]):
        exped = jnp.exp(logits[:, start : start + size] - shift[:, 0:1])
        counted = counts[:, start : start + size].astype(F32) * (1.0 / denom)
        columns.append((exped - counted).astype(BF16))
    dlogits = jnp.concatenate(columns, axis=1)
    total[...] += dot_t(dlogits, w_unit[...])
    grad[...] = dot(normed_t[...], dlogits).astype(BF16)

    @pl.when(step == pl.num_programs(0) - 1)
    def _():
        half = total.shape[0] // (chunks * halves)
        for at in range(chunks):
            base = at * halves * half
            if halves == 2:
                mine, theirs = base + where[1] * half, base + (1 - where[1]) * half
                out = parts[chunks + at]
                out[...] = total[pl.ds(pl.multiple_of(theirs, half), half), :].astype(out.dtype)
                parts[at][...] = total[pl.ds(pl.multiple_of(mine, half), half), :]
            else:
                parts[at][...] = total[base : base + half, :]


def head_grads(where, halves, chunks, stats, lengths, logits, counts, w_unit, normed, denom, ties):
    rows, vocab = logits.shape
    width = w_unit.shape[0]
    tile = tile_of(vocab, 640)
    part = (rows // (halves * chunks), width)
    shapes = [(part, F32)] * chunks + [(part, BF16)] * (chunks * (halves - 1))
    shapes += [((8, rows), F32)]
    return pl.pallas_call(
        functools.partial(head_grads_kernel, denom, halves, chunks, len(stats), len(ties)),
        grid_spec=pltpu.PrefetchScalarGridSpec(
            num_scalar_prefetch=1,
            grid=(vocab // tile,),
            in_specs=[
                *[pl.BlockSpec(memory_space=pl.ANY)] * len(ties),
                *[whole_spec((8, rows))] * len(stats),
                whole_spec((1, rows)),
                pl.BlockSpec((rows, tile), lambda t, s: (0, t)),
                pl.BlockSpec((rows, tile), lambda t, s: (0, t)),
                pl.BlockSpec((width, tile), lambda t, s: (0, t)),
                whole_spec((rows, width)),
            ],
            out_specs=[whole_spec(shape) for shape, _ in shapes]
            + [pl.BlockSpec((width, tile), lambda t, s: (0, t))],
            scratch_shapes=[
                pltpu.VMEM((rows, 128), F32),
                pltpu.VMEM((rows, width), F32),
                pltpu.VMEM((width, rows), BF16),
            ],
        ),
        out_shape=[jax.ShapeDtypeStruct(*shape) for shape in shapes]
        + [jax.ShapeDtypeStruct((width, vocab), BF16)],
        compiler_params=params(VMEM_MIB),
        cost_estimate=cost(
            flops=2 * rows * width * vocab,
            bytes_accessed=(2 * width + 6 * rows) * vocab,
            transcendentals=rows * vocab,
        ),
        name="head_grads",
    )(where, *ties, *stats, lengths, logits, counts, w_unit, normed)


def row_copies(sources, parts, me, dp_size, target, sems):
    copies = []
    base = 0
    for at, (slot, selected) in enumerate(parts):
        ref = sources[slot]
        if selected is not None:
            side, distance = selected
            ref = ref.at[side, lax.rem(me + distance, dp_size)]
        count = ref.shape[0]
        copies.append(
            pltpu.make_async_copy(ref, target.at[pl.ds(base, count), :], sems.at[at])
        )
        base += count
    return copies


def weight_kernel(x_parts, g_parts, sources, adding, share, dp_size, where, *refs):
    arrays, refs = refs[:sources], refs[sources:]
    w_in, w_out, refs = refs[0], refs[1], refs[2:]
    if adding:
        old_first, old_second, refs = refs[0], refs[1], refs[2:]
    first, second, normed, grads, normed_t, grads_t, x_sems, g_sems = refs

    @pl.when(pl.program_id(0) == 0)
    def _():
        columns = pl.ds(pl.multiple_of(where[0] * share, share), share)
        x_copies = row_copies(arrays, x_parts, where[0], dp_size, normed, x_sems)
        g_copies = row_copies(arrays, g_parts, where[0], dp_size, grads, g_sems)
        for copy in x_copies + g_copies:
            copy.start()
        for copy in x_copies:
            copy.wait()
        normed[...] = normalised(normed[...])
        normed_t[...] = normed[:, columns].astype(F32).T.astype(BF16)
        for copy in g_copies:
            copy.wait()
        grads_t[...] = grads[:, columns].astype(F32).T.astype(BF16)

    for at, size in pieces_of(w_in.shape[1]):
        value, slope = gelu_parts(dot(normed[...], w_in[:, at : at + size]))
        dpre = dot_t(grads[...], w_out[at : at + size, :]).astype(BF16) * slope
        now_first = dot(normed_t[...], dpre)
        now_second = dot(grads_t[...], value).T
        if adding:
            now_first = old_first[:, at : at + size] + now_first
            now_second = old_second[at : at + size, :] + now_second
        first[:, at : at + size] = now_first
        second[at : at + size, :] = now_second


def weight_grads(where, x_parts, g_parts, w_in, w_out, old, share):
    width, hidden = w_in.shape
    tile = tile_of(hidden, 1024)
    arrays, rows = [], 0
    slots = []
    for parts in (x_parts, g_parts):
        placed = []
        for array, selected in parts:
            known = [at for at, other in enumerate(arrays) if other is array]
            if not known:
                arrays.append(array)
            placed.append((known[0] if known else len(arrays) - 1, selected))
        slots.append(tuple(placed))
    rows = sum(array.shape[-2] for array, _ in x_parts)
    dp_size = width // share
    hbm = pl.BlockSpec(memory_space=pl.ANY)
    in_specs = [hbm] * len(arrays) + [
        pl.BlockSpec((width, tile), lambda j, s: (0, j)),
        pl.BlockSpec((tile, width), lambda j, s: (j, 0)),
    ]
    grad_specs = [
        pl.BlockSpec((share, tile), lambda j, s: (0, j)),
        pl.BlockSpec((tile, share), lambda j, s: (j, 0)),
    ]
    adding = old is not None
    aliases = {}
    if adding:
        in_specs += grad_specs
        aliases = {len(arrays) + 3: 0, len(arrays) + 4: 1}
    return pl.pallas_call(
        functools.partial(
            weight_kernel, slots[0], slots[1], len(arrays), adding, share, dp_size
        ),
        grid_spec=pltpu.PrefetchScalarGridSpec(
            num_scalar_prefetch=1,
            grid=(hidden // tile,),
            in_specs=in_specs,
            out_specs=grad_specs,
            scratch_shapes=[
                pltpu.VMEM((rows, width), BF16),
                pltpu.VMEM((rows, width), BF16),
                pltpu.VMEM((share, rows), BF16),
                pltpu.VMEM((share, rows), BF16),
                pltpu.SemaphoreType.DMA((len(x_parts),)),
                pltpu.SemaphoreType.DMA((len(g_parts),)),
            ],
        ),
        out_shape=[
            jax.ShapeDtypeStruct((share, hidden), F32),
            jax.ShapeDtypeStruct((hidden, share), F32),
        ],
        input_output_aliases=aliases,
        compiler_params=params(VMEM_MIB),
        cost_estimate=cost(
            flops=4 * rows * (width + share) * hidden,
            bytes_accessed=4 * width * hidden + 16 * share * hidden,
            transcendentals=rows * hidden,
        ),
        name="weight_grads",
    )(where, *arrays, w_in, w_out, *(old or ()))


def unit_counts(ends, targets, ids):
    positions = jnp.arange(targets.shape[1], dtype=jnp.int32)
    row_local = jnp.sum((ends[:, None, :] <= positions[None, :, None]).astype(jnp.int32), axis=-1)
    rows = jnp.arange(ends.shape[1], dtype=jnp.int32)
    row_onehot = (row_local[:, :, None] == rows[None, None, :]).astype(BF16)
    hits = (targets[:, :, None] == ids[None, None, :]).astype(BF16)
    counts = jnp.einsum("mur,muv->mrv", row_onehot, hits, preferred_element_type=F32)
    return counts.astype(BF16)


def on_device(text_rows, durations, unit_targets, w_in, w_out, w_unit):
    micro, row_count, width = text_rows.shape
    segments = lax.axis_size("segment")
    mp_size = lax.axis_size("mp")
    dp_size = lax.axis_size("dp")
    seg = lax.axis_index("segment").astype(jnp.int32)
    mp_at = lax.axis_index("mp").astype(jnp.int32)
    dp_at = lax.axis_index("dp").astype(jnp.int32)
    last = segments - 1
    pair = mp_size == 2
    halves = 2 if pair else 1
    chunks = CHUNKS
    where = jnp.stack([seg, mp_at])
    first = w_in[0]
    second = w_out[0]
    rows = micro * row_count // chunks
    text = text_rows.reshape(chunks, rows, width)
    vocab_part = w_unit.shape[1]
    unit_count = unit_targets.shape[1]
    denom = float(micro * unit_count * dp_size)
    lengths = durations[:, 0, :]
    length_f = lengths.astype(F32).reshape(1, micro * row_count)
    ends = jnp.cumsum(lengths, axis=-1)
    own_ids = (seg * mp_size + mp_at) * vocab_part + jnp.arange(vocab_part, dtype=jnp.int32)

    counts = unit_counts(ends, unit_targets, own_ids).reshape(micro * row_count, vocab_part)

    def both(part):
        return [part, swapped(part)] if pair else [part]

    def reduced(keep, send):
        return [keep, swapped(send[0])] if pair else [lax.psum(keep, "mp")]

    def gathered_rows(mine):
        if pair:
            came = lax.all_gather(mine, ("mp", "dp"))
            return came.reshape(mp_size, dp_size, *mine.shape)
        return lax.all_gather(mine, "dp")[None]

    def all_tables(table):
        if not pair:
            return [t for t in lax.all_gather(table, ("segment", "mp"))]
        count = segments * mp_size
        return [table] + [
            lax.ppermute(table, ("segment", "mp"), [(i, (i + k) % count) for i in range(count)])
            for k in range(1, count)
        ]

    every = range(chunks)
    stash = [None] * chunks
    hops = [None] * chunks
    for stage in range(segments):
        for b in every:
            arrived = []
            if stage > 0:
                arrived = both(lax.ppermute(hops[b], "segment", [(stage - 1, stage)]))
            ties = [hops[b - 1]] if b > 0 or stage > 0 else []
            if stage == 0 and b > 0:
                ties = [*ties, counts]
            outs = forward_section(
                where, stage, halves, text, b, arrived, stash[b], first, second, ties
            )
            stash[b], keep, send = outs[:halves], outs[halves], outs[halves + 1 :]
            pieces = reduced(keep, send)
            hops[b] = total_of(pieces if pair else [stash[b][0], *pieces]).astype(BF16)
    x_gathered = [gathered_rows(held[0]) for held in stash]

    finals = []
    for b in every:
        options = [(last, hops[b])]
        options += [
            (to, lax.ppermute(hops[b], "segment", [(last, to)])) for to in range(last)
        ]
        finals.append(both(chosen(seg, options)))
    logits, stats, normed = head_logits(where, finals, w_unit, counts)
    *parts, result, grad_unit = head_grads(
        where,
        halves,
        chunks,
        all_tables(stats),
        length_f,
        logits,
        counts,
        w_unit,
        normed,
        denom,
        x_gathered,
    )
    loss = (jnp.sum(result[1, :]) / denom)[None]
    sum_unit = lax.psum_scatter(grad_unit, "dp", scatter_dimension=0, tiled=True)
    for b in every:
        pieces = reduced(parts[b], parts[chunks + b : chunks + b + 1])
        dnorm = tied_sum(pieces, [hops[b - 1]] if b > 0 else [])
        dnorm = total_of(
            [dnorm] + [lax.ppermute(dnorm, "segment", [(j, last)]) for j in range(last)]
        ).astype(BF16)
        hops[b] = norm_back(finals[b][0], dnorm.astype(F32)).astype(BF16)

    grads = [[] for _ in every]
    for stage in range(last):
        owner = last - stage
        for b in every:
            came = hops[b]
            if stage > 0:
                came = lax.ppermute(came, "segment", [(owner + 1, owner)])
            ties = [] if b == 0 and stage == 0 else [hops[b - 1]]
            outs = backward_section(
                where, owner, stash[b], both(came), grads[b], first, second, ties
            )
            grads[b], keep, send = outs[:halves], outs[halves], outs[halves + 1 :]
            hops[b] = finish_backward(stash[b][0], came, reduced(keep, send))

    share = width // dp_size
    sums = None
    sources = [None] * chunks

    def own_parts(halves_of):
        return [(half, None) for half in halves_of]

    def other_parts(array):
        return [(array, (side, k)) for side in range(halves) for k in range(1, dp_size)]

    def weight_step(x_parts, g_parts, sums):
        return weight_grads(dp_at[None], x_parts, g_parts, first, second, sums, share)

    arrivals = [both(lax.ppermute(hop, "segment", [(1, 0)])) for hop in hops]
    for b in every:
        ties = [hops[-1]] if b < chunks - 1 else []
        grads[b] = pick(where, 0, arrivals[b], grads[b], ties)
        sources[b] = gathered_rows(grads[b][0])
    for b in every:
        own = every if b == 0 else []
        x_parts = [part for at in own for part in own_parts(stash[at])]
        g_parts = [part for at in own for part in own_parts(grads[at])]
        sums = weight_step(
            x_parts + other_parts(x_gathered[b]), g_parts + other_parts(sources[b]), sums
        )
    return (loss, sums[0][None], sums[1][None], sum_unit.astype(F32))


def solution(mesh):
    placed = (
        P(None, "dp", None),
        P(None, "dp", None),
        P(None, "dp"),
        P("segment", None, "mp"),
        P("segment", "mp", None),
        P(None, ("segment", "mp")),
    )
    return jax.shard_map(
        on_device,
        mesh=mesh,
        in_specs=placed,
        out_specs=(
            P("dp"),
            P("segment", "dp", "mp"),
            P("segment", "mp", "dp"),
            P("dp", ("segment", "mp")),
        ),
        check_vma=False,
    )
```

```python
import functools
import jax
import jax.numpy as jnp
from jax import lax
from jax.experimental import pallas as pl
from jax.experimental.pallas import tpu as pltpu
from jax.sharding import PartitionSpec as P

CHUNKS = 2
VMEM_MIB = 60
COST_SCALE = 4096
BF16 = jnp.bfloat16
F32 = jnp.float32
MIB = 1024 * 1024


def shifted(block, axis, distance):
    devices = range(lax.axis_size(axis))
    route = [(i - distance, i) for i in devices if i - distance in devices]
    return lax.ppermute(block, axis, route)


def swapped(block):
    return lax.ppermute(block, "mp", [(0, 1), (1, 0)])


def gelu_parts(pre_vals):
    coeff = 0.7978845608
    pre = pre_vals.astype(BF16)
    square = pre * pre
    inner = pre * (square * BF16(coeff * 0.044715) + BF16(coeff))
    half = jnp.tanh(inner) * BF16(0.5) + BF16(0.5)
    value = pre * half
    bend = square * BF16(6.0 * coeff * 0.044715) + BF16(2.0 * coeff)
    slope = half + value * (BF16(1.0) - half) * bend
    return (value, slope)


def row_scale(rows_in):
    floats = rows_in.astype(F32)
    return lax.rsqrt(jnp.mean(floats * floats, axis=-1, keepdims=True) + 1e-06)


def normalised(rows_in):
    return (rows_in.astype(F32) * row_scale(rows_in)).astype(BF16)


def norm_back(rows_in, grads):
    scale = row_scale(rows_in)
    normal = rows_in.astype(F32) * scale
    return scale * (grads - normal * jnp.mean(grads * normal, axis=-1, keepdims=True))


def dot(a, b):
    return jnp.dot(a, b, preferred_element_type=F32)


def dot_t(a, b):
    return lax.dot_general(a, b, (((1,), (1,)), ((), ())), preferred_element_type=F32)


def t_dot(a, b):
    return lax.dot_general(a, b, (((0,), (0,)), ((), ())), preferred_element_type=F32)


def tile_of(size, most):
    if size <= most:
        return size
    return max(t for t in range(128, most + 1, 128) if size % t == 0)


def pieces_of(size):
    return [(at, min(256, size - at)) for at in range(0, size, 256)]


def cost(flops, bytes_accessed, transcendentals):
    return pl.CostEstimate(
        flops=flops // COST_SCALE,
        bytes_accessed=bytes_accessed // COST_SCALE,
        transcendentals=transcendentals // COST_SCALE,
    )


def params(limit):
    return pltpu.CompilerParams(vmem_limit_bytes=limit * MIB)


def chosen(index, candidates):
    value = candidates[0][1]
    for at, option in candidates[1:]:
        value = jnp.where(index == at, option, value)
    return value


def gathered(halves, place, rows=...):
    if len(halves) == 1:
        return halves[0][rows]
    mine, theirs = (half[rows] for half in halves)
    first = jnp.where(place == 0, mine, theirs)
    second = jnp.where(place == 0, theirs, mine)
    return jnp.concatenate([first, second], axis=0)


def part_of(block, place, parts):
    rows = block.shape[0] // parts
    if parts == 1:
        return block[...]
    return block[pl.ds(pl.multiple_of(place * rows, rows), rows), :]


def whole_spec(shape):
    return pl.BlockSpec(shape, lambda *_: (0,) * len(shape))


def keep_live(live, arrived, before, after):
    for came, old, new in zip(arrived, before, after):
        new[...] = jnp.where(live, came[...], old[...])


def tile_copies(w_in, w_out, in_buf, out_buf, sems, tile):
    copies = []
    for at in range(w_in.shape[1] // tile):
        part = pl.ds(at * tile, tile)
        copies.append(
            (
                pltpu.make_async_copy(w_in.at[:, part], in_buf.at[:, part], sems.at[0, at]),
                pltpu.make_async_copy(w_out.at[part, :], out_buf.at[part, :], sems.at[1, at]),
            )
        )
    return copies


def emit(total, added, place, keep, send):
    if send:
        kept = part_of(total, place, 2)
        keep[...] = kept if added is None else kept + part_of(added, place, 2).astype(F32)
        send[0][...] = part_of(total, 1 - place, 2).astype(send[0].dtype)
    else:
        keep[...] = total[...]


def forward_kernel(halves, stage, ties, tile, where, *refs):
    refs = refs[ties:]
    if stage == 0:
        own, refs = refs[0], refs[1:]
    else:
        arrived, refs = refs[:halves], refs[halves:]
        before, refs = refs[:halves], refs[halves:]
    w_in, w_out, refs = refs[0], refs[1], refs[2:]
    after, refs = refs[:halves], refs[halves:]
    keep, *send, whole, normed, total, in_buf, out_buf, sems = refs
    live = where[0] == stage
    copies = tile_copies(w_in, w_out, in_buf, out_buf, sems, tile)

    @pl.when(live)
    def _():
        for pair in copies:
            for copy in pair:
                copy.start()

    if stage == 0:
        whole[...] = own[...]
        after[0][...] = part_of(whole, where[1], halves)
        if halves == 2:
            after[1][...] = part_of(whole, 1 - where[1], halves)
    else:
        whole[...] = gathered(arrived, where[1])
        keep_live(live, arrived, before, after)

    @pl.when(live)
    def _():
        normed[...] = normalised(whole[...])
        for index, pair in enumerate(copies):
            for copy in pair:
                copy.wait()
            values = []
            for at, size in pieces_of(tile):
                start = index * tile + at
                value, _ = gelu_parts(dot(normed[...], in_buf[:, start : start + size]))
                values.append(value)
            part = dot(
                jnp.concatenate(values, axis=1), out_buf[index * tile : (index + 1) * tile, :]
            )
            total[...] = part if index == 0 else total[...] + part
        emit(total, whole, where[1], keep, send)

    @pl.when(jnp.logical_not(live))
    def _():
        for ref in (keep, *send):
            ref[...] = jnp.zeros_like(ref)


def section_call(body, name, where, ties, operands, specs, w_in, w_out, shapes, scratch, flops):
    width, hidden = w_in.shape
    tile = tile_of(hidden, 512)
    return pl.pallas_call(
        functools.partial(body, tile),
        grid_spec=pltpu.PrefetchScalarGridSpec(
            num_scalar_prefetch=1,
            grid=(1,),
            in_specs=[pl.BlockSpec(memory_space=pl.ANY)] * len(ties)
            + specs
            + [pl.BlockSpec(memory_space=pl.ANY)] * 2,
            out_specs=[whole_spec(shape) for shape, _ in shapes],
            scratch_shapes=scratch
            + [
                pltpu.VMEM((width, hidden), BF16),
                pltpu.VMEM((hidden, width), BF16),
                pltpu.SemaphoreType.DMA((2, hidden // tile)),
            ],
        ),
        out_shape=[jax.ShapeDtypeStruct(*shape) for shape in shapes],
        compiler_params=params(VMEM_MIB),
        cost_estimate=cost(
            flops=flops, bytes_accessed=4 * width * hidden, transcendentals=flops // 4096
        ),
        name=name,
    )(where, *ties, *operands, w_in, w_out)


def forward_section(where, stage, halves, text, at, arrived, before, w_in, w_out, ties):
    _, rows, width = text.shape
    full, part = (rows, width), (rows // halves, width)
    shapes = [(part, BF16)] * halves + [(part, F32)] + [(part, BF16)] * (halves - 1)
    if stage == 0:
        operands = [text]
        specs = [pl.BlockSpec((None, rows, width), lambda j, s: (at, 0, 0))]
    else:
        operands = [*arrived, *before]
        specs = [whole_spec(part)] * len(operands)

    def body(tile, *refs):
        forward_kernel(halves, stage, len(ties), tile, *refs)

    scratch = [pltpu.VMEM(full, BF16), pltpu.VMEM(full, BF16), pltpu.VMEM(full, F32)]
    flops = 4 * rows * width * w_in.shape[1]
    return section_call(
        body, "section_forward", where, ties, operands, specs, w_in, w_out, shapes, scratch, flops
    )


def total_of(pieces):
    total = pieces[0].astype(F32)
    for piece in pieces[1:]:
        total = total + piece.astype(F32)
    return total


def tied_sum_kernel(ties, *refs):
    refs = refs[ties:]
    total = refs[0][...].astype(F32)
    for ref in refs[1:-1]:
        total = total + ref[...].astype(F32)
    refs[-1][...] = total.astype(BF16)


def tied_sum(pieces, ties):
    if not ties:
        return total_of(pieces).astype(BF16)
    shape = pieces[0].shape
    return pl.pallas_call(
        functools.partial(tied_sum_kernel, len(ties)),
        grid=(1,),
        in_specs=[pl.BlockSpec(memory_space=pl.ANY)] * len(ties)
        + [whole_spec(shape)] * len(pieces),
        out_specs=whole_spec(shape),
        out_shape=jax.ShapeDtypeStruct(shape, BF16),
        compiler_params=params(VMEM_MIB),
        name="tied_sum",
    )(*ties, *pieces)


def finish_backward(rows, grads, pieces):
    return (grads.astype(F32) + norm_back(rows, total_of(pieces))).astype(BF16)


def backward_kernel(halves, owner, old, ties, tile, where, *refs):
    refs = refs[ties:]
    stash, refs = refs[:halves], refs[halves:]
    arrived, refs = refs[:halves], refs[halves:]
    before, refs = refs[:old], refs[old:]
    w_in, w_out, refs = refs[0], refs[1], refs[2:]
    after, refs = refs[:halves], refs[halves:]
    keep, *send, grads, normed, total, in_buf, out_buf, sems = refs
    live = where[0] == owner
    copies = tile_copies(w_in, w_out, in_buf, out_buf, sems, tile)

    @pl.when(live)
    def _():
        for pair in copies:
            for copy in pair:
                copy.start()

    keep_live(live, arrived, before if old else arrived, after)

    @pl.when(live)
    def _():
        grads[...] = gathered(arrived, where[1])
        normed[...] = normalised(gathered(stash, where[1]))
        for index, pair in enumerate(copies):
            for copy in pair:
                copy.wait()
            dpres = []
            for at, size in pieces_of(tile):
                part = slice(index * tile + at, index * tile + at + size)
                _, slope = gelu_parts(dot(normed[...], in_buf[:, part]))
                dpres.append(dot_t(grads[...], out_buf[part, :]).astype(BF16) * slope)
            part = dot_t(
                jnp.concatenate(dpres, axis=1), in_buf[:, index * tile : (index + 1) * tile]
            )
            total[...] = part if index == 0 else total[...] + part
        emit(total, None, where[1], keep, send)

    @pl.when(jnp.logical_not(live))
    def _():
        for ref in (keep, *send):
            ref[...] = jnp.zeros_like(ref)


def backward_section(where, owner, stash, arrived, before, w_in, w_out, ties):
    halves = len(stash)
    part = stash[0].shape
    full = (part[0] * halves, part[1])
    shapes = [(part, BF16)] * halves + [(part, F32)] + [(part, BF16)] * (halves - 1)
    operands = [*stash, *arrived, *before]

    def body(tile, *refs):
        backward_kernel(halves, owner, len(before), len(ties), tile, *refs)

    scratch = [pltpu.VMEM(full, BF16)] * 2 + [pltpu.VMEM(full, F32)]
    flops = 6 * full[0] * full[1] * w_in.shape[1]
    specs = [whole_spec(part)] * len(operands)
    return section_call(
        body, "section_backward", where, ties, operands, specs, w_in, w_out, shapes, scratch, flops
    )


def pick_kernel(halves, owner, ties, where, *refs):
    refs = refs[ties:]
    arrived, before, after = refs[:halves], refs[halves : 2 * halves], refs[2 * halves :]
    keep_live(where[0] == owner, arrived, before, after)


def pick(where, owner, arrived, before, ties):
    halves = len(arrived)
    part = arrived[0].shape
    return pl.pallas_call(
        functools.partial(pick_kernel, halves, owner, len(ties)),
        grid_spec=pltpu.PrefetchScalarGridSpec(
            num_scalar_prefetch=1,
            grid=(1,),
            in_specs=[pl.BlockSpec(memory_space=pl.ANY)] * len(ties)
            + [whole_spec(part)] * (2 * halves),
            out_specs=[whole_spec(part)] * halves,
        ),
        out_shape=[jax.ShapeDtypeStruct(part, BF16)] * halves,
        compiler_params=params(VMEM_MIB),
        name="pick_grads",
    )(where, *ties, *arrived, *before)


def row_table(rows):
    pad = jnp.zeros((8 - len(rows), rows[0].shape[1]), F32)
    return jnp.concatenate([*rows, pad], axis=0)


def as_row(column):
    return jnp.broadcast_to(column, (column.shape[0], 128)).T[0:1, :]


def as_columns(row):
    return jnp.broadcast_to(row, (128, row.shape[1])).T


def logits_kernel(halves, chunks, where, *refs):
    finals, refs = refs[:halves], refs[halves:]
    w_unit, counts, logits, stats, normed, peak, total, target = refs
    step = pl.program_id(0)
    lanes = peak.shape[1]

    @pl.when(step == 0)
    def _():
        rows = normed.shape[0] // chunks
        half = rows // halves
        for at in range(chunks):
            final = gathered(finals, where[1], pl.ds(at * half, half))
            normed[at * rows : (at + 1) * rows, :] = normalised(final)
        peak[...] = jnp.full_like(peak, -1e30)
        total[...] = jnp.zeros_like(total)
        target[...] = jnp.zeros_like(target)

    columns = []
    for start, size in pieces_of(w_unit.shape[1]):
        values = dot(normed[...], w_unit[:, start : start + size])
        logits[:, start : start + size] = values
        counted = counts[:, start : start + size].astype(F32) * values
        columns += [
            (values[:, c : c + lanes], counted[:, c : c + lanes]) for c in range(0, size, lanes)
        ]
    higher = peak[...]
    for values, _ in columns:
        higher = jnp.maximum(higher, values)
    mass = total[...] * jnp.exp(peak[...] - higher)
    summed = target[...]
    for values, counted in columns:
        mass = mass + jnp.exp(values - higher)
        summed = summed + counted
    peak[...] = higher
    total[...] = mass
    target[...] = summed

    @pl.when(step == pl.num_programs(0) - 1)
    def _():
        top = jnp.max(peak[...], axis=-1, keepdims=True)
        mass = jnp.sum(total[...] * jnp.exp(peak[...] - top), axis=-1, keepdims=True)
        summed = jnp.sum(target[...], axis=-1, keepdims=True)
        stats[...] = row_table([as_row(top), as_row(mass), as_row(summed)])


def head_logits(where, chunks, finals, w_unit, counts):
    halves = len(finals)
    half, width = finals[0].shape
    rows = half * halves
    vocab = w_unit.shape[1]
    lanes = 128 if vocab % 128 == 0 else vocab
    tile = tile_of(vocab, 640)
    return pl.pallas_call(
        functools.partial(logits_kernel, halves, chunks),
        grid_spec=pltpu.PrefetchScalarGridSpec(
            num_scalar_prefetch=1,
            grid=(vocab // tile,),
            in_specs=[
                *[whole_spec((half, width))] * halves,
                pl.BlockSpec((width, tile), lambda t, s: (0, t)),
                pl.BlockSpec((rows, tile), lambda t, s: (0, t)),
            ],
            out_specs=[
                pl.BlockSpec((rows, tile), lambda t, s: (0, t)),
                whole_spec((8, rows)),
                whole_spec((rows, width)),
            ],
            scratch_shapes=[pltpu.VMEM((rows, lanes), F32)] * 3,
        ),
        out_shape=[
            jax.ShapeDtypeStruct((rows, vocab), F32),
            jax.ShapeDtypeStruct((8, rows), F32),
            jax.ShapeDtypeStruct((rows, width), BF16),
        ],
        compiler_params=params(VMEM_MIB),
        cost_estimate=cost(
            flops=2 * rows * width * vocab,
            bytes_accessed=(2 * width + 6 * rows) * vocab,
            transcendentals=rows * vocab,
        ),
        name="head_logits",
    )(where, *finals, w_unit, counts)


def head_grads_kernel(denom, halves, chunks, tables, ties, where, *refs):
    refs = refs[ties:]
    stats, refs = refs[:tables], refs[tables:]
    lengths, logits, counts, w_unit, normed, *parts, results, grad, shift, total, normed_t = refs
    step = pl.program_id(0)

    @pl.when(step == 0)
    def _():
        values = [ref[...] for ref in stats]
        top = values[0][0:1, :]
        for table in values[1:]:
            top = jnp.maximum(top, table[0:1, :])
        mass = sum(table[1:2, :] * jnp.exp(table[0:1, :] - top) for table in values)
        target = sum(table[2:3, :] for table in values)
        lse = top + jnp.log(mass)
        moved = lse - jnp.log(lengths[...] * (1.0 / denom))
        shift[...] = as_columns(moved)
        results[...] = row_table([moved, lengths[...] * lse - target])
        normed_t[...] = normed[...].astype(F32).T.astype(BF16)
        total[...] = jnp.zeros_like(total)

    columns = []
    for start, size in pieces_of(w_unit.shape[1]):
        exped = jnp.exp(logits[:, start : start + size] - shift[:, 0:1])
        counted = counts[:, start : start + size].astype(F32) * (1.0 / denom)
        columns.append((exped - counted).astype(BF16))
    dlogits = jnp.concatenate(columns, axis=1)
    total[...] += dot_t(dlogits, w_unit[...])
    grad[...] = dot(normed_t[...], dlogits).astype(BF16)

    @pl.when(step == pl.num_programs(0) - 1)
    def _():
        half = total.shape[0] // (chunks * halves)
        for at in range(chunks):
            base = at * halves * half
            if halves == 2:
                mine, theirs = base + where[1] * half, base + (1 - where[1]) * half
                out = parts[chunks + at]
                out[...] = total[pl.ds(pl.multiple_of(theirs, half), half), :].astype(out.dtype)
                parts[at][...] = total[pl.ds(pl.multiple_of(mine, half), half), :]
            else:
                parts[at][...] = total[base : base + half, :]


def head_grads(where, halves, chunks, stats, lengths, logits, counts, w_unit, normed, denom, ties):
    rows, vocab = logits.shape
    width = w_unit.shape[0]
    tile = tile_of(vocab, 640)
    part = (rows // (halves * chunks), width)
    shapes = [(part, F32)] * chunks + [(part, BF16)] * (chunks * (halves - 1))
    shapes += [((8, rows), F32)]
    return pl.pallas_call(
        functools.partial(head_grads_kernel, denom, halves, chunks, len(stats), len(ties)),
        grid_spec=pltpu.PrefetchScalarGridSpec(
            num_scalar_prefetch=1,
            grid=(vocab // tile,),
            in_specs=[
                *[pl.BlockSpec(memory_space=pl.ANY)] * len(ties),
                *[whole_spec((8, rows))] * len(stats),
                whole_spec((1, rows)),
                pl.BlockSpec((rows, tile), lambda t, s: (0, t)),
                pl.BlockSpec((rows, tile), lambda t, s: (0, t)),
                pl.BlockSpec((width, tile), lambda t, s: (0, t)),
                whole_spec((rows, width)),
            ],
            out_specs=[whole_spec(shape) for shape, _ in shapes]
            + [pl.BlockSpec((width, tile), lambda t, s: (0, t))],
            scratch_shapes=[
                pltpu.VMEM((rows, 128), F32),
                pltpu.VMEM((rows, width), F32),
                pltpu.VMEM((width, rows), BF16),
            ],
        ),
        out_shape=[jax.ShapeDtypeStruct(*shape) for shape in shapes]
        + [jax.ShapeDtypeStruct((width, vocab), BF16)],
        compiler_params=params(VMEM_MIB),
        cost_estimate=cost(
            flops=2 * rows * width * vocab,
            bytes_accessed=(2 * width + 6 * rows) * vocab,
            transcendentals=rows * vocab,
        ),
        name="head_grads",
    )(where, *ties, *stats, lengths, logits, counts, w_unit, normed)


def row_copies(sources, parts, me, dp_size, target, sems):
    copies = []
    base = 0
    for at, (slot, selected) in enumerate(parts):
        ref = sources[slot]
        if selected is not None:
            side, distance = selected
            ref = ref.at[side, lax.rem(me + distance, dp_size)]
        count = ref.shape[0]
        copies.append(
            pltpu.make_async_copy(ref, target.at[pl.ds(base, count), :], sems.at[at])
        )
        base += count
    return copies


def weight_kernel(x_parts, g_parts, sources, adding, share, dp_size, where, *refs):
    arrays, refs = refs[:sources], refs[sources:]
    w_in, w_out, refs = refs[0], refs[1], refs[2:]
    if adding:
        old_first, old_second, refs = refs[0], refs[1], refs[2:]
    first, second, normed, grads, normed_t, grads_t, x_sems, g_sems = refs

    @pl.when(pl.program_id(0) == 0)
    def _():
        columns = pl.ds(pl.multiple_of(where[0] * share, share), share)
        x_copies = row_copies(arrays, x_parts, where[0], dp_size, normed, x_sems)
        g_copies = row_copies(arrays, g_parts, where[0], dp_size, grads, g_sems)
        for copy in x_copies + g_copies:
            copy.start()
        for copy in x_copies:
            copy.wait()
        normed[...] = normalised(normed[...])
        normed_t[...] = normed[:, columns].astype(F32).T.astype(BF16)
        for copy in g_copies:
            copy.wait()
        grads_t[...] = grads[:, columns].astype(F32).T.astype(BF16)

    for at, size in pieces_of(w_in.shape[1]):
        value, slope = gelu_parts(dot(normed[...], w_in[:, at : at + size]))
        dpre = dot_t(grads[...], w_out[at : at + size, :]).astype(BF16) * slope
        now_first = dot(normed_t[...], dpre)
        now_second = dot(grads_t[...], value).T
        if adding:
            now_first = old_first[:, at : at + size] + now_first
            now_second = old_second[at : at + size, :] + now_second
        first[:, at : at + size] = now_first
        second[at : at + size, :] = now_second


def weight_grads(where, x_parts, g_parts, w_in, w_out, old, share):
    width, hidden = w_in.shape
    tile = tile_of(hidden, 512)
    arrays, rows = [], 0
    slots = []
    for parts in (x_parts, g_parts):
        placed = []
        for array, selected in parts:
            known = [at for at, other in enumerate(arrays) if other is array]
            if not known:
                arrays.append(array)
            placed.append((known[0] if known else len(arrays) - 1, selected))
        slots.append(tuple(placed))
    rows = sum(array.shape[-2] for array, _ in x_parts)
    dp_size = width // share
    hbm = pl.BlockSpec(memory_space=pl.ANY)
    in_specs = [hbm] * len(arrays) + [
        pl.BlockSpec((width, tile), lambda j, s: (0, j)),
        pl.BlockSpec((tile, width), lambda j, s: (j, 0)),
    ]
    grad_specs = [
        pl.BlockSpec((share, tile), lambda j, s: (0, j)),
        pl.BlockSpec((tile, share), lambda j, s: (j, 0)),
    ]
    adding = old is not None
    aliases = {}
    if adding:
        in_specs += grad_specs
        aliases = {len(arrays) + 3: 0, len(arrays) + 4: 1}
    return pl.pallas_call(
        functools.partial(
            weight_kernel, slots[0], slots[1], len(arrays), adding, share, dp_size
        ),
        grid_spec=pltpu.PrefetchScalarGridSpec(
            num_scalar_prefetch=1,
            grid=(hidden // tile,),
            in_specs=in_specs,
            out_specs=grad_specs,
            scratch_shapes=[
                pltpu.VMEM((rows, width), BF16),
                pltpu.VMEM((rows, width), BF16),
                pltpu.VMEM((share, rows), BF16),
                pltpu.VMEM((share, rows), BF16),
                pltpu.SemaphoreType.DMA((len(x_parts),)),
                pltpu.SemaphoreType.DMA((len(g_parts),)),
            ],
        ),
        out_shape=[
            jax.ShapeDtypeStruct((share, hidden), F32),
            jax.ShapeDtypeStruct((hidden, share), F32),
        ],
        input_output_aliases=aliases,
        compiler_params=params(VMEM_MIB),
        cost_estimate=cost(
            flops=4 * rows * (width + share) * hidden,
            bytes_accessed=4 * width * hidden + 16 * share * hidden,
            transcendentals=rows * hidden,
        ),
        name="weight_grads",
    )(where, *arrays, w_in, w_out, *(old or ()))


def unit_counts(ends, targets, ids):
    positions = jnp.arange(targets.shape[1], dtype=jnp.int32)
    row_local = jnp.sum((ends[:, None, :] <= positions[None, :, None]).astype(jnp.int32), axis=-1)
    rows = jnp.arange(ends.shape[1], dtype=jnp.int32)
    row_onehot = (row_local[:, :, None] == rows[None, None, :]).astype(BF16)
    hits = (targets[:, :, None] == ids[None, None, :]).astype(BF16)
    counts = jnp.einsum("mur,muv->mrv", row_onehot, hits, preferred_element_type=F32)
    return counts.astype(BF16)


def on_device(text_rows, durations, unit_targets, w_in, w_out, w_unit):
    micro, row_count, width = text_rows.shape
    segments = lax.axis_size("segment")
    mp_size = lax.axis_size("mp")
    dp_size = lax.axis_size("dp")
    seg = lax.axis_index("segment").astype(jnp.int32)
    mp_at = lax.axis_index("mp").astype(jnp.int32)
    dp_at = lax.axis_index("dp").astype(jnp.int32)
    last = segments - 1
    pair = mp_size == 2
    halves = 2 if pair else 1
    chunks = CHUNKS
    where = jnp.stack([seg, mp_at])
    first = w_in[0]
    second = w_out[0]
    rows = micro * row_count // chunks
    text = text_rows.reshape(chunks, rows, width)
    vocab_part = w_unit.shape[1]
    unit_count = unit_targets.shape[1]
    denom = float(micro * unit_count * dp_size)
    lengths = durations[:, 0, :]
    length_f = lengths.astype(F32).reshape(1, micro * row_count)
    ends = jnp.cumsum(lengths, axis=-1)
    own_ids = (seg * mp_size + mp_at) * vocab_part + jnp.arange(vocab_part, dtype=jnp.int32)

    counts = unit_counts(ends, unit_targets, own_ids).reshape(micro * row_count, vocab_part)

    def both(part):
        return [part, swapped(part)] if pair else [part]

    def reduced(keep, send):
        return [keep, swapped(send[0])] if pair else [lax.psum(keep, "mp")]

    def gathered_rows(mine):
        if pair:
            came = lax.all_gather(mine, ("mp", "dp"))
            return came.reshape(mp_size, dp_size, *mine.shape)
        return lax.all_gather(mine, "dp")[None]

    def all_tables(table):
        if not pair:
            return [t for t in lax.all_gather(table, ("segment", "mp"))]
        count = segments * mp_size
        return [table] + [
            lax.ppermute(table, ("segment", "mp"), [(i, (i + k) % count) for i in range(count)])
            for k in range(1, count)
        ]

    every = range(chunks)
    stash = [None] * chunks
    hops = [None] * chunks
    for stage in range(segments):
        for b in every:
            arrived = []
            if stage > 0:
                arrived = both(lax.ppermute(hops[b], "segment", [(stage - 1, stage)]))
            ties = [hops[b - 1]] if b > 0 or stage > 0 else []
            if stage == 0 and b > 0:
                ties = [*ties, counts]
            outs = forward_section(
                where, stage, halves, text, b, arrived, stash[b], first, second, ties
            )
            stash[b], keep, send = outs[:halves], outs[halves], outs[halves + 1 :]
            pieces = reduced(keep, send)
            hops[b] = total_of(pieces if pair else [stash[b][0], *pieces]).astype(BF16)
    x_gathered = [gathered_rows(held[0]) for held in stash]

    joined = jnp.concatenate(hops)
    options = [(last, joined)]
    options += [(to, lax.ppermute(joined, "segment", [(last, to)])) for to in range(last)]
    final = chosen(seg, options)
    logits, stats, normed = head_logits(where, chunks, both(final), w_unit, counts)
    *parts, result, grad_unit = head_grads(
        where,
        halves,
        chunks,
        all_tables(stats),
        length_f,
        logits,
        counts,
        w_unit,
        normed,
        denom,
        x_gathered,
    )
    loss = (jnp.sum(result[1, :]) / denom)[None]
    sum_unit = lax.psum_scatter(grad_unit, "dp", scatter_dimension=0, tiled=True)
    for b in every:
        pieces = reduced(parts[b], parts[chunks + b : chunks + b + 1])
        dnorm = tied_sum(pieces, [hops[b - 1]] if b > 0 else [])
        dnorm = total_of(
            [dnorm] + [lax.ppermute(dnorm, "segment", [(j, last)]) for j in range(last)]
        ).astype(BF16)
        half = rows // halves
        hops[b] = norm_back(final[b * half : (b + 1) * half], dnorm.astype(F32)).astype(BF16)

    grads = [[] for _ in every]
    for stage in range(last):
        owner = last - stage
        for b in every:
            came = hops[b]
            if stage > 0:
                came = lax.ppermute(came, "segment", [(owner + 1, owner)])
            ties = [] if b == 0 and stage == 0 else [hops[b - 1]]
            arrived = both(came)
            outs = backward_section(
                where, owner, stash[b], arrived, grads[b], first, second, ties
            )
            grads[b], keep, send = outs[:halves], outs[halves], outs[halves + 1 :]
            hops[b] = finish_backward(stash[b][0], came, reduced(keep, send))

    share = width // dp_size
    sums = None
    sources = [None] * chunks

    def own_parts(halves_of):
        return [(half, None) for half in halves_of]

    def other_parts(array):
        return [(array, (side, k)) for side in range(halves) for k in range(1, dp_size)]

    def weight_step(x_parts, g_parts, sums):
        return weight_grads(dp_at[None], x_parts, g_parts, first, second, sums, share)

    arrivals = [both(lax.ppermute(hop, "segment", [(1, 0)])) for hop in hops]
    for b in every:
        ties = arrived if b < chunks - 1 else []
        grads[b] = pick(where, 0, arrivals[b], grads[b], ties)
        sources[b] = gathered_rows(grads[b][0])
    for b in every:
        own = every if b == 0 else []
        x_parts = [part for at in own for part in own_parts(stash[at])]
        g_parts = [part for at in own for part in own_parts(grads[at])]
        sums = weight_step(
            x_parts + other_parts(x_gathered[b]), g_parts + other_parts(sources[b]), sums
        )
    return (loss, sums[0][None], sums[1][None], sum_unit.astype(F32))


def solution(mesh):
    placed = (
        P(None, "dp", None),
        P(None, "dp", None),
        P(None, "dp"),
        P("segment", None, "mp"),
        P("segment", "mp", None),
        P(None, ("segment", "mp")),
    )
    return jax.shard_map(
        on_device,
        mesh=mesh,
        in_specs=placed,
        out_specs=(
            P("dp"),
            P("segment", "dp", "mp"),
            P("segment", "mp", "dp"),
            P("dp", ("segment", "mp")),
        ),
        check_vma=False,
    )
```

```python
import functools
import jax
import jax.numpy as jnp
from jax import lax
from jax.experimental import pallas as pl
from jax.experimental.pallas import tpu as pltpu
from jax.sharding import PartitionSpec as P

CHUNKS = 2
VMEM_MIB = 60
COST_SCALE = 4096
BF16 = jnp.bfloat16
F32 = jnp.float32
MIB = 1024 * 1024


def shifted(block, axis, distance):
    devices = range(lax.axis_size(axis))
    route = [(i - distance, i) for i in devices if i - distance in devices]
    return lax.ppermute(block, axis, route)


def swapped(block):
    return lax.ppermute(block, "mp", [(0, 1), (1, 0)])


def gelu_parts(pre_vals):
    coeff = 0.7978845608
    pre = pre_vals.astype(BF16)
    square = pre * pre
    inner = pre * (square * BF16(coeff * 0.044715) + BF16(coeff))
    half = jnp.tanh(inner) * BF16(0.5) + BF16(0.5)
    value = pre * half
    bend = square * BF16(6.0 * coeff * 0.044715) + BF16(2.0 * coeff)
    slope = half + value * (BF16(1.0) - half) * bend
    return (value, slope)


def row_scale(rows_in):
    floats = rows_in.astype(F32)
    return lax.rsqrt(jnp.mean(floats * floats, axis=-1, keepdims=True) + 1e-06)


def normalised(rows_in):
    return (rows_in.astype(F32) * row_scale(rows_in)).astype(BF16)


def norm_back(rows_in, grads):
    scale = row_scale(rows_in)
    normal = rows_in.astype(F32) * scale
    return scale * (grads - normal * jnp.mean(grads * normal, axis=-1, keepdims=True))


def dot(a, b):
    return jnp.dot(a, b, preferred_element_type=F32)


def dot_t(a, b):
    return lax.dot_general(a, b, (((1,), (1,)), ((), ())), preferred_element_type=F32)


def t_dot(a, b):
    return lax.dot_general(a, b, (((0,), (0,)), ((), ())), preferred_element_type=F32)


def tile_of(size, most):
    if size <= most:
        return size
    return max(t for t in range(128, most + 1, 128) if size % t == 0)


def pieces_of(size):
    return [(at, min(256, size - at)) for at in range(0, size, 256)]


def cost(flops, bytes_accessed, transcendentals):
    return pl.CostEstimate(
        flops=flops // COST_SCALE,
        bytes_accessed=bytes_accessed // COST_SCALE,
        transcendentals=transcendentals // COST_SCALE,
    )


def params(limit):
    return pltpu.CompilerParams(vmem_limit_bytes=limit * MIB)


def chosen(index, candidates):
    value = candidates[0][1]
    for at, option in candidates[1:]:
        value = jnp.where(index == at, option, value)
    return value


def gathered(halves, place):
    if len(halves) == 1:
        return halves[0][...]
    mine, theirs = (half[...] for half in halves)
    first = jnp.where(place == 0, mine, theirs)
    second = jnp.where(place == 0, theirs, mine)
    return jnp.concatenate([first, second], axis=0)


def part_of(block, place, parts):
    rows = block.shape[0] // parts
    if parts == 1:
        return block[...]
    return block[pl.ds(pl.multiple_of(place * rows, rows), rows), :]


def whole_spec(shape):
    return pl.BlockSpec(shape, lambda *_: (0,) * len(shape))


def keep_live(live, arrived, before, after):
    for came, old, new in zip(arrived, before, after):
        new[...] = jnp.where(live, came[...], old[...])


def tile_copies(w_in, w_out, in_buf, out_buf, sems, tile):
    copies = []
    for at in range(w_in.shape[1] // tile):
        part = pl.ds(at * tile, tile)
        copies.append(
            (
                pltpu.make_async_copy(w_in.at[:, part], in_buf.at[:, part], sems.at[0, at]),
                pltpu.make_async_copy(w_out.at[part, :], out_buf.at[part, :], sems.at[1, at]),
            )
        )
    return copies


def emit(total, added, place, keep, send):
    if send:
        kept = part_of(total, place, 2)
        keep[...] = kept if added is None else kept + part_of(added, place, 2).astype(F32)
        send[0][...] = part_of(total, 1 - place, 2).astype(send[0].dtype)
    else:
        keep[...] = total[...]


def forward_kernel(halves, stage, ties, tile, where, *refs):
    refs = refs[ties:]
    if stage == 0:
        own, refs = refs[0], refs[1:]
    else:
        arrived, refs = refs[:halves], refs[halves:]
        before, refs = refs[:halves], refs[halves:]
    w_in, w_out, refs = refs[0], refs[1], refs[2:]
    after, refs = refs[:halves], refs[halves:]
    keep, *send, whole, normed, total, in_buf, out_buf, sems = refs
    live = where[0] == stage
    copies = tile_copies(w_in, w_out, in_buf, out_buf, sems, tile)

    @pl.when(live)
    def _():
        for pair in copies:
            for copy in pair:
                copy.start()

    if stage == 0:
        whole[...] = own[...]
        after[0][...] = part_of(whole, where[1], halves)
        if halves == 2:
            after[1][...] = part_of(whole, 1 - where[1], halves)
    else:
        whole[...] = gathered(arrived, where[1])
        keep_live(live, arrived, before, after)

    @pl.when(live)
    def _():
        normed[...] = normalised(whole[...])
        for index, pair in enumerate(copies):
            for copy in pair:
                copy.wait()
            values = []
            for at, size in pieces_of(tile):
                start = index * tile + at
                value, _ = gelu_parts(dot(normed[...], in_buf[:, start : start + size]))
                values.append(value)
            part = dot(
                jnp.concatenate(values, axis=1), out_buf[index * tile : (index + 1) * tile, :]
            )
            total[...] = part if index == 0 else total[...] + part
        emit(total, whole, where[1], keep, send)

    @pl.when(jnp.logical_not(live))
    def _():
        for ref in (keep, *send):
            ref[...] = jnp.zeros_like(ref)


def section_call(body, name, where, ties, operands, specs, w_in, w_out, shapes, scratch, flops):
    width, hidden = w_in.shape
    tile = tile_of(hidden, 1024 if name == "section_forward" else 512)
    return pl.pallas_call(
        functools.partial(body, tile),
        grid_spec=pltpu.PrefetchScalarGridSpec(
            num_scalar_prefetch=1,
            grid=(1,),
            in_specs=[pl.BlockSpec(memory_space=pl.ANY)] * len(ties)
            + specs
            + [pl.BlockSpec(memory_space=pl.ANY)] * 2,
            out_specs=[whole_spec(shape) for shape, _ in shapes],
            scratch_shapes=scratch
            + [
                pltpu.VMEM((width, hidden), BF16),
                pltpu.VMEM((hidden, width), BF16),
                pltpu.SemaphoreType.DMA((2, hidden // tile)),
            ],
        ),
        out_shape=[jax.ShapeDtypeStruct(*shape) for shape in shapes],
        compiler_params=params(VMEM_MIB),
        cost_estimate=cost(
            flops=flops, bytes_accessed=4 * width * hidden, transcendentals=flops // 4096
        ),
        name=name,
    )(where, *ties, *operands, w_in, w_out)


def forward_section(where, stage, halves, text, at, arrived, before, w_in, w_out, ties):
    _, rows, width = text.shape
    full, part = (rows, width), (rows // halves, width)
    shapes = [(part, BF16)] * halves + [(part, F32)] + [(part, BF16)] * (halves - 1)
    if stage == 0:
        operands = [text]
        specs = [pl.BlockSpec((None, rows, width), lambda j, s: (at, 0, 0))]
    else:
        operands = [*arrived, *before]
        specs = [whole_spec(part)] * len(operands)

    def body(tile, *refs):
        forward_kernel(halves, stage, len(ties), tile, *refs)

    scratch = [pltpu.VMEM(full, BF16), pltpu.VMEM(full, BF16), pltpu.VMEM(full, F32)]
    flops = 4 * rows * width * w_in.shape[1]
    return section_call(
        body, "section_forward", where, ties, operands, specs, w_in, w_out, shapes, scratch, flops
    )


def total_of(pieces):
    total = pieces[0].astype(F32)
    for piece in pieces[1:]:
        total = total + piece.astype(F32)
    return total


def tied_sum_kernel(ties, *refs):
    refs = refs[ties:]
    total = refs[0][...].astype(F32)
    for ref in refs[1:-1]:
        total = total + ref[...].astype(F32)
    refs[-1][...] = total.astype(BF16)


def tied_sum(pieces, ties):
    if not ties:
        return total_of(pieces).astype(BF16)
    shape = pieces[0].shape
    return pl.pallas_call(
        functools.partial(tied_sum_kernel, len(ties)),
        grid=(1,),
        in_specs=[pl.BlockSpec(memory_space=pl.ANY)] * len(ties)
        + [whole_spec(shape)] * len(pieces),
        out_specs=whole_spec(shape),
        out_shape=jax.ShapeDtypeStruct(shape, BF16),
        compiler_params=params(VMEM_MIB),
        name="tied_sum",
    )(*ties, *pieces)


def finish_backward(rows, grads, pieces):
    return (grads.astype(F32) + norm_back(rows, total_of(pieces))).astype(BF16)


def backward_kernel(halves, owner, old, ties, tile, where, *refs):
    refs = refs[ties:]
    stash, refs = refs[:halves], refs[halves:]
    arrived, refs = refs[:halves], refs[halves:]
    before, refs = refs[:old], refs[old:]
    w_in, w_out, refs = refs[0], refs[1], refs[2:]
    after, refs = refs[:halves], refs[halves:]
    keep, *send, grads, normed, total, in_buf, out_buf, sems = refs
    live = where[0] == owner
    copies = tile_copies(w_in, w_out, in_buf, out_buf, sems, tile)

    @pl.when(live)
    def _():
        for pair in copies:
            for copy in pair:
                copy.start()

    keep_live(live, arrived, before if old else arrived, after)

    @pl.when(live)
    def _():
        grads[...] = gathered(arrived, where[1])
        normed[...] = normalised(gathered(stash, where[1]))
        for index, pair in enumerate(copies):
            for copy in pair:
                copy.wait()
            dpres = []
            for at, size in pieces_of(tile):
                part = slice(index * tile + at, index * tile + at + size)
                _, slope = gelu_parts(dot(normed[...], in_buf[:, part]))
                dpres.append(dot_t(grads[...], out_buf[part, :]).astype(BF16) * slope)
            part = dot_t(
                jnp.concatenate(dpres, axis=1), in_buf[:, index * tile : (index + 1) * tile]
            )
            total[...] = part if index == 0 else total[...] + part
        emit(total, None, where[1], keep, send)

    @pl.when(jnp.logical_not(live))
    def _():
        for ref in (keep, *send):
            ref[...] = jnp.zeros_like(ref)


def backward_section(where, owner, stash, arrived, before, w_in, w_out, ties):
    halves = len(stash)
    part = stash[0].shape
    full = (part[0] * halves, part[1])
    shapes = [(part, BF16)] * halves + [(part, F32)] + [(part, BF16)] * (halves - 1)
    operands = [*stash, *arrived, *before]

    def body(tile, *refs):
        backward_kernel(halves, owner, len(before), len(ties), tile, *refs)

    scratch = [pltpu.VMEM(full, BF16)] * 2 + [pltpu.VMEM(full, F32)]
    flops = 6 * full[0] * full[1] * w_in.shape[1]
    specs = [whole_spec(part)] * len(operands)
    return section_call(
        body, "section_backward", where, ties, operands, specs, w_in, w_out, shapes, scratch, flops
    )


def pick_kernel(halves, owner, ties, where, *refs):
    refs = refs[ties:]
    arrived, before, after = refs[:halves], refs[halves : 2 * halves], refs[2 * halves :]
    keep_live(where[0] == owner, arrived, before, after)


def pick(where, owner, arrived, before, ties):
    halves = len(arrived)
    part = arrived[0].shape
    return pl.pallas_call(
        functools.partial(pick_kernel, halves, owner, len(ties)),
        grid_spec=pltpu.PrefetchScalarGridSpec(
            num_scalar_prefetch=1,
            grid=(1,),
            in_specs=[pl.BlockSpec(memory_space=pl.ANY)] * len(ties)
            + [whole_spec(part)] * (2 * halves),
            out_specs=[whole_spec(part)] * halves,
        ),
        out_shape=[jax.ShapeDtypeStruct(part, BF16)] * halves,
        compiler_params=params(VMEM_MIB),
        name="pick_grads",
    )(where, *ties, *arrived, *before)


def row_table(rows):
    pad = jnp.zeros((8 - len(rows), rows[0].shape[1]), F32)
    return jnp.concatenate([*rows, pad], axis=0)


def as_row(column):
    return jnp.broadcast_to(column, (column.shape[0], 128)).T[0:1, :]


def as_columns(row):
    return jnp.broadcast_to(row, (128, row.shape[1])).T


def logits_kernel(halves, chunks, where, *refs):
    finals, refs = refs[: halves * chunks], refs[halves * chunks :]
    w_unit, counts, logits, stats, normed, peak, total, target = refs
    step = pl.program_id(0)
    lanes = peak.shape[1]

    @pl.when(step == 0)
    def _():
        rows = normed.shape[0] // chunks
        for at in range(chunks):
            final = finals[at * halves : (at + 1) * halves]
            normed[at * rows : (at + 1) * rows, :] = normalised(gathered(final, where[1]))
        peak[...] = jnp.full_like(peak, -1e30)
        total[...] = jnp.zeros_like(total)
        target[...] = jnp.zeros_like(target)

    columns = []
    for start, size in pieces_of(w_unit.shape[1]):
        values = dot(normed[...], w_unit[:, start : start + size])
        logits[:, start : start + size] = values
        counted = counts[:, start : start + size].astype(F32) * values
        columns += [
            (values[:, c : c + lanes], counted[:, c : c + lanes]) for c in range(0, size, lanes)
        ]
    higher = peak[...]
    for values, _ in columns:
        higher = jnp.maximum(higher, values)
    mass = total[...] * jnp.exp(peak[...] - higher)
    summed = target[...]
    for values, counted in columns:
        mass = mass + jnp.exp(values - higher)
        summed = summed + counted
    peak[...] = higher
    total[...] = mass
    target[...] = summed

    @pl.when(step == pl.num_programs(0) - 1)
    def _():
        top = jnp.max(peak[...], axis=-1, keepdims=True)
        mass = jnp.sum(total[...] * jnp.exp(peak[...] - top), axis=-1, keepdims=True)
        summed = jnp.sum(target[...], axis=-1, keepdims=True)
        stats[...] = row_table([as_row(top), as_row(mass), as_row(summed)])


def head_logits(where, finals, w_unit, counts):
    halves, chunks = len(finals[0]), len(finals)
    half, width = finals[0][0].shape
    rows = half * halves * chunks
    vocab = w_unit.shape[1]
    lanes = 128 if vocab % 128 == 0 else vocab
    tile = tile_of(vocab, 640)
    return pl.pallas_call(
        functools.partial(logits_kernel, halves, chunks),
        grid_spec=pltpu.PrefetchScalarGridSpec(
            num_scalar_prefetch=1,
            grid=(vocab // tile,),
            in_specs=[
                *[whole_spec((half, width))] * (halves * chunks),
                pl.BlockSpec((width, tile), lambda t, s: (0, t)),
                pl.BlockSpec((rows, tile), lambda t, s: (0, t)),
            ],
            out_specs=[
                pl.BlockSpec((rows, tile), lambda t, s: (0, t)),
                whole_spec((8, rows)),
                whole_spec((rows, width)),
            ],
            scratch_shapes=[pltpu.VMEM((rows, lanes), F32)] * 3,
        ),
        out_shape=[
            jax.ShapeDtypeStruct((rows, vocab), F32),
            jax.ShapeDtypeStruct((8, rows), F32),
            jax.ShapeDtypeStruct((rows, width), BF16),
        ],
        compiler_params=params(VMEM_MIB),
        cost_estimate=cost(
            flops=2 * rows * width * vocab,
            bytes_accessed=(2 * width + 6 * rows) * vocab,
            transcendentals=rows * vocab,
        ),
        name="head_logits",
    )(where, *[half for final in finals for half in final], w_unit, counts)


def head_grads_kernel(denom, halves, chunks, tables, ties, where, *refs):
    refs = refs[ties:]
    stats, refs = refs[:tables], refs[tables:]
    lengths, logits, counts, w_unit, normed, *parts, results, grad, shift, total, normed_t = refs
    step = pl.program_id(0)

    @pl.when(step == 0)
    def _():
        values = [ref[...] for ref in stats]
        top = values[0][0:1, :]
        for table in values[1:]:
            top = jnp.maximum(top, table[0:1, :])
        mass = sum(table[1:2, :] * jnp.exp(table[0:1, :] - top) for table in values)
        target = sum(table[2:3, :] for table in values)
        lse = top + jnp.log(mass)
        moved = lse - jnp.log(lengths[...] * (1.0 / denom))
        shift[...] = as_columns(moved)
        results[...] = row_table([moved, lengths[...] * lse - target])
        normed_t[...] = normed[...].astype(F32).T.astype(BF16)
        total[...] = jnp.zeros_like(total)

    columns = []
    for start, size in pieces_of(w_unit.shape[1]):
        exped = jnp.exp(logits[:, start : start + size] - shift[:, 0:1])
        counted = counts[:, start : start + size].astype(F32) * (1.0 / denom)
        columns.append((exped - counted).astype(BF16))
    dlogits = jnp.concatenate(columns, axis=1)
    total[...] += dot_t(dlogits, w_unit[...])
    grad[...] = dot(normed_t[...], dlogits).astype(BF16)

    @pl.when(step == pl.num_programs(0) - 1)
    def _():
        half = total.shape[0] // (chunks * halves)
        for at in range(chunks):
            base = at * halves * half
            if halves == 2:
                mine, theirs = base + where[1] * half, base + (1 - where[1]) * half
                out = parts[chunks + at]
                out[...] = total[pl.ds(pl.multiple_of(theirs, half), half), :].astype(out.dtype)
                parts[at][...] = total[pl.ds(pl.multiple_of(mine, half), half), :]
            else:
                parts[at][...] = total[base : base + half, :]


def head_grads(where, halves, chunks, stats, lengths, logits, counts, w_unit, normed, denom, ties):
    rows, vocab = logits.shape
    width = w_unit.shape[0]
    tile = tile_of(vocab, 640)
    part = (rows // (halves * chunks), width)
    shapes = [(part, F32)] * chunks + [(part, BF16)] * (chunks * (halves - 1))
    shapes += [((8, rows), F32)]
    return pl.pallas_call(
        functools.partial(head_grads_kernel, denom, halves, chunks, len(stats), len(ties)),
        grid_spec=pltpu.PrefetchScalarGridSpec(
            num_scalar_prefetch=1,
            grid=(vocab // tile,),
            in_specs=[
                *[pl.BlockSpec(memory_space=pl.ANY)] * len(ties),
                *[whole_spec((8, rows))] * len(stats),
                whole_spec((1, rows)),
                pl.BlockSpec((rows, tile), lambda t, s: (0, t)),
                pl.BlockSpec((rows, tile), lambda t, s: (0, t)),
                pl.BlockSpec((width, tile), lambda t, s: (0, t)),
                whole_spec((rows, width)),
            ],
            out_specs=[whole_spec(shape) for shape, _ in shapes]
            + [pl.BlockSpec((width, tile), lambda t, s: (0, t))],
            scratch_shapes=[
                pltpu.VMEM((rows, 128), F32),
                pltpu.VMEM((rows, width), F32),
                pltpu.VMEM((width, rows), BF16),
            ],
        ),
        out_shape=[jax.ShapeDtypeStruct(*shape) for shape in shapes]
        + [jax.ShapeDtypeStruct((width, vocab), BF16)],
        compiler_params=params(VMEM_MIB),
        cost_estimate=cost(
            flops=2 * rows * width * vocab,
            bytes_accessed=(2 * width + 6 * rows) * vocab,
            transcendentals=rows * vocab,
        ),
        name="head_grads",
    )(where, *ties, *stats, lengths, logits, counts, w_unit, normed)


def row_copies(sources, parts, me, dp_size, target, sems):
    copies = []
    base = 0
    for at, (slot, selected) in enumerate(parts):
        ref = sources[slot]
        if selected is not None:
            side, distance, rest = selected
            ref = ref.at[(side, lax.rem(me + distance, dp_size), *rest)]
        count = ref.shape[0]
        copies.append(
            pltpu.make_async_copy(ref, target.at[pl.ds(base, count), :], sems.at[at])
        )
        base += count
    return copies


def weight_kernel(x_parts, g_parts, sources, adding, share, dp_size, where, *refs):
    arrays, refs = refs[:sources], refs[sources:]
    w_in, w_out, refs = refs[0], refs[1], refs[2:]
    if adding:
        old_first, old_second, refs = refs[0], refs[1], refs[2:]
    first, second, normed, grads, normed_t, grads_t, x_sems, g_sems = refs

    @pl.when(pl.program_id(0) == 0)
    def _():
        columns = pl.ds(pl.multiple_of(where[0] * share, share), share)
        x_copies = row_copies(arrays, x_parts, where[0], dp_size, normed, x_sems)
        g_copies = row_copies(arrays, g_parts, where[0], dp_size, grads, g_sems)
        for copy in x_copies + g_copies:
            copy.start()
        for copy in x_copies:
            copy.wait()
        normed[...] = normalised(normed[...])
        normed_t[...] = normed[:, columns].astype(F32).T.astype(BF16)
        for copy in g_copies:
            copy.wait()
        grads_t[...] = grads[:, columns].astype(F32).T.astype(BF16)

    for at, size in pieces_of(w_in.shape[1]):
        value, slope = gelu_parts(dot(normed[...], w_in[:, at : at + size]))
        dpre = dot_t(grads[...], w_out[at : at + size, :]).astype(BF16) * slope
        now_first = dot(normed_t[...], dpre)
        now_second = dot(grads_t[...], value).T
        if adding:
            now_first = old_first[:, at : at + size] + now_first
            now_second = old_second[at : at + size, :] + now_second
        first[:, at : at + size] = now_first
        second[at : at + size, :] = now_second


def weight_grads(where, x_parts, g_parts, w_in, w_out, old, share):
    width, hidden = w_in.shape
    tile = tile_of(hidden, 512)
    arrays, rows = [], 0
    slots = []
    for parts in (x_parts, g_parts):
        placed = []
        for array, selected in parts:
            known = [at for at, other in enumerate(arrays) if other is array]
            if not known:
                arrays.append(array)
            placed.append((known[0] if known else len(arrays) - 1, selected))
        slots.append(tuple(placed))
    rows = sum(array.shape[-2] for array, _ in x_parts)
    dp_size = width // share
    hbm = pl.BlockSpec(memory_space=pl.ANY)
    in_specs = [hbm] * len(arrays) + [
        pl.BlockSpec((width, tile), lambda j, s: (0, j)),
        pl.BlockSpec((tile, width), lambda j, s: (j, 0)),
    ]
    grad_specs = [
        pl.BlockSpec((share, tile), lambda j, s: (0, j)),
        pl.BlockSpec((tile, share), lambda j, s: (j, 0)),
    ]
    adding = old is not None
    aliases = {}
    if adding:
        in_specs += grad_specs
        aliases = {len(arrays) + 3: 0, len(arrays) + 4: 1}
    return pl.pallas_call(
        functools.partial(
            weight_kernel, slots[0], slots[1], len(arrays), adding, share, dp_size
        ),
        grid_spec=pltpu.PrefetchScalarGridSpec(
            num_scalar_prefetch=1,
            grid=(hidden // tile,),
            in_specs=in_specs,
            out_specs=grad_specs,
            scratch_shapes=[
                pltpu.VMEM((rows, width), BF16),
                pltpu.VMEM((rows, width), BF16),
                pltpu.VMEM((share, rows), BF16),
                pltpu.VMEM((share, rows), BF16),
                pltpu.SemaphoreType.DMA((len(x_parts),)),
                pltpu.SemaphoreType.DMA((len(g_parts),)),
            ],
        ),
        out_shape=[
            jax.ShapeDtypeStruct((share, hidden), F32),
            jax.ShapeDtypeStruct((hidden, share), F32),
        ],
        input_output_aliases=aliases,
        compiler_params=params(VMEM_MIB),
        cost_estimate=cost(
            flops=4 * rows * (width + share) * hidden,
            bytes_accessed=4 * width * hidden + 16 * share * hidden,
            transcendentals=rows * hidden,
        ),
        name="weight_grads",
    )(where, *arrays, w_in, w_out, *(old or ()))


def unit_counts(ends, targets, ids):
    positions = jnp.arange(targets.shape[1], dtype=jnp.int32)
    row_local = jnp.sum((ends[:, None, :] <= positions[None, :, None]).astype(jnp.int32), axis=-1)
    rows = jnp.arange(ends.shape[1], dtype=jnp.int32)
    row_onehot = (row_local[:, :, None] == rows[None, None, :]).astype(BF16)
    hits = (targets[:, :, None] == ids[None, None, :]).astype(BF16)
    counts = jnp.einsum("mur,muv->mrv", row_onehot, hits, preferred_element_type=F32)
    return counts.astype(BF16)


def on_device(text_rows, durations, unit_targets, w_in, w_out, w_unit):
    micro, row_count, width = text_rows.shape
    segments = lax.axis_size("segment")
    mp_size = lax.axis_size("mp")
    dp_size = lax.axis_size("dp")
    seg = lax.axis_index("segment").astype(jnp.int32)
    mp_at = lax.axis_index("mp").astype(jnp.int32)
    dp_at = lax.axis_index("dp").astype(jnp.int32)
    last = segments - 1
    pair = mp_size == 2
    halves = 2 if pair else 1
    chunks = CHUNKS
    where = jnp.stack([seg, mp_at])
    first = w_in[0]
    second = w_out[0]
    rows = micro * row_count // chunks
    text = text_rows.reshape(chunks, rows, width)
    vocab_part = w_unit.shape[1]
    unit_count = unit_targets.shape[1]
    denom = float(micro * unit_count * dp_size)
    lengths = durations[:, 0, :]
    length_f = lengths.astype(F32).reshape(1, micro * row_count)
    ends = jnp.cumsum(lengths, axis=-1)
    own_ids = (seg * mp_size + mp_at) * vocab_part + jnp.arange(vocab_part, dtype=jnp.int32)

    counts = unit_counts(ends, unit_targets, own_ids).reshape(micro * row_count, vocab_part)

    def both(part):
        return [part, swapped(part)] if pair else [part]

    def reduced(keep, send):
        return [keep, swapped(send[0])] if pair else [lax.psum(keep, "mp")]

    def gathered_rows(mine):
        if pair:
            came = lax.all_gather(mine, ("mp", "dp"))
            return came.reshape(mp_size, dp_size, *mine.shape)
        return lax.all_gather(mine, "dp")[None]

    def all_tables(table):
        if not pair:
            return [t for t in lax.all_gather(table, ("segment", "mp"))]
        count = segments * mp_size
        return [table] + [
            lax.ppermute(table, ("segment", "mp"), [(i, (i + k) % count) for i in range(count)])
            for k in range(1, count)
        ]

    every = range(chunks)
    stash = [None] * chunks
    hops = [None] * chunks
    for stage in range(segments):
        for b in every:
            arrived = []
            if stage > 0:
                arrived = both(lax.ppermute(hops[b], "segment", [(stage - 1, stage)]))
            ties = [hops[b - 1]] if b > 0 or stage > 0 else []
            if stage == 0 and b > 0:
                ties = [*ties, counts]
            outs = forward_section(
                where, stage, halves, text, b, arrived, stash[b], first, second, ties
            )
            stash[b], keep, send = outs[:halves], outs[halves], outs[halves + 1 :]
            pieces = reduced(keep, send)
            hops[b] = total_of(pieces if pair else [stash[b][0], *pieces]).astype(BF16)
    x_gathered = gathered_rows(jnp.stack([held[0] for held in stash]))

    finals = []
    for b in every:
        options = [(last, hops[b])]
        options += [
            (to, lax.ppermute(hops[b], "segment", [(last, to)])) for to in range(last)
        ]
        finals.append(both(chosen(seg, options)))
    logits, stats, normed = head_logits(where, finals, w_unit, counts)
    *parts, result, grad_unit = head_grads(
        where,
        halves,
        chunks,
        all_tables(stats),
        length_f,
        logits,
        counts,
        w_unit,
        normed,
        denom,
        [x_gathered],
    )
    loss = (jnp.sum(result[1, :]) / denom)[None]
    sum_unit = lax.psum_scatter(grad_unit, "dp", scatter_dimension=0, tiled=True)
    for b in every:
        pieces = reduced(parts[b], parts[chunks + b : chunks + b + 1])
        dnorm = tied_sum(pieces, [hops[b - 1]] if b > 0 else [])
        dnorm = total_of(
            [dnorm] + [lax.ppermute(dnorm, "segment", [(j, last)]) for j in range(last)]
        ).astype(BF16)
        hops[b] = norm_back(finals[b][0], dnorm.astype(F32)).astype(BF16)

    grads = [[] for _ in every]
    for stage in range(last):
        owner = last - stage
        for b in every:
            came = hops[b]
            if stage > 0:
                came = lax.ppermute(came, "segment", [(owner + 1, owner)])
            ties = [] if b == 0 and stage == 0 else [hops[b - 1]]
            arrived = both(came)
            outs = backward_section(
                where, owner, stash[b], arrived, grads[b], first, second, ties
            )
            grads[b], keep, send = outs[:halves], outs[halves], outs[halves + 1 :]
            hops[b] = finish_backward(stash[b][0], came, reduced(keep, send))

    share = width // dp_size
    sums = None
    sources = [None] * chunks

    def own_parts(halves_of):
        return [(half, None) for half in halves_of]

    def other_parts(array, rest):
        return [(array, (side, k, rest)) for side in range(halves) for k in range(1, dp_size)]

    def weight_step(x_parts, g_parts, sums):
        return weight_grads(dp_at[None], x_parts, g_parts, first, second, sums, share)

    arrivals = [both(lax.ppermute(hop, "segment", [(1, 0)])) for hop in hops]
    for b in every:
        ties = arrived if b < chunks - 1 else []
        grads[b] = pick(where, 0, arrivals[b], grads[b], ties)
        sources[b] = gathered_rows(grads[b][0])
    for b in every:
        own = every if b == 0 else []
        x_parts = [part for at in own for part in own_parts(stash[at])]
        g_parts = [part for at in own for part in own_parts(grads[at])]
        sums = weight_step(
            x_parts + other_parts(x_gathered, (b,)), g_parts + other_parts(sources[b], ()), sums
        )
    return (loss, sums[0][None], sums[1][None], sum_unit.astype(F32))


def solution(mesh):
    placed = (
        P(None, "dp", None),
        P(None, "dp", None),
        P(None, "dp"),
        P("segment", None, "mp"),
        P("segment", "mp", None),
        P(None, ("segment", "mp")),
    )
    return jax.shard_map(
        on_device,
        mesh=mesh,
        in_specs=placed,
        out_specs=(
            P("dp"),
            P("segment", "dp", "mp"),
            P("segment", "mp", "dp"),
            P("dp", ("segment", "mp")),
        ),
        check_vma=False,
    )
```

```python
import functools
import jax
import jax.numpy as jnp
from jax import lax
from jax.experimental import pallas as pl
from jax.experimental.pallas import tpu as pltpu
from jax.sharding import PartitionSpec as P

CHUNKS = 2
VMEM_MIB = 60
COST_SCALE = 4096
BF16 = jnp.bfloat16
F32 = jnp.float32
MIB = 1024 * 1024


def shifted(block, axis, distance):
    devices = range(lax.axis_size(axis))
    route = [(i - distance, i) for i in devices if i - distance in devices]
    return lax.ppermute(block, axis, route)


def swapped(block):
    return lax.ppermute(block, "mp", [(0, 1), (1, 0)])


def gelu_parts(pre_vals):
    coeff = 0.7978845608
    pre = pre_vals.astype(BF16)
    square = pre * pre
    inner = pre * (square * BF16(coeff * 0.044715) + BF16(coeff))
    half = jnp.tanh(inner) * BF16(0.5) + BF16(0.5)
    value = pre * half
    bend = square * BF16(6.0 * coeff * 0.044715) + BF16(2.0 * coeff)
    slope = half + value * (BF16(1.0) - half) * bend
    return (value, slope)


def row_scale(rows_in):
    floats = rows_in.astype(F32)
    return lax.rsqrt(jnp.mean(floats * floats, axis=-1, keepdims=True) + 1e-06)


def normalised(rows_in):
    return (rows_in.astype(F32) * row_scale(rows_in)).astype(BF16)


def norm_back(rows_in, grads):
    scale = row_scale(rows_in)
    normal = rows_in.astype(F32) * scale
    return scale * (grads - normal * jnp.mean(grads * normal, axis=-1, keepdims=True))


def dot(a, b):
    return jnp.dot(a, b, preferred_element_type=F32)


def dot_t(a, b):
    return lax.dot_general(a, b, (((1,), (1,)), ((), ())), preferred_element_type=F32)


def t_dot(a, b):
    return lax.dot_general(a, b, (((0,), (0,)), ((), ())), preferred_element_type=F32)


def tile_of(size, most):
    if size <= most:
        return size
    return max(t for t in range(128, most + 1, 128) if size % t == 0)


def pieces_of(size):
    return [(at, min(256, size - at)) for at in range(0, size, 256)]


def cost(flops, bytes_accessed, transcendentals):
    return pl.CostEstimate(
        flops=flops // COST_SCALE,
        bytes_accessed=bytes_accessed // COST_SCALE,
        transcendentals=transcendentals // COST_SCALE,
    )


def params(limit):
    return pltpu.CompilerParams(vmem_limit_bytes=limit * MIB)


def chosen(index, candidates):
    value = candidates[0][1]
    for at, option in candidates[1:]:
        value = jnp.where(index == at, option, value)
    return value


def gathered(halves, place):
    if len(halves) == 1:
        return halves[0][...]
    mine, theirs = (half[...] for half in halves)
    first = jnp.where(place == 0, mine, theirs)
    second = jnp.where(place == 0, theirs, mine)
    return jnp.concatenate([first, second], axis=0)


def part_of(block, place, parts):
    rows = block.shape[0] // parts
    if parts == 1:
        return block[...]
    return block[pl.ds(pl.multiple_of(place * rows, rows), rows), :]


def whole_spec(shape):
    return pl.BlockSpec(shape, lambda *_: (0,) * len(shape))


def keep_live(live, arrived, before, after):
    for came, old, new in zip(arrived, before, after):
        new[...] = jnp.where(live, came[...], old[...])


def tile_copies(w_in, w_out, in_buf, out_buf, sems, tile):
    copies = []
    for at in range(w_in.shape[1] // tile):
        part = pl.ds(at * tile, tile)
        copies.append(
            (
                pltpu.make_async_copy(w_in.at[:, part], in_buf.at[:, part], sems.at[0, at]),
                pltpu.make_async_copy(w_out.at[part, :], out_buf.at[part, :], sems.at[1, at]),
            )
        )
    return copies


def emit(total, added, place, keep, send):
    if send:
        kept = part_of(total, place, 2)
        keep[...] = kept if added is None else kept + part_of(added, place, 2).astype(F32)
        send[0][...] = part_of(total, 1 - place, 2).astype(send[0].dtype)
    else:
        keep[...] = total[...]


def forward_kernel(halves, stage, ties, tile, where, *refs):
    refs = refs[ties:]
    if stage == 0:
        own, refs = refs[0], refs[1:]
    else:
        arrived, refs = refs[:halves], refs[halves:]
        before, refs = refs[:halves], refs[halves:]
    w_in, w_out, refs = refs[0], refs[1], refs[2:]
    after, refs = refs[:halves], refs[halves:]
    keep, *send, whole, normed, total, in_buf, out_buf, sems = refs
    live = where[0] == stage
    copies = tile_copies(w_in, w_out, in_buf, out_buf, sems, tile)

    @pl.when(live)
    def _():
        for pair in copies:
            for copy in pair:
                copy.start()

    if stage == 0:
        whole[...] = own[...]
        after[0][...] = part_of(whole, where[1], halves)
        if halves == 2:
            after[1][...] = part_of(whole, 1 - where[1], halves)
    else:
        whole[...] = gathered(arrived, where[1])
        keep_live(live, arrived, before, after)

    @pl.when(live)
    def _():
        normed[...] = normalised(whole[...])
        for index, pair in enumerate(copies):
            for copy in pair:
                copy.wait()
            values = []
            for at, size in pieces_of(tile):
                start = index * tile + at
                value, _ = gelu_parts(dot(normed[...], in_buf[:, start : start + size]))
                values.append(value)
            part = dot(
                jnp.concatenate(values, axis=1), out_buf[index * tile : (index + 1) * tile, :]
            )
            total[...] = part if index == 0 else total[...] + part
        emit(total, whole, where[1], keep, send)

    @pl.when(jnp.logical_not(live))
    def _():
        for ref in (keep, *send):
            ref[...] = jnp.zeros_like(ref)


def section_call(body, name, where, ties, operands, specs, w_in, w_out, shapes, scratch, flops):
    width, hidden = w_in.shape
    tile = tile_of(hidden, 1024 if name == "section_forward" else 512)
    return pl.pallas_call(
        functools.partial(body, tile),
        grid_spec=pltpu.PrefetchScalarGridSpec(
            num_scalar_prefetch=1,
            grid=(1,),
            in_specs=[pl.BlockSpec(memory_space=pl.ANY)] * len(ties)
            + specs
            + [pl.BlockSpec(memory_space=pl.ANY)] * 2,
            out_specs=[whole_spec(shape) for shape, _ in shapes],
            scratch_shapes=scratch
            + [
                pltpu.VMEM((width, hidden), BF16),
                pltpu.VMEM((hidden, width), BF16),
                pltpu.SemaphoreType.DMA((2, hidden // tile)),
            ],
        ),
        out_shape=[jax.ShapeDtypeStruct(*shape) for shape in shapes],
        compiler_params=params(VMEM_MIB),
        cost_estimate=cost(
            flops=flops, bytes_accessed=4 * width * hidden, transcendentals=flops // 4096
        ),
        name=name,
    )(where, *ties, *operands, w_in, w_out)


def forward_section(where, stage, halves, text, at, arrived, before, w_in, w_out, ties):
    _, rows, width = text.shape
    full, part = (rows, width), (rows // halves, width)
    shapes = [(part, BF16)] * halves + [(part, F32)] + [(part, BF16)] * (halves - 1)
    if stage == 0:
        operands = [text]
        specs = [pl.BlockSpec((None, rows, width), lambda j, s: (at, 0, 0))]
    else:
        operands = [*arrived, *before]
        specs = [whole_spec(part)] * len(operands)

    def body(tile, *refs):
        forward_kernel(halves, stage, len(ties), tile, *refs)

    scratch = [pltpu.VMEM(full, BF16), pltpu.VMEM(full, BF16), pltpu.VMEM(full, F32)]
    flops = 4 * rows * width * w_in.shape[1]
    return section_call(
        body, "section_forward", where, ties, operands, specs, w_in, w_out, shapes, scratch, flops
    )


def total_of(pieces):
    total = pieces[0].astype(F32)
    for piece in pieces[1:]:
        total = total + piece.astype(F32)
    return total


def tied_sum_kernel(ties, *refs):
    refs = refs[ties:]
    total = refs[0][...].astype(F32)
    for ref in refs[1:-1]:
        total = total + ref[...].astype(F32)
    refs[-1][...] = total.astype(BF16)


def tied_sum(pieces, ties):
    if not ties:
        return total_of(pieces).astype(BF16)
    shape = pieces[0].shape
    return pl.pallas_call(
        functools.partial(tied_sum_kernel, len(ties)),
        grid=(1,),
        in_specs=[pl.BlockSpec(memory_space=pl.ANY)] * len(ties)
        + [whole_spec(shape)] * len(pieces),
        out_specs=whole_spec(shape),
        out_shape=jax.ShapeDtypeStruct(shape, BF16),
        compiler_params=params(VMEM_MIB),
        name="tied_sum",
    )(*ties, *pieces)


def finish_backward(rows, grads, pieces):
    return (grads.astype(F32) + norm_back(rows, total_of(pieces))).astype(BF16)


def backward_kernel(halves, owner, old, ties, tile, where, *refs):
    refs = refs[ties:]
    stash, refs = refs[:halves], refs[halves:]
    arrived, refs = refs[:halves], refs[halves:]
    before, refs = refs[:old], refs[old:]
    w_in, w_out, refs = refs[0], refs[1], refs[2:]
    after, refs = refs[:halves], refs[halves:]
    keep, *send, grads, normed, total, in_buf, out_buf, sems = refs
    live = where[0] == owner
    copies = tile_copies(w_in, w_out, in_buf, out_buf, sems, tile)

    @pl.when(live)
    def _():
        for pair in copies:
            for copy in pair:
                copy.start()

    keep_live(live, arrived, before if old else arrived, after)

    @pl.when(live)
    def _():
        grads[...] = gathered(arrived, where[1])
        normed[...] = normalised(gathered(stash, where[1]))
        for index, pair in enumerate(copies):
            for copy in pair:
                copy.wait()
            dpres = []
            for at, size in pieces_of(tile):
                part = slice(index * tile + at, index * tile + at + size)
                _, slope = gelu_parts(dot(normed[...], in_buf[:, part]))
                dpres.append(dot_t(grads[...], out_buf[part, :]).astype(BF16) * slope)
            part = dot_t(
                jnp.concatenate(dpres, axis=1), in_buf[:, index * tile : (index + 1) * tile]
            )
            total[...] = part if index == 0 else total[...] + part
        emit(total, None, where[1], keep, send)

    @pl.when(jnp.logical_not(live))
    def _():
        for ref in (keep, *send):
            ref[...] = jnp.zeros_like(ref)


def backward_section(where, owner, stash, arrived, before, w_in, w_out, ties):
    halves = len(stash)
    part = stash[0].shape
    full = (part[0] * halves, part[1])
    shapes = [(part, BF16)] * halves + [(part, F32)] + [(part, BF16)] * (halves - 1)
    operands = [*stash, *arrived, *before]

    def body(tile, *refs):
        backward_kernel(halves, owner, len(before), len(ties), tile, *refs)

    scratch = [pltpu.VMEM(full, BF16)] * 2 + [pltpu.VMEM(full, F32)]
    flops = 6 * full[0] * full[1] * w_in.shape[1]
    specs = [whole_spec(part)] * len(operands)
    return section_call(
        body, "section_backward", where, ties, operands, specs, w_in, w_out, shapes, scratch, flops
    )


def pick_kernel(halves, owner, ties, where, *refs):
    refs = refs[ties:]
    arrived, before, after = refs[:halves], refs[halves : 2 * halves], refs[2 * halves :]
    keep_live(where[0] == owner, arrived, before, after)


def pick(where, owner, arrived, before, ties):
    halves = len(arrived)
    part = arrived[0].shape
    return pl.pallas_call(
        functools.partial(pick_kernel, halves, owner, len(ties)),
        grid_spec=pltpu.PrefetchScalarGridSpec(
            num_scalar_prefetch=1,
            grid=(1,),
            in_specs=[pl.BlockSpec(memory_space=pl.ANY)] * len(ties)
            + [whole_spec(part)] * (2 * halves),
            out_specs=[whole_spec(part)] * halves,
        ),
        out_shape=[jax.ShapeDtypeStruct(part, BF16)] * halves,
        compiler_params=params(VMEM_MIB),
        name="pick_grads",
    )(where, *ties, *arrived, *before)


def row_table(rows):
    pad = jnp.zeros((8 - len(rows), rows[0].shape[1]), F32)
    return jnp.concatenate([*rows, pad], axis=0)


def as_row(column):
    return jnp.broadcast_to(column, (column.shape[0], 128)).T[0:1, :]


def as_columns(row):
    return jnp.broadcast_to(row, (128, row.shape[1])).T


def logits_kernel(halves, chunks, where, *refs):
    finals, refs = refs[: halves * chunks], refs[halves * chunks :]
    w_unit, counts, logits, stats, normed, peak, total, target = refs
    step = pl.program_id(0)
    lanes = peak.shape[1]

    @pl.when(step == 0)
    def _():
        rows = normed.shape[0] // chunks
        for at in range(chunks):
            final = finals[at * halves : (at + 1) * halves]
            normed[at * rows : (at + 1) * rows, :] = normalised(gathered(final, where[1]))
        peak[...] = jnp.full_like(peak, -1e30)
        total[...] = jnp.zeros_like(total)
        target[...] = jnp.zeros_like(target)

    columns = []
    for start, size in pieces_of(w_unit.shape[1]):
        values = dot(normed[...], w_unit[:, start : start + size])
        logits[:, start : start + size] = values
        counted = counts[:, start : start + size].astype(F32) * values
        columns += [
            (values[:, c : c + lanes], counted[:, c : c + lanes]) for c in range(0, size, lanes)
        ]
    higher = peak[...]
    for values, _ in columns:
        higher = jnp.maximum(higher, values)
    mass = total[...] * jnp.exp(peak[...] - higher)
    summed = target[...]
    for values, counted in columns:
        mass = mass + jnp.exp(values - higher)
        summed = summed + counted
    peak[...] = higher
    total[...] = mass
    target[...] = summed

    @pl.when(step == pl.num_programs(0) - 1)
    def _():
        top = jnp.max(peak[...], axis=-1, keepdims=True)
        mass = jnp.sum(total[...] * jnp.exp(peak[...] - top), axis=-1, keepdims=True)
        summed = jnp.sum(target[...], axis=-1, keepdims=True)
        stats[...] = row_table([as_row(top), as_row(mass), as_row(summed)])


def head_logits(where, finals, w_unit, counts):
    halves, chunks = len(finals[0]), len(finals)
    half, width = finals[0][0].shape
    rows = half * halves * chunks
    vocab = w_unit.shape[1]
    lanes = 128 if vocab % 128 == 0 else vocab
    tile = tile_of(vocab, 640)
    return pl.pallas_call(
        functools.partial(logits_kernel, halves, chunks),
        grid_spec=pltpu.PrefetchScalarGridSpec(
            num_scalar_prefetch=1,
            grid=(vocab // tile,),
            in_specs=[
                *[whole_spec((half, width))] * (halves * chunks),
                pl.BlockSpec((width, tile), lambda t, s: (0, t)),
                pl.BlockSpec((rows, tile), lambda t, s: (0, t)),
            ],
            out_specs=[
                pl.BlockSpec((rows, tile), lambda t, s: (0, t)),
                whole_spec((8, rows)),
                whole_spec((rows, width)),
            ],
            scratch_shapes=[pltpu.VMEM((rows, lanes), F32)] * 3,
        ),
        out_shape=[
            jax.ShapeDtypeStruct((rows, vocab), F32),
            jax.ShapeDtypeStruct((8, rows), F32),
            jax.ShapeDtypeStruct((rows, width), BF16),
        ],
        compiler_params=params(VMEM_MIB),
        cost_estimate=cost(
            flops=2 * rows * width * vocab,
            bytes_accessed=(2 * width + 6 * rows) * vocab,
            transcendentals=rows * vocab,
        ),
        name="head_logits",
    )(where, *[half for final in finals for half in final], w_unit, counts)


def head_grads_kernel(denom, halves, chunks, tables, ties, where, *refs):
    refs = refs[ties:]
    stats, refs = refs[:tables], refs[tables:]
    lengths, logits, counts, w_unit, normed, *parts, results, grad, shift, total, normed_t = refs
    step = pl.program_id(0)

    @pl.when(step == 0)
    def _():
        values = [ref[...] for ref in stats]
        top = values[0][0:1, :]
        for table in values[1:]:
            top = jnp.maximum(top, table[0:1, :])
        mass = sum(table[1:2, :] * jnp.exp(table[0:1, :] - top) for table in values)
        target = sum(table[2:3, :] for table in values)
        lse = top + jnp.log(mass)
        moved = lse - jnp.log(lengths[...] * (1.0 / denom))
        shift[...] = as_columns(moved)
        results[...] = row_table([moved, lengths[...] * lse - target])
        normed_t[...] = normed[...].astype(F32).T.astype(BF16)
        total[...] = jnp.zeros_like(total)

    columns = []
    for start, size in pieces_of(w_unit.shape[1]):
        exped = jnp.exp(logits[:, start : start + size] - shift[:, 0:1])
        counted = counts[:, start : start + size].astype(F32) * (1.0 / denom)
        columns.append((exped - counted).astype(BF16))
    dlogits = jnp.concatenate(columns, axis=1)
    total[...] += dot_t(dlogits, w_unit[...])
    grad[...] = dot(normed_t[...], dlogits).astype(BF16)

    @pl.when(step == pl.num_programs(0) - 1)
    def _():
        half = total.shape[0] // (chunks * halves)
        for at in range(chunks):
            base = at * halves * half
            if halves == 2:
                mine, theirs = base + where[1] * half, base + (1 - where[1]) * half
                out = parts[chunks + at]
                out[...] = total[pl.ds(pl.multiple_of(theirs, half), half), :].astype(out.dtype)
                parts[at][...] = total[pl.ds(pl.multiple_of(mine, half), half), :]
            else:
                parts[at][...] = total[base : base + half, :]


def head_grads(where, halves, chunks, stats, lengths, logits, counts, w_unit, normed, denom, ties):
    rows, vocab = logits.shape
    width = w_unit.shape[0]
    tile = tile_of(vocab, 640)
    part = (rows // (halves * chunks), width)
    shapes = [(part, F32)] * chunks + [(part, BF16)] * (chunks * (halves - 1))
    shapes += [((8, rows), F32)]
    return pl.pallas_call(
        functools.partial(head_grads_kernel, denom, halves, chunks, len(stats), len(ties)),
        grid_spec=pltpu.PrefetchScalarGridSpec(
            num_scalar_prefetch=1,
            grid=(vocab // tile,),
            in_specs=[
                *[pl.BlockSpec(memory_space=pl.ANY)] * len(ties),
                *[whole_spec((8, rows))] * len(stats),
                whole_spec((1, rows)),
                pl.BlockSpec((rows, tile), lambda t, s: (0, t)),
                pl.BlockSpec((rows, tile), lambda t, s: (0, t)),
                pl.BlockSpec((width, tile), lambda t, s: (0, t)),
                whole_spec((rows, width)),
            ],
            out_specs=[whole_spec(shape) for shape, _ in shapes]
            + [pl.BlockSpec((width, tile), lambda t, s: (0, t))],
            scratch_shapes=[
                pltpu.VMEM((rows, 128), F32),
                pltpu.VMEM((rows, width), F32),
                pltpu.VMEM((width, rows), BF16),
            ],
        ),
        out_shape=[jax.ShapeDtypeStruct(*shape) for shape in shapes]
        + [jax.ShapeDtypeStruct((width, vocab), BF16)],
        compiler_params=params(VMEM_MIB),
        cost_estimate=cost(
            flops=2 * rows * width * vocab,
            bytes_accessed=(2 * width + 6 * rows) * vocab,
            transcendentals=rows * vocab,
        ),
        name="head_grads",
    )(where, *ties, *stats, lengths, logits, counts, w_unit, normed)


def row_copies(sources, parts, me, dp_size, target, sems):
    copies = []
    base = 0
    for at, (slot, selected) in enumerate(parts):
        ref = sources[slot]
        if selected is not None:
            side, distance, rest = selected
            ref = ref.at[(side, lax.rem(me + distance, dp_size), *rest)]
        count = ref.shape[0]
        copies.append(
            pltpu.make_async_copy(ref, target.at[pl.ds(base, count), :], sems.at[at])
        )
        base += count
    return copies


def weight_kernel(x_parts, g_parts, sources, adding, share, dp_size, where, *refs):
    arrays, refs = refs[:sources], refs[sources:]
    w_in, w_out, refs = refs[0], refs[1], refs[2:]
    if adding:
        old_first, old_second, refs = refs[0], refs[1], refs[2:]
    first, second, normed, grads, normed_t, grads_t, x_sems, g_sems = refs

    @pl.when(pl.program_id(0) == 0)
    def _():
        columns = pl.ds(pl.multiple_of(where[0] * share, share), share)
        x_copies = row_copies(arrays, x_parts, where[0], dp_size, normed, x_sems)
        g_copies = row_copies(arrays, g_parts, where[0], dp_size, grads, g_sems)
        for copy in x_copies + g_copies:
            copy.start()
        for copy in x_copies:
            copy.wait()
        normed[...] = normalised(normed[...])
        normed_t[...] = normed[:, columns].astype(F32).T.astype(BF16)
        for copy in g_copies:
            copy.wait()
        grads_t[...] = grads[:, columns].astype(F32).T.astype(BF16)

    for at, size in pieces_of(w_in.shape[1]):
        value, slope = gelu_parts(dot(normed[...], w_in[:, at : at + size]))
        dpre = dot_t(grads[...], w_out[at : at + size, :]).astype(BF16) * slope
        now_first = dot(normed_t[...], dpre)
        now_second = dot(grads_t[...], value).T
        if adding:
            now_first = old_first[:, at : at + size] + now_first
            now_second = old_second[at : at + size, :] + now_second
        first[:, at : at + size] = now_first
        second[at : at + size, :] = now_second


def weight_grads(where, x_parts, g_parts, w_in, w_out, old, share):
    width, hidden = w_in.shape
    tile = tile_of(hidden, 512)
    arrays, rows = [], 0
    slots = []
    for parts in (x_parts, g_parts):
        placed = []
        for array, selected in parts:
            known = [at for at, other in enumerate(arrays) if other is array]
            if not known:
                arrays.append(array)
            placed.append((known[0] if known else len(arrays) - 1, selected))
        slots.append(tuple(placed))
    rows = sum(array.shape[-2] for array, _ in x_parts)
    dp_size = width // share
    hbm = pl.BlockSpec(memory_space=pl.ANY)
    in_specs = [hbm] * len(arrays) + [
        pl.BlockSpec((width, tile), lambda j, s: (0, j)),
        pl.BlockSpec((tile, width), lambda j, s: (j, 0)),
    ]
    grad_specs = [
        pl.BlockSpec((share, tile), lambda j, s: (0, j)),
        pl.BlockSpec((tile, share), lambda j, s: (j, 0)),
    ]
    adding = old is not None
    aliases = {}
    if adding:
        in_specs += grad_specs
        aliases = {len(arrays) + 3: 0, len(arrays) + 4: 1}
    return pl.pallas_call(
        functools.partial(
            weight_kernel, slots[0], slots[1], len(arrays), adding, share, dp_size
        ),
        grid_spec=pltpu.PrefetchScalarGridSpec(
            num_scalar_prefetch=1,
            grid=(hidden // tile,),
            in_specs=in_specs,
            out_specs=grad_specs,
            scratch_shapes=[
                pltpu.VMEM((rows, width), BF16),
                pltpu.VMEM((rows, width), BF16),
                pltpu.VMEM((share, rows), BF16),
                pltpu.VMEM((share, rows), BF16),
                pltpu.SemaphoreType.DMA((len(x_parts),)),
                pltpu.SemaphoreType.DMA((len(g_parts),)),
            ],
        ),
        out_shape=[
            jax.ShapeDtypeStruct((share, hidden), F32),
            jax.ShapeDtypeStruct((hidden, share), F32),
        ],
        input_output_aliases=aliases,
        compiler_params=params(VMEM_MIB),
        cost_estimate=cost(
            flops=4 * rows * (width + share) * hidden,
            bytes_accessed=4 * width * hidden + 16 * share * hidden,
            transcendentals=rows * hidden,
        ),
        name="weight_grads",
    )(where, *arrays, w_in, w_out, *(old or ()))


def unit_counts(ends, targets, ids):
    positions = jnp.arange(targets.shape[1], dtype=jnp.int32)
    row_local = jnp.sum((ends[:, None, :] <= positions[None, :, None]).astype(jnp.int32), axis=-1)
    rows = jnp.arange(ends.shape[1], dtype=jnp.int32)
    row_onehot = (row_local[:, :, None] == rows[None, None, :]).astype(BF16)
    hits = (targets[:, :, None] == ids[None, None, :]).astype(BF16)
    counts = jnp.einsum("mur,muv->mrv", row_onehot, hits, preferred_element_type=F32)
    return counts.astype(BF16)


def on_device(text_rows, durations, unit_targets, w_in, w_out, w_unit):
    micro, row_count, width = text_rows.shape
    segments = lax.axis_size("segment")
    mp_size = lax.axis_size("mp")
    dp_size = lax.axis_size("dp")
    seg = lax.axis_index("segment").astype(jnp.int32)
    mp_at = lax.axis_index("mp").astype(jnp.int32)
    dp_at = lax.axis_index("dp").astype(jnp.int32)
    last = segments - 1
    pair = mp_size == 2
    halves = 2 if pair else 1
    chunks = CHUNKS
    where = jnp.stack([seg, mp_at])
    first = w_in[0]
    second = w_out[0]
    rows = micro * row_count // chunks
    text = text_rows.reshape(chunks, rows, width)
    vocab_part = w_unit.shape[1]
    unit_count = unit_targets.shape[1]
    denom = float(micro * unit_count * dp_size)
    lengths = durations[:, 0, :]
    length_f = lengths.astype(F32).reshape(1, micro * row_count)
    ends = jnp.cumsum(lengths, axis=-1)
    own_ids = (seg * mp_size + mp_at) * vocab_part + jnp.arange(vocab_part, dtype=jnp.int32)

    counts = unit_counts(ends, unit_targets, own_ids).reshape(micro * row_count, vocab_part)

    def both(part):
        return [part, swapped(part)] if pair else [part]

    def reduced(keep, send):
        return [keep, swapped(send[0])] if pair else [lax.psum(keep, "mp")]

    def gathered_rows(mine):
        if pair:
            came = lax.all_gather(mine, ("mp", "dp"))
            return came.reshape(mp_size, dp_size, *mine.shape)
        return lax.all_gather(mine, "dp")[None]

    def all_tables(table):
        if not pair:
            return [t for t in lax.all_gather(table, ("segment", "mp"))]
        count = segments * mp_size
        return [table] + [
            lax.ppermute(table, ("segment", "mp"), [(i, (i + k) % count) for i in range(count)])
            for k in range(1, count)
        ]

    every = range(chunks)
    stash = [None] * chunks
    hops = [None] * chunks
    for stage in range(segments):
        for b in every:
            arrived = []
            if stage > 0:
                arrived = both(lax.ppermute(hops[b], "segment", [(stage - 1, stage)]))
            ties = [hops[b - 1]] if b > 0 or stage > 0 else []
            if stage == 0 and b > 0:
                ties = [*ties, counts]
            outs = forward_section(
                where, stage, halves, text, b, arrived, stash[b], first, second, ties
            )
            stash[b], keep, send = outs[:halves], outs[halves], outs[halves + 1 :]
            pieces = reduced(keep, send)
            hops[b] = total_of(pieces if pair else [stash[b][0], *pieces]).astype(BF16)
    x_gathered = gathered_rows(jnp.stack([held[0] for held in stash]))

    finals = []
    for b in every:
        options = [(last, hops[b])]
        options += [
            (to, lax.ppermute(hops[b], "segment", [(last, to)])) for to in range(last)
        ]
        finals.append(both(chosen(seg, options)))
    logits, stats, normed = head_logits(where, finals, w_unit, counts)
    *parts, result, grad_unit = head_grads(
        where,
        halves,
        chunks,
        all_tables(stats),
        length_f,
        logits,
        counts,
        w_unit,
        normed,
        denom,
        [x_gathered],
    )
    loss = (jnp.sum(result[1, :]) / denom)[None]
    sum_unit = lax.psum_scatter(grad_unit, "dp", scatter_dimension=0, tiled=True).astype(F32)
    for b in every:
        pieces = reduced(parts[b], parts[chunks + b : chunks + b + 1])
        dnorm = tied_sum(pieces, [hops[b - 1]] if b > 0 else [])
        dnorm = total_of(
            [dnorm] + [lax.ppermute(dnorm, "segment", [(j, last)]) for j in range(last)]
        ).astype(BF16)
        hops[b] = norm_back(finals[b][0], dnorm.astype(F32)).astype(BF16)

    grads = [[] for _ in every]
    for stage in range(last):
        owner = last - stage
        for b in every:
            came = hops[b]
            if stage > 0:
                came = lax.ppermute(came, "segment", [(owner + 1, owner)])
            ties = [] if b == 0 and stage == 0 else [hops[b - 1]]
            arrived = both(came)
            outs = backward_section(
                where, owner, stash[b], arrived, grads[b], first, second, ties
            )
            grads[b], keep, send = outs[:halves], outs[halves], outs[halves + 1 :]
            hops[b] = finish_backward(stash[b][0], came, reduced(keep, send))

    share = width // dp_size
    sums = None
    sources = [None] * chunks

    def own_parts(halves_of):
        return [(half, None) for half in halves_of]

    def other_parts(array, rest):
        return [(array, (side, k, rest)) for side in range(halves) for k in range(1, dp_size)]

    def weight_step(x_parts, g_parts, sums):
        return weight_grads(dp_at[None], x_parts, g_parts, first, second, sums, share)

    arrivals = [both(lax.ppermute(hop, "segment", [(1, 0)])) for hop in hops]
    for b in every:
        ties = [*arrived, sum_unit, loss] if b < chunks - 1 else []
        grads[b] = pick(where, 0, arrivals[b], grads[b], ties)
        sources[b] = gathered_rows(grads[b][0])
    for b in every:
        own = every if b == 0 else []
        x_parts = [part for at in own for part in own_parts(stash[at])]
        g_parts = [part for at in own for part in own_parts(grads[at])]
        sums = weight_step(
            x_parts + other_parts(x_gathered, (b,)), g_parts + other_parts(sources[b], ()), sums
        )
    return (loss, sums[0][None], sums[1][None], sum_unit)


def solution(mesh):
    placed = (
        P(None, "dp", None),
        P(None, "dp", None),
        P(None, "dp"),
        P("segment", None, "mp"),
        P("segment", "mp", None),
        P(None, ("segment", "mp")),
    )
    return jax.shard_map(
        on_device,
        mesh=mesh,
        in_specs=placed,
        out_specs=(
            P("dp"),
            P("segment", "dp", "mp"),
            P("segment", "mp", "dp"),
            P("dp", ("segment", "mp")),
        ),
        check_vma=False,
    )
```

```python
import functools
import jax
import jax.numpy as jnp
from jax import lax
from jax.experimental import pallas as pl
from jax.experimental.pallas import tpu as pltpu
from jax.sharding import PartitionSpec as P

CHUNKS = 2
VMEM_MIB = 63
COST_SCALE = 4096
BF16 = jnp.bfloat16
F32 = jnp.float32
MIB = 1024 * 1024


def shifted(block, axis, distance):
    devices = range(lax.axis_size(axis))
    route = [(i - distance, i) for i in devices if i - distance in devices]
    return lax.ppermute(block, axis, route)


def swapped(block):
    return lax.ppermute(block, "mp", [(0, 1), (1, 0)])


def gelu_parts(pre_vals):
    coeff = 0.7978845608
    pre = pre_vals.astype(BF16)
    square = pre * pre
    inner = pre * (square * BF16(coeff * 0.044715) + BF16(coeff))
    half = jnp.tanh(inner) * BF16(0.5) + BF16(0.5)
    value = pre * half
    bend = square * BF16(6.0 * coeff * 0.044715) + BF16(2.0 * coeff)
    slope = half + value * (BF16(1.0) - half) * bend
    return (value, slope)


def row_scale(rows_in):
    floats = rows_in.astype(F32)
    return lax.rsqrt(jnp.mean(floats * floats, axis=-1, keepdims=True) + 1e-06)


def normalised(rows_in):
    return (rows_in.astype(F32) * row_scale(rows_in)).astype(BF16)


def norm_back(rows_in, grads):
    scale = row_scale(rows_in)
    normal = rows_in.astype(F32) * scale
    return scale * (grads - normal * jnp.mean(grads * normal, axis=-1, keepdims=True))


def dot(a, b):
    return jnp.dot(a, b, preferred_element_type=F32)


def dot_t(a, b):
    return lax.dot_general(a, b, (((1,), (1,)), ((), ())), preferred_element_type=F32)


def t_dot(a, b):
    return lax.dot_general(a, b, (((0,), (0,)), ((), ())), preferred_element_type=F32)


def tile_of(size, most):
    if size <= most:
        return size
    return max(t for t in range(128, most + 1, 128) if size % t == 0)


def pieces_of(size):
    return [(at, min(256, size - at)) for at in range(0, size, 256)]


def cost(flops, bytes_accessed, transcendentals):
    return pl.CostEstimate(
        flops=flops // COST_SCALE,
        bytes_accessed=bytes_accessed // COST_SCALE,
        transcendentals=transcendentals // COST_SCALE,
    )


def params(limit):
    return pltpu.CompilerParams(vmem_limit_bytes=limit * MIB)


def chosen(index, candidates):
    value = candidates[0][1]
    for at, option in candidates[1:]:
        value = jnp.where(index == at, option, value)
    return value


def gathered(halves, place):
    if len(halves) == 1:
        return halves[0][...]
    mine, theirs = (half[...] for half in halves)
    first = jnp.where(place == 0, mine, theirs)
    second = jnp.where(place == 0, theirs, mine)
    return jnp.concatenate([first, second], axis=0)


def part_of(block, place, parts):
    rows = block.shape[0] // parts
    if parts == 1:
        return block[...]
    return block[pl.ds(pl.multiple_of(place * rows, rows), rows), :]


def whole_spec(shape):
    return pl.BlockSpec(shape, lambda *_: (0,) * len(shape))


def keep_live(live, arrived, before, after):
    for came, old, new in zip(arrived, before, after):
        new[...] = jnp.where(live, came[...], old[...])


def tile_copies(w_in, w_out, in_buf, out_buf, sems, tile):
    copies = []
    for at in range(w_in.shape[1] // tile):
        part = pl.ds(at * tile, tile)
        copies.append(
            (
                pltpu.make_async_copy(w_in.at[:, part], in_buf.at[:, part], sems.at[0, at]),
                pltpu.make_async_copy(w_out.at[part, :], out_buf.at[part, :], sems.at[1, at]),
            )
        )
    return copies


def emit(total, added, place, keep, send):
    if send:
        kept = part_of(total, place, 2)
        keep[...] = kept if added is None else kept + part_of(added, place, 2).astype(F32)
        send[0][...] = part_of(total, 1 - place, 2).astype(send[0].dtype)
    else:
        keep[...] = total[...]


def forward_kernel(halves, stage, ties, tile, where, *refs):
    refs = refs[ties:]
    if stage == 0:
        own, refs = refs[0], refs[1:]
    else:
        arrived, refs = refs[:halves], refs[halves:]
        before, refs = refs[:halves], refs[halves:]
    w_in, w_out, refs = refs[0], refs[1], refs[2:]
    after, refs = refs[:halves], refs[halves:]
    keep, *send, whole, normed, total, in_buf, out_buf, sems = refs
    live = where[0] == stage
    copies = tile_copies(w_in, w_out, in_buf, out_buf, sems, tile)

    @pl.when(live)
    def _():
        for pair in copies:
            for copy in pair:
                copy.start()

    if stage == 0:
        whole[...] = own[...]
        after[0][...] = part_of(whole, where[1], halves)
        if halves == 2:
            after[1][...] = part_of(whole, 1 - where[1], halves)
    else:
        whole[...] = gathered(arrived, where[1])
        keep_live(live, arrived, before, after)

    @pl.when(live)
    def _():
        normed[...] = normalised(whole[...])
        for index, pair in enumerate(copies):
            for copy in pair:
                copy.wait()
            values = []
            for at, size in pieces_of(tile):
                start = index * tile + at
                value, _ = gelu_parts(dot(normed[...], in_buf[:, start : start + size]))
                values.append(value)
            part = dot(
                jnp.concatenate(values, axis=1), out_buf[index * tile : (index + 1) * tile, :]
            )
            total[...] = part if index == 0 else total[...] + part
        emit(total, whole, where[1], keep, send)

    @pl.when(jnp.logical_not(live))
    def _():
        for ref in (keep, *send):
            ref[...] = jnp.zeros_like(ref)


def section_call(body, name, where, ties, operands, specs, w_in, w_out, shapes, scratch, flops):
    width, hidden = w_in.shape
    tile = tile_of(hidden, 1024 if name == "section_forward" else 512)
    return pl.pallas_call(
        functools.partial(body, tile),
        grid_spec=pltpu.PrefetchScalarGridSpec(
            num_scalar_prefetch=1,
            grid=(1,),
            in_specs=[pl.BlockSpec(memory_space=pl.ANY)] * len(ties)
            + specs
            + [pl.BlockSpec(memory_space=pl.ANY)] * 2,
            out_specs=[whole_spec(shape) for shape, _ in shapes],
            scratch_shapes=scratch
            + [
                pltpu.VMEM((width, hidden), BF16),
                pltpu.VMEM((hidden, width), BF16),
                pltpu.SemaphoreType.DMA((2, hidden // tile)),
            ],
        ),
        out_shape=[jax.ShapeDtypeStruct(*shape) for shape in shapes],
        compiler_params=params(VMEM_MIB),
        cost_estimate=cost(
            flops=flops, bytes_accessed=4 * width * hidden, transcendentals=flops // 4096
        ),
        name=name,
    )(where, *ties, *operands, w_in, w_out)


def forward_section(where, stage, halves, text, at, arrived, before, w_in, w_out, ties):
    _, rows, width = text.shape
    full, part = (rows, width), (rows // halves, width)
    shapes = [(part, BF16)] * halves + [(part, F32)] + [(part, BF16)] * (halves - 1)
    if stage == 0:
        operands = [text]
        specs = [pl.BlockSpec((None, rows, width), lambda j, s: (at, 0, 0))]
    else:
        operands = [*arrived, *before]
        specs = [whole_spec(part)] * len(operands)

    def body(tile, *refs):
        forward_kernel(halves, stage, len(ties), tile, *refs)

    scratch = [pltpu.VMEM(full, BF16), pltpu.VMEM(full, BF16), pltpu.VMEM(full, F32)]
    flops = 4 * rows * width * w_in.shape[1]
    return section_call(
        body, "section_forward", where, ties, operands, specs, w_in, w_out, shapes, scratch, flops
    )


def total_of(pieces):
    total = pieces[0].astype(F32)
    for piece in pieces[1:]:
        total = total + piece.astype(F32)
    return total


def tied_sum_kernel(ties, *refs):
    refs = refs[ties:]
    total = refs[0][...].astype(F32)
    for ref in refs[1:-1]:
        total = total + ref[...].astype(F32)
    refs[-1][...] = total.astype(BF16)


def tied_sum(pieces, ties):
    if not ties:
        return total_of(pieces).astype(BF16)
    shape = pieces[0].shape
    return pl.pallas_call(
        functools.partial(tied_sum_kernel, len(ties)),
        grid=(1,),
        in_specs=[pl.BlockSpec(memory_space=pl.ANY)] * len(ties)
        + [whole_spec(shape)] * len(pieces),
        out_specs=whole_spec(shape),
        out_shape=jax.ShapeDtypeStruct(shape, BF16),
        compiler_params=params(VMEM_MIB),
        name="tied_sum",
    )(*ties, *pieces)


def finish_backward(rows, grads, pieces):
    return (grads.astype(F32) + norm_back(rows, total_of(pieces))).astype(BF16)


def backward_kernel(halves, owner, old, ties, tile, where, *refs):
    refs = refs[ties:]
    stash, refs = refs[:halves], refs[halves:]
    arrived, refs = refs[:halves], refs[halves:]
    before, refs = refs[:old], refs[old:]
    w_in, w_out, refs = refs[0], refs[1], refs[2:]
    after, refs = refs[:halves], refs[halves:]
    keep, *send, grads, normed, total, in_buf, out_buf, sems = refs
    live = where[0] == owner
    copies = tile_copies(w_in, w_out, in_buf, out_buf, sems, tile)

    @pl.when(live)
    def _():
        for pair in copies:
            for copy in pair:
                copy.start()

    keep_live(live, arrived, before if old else arrived, after)

    @pl.when(live)
    def _():
        grads[...] = gathered(arrived, where[1])
        normed[...] = normalised(gathered(stash, where[1]))
        for index, pair in enumerate(copies):
            for copy in pair:
                copy.wait()
            dpres = []
            for at, size in pieces_of(tile):
                part = slice(index * tile + at, index * tile + at + size)
                _, slope = gelu_parts(dot(normed[...], in_buf[:, part]))
                dpres.append(dot_t(grads[...], out_buf[part, :]).astype(BF16) * slope)
            part = dot_t(
                jnp.concatenate(dpres, axis=1), in_buf[:, index * tile : (index + 1) * tile]
            )
            total[...] = part if index == 0 else total[...] + part
        emit(total, None, where[1], keep, send)

    @pl.when(jnp.logical_not(live))
    def _():
        for ref in (keep, *send):
            ref[...] = jnp.zeros_like(ref)


def backward_section(where, owner, stash, arrived, before, w_in, w_out, ties):
    halves = len(stash)
    part = stash[0].shape
    full = (part[0] * halves, part[1])
    shapes = [(part, BF16)] * halves + [(part, F32)] + [(part, BF16)] * (halves - 1)
    operands = [*stash, *arrived, *before]

    def body(tile, *refs):
        backward_kernel(halves, owner, len(before), len(ties), tile, *refs)

    scratch = [pltpu.VMEM(full, BF16)] * 2 + [pltpu.VMEM(full, F32)]
    flops = 6 * full[0] * full[1] * w_in.shape[1]
    specs = [whole_spec(part)] * len(operands)
    return section_call(
        body, "section_backward", where, ties, operands, specs, w_in, w_out, shapes, scratch, flops
    )


def pick_kernel(halves, owner, ties, where, *refs):
    refs = refs[ties:]
    arrived, before, after = refs[:halves], refs[halves : 2 * halves], refs[2 * halves :]
    keep_live(where[0] == owner, arrived, before, after)


def pick(where, owner, arrived, before, ties):
    halves = len(arrived)
    part = arrived[0].shape
    return pl.pallas_call(
        functools.partial(pick_kernel, halves, owner, len(ties)),
        grid_spec=pltpu.PrefetchScalarGridSpec(
            num_scalar_prefetch=1,
            grid=(1,),
            in_specs=[pl.BlockSpec(memory_space=pl.ANY)] * len(ties)
            + [whole_spec(part)] * (2 * halves),
            out_specs=[whole_spec(part)] * halves,
        ),
        out_shape=[jax.ShapeDtypeStruct(part, BF16)] * halves,
        compiler_params=params(VMEM_MIB),
        name="pick_grads",
    )(where, *ties, *arrived, *before)


def row_table(rows):
    pad = jnp.zeros((8 - len(rows), rows[0].shape[1]), F32)
    return jnp.concatenate([*rows, pad], axis=0)


def as_row(column):
    return jnp.broadcast_to(column, (column.shape[0], 128)).T[0:1, :]


def as_columns(row):
    return jnp.broadcast_to(row, (128, row.shape[1])).T


def logits_kernel(halves, chunks, where, *refs):
    finals, refs = refs[: halves * chunks], refs[halves * chunks :]
    w_unit, counts, logits, stats, normed, peak, total, target = refs
    step = pl.program_id(0)
    lanes = peak.shape[1]

    @pl.when(step == 0)
    def _():
        rows = normed.shape[0] // chunks
        for at in range(chunks):
            final = finals[at * halves : (at + 1) * halves]
            normed[at * rows : (at + 1) * rows, :] = normalised(gathered(final, where[1]))
        peak[...] = jnp.full_like(peak, -1e30)
        total[...] = jnp.zeros_like(total)
        target[...] = jnp.zeros_like(target)

    columns = []
    for start, size in pieces_of(w_unit.shape[1]):
        values = dot(normed[...], w_unit[:, start : start + size])
        logits[:, start : start + size] = values
        counted = counts[:, start : start + size].astype(F32) * values
        columns += [
            (values[:, c : c + lanes], counted[:, c : c + lanes]) for c in range(0, size, lanes)
        ]
    higher = peak[...]
    for values, _ in columns:
        higher = jnp.maximum(higher, values)
    mass = total[...] * jnp.exp(peak[...] - higher)
    summed = target[...]
    for values, counted in columns:
        mass = mass + jnp.exp(values - higher)
        summed = summed + counted
    peak[...] = higher
    total[...] = mass
    target[...] = summed

    @pl.when(step == pl.num_programs(0) - 1)
    def _():
        top = jnp.max(peak[...], axis=-1, keepdims=True)
        mass = jnp.sum(total[...] * jnp.exp(peak[...] - top), axis=-1, keepdims=True)
        summed = jnp.sum(target[...], axis=-1, keepdims=True)
        stats[...] = row_table([as_row(top), as_row(mass), as_row(summed)])


def head_logits(where, finals, w_unit, counts):
    halves, chunks = len(finals[0]), len(finals)
    half, width = finals[0][0].shape
    rows = half * halves * chunks
    vocab = w_unit.shape[1]
    lanes = 128 if vocab % 128 == 0 else vocab
    tile = tile_of(vocab, 640)
    return pl.pallas_call(
        functools.partial(logits_kernel, halves, chunks),
        grid_spec=pltpu.PrefetchScalarGridSpec(
            num_scalar_prefetch=1,
            grid=(vocab // tile,),
            in_specs=[
                *[whole_spec((half, width))] * (halves * chunks),
                pl.BlockSpec((width, tile), lambda t, s: (0, t)),
                pl.BlockSpec((rows, tile), lambda t, s: (0, t)),
            ],
            out_specs=[
                pl.BlockSpec((rows, tile), lambda t, s: (0, t)),
                whole_spec((8, rows)),
                whole_spec((rows, width)),
            ],
            scratch_shapes=[pltpu.VMEM((rows, lanes), F32)] * 3,
        ),
        out_shape=[
            jax.ShapeDtypeStruct((rows, vocab), F32),
            jax.ShapeDtypeStruct((8, rows), F32),
            jax.ShapeDtypeStruct((rows, width), BF16),
        ],
        compiler_params=params(VMEM_MIB),
        cost_estimate=cost(
            flops=2 * rows * width * vocab,
            bytes_accessed=(2 * width + 6 * rows) * vocab,
            transcendentals=rows * vocab,
        ),
        name="head_logits",
    )(where, *[half for final in finals for half in final], w_unit, counts)


def head_grads_kernel(denom, halves, chunks, tables, ties, where, *refs):
    refs = refs[ties:]
    stats, refs = refs[:tables], refs[tables:]
    lengths, logits, counts, w_unit, normed, *parts, results, grad, shift, total, normed_t = refs
    step = pl.program_id(0)

    @pl.when(step == 0)
    def _():
        values = [ref[...] for ref in stats]
        top = values[0][0:1, :]
        for table in values[1:]:
            top = jnp.maximum(top, table[0:1, :])
        mass = sum(table[1:2, :] * jnp.exp(table[0:1, :] - top) for table in values)
        target = sum(table[2:3, :] for table in values)
        lse = top + jnp.log(mass)
        moved = lse - jnp.log(lengths[...] * (1.0 / denom))
        shift[...] = as_columns(moved)
        results[...] = row_table([moved, lengths[...] * lse - target])
        normed_t[...] = normed[...].astype(F32).T.astype(BF16)
        total[...] = jnp.zeros_like(total)

    columns = []
    for start, size in pieces_of(w_unit.shape[1]):
        exped = jnp.exp(logits[:, start : start + size] - shift[:, 0:1])
        counted = counts[:, start : start + size].astype(F32) * (1.0 / denom)
        columns.append((exped - counted).astype(BF16))
    dlogits = jnp.concatenate(columns, axis=1)
    total[...] += dot_t(dlogits, w_unit[...])
    grad[...] = dot(normed_t[...], dlogits).astype(BF16)

    @pl.when(step == pl.num_programs(0) - 1)
    def _():
        half = total.shape[0] // (chunks * halves)
        for at in range(chunks):
            base = at * halves * half
            if halves == 2:
                mine, theirs = base + where[1] * half, base + (1 - where[1]) * half
                out = parts[chunks + at]
                out[...] = total[pl.ds(pl.multiple_of(theirs, half), half), :].astype(out.dtype)
                parts[at][...] = total[pl.ds(pl.multiple_of(mine, half), half), :]
            else:
                parts[at][...] = total[base : base + half, :]


def head_grads(where, halves, chunks, stats, lengths, logits, counts, w_unit, normed, denom, ties):
    rows, vocab = logits.shape
    width = w_unit.shape[0]
    tile = tile_of(vocab, 640)
    part = (rows // (halves * chunks), width)
    shapes = [(part, F32)] * chunks + [(part, BF16)] * (chunks * (halves - 1))
    shapes += [((8, rows), F32)]
    return pl.pallas_call(
        functools.partial(head_grads_kernel, denom, halves, chunks, len(stats), len(ties)),
        grid_spec=pltpu.PrefetchScalarGridSpec(
            num_scalar_prefetch=1,
            grid=(vocab // tile,),
            in_specs=[
                *[pl.BlockSpec(memory_space=pl.ANY)] * len(ties),
                *[whole_spec((8, rows))] * len(stats),
                whole_spec((1, rows)),
                pl.BlockSpec((rows, tile), lambda t, s: (0, t)),
                pl.BlockSpec((rows, tile), lambda t, s: (0, t)),
                pl.BlockSpec((width, tile), lambda t, s: (0, t)),
                whole_spec((rows, width)),
            ],
            out_specs=[whole_spec(shape) for shape, _ in shapes]
            + [pl.BlockSpec((width, tile), lambda t, s: (0, t))],
            scratch_shapes=[
                pltpu.VMEM((rows, 128), F32),
                pltpu.VMEM((rows, width), F32),
                pltpu.VMEM((width, rows), BF16),
            ],
        ),
        out_shape=[jax.ShapeDtypeStruct(*shape) for shape in shapes]
        + [jax.ShapeDtypeStruct((width, vocab), BF16)],
        compiler_params=params(VMEM_MIB),
        cost_estimate=cost(
            flops=2 * rows * width * vocab,
            bytes_accessed=(2 * width + 6 * rows) * vocab,
            transcendentals=rows * vocab,
        ),
        name="head_grads",
    )(where, *ties, *stats, lengths, logits, counts, w_unit, normed)


def row_copies(sources, parts, me, dp_size, target, sems):
    copies = []
    base = 0
    for at, (slot, selected) in enumerate(parts):
        ref = sources[slot]
        if selected is not None:
            side, distance, rest = selected
            ref = ref.at[(side, lax.rem(me + distance, dp_size), *rest)]
        count = ref.shape[0]
        copies.append(
            pltpu.make_async_copy(ref, target.at[pl.ds(base, count), :], sems.at[at])
        )
        base += count
    return copies


def weight_kernel(x_parts, g_parts, sources, adding, share, dp_size, where, *refs):
    arrays, refs = refs[:sources], refs[sources:]
    w_in, w_out, refs = refs[0], refs[1], refs[2:]
    if adding:
        old_first, old_second, refs = refs[0], refs[1], refs[2:]
    first, second, normed, grads, normed_t, grads_t, x_sems, g_sems = refs

    @pl.when(pl.program_id(0) == 0)
    def _():
        columns = pl.ds(pl.multiple_of(where[0] * share, share), share)
        x_copies = row_copies(arrays, x_parts, where[0], dp_size, normed, x_sems)
        g_copies = row_copies(arrays, g_parts, where[0], dp_size, grads, g_sems)
        for copy in x_copies + g_copies:
            copy.start()
        for copy in x_copies:
            copy.wait()
        normed[...] = normalised(normed[...])
        normed_t[...] = normed[:, columns].astype(F32).T.astype(BF16)
        for copy in g_copies:
            copy.wait()
        grads_t[...] = grads[:, columns].astype(F32).T.astype(BF16)

    for at, size in pieces_of(w_in.shape[1]):
        value, slope = gelu_parts(dot(normed[...], w_in[:, at : at + size]))
        dpre = dot_t(grads[...], w_out[at : at + size, :]).astype(BF16) * slope
        now_first = dot(normed_t[...], dpre)
        now_second = dot(grads_t[...], value).T
        if adding:
            now_first = old_first[:, at : at + size] + now_first
            now_second = old_second[at : at + size, :] + now_second
        first[:, at : at + size] = now_first
        second[at : at + size, :] = now_second


def weight_grads(where, x_parts, g_parts, w_in, w_out, old, share):
    width, hidden = w_in.shape
    tile = tile_of(hidden, 512)
    arrays, rows = [], 0
    slots = []
    for parts in (x_parts, g_parts):
        placed = []
        for array, selected in parts:
            known = [at for at, other in enumerate(arrays) if other is array]
            if not known:
                arrays.append(array)
            placed.append((known[0] if known else len(arrays) - 1, selected))
        slots.append(tuple(placed))
    rows = sum(array.shape[-2] for array, _ in x_parts)
    dp_size = width // share
    hbm = pl.BlockSpec(memory_space=pl.ANY)
    in_specs = [hbm] * len(arrays) + [
        pl.BlockSpec((width, tile), lambda j, s: (0, j)),
        pl.BlockSpec((tile, width), lambda j, s: (j, 0)),
    ]
    grad_specs = [
        pl.BlockSpec((share, tile), lambda j, s: (0, j)),
        pl.BlockSpec((tile, share), lambda j, s: (j, 0)),
    ]
    adding = old is not None
    aliases = {}
    if adding:
        in_specs += grad_specs
        aliases = {len(arrays) + 3: 0, len(arrays) + 4: 1}
    return pl.pallas_call(
        functools.partial(
            weight_kernel, slots[0], slots[1], len(arrays), adding, share, dp_size
        ),
        grid_spec=pltpu.PrefetchScalarGridSpec(
            num_scalar_prefetch=1,
            grid=(hidden // tile,),
            in_specs=in_specs,
            out_specs=grad_specs,
            scratch_shapes=[
                pltpu.VMEM((rows, width), BF16),
                pltpu.VMEM((rows, width), BF16),
                pltpu.VMEM((share, rows), BF16),
                pltpu.VMEM((share, rows), BF16),
                pltpu.SemaphoreType.DMA((len(x_parts),)),
                pltpu.SemaphoreType.DMA((len(g_parts),)),
            ],
        ),
        out_shape=[
            jax.ShapeDtypeStruct((share, hidden), F32),
            jax.ShapeDtypeStruct((hidden, share), F32),
        ],
        input_output_aliases=aliases,
        compiler_params=params(VMEM_MIB),
        cost_estimate=cost(
            flops=4 * rows * (width + share) * hidden,
            bytes_accessed=4 * width * hidden + 16 * share * hidden,
            transcendentals=rows * hidden,
        ),
        name="weight_grads",
    )(where, *arrays, w_in, w_out, *(old or ()))


def unit_counts(ends, targets, ids):
    positions = jnp.arange(targets.shape[1], dtype=jnp.int32)
    row_local = jnp.sum((ends[:, None, :] <= positions[None, :, None]).astype(jnp.int32), axis=-1)
    rows = jnp.arange(ends.shape[1], dtype=jnp.int32)
    row_onehot = (row_local[:, :, None] == rows[None, None, :]).astype(BF16)
    hits = (targets[:, :, None] == ids[None, None, :]).astype(BF16)
    counts = jnp.einsum("mur,muv->mrv", row_onehot, hits, preferred_element_type=F32)
    return counts.astype(BF16)


def on_device(text_rows, durations, unit_targets, w_in, w_out, w_unit):
    micro, row_count, width = text_rows.shape
    segments = lax.axis_size("segment")
    mp_size = lax.axis_size("mp")
    dp_size = lax.axis_size("dp")
    seg = lax.axis_index("segment").astype(jnp.int32)
    mp_at = lax.axis_index("mp").astype(jnp.int32)
    dp_at = lax.axis_index("dp").astype(jnp.int32)
    last = segments - 1
    pair = mp_size == 2
    halves = 2 if pair else 1
    chunks = CHUNKS
    where = jnp.stack([seg, mp_at])
    first = w_in[0]
    second = w_out[0]
    rows = micro * row_count // chunks
    text = text_rows.reshape(chunks, rows, width)
    vocab_part = w_unit.shape[1]
    unit_count = unit_targets.shape[1]
    denom = float(micro * unit_count * dp_size)
    lengths = durations[:, 0, :]
    length_f = lengths.astype(F32).reshape(1, micro * row_count)
    ends = jnp.cumsum(lengths, axis=-1)
    own_ids = (seg * mp_size + mp_at) * vocab_part + jnp.arange(vocab_part, dtype=jnp.int32)

    counts = unit_counts(ends, unit_targets, own_ids).reshape(micro * row_count, vocab_part)

    def both(part):
        return [part, swapped(part)] if pair else [part]

    def reduced(keep, send):
        return [keep, swapped(send[0])] if pair else [lax.psum(keep, "mp")]

    def gathered_rows(mine):
        if pair:
            came = lax.all_gather(mine, ("mp", "dp"))
            return came.reshape(mp_size, dp_size, *mine.shape)
        return lax.all_gather(mine, "dp")[None]

    def all_tables(table):
        if not pair:
            return [t for t in lax.all_gather(table, ("segment", "mp"))]
        count = segments * mp_size
        return [table] + [
            lax.ppermute(table, ("segment", "mp"), [(i, (i + k) % count) for i in range(count)])
            for k in range(1, count)
        ]

    every = range(chunks)
    stash = [None] * chunks
    hops = [None] * chunks
    for stage in range(segments):
        for b in every:
            arrived = []
            if stage > 0:
                arrived = both(lax.ppermute(hops[b], "segment", [(stage - 1, stage)]))
            ties = [hops[b - 1]] if b > 0 or stage > 0 else []
            if stage == 0 and b > 0:
                ties = [*ties, counts]
            outs = forward_section(
                where, stage, halves, text, b, arrived, stash[b], first, second, ties
            )
            stash[b], keep, send = outs[:halves], outs[halves], outs[halves + 1 :]
            pieces = reduced(keep, send)
            hops[b] = total_of(pieces if pair else [stash[b][0], *pieces]).astype(BF16)
    x_gathered = gathered_rows(jnp.stack([held[0] for held in stash]))

    finals = []
    for b in every:
        options = [(last, hops[b])]
        options += [
            (to, lax.ppermute(hops[b], "segment", [(last, to)])) for to in range(last)
        ]
        finals.append(both(chosen(seg, options)))
    logits, stats, normed = head_logits(where, finals, w_unit, counts)
    *parts, result, grad_unit = head_grads(
        where,
        halves,
        chunks,
        all_tables(stats),
        length_f,
        logits,
        counts,
        w_unit,
        normed,
        denom,
        [x_gathered],
    )
    loss = (jnp.sum(result[1, :]) / denom)[None]
    sum_unit = lax.psum_scatter(grad_unit, "dp", scatter_dimension=0, tiled=True).astype(F32)
    for b in every:
        pieces = reduced(parts[b], parts[chunks + b : chunks + b + 1])
        dnorm = tied_sum(pieces, [hops[b - 1]] if b > 0 else [])
        dnorm = total_of(
            [dnorm] + [lax.ppermute(dnorm, "segment", [(j, last)]) for j in range(last)]
        ).astype(BF16)
        hops[b] = norm_back(finals[b][0], dnorm.astype(F32)).astype(BF16)

    grads = [[] for _ in every]
    for stage in range(last):
        owner = last - stage
        for b in every:
            came = hops[b]
            if stage > 0:
                came = lax.ppermute(came, "segment", [(owner + 1, owner)])
            ties = [] if b == 0 and stage == 0 else [hops[b - 1]]
            arrived = both(came)
            outs = backward_section(
                where, owner, stash[b], arrived, grads[b], first, second, ties
            )
            grads[b], keep, send = outs[:halves], outs[halves], outs[halves + 1 :]
            hops[b] = finish_backward(stash[b][0], came, reduced(keep, send))

    share = width // dp_size
    sums = None
    sources = [None] * chunks

    def own_parts(halves_of):
        return [(half, None) for half in halves_of]

    def other_parts(array, rest):
        return [(array, (side, k, rest)) for side in range(halves) for k in range(1, dp_size)]

    def weight_step(x_parts, g_parts, sums):
        return weight_grads(dp_at[None], x_parts, g_parts, first, second, sums, share)

    arrivals = [both(lax.ppermute(hop, "segment", [(1, 0)])) for hop in hops]
    for b in every:
        ties = [*arrived, sum_unit, loss] if b < chunks - 1 else []
        grads[b] = pick(where, 0, arrivals[b], grads[b], ties)
        sources[b] = gathered_rows(grads[b][0])
    for b in every:
        own = every if b == 0 else []
        x_parts = [part for at in own for part in own_parts(stash[at])]
        g_parts = [part for at in own for part in own_parts(grads[at])]
        sums = weight_step(
            x_parts + other_parts(x_gathered, (b,)), g_parts + other_parts(sources[b], ()), sums
        )
    return (loss, sums[0][None], sums[1][None], sum_unit)


def solution(mesh):
    placed = (
        P(None, "dp", None),
        P(None, "dp", None),
        P(None, "dp"),
        P("segment", None, "mp"),
        P("segment", "mp", None),
        P(None, ("segment", "mp")),
    )
    return jax.shard_map(
        on_device,
        mesh=mesh,
        in_specs=placed,
        out_specs=(
            P("dp"),
            P("segment", "dp", "mp"),
            P("segment", "mp", "dp"),
            P("dp", ("segment", "mp")),
        ),
        check_vma=False,
    )
```
